32 devices in a mesh: fsdp: 8 (over z, core), tp: 4 (over y, x).
Axes of the slice: x: 2, y: 2, z: 4, core: 2. Of those that a mesh axis runs over, the one named last changes fastest.
Arguments:
- momentum: float32 [1024, 16384], P('fsdp', 'tp'), may hold values from -6 to 6
- grad: bfloat16 [1024, 16384], P('fsdp', 'tp'), may hold values from -6 to 6
- q_stored: bfloat16 [256, 16384], P('fsdp', 'tp'), may hold values from -6 to 6
- perm: int32 [8], replicated, may hold values from 0 to 7, each once
Outputs:
- momentum_next: float32 [1024, 16384], P('fsdp', 'tp')
- q_next: float32 [16384, 256], P('tp')
- update: bfloat16 [1024, 16384], P('fsdp', 'tp')
The draws below stay inside these ranges and needn't reach their ends.
Inputs may be any that keep to these rules, and one draw needn't show every extreme that they name: perm names every rank block exactly once.
All inputs are finite; a program needn't handle non-finite values.
Results may differ from the reference program's by a relative error of at most 0.0008.
Values may be sent and summed in bfloat16 or wider, within the bound.
No kernel may reach another device: no remote copies, remote signals or barrier semaphores. Data moves between devices by JAX's collectives and lax.ppermute only.
A program may use at most 64 MiB of HBM per device.

```python
import math
import jax
import jax.numpy as jnp
from jax import lax

NCOL = 16384
RANK = 256
NROW = 1024
N_FSDP = 8


def shard_levels(key, dims, shards, smallest, top_value):
    def one(dim, blocks):
        heights = jax.random.uniform(jax.random.fold_in(jax.random.fold_in(key, 6), dim), (blocks,), jnp.float32, smallest / len(shards), top_value / len(shards))
        return jnp.repeat(jnp.exp(heights), dims[dim] // blocks).reshape((-1,) + (1,) * (len(dims) - dim - 1))

    loudness = one(*shards[0])
    for cut in shards[1:]:
        loudness = loudness * one(*cut)
    return loudness


def bell_draw(key, dims, spread, bound, pieces=(), held_as=jnp.bfloat16):
    drawn = jax.random.normal(key, dims, jnp.float32) * spread
    if len(pieces) > 0:
        drawn = shard_levels(key, dims, pieces, -0.22, 0.18) * drawn
    return jnp.clip(drawn, min=-bound, max=bound).astype(held_as)


def setup_inputs(seed: int = 0) -> dict:
    key_of = jax.random.split(jax.random.key(seed), 5)
    return {
        "momentum": bell_draw(key_of[0], (NROW, NCOL), 1.0, 6.0, ((0, 8), (1, 4)), jnp.float32),
        "grad": bell_draw(key_of[1], (NROW, NCOL), 1.0, 6.0, ((0, 8), (1, 4))),
        "q_stored": bell_draw(key_of[2], (RANK, NCOL), 1.0, 6.0, ((0, 8), (1, 4))),
        "perm": jax.random.permutation(key_of[3], N_FSDP).astype(jnp.int32),
    }


EPSILON = 1e-06
KEEP_SHARE = 0.5
HIGH = lax.Precision.HIGHEST

def reference(momentum, grad, q_stored, perm):
    block_rows = RANK // N_FSDP
    blocks = jnp.arange(N_FSDP, dtype=jnp.int32)
    inverse = lax.optimization_barrier(jnp.sum(jnp.where(perm[:, None] == blocks[None, :], blocks[:, None], 0), axis=0)).astype(jnp.int32)
    row_ids = jnp.arange(RANK, dtype=jnp.int32)
    order_index = (inverse[row_ids // block_rows] * block_rows + row_ids % block_rows).astype(jnp.int32)
    restored = q_stored[order_index]
    combined = momentum + grad.astype(jnp.float32)
    projected = lax.dot_general(combined, restored.astype(jnp.float32), (((1,), (1,)), ((), ())), precision=HIGH)
    gram_total = lax.dot_general(projected, projected, (((0,), (0,)), ((), ())), precision=HIGH)
    factor_low = jnp.linalg.cholesky(gram_total)
    orthonormal = jax.scipy.linalg.solve_triangular(factor_low, projected.T, lower=True).T
    right = lax.dot_general(combined, orthonormal, (((0,), (0,)), ((), ())), precision=HIGH)
    scale = lax.rsqrt(lax.optimization_barrier(jnp.mean(right * right, axis=0)) + EPSILON)
    q_next = right * scale[None, :]
    outer = lax.dot_general(orthonormal, right, (((1,), (1,)), ((), ())), precision=HIGH)
    momentum_next = combined - KEEP_SHARE * outer
    direction = lax.dot_general(orthonormal, q_next, (((1,), (1,)), ((), ())), precision=HIGH)
    update = (direction * math.sqrt(NROW / RANK)).astype(jnp.bfloat16)
    return (momentum_next, q_next, update)
```

```python
import math

import jax
import jax.numpy as jnp
from jax import lax
from jax.experimental import pallas as pl
from jax.experimental.pallas import tpu as pltpu
from jax.sharding import PartitionSpec as P

EPSILON = 1e-06
KEEP_SHARE = 0.5
HIGH = lax.Precision.HIGHEST
PANEL = 64
TILE = 8


def split_two(x):
    high = lax.reduce_precision(x, 8, 7)
    return high.astype(jnp.bfloat16), (x - high).astype(jnp.bfloat16)


def butterfly_sum(x, axis):
    n = lax.axis_size(axis)
    step = 1
    while step < n:
        x = x + lax.ppermute(x, axis, [(i, i ^ step) for i in range(n)])
        step *= 2
    return x


def gather_list(x, axis):
    n = lax.axis_size(axis)
    return [x] + [lax.ppermute(x, axis, [(i, i ^ k) for i in range(n)]) for k in range(1, n)]


def spread(row):
    return jnp.broadcast_to(row, (TILE, 2 * PANEL))


def panel_inverse(block):
    rows = lax.broadcasted_iota(jnp.int32, (PANEL, PANEL), 0)
    cols = lax.broadcasted_iota(jnp.int32, (PANEL, PANEL), 1)
    both = jnp.concatenate([block, (rows == cols).astype(jnp.float32)], axis=1)
    count = PANEL // TILE
    tiles = [both[TILE * i : TILE * (i + 1)] for i in range(count)]
    sub = lax.broadcasted_iota(jnp.int32, (TILE, 2 * PANEL), 0)
    done = []
    for k in range(count):
        columns = [
            [spread(tiles[i][:, TILE * k + j : TILE * k + j + 1]) for j in range(TILE)] for i in range(k, count)
        ]
        own, body = columns[0], tiles[k]
        final = jnp.zeros_like(body)
        for j in range(TILE):
            here = sub == j
            pivot = spread(own[j][j : j + 1])
            inverse = 1.0 / pivot
            final = jnp.where(here, body * lax.rsqrt(pivot), final)
            reduced = spread(body[j : j + 1]) * inverse
            body = jnp.where(here, reduced, body - own[j] * reduced)
            for other in range(j + 1, TILE):
                ratio = spread(own[other][j : j + 1]) * inverse
                own[other] = jnp.where(here, ratio, own[other] - own[j] * ratio)
        done.append(final)
        for i in range(k + 1, count):
            tile = tiles[i]
            for j in range(TILE):
                tile = tile - columns[i - k][j] * spread(body[j : j + 1])
            tiles[i] = tile
    return jnp.concatenate(done, axis=0)[:, PANEL:]


def factor_kernel(gram_ref, out_ref, work):
    rank = gram_ref.shape[0]
    work[:, :rank] = gram_ref[...]
    rows = lax.broadcasted_iota(jnp.int32, (rank, rank), 0)
    cols = lax.broadcasted_iota(jnp.int32, (rank, rank), 1)
    work[:, rank:] = (rows == cols).astype(jnp.float32)
    for start in range(0, rank, PANEL):
        end = start + PANEL
        inverse = panel_inverse(work[start:end, start:end])
        scaled = jnp.dot(inverse, work[start:end, :], precision=HIGH, preferred_element_type=jnp.float32)
        out_ref[start:end, :] = scaled[:, rank:]
        if end < rank:
            low = end // 128 * 128
            change = lax.dot_general(
                scaled[:, low:rank],
                scaled,
                (((0,), (0,)), ((), ())),
                precision=HIGH,
                preferred_element_type=jnp.float32,
            )
            work[end:, :] = work[end:, :] - change[end - low :, :]


def factor_inverse(gram):
    rank = gram.shape[0]
    return pl.pallas_call(
        factor_kernel,
        out_shape=jax.ShapeDtypeStruct((rank, rank), jnp.float32),
        scratch_shapes=[pltpu.VMEM((rank, 2 * rank), jnp.float32)],
        compiler_params=pltpu.CompilerParams(vmem_limit_bytes=32 * 1024 * 1024),
        cost_estimate=pl.CostEstimate(flops=6 * 2 * rank**3, bytes_accessed=2 * rank * rank * 4, transcendentals=rank),
    )(gram)


def finish_kernel(momentum_ref, grad_ref, right_ref, high_ref, low_ref, scale_ref, next_ref, basis_ref, update_ref):
    right = right_ref[...]
    basis_ref[...] = right * scale_ref[...]
    right_high = right.astype(jnp.bfloat16)
    right_low = (right - right_high.astype(jnp.float32)).astype(jnp.bfloat16)

    def times(a, b):
        return lax.dot_general(a, b, (((1,), (1,)), ((), ())), preferred_element_type=jnp.float32)

    high = high_ref[...]
    both = times(high, right_high) + (times(low_ref[...], right_high) + times(high, right_low))
    rows = momentum_ref.shape[0]
    next_ref[...] = momentum_ref[...] + grad_ref[...].astype(jnp.float32) + both[:rows]
    update_ref[...] = both[rows:].astype(jnp.bfloat16)


def finish(momentum, grad, right, factors, scale):
    rows, cols = momentum.shape
    rank = right.shape[1]
    block = min(512, cols)
    high, low = split_two(factors)
    wide = lambda: pl.BlockSpec((rows, block), lambda i: (0, i))
    tall = lambda: pl.BlockSpec((block, rank), lambda i: (i, 0))
    whole = lambda a: pl.BlockSpec(a.shape, lambda i: (0, 0))
    return pl.pallas_call(
        finish_kernel,
        grid=(cols // block,),
        in_specs=[wide(), wide(), tall(), whole(high), whole(low), whole(scale)],
        out_specs=[wide(), tall(), wide()],
        out_shape=[
            jax.ShapeDtypeStruct((rows, cols), jnp.float32),
            jax.ShapeDtypeStruct((cols, rank), jnp.float32),
            jax.ShapeDtypeStruct((rows, cols), jnp.bfloat16),
        ],
        compiler_params=pltpu.CompilerParams(vmem_limit_bytes=32 * 1024 * 1024),
        cost_estimate=pl.CostEstimate(
            flops=6 * 2 * rows * cols * rank, bytes_accessed=rows * cols * 12 + cols * rank * 8, transcendentals=0
        ),
    )(momentum, grad, right, high, low, scale)


def on_device(momentum, grad, q_stored, perm):
    block_rows = q_stored.shape[0]
    num_blocks = lax.axis_size("fsdp")
    num_cols = lax.axis_size("tp")
    rank_total = block_rows * num_blocks
    row_total = momentum.shape[0] * num_blocks
    col_total = momentum.shape[1] * num_cols
    rows = momentum.shape[0]

    combined = momentum + grad.astype(jnp.float32)
    comb_high, comb_low = split_two(combined)
    basis = lax.all_gather(q_stored, "fsdp", axis=0, tiled=True)
    stacked = lax.dot_general(
        jnp.concatenate([comb_high, comb_low], axis=0),
        basis,
        (((1,), (1,)), ((), ())),
        preferred_element_type=jnp.float32,
    )
    stored_order = stacked[:rows] + stacked[rows:]
    blocks = jnp.arange(num_blocks, dtype=jnp.int32)
    inverse = jnp.sum(jnp.where(perm[:, None] == blocks[None, :], blocks[:, None], 0), axis=0)
    row_ids = jnp.arange(rank_total, dtype=jnp.int32)
    order_index = inverse[row_ids // block_rows] * block_rows + row_ids % block_rows
    projected = butterfly_sum(jnp.take(stored_order, order_index, axis=1), "tp")

    mixed = lax.dot_general(combined, projected, (((0,), (0,)), ((), ())), precision=HIGH)
    mixed_share = lax.psum_scatter(mixed, "fsdp", scatter_dimension=0, tiled=True)

    gram_part = lax.dot_general(projected, projected, (((0,), (0,)), ((), ())), precision=HIGH)
    piece_rows = rank_total // num_cols
    piece = lax.dynamic_slice_in_dim(gram_part, lax.axis_index("tp") * piece_rows, piece_rows, axis=0)
    pieces = gather_list(butterfly_sum(piece, "fsdp"), "tp")
    gram = jnp.zeros((rank_total, rank_total), jnp.float32)
    for k, part in enumerate(pieces):
        place = (lax.axis_index("tp") ^ k) * piece_rows
        gram = lax.dynamic_update_slice_in_dim(gram, part, place, axis=0)
    inverse_low = factor_inverse(gram)

    orthonormal = lax.dot_general(projected, inverse_low, (((1,), (1,)), ((), ())), precision=HIGH)
    right_share = lax.dot_general(mixed_share, inverse_low, (((1,), (1,)), ((), ())), precision=HIGH)
    right = lax.all_gather(right_share, "fsdp", axis=0, tiled=True)
    squares = butterfly_sum(butterfly_sum(jnp.sum(right_share * right_share, axis=0, keepdims=True), "fsdp"), "tp")
    scale = lax.rsqrt(squares / col_total + EPSILON)
    factors = jnp.concatenate(
        [-KEEP_SHARE * orthonormal, math.sqrt(row_total / rank_total) * orthonormal * scale], axis=0
    )
    return tuple(finish(momentum, grad, right, factors, scale))


def solution(mesh):
    return jax.shard_map(
        on_device,
        mesh=mesh,
        in_specs=(P("fsdp", "tp"), P("fsdp", "tp"), P("fsdp", "tp"), P()),
        out_specs=(P("fsdp", "tp"), P("tp", None), P("fsdp", "tp")),
        check_vma=False,
    )
```

```python
import math

import jax
import jax.numpy as jnp
from jax import lax
from jax.experimental import pallas as pl
from jax.experimental.pallas import tpu as pltpu
from jax.sharding import PartitionSpec as P

EPSILON = 1e-06
KEEP_SHARE = 0.5
HIGH = lax.Precision.HIGHEST
PANEL = 64
TILE = 8
HEAD = 16


def split_two(x):
    high = lax.reduce_precision(x, 8, 7)
    return high.astype(jnp.bfloat16), (x - high).astype(jnp.bfloat16)


def butterfly_sum(x, axis, step=1):
    n = lax.axis_size(axis)
    while step < n:
        x = x + lax.ppermute(x, axis, [(i, i ^ step) for i in range(n)])
        step *= 2
    return x


def gather_list(x, axis):
    n = lax.axis_size(axis)
    return [x] + [lax.ppermute(x, axis, [(i, i ^ k) for i in range(n)]) for k in range(1, n)]


def spread(row):
    return jnp.broadcast_to(row, (TILE, 2 * PANEL))


def panel_inverse(block):
    rows = lax.broadcasted_iota(jnp.int32, (PANEL, PANEL), 0)
    cols = lax.broadcasted_iota(jnp.int32, (PANEL, PANEL), 1)
    both = jnp.concatenate([block, (rows == cols).astype(jnp.float32)], axis=1)
    count = PANEL // TILE
    tiles = [both[TILE * i : TILE * (i + 1)] for i in range(count)]
    sub = lax.broadcasted_iota(jnp.int32, (TILE, 2 * PANEL), 0)
    done = []
    for k in range(count):
        columns = [
            [spread(tiles[i][:, TILE * k + j : TILE * k + j + 1]) for j in range(TILE)] for i in range(k, count)
        ]
        own, body = columns[0], tiles[k]
        final = jnp.zeros_like(body)
        for j in range(TILE):
            here = sub == j
            pivot = spread(own[j][j : j + 1])
            inverse = 1.0 / pivot
            final = jnp.where(here, body * lax.rsqrt(pivot), final)
            reduced = spread(body[j : j + 1]) * inverse
            body = jnp.where(here, reduced, body - own[j] * reduced)
            for other in range(j + 1, TILE):
                ratio = spread(own[other][j : j + 1]) * inverse
                own[other] = jnp.where(here, ratio, own[other] - own[j] * ratio)
        done.append(final)
        for i in range(k + 1, count):
            tile = tiles[i]
            for j in range(TILE):
                tile = tile - columns[i - k][j] * spread(body[j : j + 1])
            tiles[i] = tile
    return jnp.concatenate(done, axis=0)[:, PANEL:]


def factor_kernel(gram_ref, out_ref, work):
    rank = gram_ref.shape[0]
    work[:, :rank] = gram_ref[...]
    rows = lax.broadcasted_iota(jnp.int32, (rank, rank), 0)
    cols = lax.broadcasted_iota(jnp.int32, (rank, rank), 1)
    work[:, rank:] = (rows == cols).astype(jnp.float32)
    for start in range(0, rank, PANEL):
        end = start + PANEL
        inverse = panel_inverse(work[start:end, start:end])
        scaled = jnp.dot(inverse, work[start:end, :], precision=HIGH, preferred_element_type=jnp.float32)
        out_ref[start:end, :] = scaled[:, rank:]
        if end < rank:
            low = end // 128 * 128
            change = lax.dot_general(
                scaled[:, low:rank],
                scaled,
                (((0,), (0,)), ((), ())),
                precision=HIGH,
                preferred_element_type=jnp.float32,
            )
            work[end:, :] = work[end:, :] - change[end - low :, :]


def factor_inverse(gram):
    rank = gram.shape[0]
    return pl.pallas_call(
        factor_kernel,
        out_shape=jax.ShapeDtypeStruct((rank, rank), jnp.float32),
        scratch_shapes=[pltpu.VMEM((rank, 2 * rank), jnp.float32)],
        compiler_params=pltpu.CompilerParams(vmem_limit_bytes=32 * 1024 * 1024),
        cost_estimate=pl.CostEstimate(flops=6 * 2 * rank**3, bytes_accessed=2 * rank * rank * 4, transcendentals=rank),
    )(gram)


def dot_rows(a, b):
    return lax.dot_general(a, b, (((1,), (1,)), ((), ())), precision=HIGH, preferred_element_type=jnp.float32)


def halves(x):
    high = x.astype(jnp.bfloat16)
    return high, (x - high.astype(jnp.float32)).astype(jnp.bfloat16)


def mix_kernel(core_ref, high_ref, low_ref, proj_ref, out_ref):
    def times(a, b):
        return lax.dot_general(a, b, (((0,), (0,)), ((), ())), preferred_element_type=jnp.float32)

    proj_high, proj_low = halves(proj_ref[...])
    high = high_ref[...]
    out_ref[...] = times(high, proj_high) + (times(low_ref[...], proj_high) + times(high, proj_low))


def mix(core, pair_high, pair_low, projected):
    rows, cols = pair_high.shape
    rank = projected.shape[1]
    block = min(512, cols // 2)
    steps = cols // 2 // block
    wide = pl.BlockSpec((rows, block), lambda i, core: (0, core[0] * steps + i))
    return pl.pallas_call(
        mix_kernel,
        grid_spec=pltpu.PrefetchScalarGridSpec(
            num_scalar_prefetch=1,
            grid=(steps,),
            in_specs=[wide, wide, pl.BlockSpec(projected.shape, lambda i, core: (0, 0))],
            out_specs=pl.BlockSpec((block, rank), lambda i, core: (i, 0)),
        ),
        out_shape=jax.ShapeDtypeStruct((cols // 2, rank), jnp.float32),
        compiler_params=pltpu.CompilerParams(vmem_limit_bytes=32 * 1024 * 1024),
        cost_estimate=pl.CostEstimate(
            flops=3 * rows * cols * rank, bytes_accessed=rows * cols * 2 + cols * rank * 2, transcendentals=0
        ),
    )(core, pair_high, pair_low, projected)


def unit_of(exponent, mantissa):
    return mantissa * jnp.exp2(exponent - 13.0)


def encode_kernel(share_ref, inverse_ref, code_ref, squares_ref):
    right = dot_rows(share_ref[...], inverse_ref[...])
    rows, rank = right.shape
    squares_ref[...] = jnp.broadcast_to(jnp.sum(right * right, axis=0, keepdims=True), squares_ref.shape)
    top = jnp.maximum(jnp.max(jnp.abs(right), axis=0, keepdims=True), 1e-30) * (1.0 / 32766.0)
    exponent = jnp.floor(jnp.log2(top))
    mantissa = jnp.floor(top * jnp.exp2(13.0 - exponent)) + 1.0
    unit = unit_of(exponent, mantissa)
    code_ref[:rows, :] = jnp.floor(right * (1.0 / unit) + 0.5).astype(jnp.int32).astype(jnp.int16)
    place = lax.broadcasted_iota(jnp.int32, (HEAD, rank), 0)
    head = jnp.where(place == 0, exponent, mantissa)
    code_ref[rows:, :] = head.astype(jnp.int32).astype(jnp.int16)


def encode(share, inverse_low):
    rows, rank = share.shape
    return pl.pallas_call(
        encode_kernel,
        out_shape=[
            jax.ShapeDtypeStruct((rows + HEAD, rank), jnp.int16),
            jax.ShapeDtypeStruct((TILE, rank), jnp.float32),
        ],
        compiler_params=pltpu.CompilerParams(vmem_limit_bytes=32 * 1024 * 1024),
        cost_estimate=pl.CostEstimate(flops=12 * rows * rank * rank, bytes_accessed=rows * rank * 6, transcendentals=0),
    )(share, inverse_low)


def finish_kernel(
    core_ref, momentum_ref, grad_ref, mine_ref, other_ref, high_ref, low_ref, scale_ref, next_ref, basis_ref, update_ref
):
    code = jnp.where(pl.program_id(0) == 0, mine_ref[...].astype(jnp.int32), other_ref[...].astype(jnp.int32))
    code = code.astype(jnp.float32)
    share = code.shape[1] - HEAD
    right = code[:, :share] * unit_of(code[:, share : share + 1], code[:, share + 1 : share + 2])
    right = right.reshape(basis_ref.shape)
    basis_ref[...] = right * scale_ref[...]
    right_high, right_low = halves(right)

    def times(a, b):
        return lax.dot_general(a, b, (((1,), (1,)), ((), ())), preferred_element_type=jnp.float32)

    high = high_ref[...]
    both = times(high, right_high) + (times(low_ref[...], right_high) + times(high, right_low))
    rows = momentum_ref.shape[0]
    next_ref[...] = momentum_ref[...] + grad_ref[...].astype(jnp.float32) + both[:rows]
    update_ref[...] = both[rows:].astype(jnp.bfloat16)


def finish(core, momentum, grad, mine, other, factors, scale):
    rows, cols = momentum.shape
    shares, share, rank = mine.shape
    share -= HEAD
    group = max(1, min(512 // share, shares))
    block, steps = group * share, shares // group
    high, low = split_two(factors)
    column = lambda a, i, core: (a ^ core[0]) * steps + i
    wide = lambda: pl.BlockSpec((rows, block), lambda a, i, core: (0, column(a, i, core)))
    tall = lambda: pl.BlockSpec((block, rank), lambda a, i, core: (column(a, i, core), 0))
    whole = lambda x: pl.BlockSpec(x.shape, lambda a, i, core: (0, 0))
    first = pl.BlockSpec((group, share + HEAD, rank), lambda a, i, core: (jnp.where(a == 0, i, steps - 1), 0, 0))
    second = pl.BlockSpec((group, share + HEAD, rank), lambda a, i, core: (jnp.where(a == 0, 0, i), 0, 0))
    return pl.pallas_call(
        finish_kernel,
        grid_spec=pltpu.PrefetchScalarGridSpec(
            num_scalar_prefetch=1,
            grid=(2, steps),
            in_specs=[wide(), wide(), first, second, whole(high), whole(low), whole(scale)],
            out_specs=[wide(), tall(), wide()],
        ),
        out_shape=[
            jax.ShapeDtypeStruct((rows, cols), jnp.float32),
            jax.ShapeDtypeStruct((cols, rank), jnp.float32),
            jax.ShapeDtypeStruct((rows, cols), jnp.bfloat16),
        ],
        compiler_params=pltpu.CompilerParams(vmem_limit_bytes=32 * 1024 * 1024),
        cost_estimate=pl.CostEstimate(
            flops=6 * 2 * rows * cols * rank, bytes_accessed=rows * cols * 12 + cols * rank * 8, transcendentals=0
        ),
    )(core, momentum, grad, mine, other, high, low, scale)


def on_device(momentum, grad, q_stored, perm):
    block_rows = q_stored.shape[0]
    num_blocks = lax.axis_size("fsdp")
    num_cols = lax.axis_size("tp")
    rank_total = block_rows * num_blocks
    row_total = momentum.shape[0] * num_blocks
    col_total = momentum.shape[1] * num_cols
    rows = momentum.shape[0]
    core = lax.axis_index("fsdp") % 2
    lines = [list(range(0, num_blocks, 2)), list(range(1, num_blocks, 2))]
    swap = lambda x: lax.ppermute(x, "fsdp", [(i, i ^ 1) for i in range(num_blocks)])

    comb_high, comb_low = split_two(momentum + grad.astype(jnp.float32))
    pair_high = jnp.concatenate([comb_high, swap(comb_high)], axis=0)
    pair_low = jnp.concatenate([comb_low, swap(comb_low)], axis=0)

    basis = lax.all_gather(q_stored, "fsdp", axis=0, tiled=True, axis_index_groups=lines)
    product = lax.dot_general(
        jnp.concatenate([pair_high, pair_low], axis=0),
        basis,
        (((1,), (1,)), ((), ())),
        preferred_element_type=jnp.float32,
    )
    mine = butterfly_sum(product[: 2 * rows] + product[2 * rows :], "tp")
    other = swap(mine)
    other = jnp.concatenate([other[rows:], other[:rows]], axis=0)
    blocks = jnp.arange(num_blocks, dtype=jnp.int32)
    inverse = jnp.sum(jnp.where(perm[:, None] == blocks[None, :], blocks[:, None], 0), axis=0)
    inverse = ((inverse % 2) ^ core) * (num_blocks // 2) + inverse // 2
    row_ids = jnp.arange(rank_total, dtype=jnp.int32)
    order_index = inverse[row_ids // block_rows] * block_rows + row_ids % block_rows
    projected = jnp.take(jnp.concatenate([mine, other], axis=1), order_index, axis=1)

    mixed = mix(core.reshape(1), pair_high, pair_low, projected)
    mixed_share = lax.psum_scatter(mixed, "fsdp", scatter_dimension=0, tiled=True, axis_index_groups=lines)

    gram_part = lax.dot_general(projected, projected, (((0,), (0,)), ((), ())), precision=HIGH)
    piece_rows = rank_total // num_cols
    piece = lax.dynamic_slice_in_dim(gram_part, lax.axis_index("tp") * piece_rows, piece_rows, axis=0)
    pieces = gather_list(butterfly_sum(piece, "fsdp", 2), "tp")
    gram = jnp.zeros((rank_total, rank_total), jnp.float32)
    for k, part in enumerate(pieces):
        place = (lax.axis_index("tp") ^ k) * piece_rows
        gram = lax.dynamic_update_slice_in_dim(gram, part, place, axis=0)
    inverse_low = factor_inverse(gram)

    orthonormal = dot_rows(projected[:rows], inverse_low)
    code, squares = encode(mixed_share, inverse_low)
    codes = lax.all_gather(code, "fsdp", axis=0, axis_index_groups=lines)
    squares = butterfly_sum(butterfly_sum(squares[:1], "fsdp"), "tp")
    scale = lax.rsqrt(squares / col_total + EPSILON)
    factors = jnp.concatenate(
        [-KEEP_SHARE * orthonormal, math.sqrt(row_total / rank_total) * orthonormal * scale], axis=0
    )
    return tuple(finish(core.reshape(1), momentum, grad, codes, swap(codes), factors, scale))


def solution(mesh):
    return jax.shard_map(
        on_device,
        mesh=mesh,
        in_specs=(P("fsdp", "tp"), P("fsdp", "tp"), P("fsdp", "tp"), P()),
        out_specs=(P("fsdp", "tp"), P("tp", None), P("fsdp", "tp")),
        check_vma=False,
    )
```

```python
import functools
import math

import jax
import jax.numpy as jnp
from jax import lax
from jax.experimental import pallas as pl
from jax.experimental.pallas import tpu as pltpu
from jax.sharding import PartitionSpec as P

EPSILON = 1e-06
KEEP_SHARE = 0.5
HIGH = lax.Precision.HIGHEST
PANEL = 64
TILE = 8
HEAD = 16


def split_two(x):
    high = lax.reduce_precision(x, 8, 7)
    return high.astype(jnp.bfloat16), (x - high).astype(jnp.bfloat16)


def butterfly_sum(x, axis, step=1):
    n = lax.axis_size(axis)
    while step < n:
        x = x + lax.ppermute(x, axis, [(i, i ^ step) for i in range(n)])
        step *= 2
    return x


def quad_sum(x, axis, step=1):
    if lax.axis_size(axis) != 4 * step:
        return butterfly_sum(x, axis, step)
    near, far, across = [
        lax.ppermute(x, axis, [(i, i ^ (k * step)) for i in range(4 * step)]) for k in range(1, 4)
    ]
    return (x + near) + (far + across)


def gather_list(x, axis):
    n = lax.axis_size(axis)
    return [x] + [lax.ppermute(x, axis, [(i, i ^ k) for i in range(n)]) for k in range(1, n)]


def line_gather(chunks):
    n = lax.axis_size("fsdp")
    length = n // 2
    place = lax.axis_index("fsdp") // 2
    if length > 4:
        groups = [list(range(0, n, 2)), list(range(1, n, 2))]
        order = (place - jnp.arange(length)) % length
        return [jnp.take(lax.all_gather(c, "fsdp", axis_index_groups=groups), order, axis=0) for c in chunks]
    ups = [(i, i + 2) for i in range(n - 2)]
    downs = [(i + 2, i) for i in range(n - 2)]
    from_below, from_above = [list(chunks)], [list(chunks)]
    for _ in range(length - 1):
        below, above = from_below[-1], from_above[-1]
        moved = [(lax.ppermute(b, "fsdp", ups), lax.ppermute(a, "fsdp", downs)) for b, a in zip(below, above)]
        from_below.append([m[0] for m in moved])
        from_above.append([m[1] for m in moved])
    results = []
    for c, chunk in enumerate(chunks):
        blocks = [chunk]
        for k in range(1, length):
            blocks.append(jnp.where(place >= k, from_below[k][c], from_above[length - k][c]))
        results.append(blocks)
    return results


def spread(row):
    return jnp.broadcast_to(row, (TILE, 2 * PANEL))


def panel_inverse(block):
    rows = lax.broadcasted_iota(jnp.int32, (PANEL, PANEL), 0)
    cols = lax.broadcasted_iota(jnp.int32, (PANEL, PANEL), 1)
    both = jnp.concatenate([block, (rows == cols).astype(jnp.float32)], axis=1)
    count = PANEL // TILE
    tiles = [both[TILE * i : TILE * (i + 1)] for i in range(count)]
    sub = lax.broadcasted_iota(jnp.int32, (TILE, 2 * PANEL), 0)
    done = []
    for k in range(count):
        columns = [
            [spread(tiles[i][:, TILE * k + j : TILE * k + j + 1]) for j in range(TILE)] for i in range(k, count)
        ]
        own, body = columns[0], tiles[k]
        final = jnp.zeros_like(body)
        for j in range(TILE):
            here = sub == j
            pivot = spread(own[j][j : j + 1])
            inverse = 1.0 / pivot
            final = jnp.where(here, body * lax.rsqrt(pivot), final)
            reduced = spread(body[j : j + 1]) * inverse
            body = jnp.where(here, reduced, body - own[j] * reduced)
            for other in range(j + 1, TILE):
                ratio = spread(own[other][j : j + 1]) * inverse
                own[other] = jnp.where(here, ratio, own[other] - own[j] * ratio)
        done.append(final)
        for i in range(k + 1, count):
            tile = tiles[i]
            for j in range(TILE):
                tile = tile - columns[i - k][j] * spread(body[j : j + 1])
            tiles[i] = tile
    return jnp.concatenate(done, axis=0)[:, PANEL:]


def factor_kernel(gram_ref, out_ref, work):
    rank = gram_ref.shape[0]
    work[:, :rank] = gram_ref[...]
    rows = lax.broadcasted_iota(jnp.int32, (rank, rank), 0)
    cols = lax.broadcasted_iota(jnp.int32, (rank, rank), 1)
    work[:, rank:] = (rows == cols).astype(jnp.float32)
    for start in range(0, rank, PANEL):
        end = start + PANEL
        inverse = panel_inverse(work[start:end, start:end])
        scaled = jnp.dot(inverse, work[start:end, :], precision=HIGH, preferred_element_type=jnp.float32)
        out_ref[start:end, :] = scaled[:, rank:]
        if end < rank:
            low = end // 128 * 128
            change = lax.dot_general(
                scaled[:, low:rank],
                scaled,
                (((0,), (0,)), ((), ())),
                precision=HIGH,
                preferred_element_type=jnp.float32,
            )
            work[end:, :] = work[end:, :] - change[end - low :, :]


def factor_inverse(gram):
    rank = gram.shape[0]
    return pl.pallas_call(
        factor_kernel,
        out_shape=jax.ShapeDtypeStruct((rank, rank), jnp.float32),
        scratch_shapes=[pltpu.VMEM((rank, 2 * rank), jnp.float32)],
        compiler_params=pltpu.CompilerParams(vmem_limit_bytes=32 * 1024 * 1024),
        cost_estimate=pl.CostEstimate(flops=6 * 2 * rank**3, bytes_accessed=2 * rank * rank * 4, transcendentals=rank),
    )(gram)


def dot_rows(a, b):
    return lax.dot_general(a, b, (((1,), (1,)), ((), ())), precision=HIGH, preferred_element_type=jnp.float32)


def halves(x):
    high = x.astype(jnp.bfloat16)
    return high, (x - high.astype(jnp.float32)).astype(jnp.bfloat16)


def mix_kernel(core_ref, high_ref, low_ref, proj_ref, out_ref):
    def times(a, b):
        return lax.dot_general(a, b, (((0,), (0,)), ((), ())), preferred_element_type=jnp.float32)

    proj_high, proj_low = halves(proj_ref[...])
    high = high_ref[...]
    out_ref[...] = times(high, proj_high) + (times(low_ref[...], proj_high) + times(high, proj_low))


def mix(core, pair_high, pair_low, projected):
    rows, cols = pair_high.shape
    rank = projected.shape[1]
    block = min(512, cols // 2)
    steps = cols // 2 // block
    wide = pl.BlockSpec((rows, block), lambda i, core: (0, core[0] * steps + i))
    return pl.pallas_call(
        mix_kernel,
        grid_spec=pltpu.PrefetchScalarGridSpec(
            num_scalar_prefetch=1,
            grid=(steps,),
            in_specs=[wide, wide, pl.BlockSpec(projected.shape, lambda i, core: (0, 0))],
            out_specs=pl.BlockSpec((block, rank), lambda i, core: (i, 0)),
        ),
        out_shape=jax.ShapeDtypeStruct((cols // 2, rank), jnp.float32),
        compiler_params=pltpu.CompilerParams(vmem_limit_bytes=32 * 1024 * 1024),
        cost_estimate=pl.CostEstimate(
            flops=3 * rows * cols * rank, bytes_accessed=rows * cols * 2 + cols * rank * 2, transcendentals=0
        ),
    )(core, pair_high, pair_low, projected)


def unit_of(exponent, mantissa):
    return mantissa * jnp.exp2(exponent - 13.0)


def encode_kernel(share_ref, inverse_ref, *out_refs):
    squares_ref, code_refs = out_refs[-1], out_refs[:-1]
    right = dot_rows(share_ref[...], inverse_ref[...])
    squares_ref[...] = jnp.broadcast_to(jnp.sum(right * right, axis=0, keepdims=True), squares_ref.shape)
    rows = right.shape[0] // len(code_refs)
    place = lax.broadcasted_iota(jnp.int32, (HEAD, right.shape[1]), 0)
    for c, code_ref in enumerate(code_refs):
        part = right[rows * c : rows * (c + 1)]
        top = jnp.maximum(jnp.max(jnp.abs(part), axis=0, keepdims=True), 1e-28) * (1.0 / 32766.0)
        exponent = jnp.floor(jnp.log2(top))
        mantissa = jnp.floor(top * jnp.exp2(13.0 - exponent)) + 1.0
        scaled = part * (1.0 / unit_of(exponent, mantissa))
        code_ref[:rows, :] = jnp.floor(scaled + 0.5).astype(jnp.int32).astype(jnp.int16)
        head = jnp.where(place == 0, exponent, mantissa)
        code_ref[rows:, :] = head.astype(jnp.int32).astype(jnp.int16)


def encode(share, inverse_low):
    rows, rank = share.shape
    parts = 2 if rows % 256 == 0 else 1
    out = pl.pallas_call(
        encode_kernel,
        out_shape=[jax.ShapeDtypeStruct((rows // parts + HEAD, rank), jnp.int16)] * parts
        + [jax.ShapeDtypeStruct((TILE, rank), jnp.float32)],
        compiler_params=pltpu.CompilerParams(vmem_limit_bytes=32 * 1024 * 1024),
        cost_estimate=pl.CostEstimate(flops=12 * rows * rank * rank, bytes_accessed=rows * rank * 6, transcendentals=0),
    )(share, inverse_low)
    return out[:-1], out[-1]


def finish_kernel(parts, pieces, column_ref, momentum_ref, grad_ref, high_ref, low_ref, scale_ref, *refs):
    code_refs, (next_ref, basis_ref, update_ref, right_ref) = refs[: parts * pieces], refs[parts * pieces :]
    rank = basis_ref.shape[1]
    for piece in range(pieces):

        @pl.when(pl.program_id(0) == piece)
        def _():
            for c, code_ref in enumerate(code_refs[parts * piece : parts * (piece + 1)]):
                code = code_ref[...].astype(jnp.int32).astype(jnp.float32)
                share = code.shape[1] - HEAD
                decoded = code[:, :share] * unit_of(code[:, share : share + 1], code[:, share + 1 : share + 2])
                size = code.shape[0] * share
                right_ref[size * c : size * (c + 1), :] = decoded.reshape(size, rank)

    right = right_ref[...]
    basis_ref[...] = right * scale_ref[...]
    right_high, right_low = halves(right)

    def times(a, b):
        return lax.dot_general(a, b, (((1,), (1,)), ((), ())), preferred_element_type=jnp.float32)

    high = high_ref[...]
    both = times(high, right_high) + (times(low_ref[...], right_high) + times(high, right_low))
    rows = momentum_ref.shape[0]
    next_ref[...] = momentum_ref[...] + grad_ref[...].astype(jnp.float32) + both[:rows]
    update_ref[...] = both[rows:].astype(jnp.bfloat16)


def finish(momentum, grad, codes, columns, factors, scale):
    rows, cols = momentum.shape
    pieces, parts, rank = len(codes), len(codes[0]), scale.shape[1]
    block = cols // pieces
    high, low = split_two(factors)
    wide = lambda: pl.BlockSpec((rows, block), lambda i, column: (0, column[i]))
    tall = lambda: pl.BlockSpec((block, rank), lambda i, column: (column[i], 0))
    whole = lambda x: pl.BlockSpec(x.shape, lambda i, column: (0,) * x.ndim)
    flat = [c for piece in codes for c in piece]
    return pl.pallas_call(
        functools.partial(finish_kernel, parts, pieces),
        grid_spec=pltpu.PrefetchScalarGridSpec(
            num_scalar_prefetch=1,
            grid=(pieces,),
            in_specs=[wide(), wide(), whole(high), whole(low), whole(scale)] + [whole(c) for c in flat],
            out_specs=[wide(), tall(), wide()],
            scratch_shapes=[pltpu.VMEM((block, rank), jnp.float32)],
        ),
        out_shape=[
            jax.ShapeDtypeStruct((rows, cols), jnp.float32),
            jax.ShapeDtypeStruct((cols, rank), jnp.float32),
            jax.ShapeDtypeStruct((rows, cols), jnp.bfloat16),
        ],
        compiler_params=pltpu.CompilerParams(vmem_limit_bytes=40 * 1024 * 1024),
        cost_estimate=pl.CostEstimate(
            flops=6 * 2 * rows * cols * rank, bytes_accessed=rows * cols * 12 + cols * rank * 8, transcendentals=0
        ),
    )(columns, momentum, grad, high, low, scale, *flat)


def on_device(momentum, grad, q_stored, perm):
    block_rows = q_stored.shape[0]
    num_blocks = lax.axis_size("fsdp")
    num_cols = lax.axis_size("tp")
    rank_total = block_rows * num_blocks
    row_total = momentum.shape[0] * num_blocks
    col_total = momentum.shape[1] * num_cols
    rows = momentum.shape[0]
    core = lax.axis_index("fsdp") % 2
    lines = [list(range(0, num_blocks, 2)), list(range(1, num_blocks, 2))]
    swap = lambda x: lax.ppermute(x, "fsdp", [(i, i ^ 1) for i in range(num_blocks)])

    comb_high, comb_low = split_two(momentum + grad.astype(jnp.float32))
    pair_high = jnp.concatenate([comb_high, swap(comb_high)], axis=0)
    pair_low = jnp.concatenate([comb_low, swap(comb_low)], axis=0)

    parts = 2 if block_rows % 32 == 0 else 1
    chunk_rows = block_rows // parts
    chunks = line_gather([q_stored[chunk_rows * c : chunk_rows * (c + 1)] for c in range(parts)])
    basis = jnp.concatenate([jnp.concatenate(list(blocks), axis=0) for blocks in chunks], axis=0)
    product = lax.dot_general(
        jnp.concatenate([pair_high, pair_low], axis=0),
        basis,
        (((1,), (1,)), ((), ())),
        preferred_element_type=jnp.float32,
    )
    mine = butterfly_sum(product[: 2 * rows] + product[2 * rows :], "tp")
    other = swap(mine)
    other = jnp.concatenate([other[rows:], other[:rows]], axis=0)
    blocks = jnp.arange(num_blocks, dtype=jnp.int32)
    inverse = jnp.sum(jnp.where(perm[:, None] == blocks[None, :], blocks[:, None], 0), axis=0)
    line = num_blocks // 2
    row_ids = jnp.arange(rank_total, dtype=jnp.int32)
    source = inverse[row_ids // block_rows]
    within = row_ids % block_rows
    away = (lax.axis_index("fsdp") // 2 - source // 2) % line
    order_index = ((source % 2) ^ core) * (rank_total // 2)
    order_index += (within // chunk_rows * line + away) * chunk_rows + within % chunk_rows
    projected = jnp.take(jnp.concatenate([mine, other], axis=1), order_index, axis=1)

    mixed = mix(core.reshape(1), pair_high, pair_low, projected)
    mixed_share = lax.psum_scatter(mixed, "fsdp", scatter_dimension=0, tiled=True, axis_index_groups=lines)

    gram_part = lax.dot_general(projected, projected, (((0,), (0,)), ((), ())), precision=HIGH)
    piece_rows = rank_total // num_cols
    piece = lax.dynamic_slice_in_dim(gram_part, lax.axis_index("tp") * piece_rows, piece_rows, axis=0)
    pieces = gather_list(butterfly_sum(piece, "fsdp", 2), "tp")
    gram = jnp.zeros((rank_total, rank_total), jnp.float32)
    for k, part in enumerate(pieces):
        place = (lax.axis_index("tp") ^ k) * piece_rows
        gram = lax.dynamic_update_slice_in_dim(gram, part, place, axis=0)
    inverse_low = factor_inverse(gram)

    orthonormal = dot_rows(projected[:rows], inverse_low)
    codes, squares = encode(mixed_share, inverse_low)
    squares = quad_sum(quad_sum(squares[:1], "tp"), "fsdp", 2)
    squares = squares + swap(squares)
    scale = lax.rsqrt(squares / col_total + EPSILON)
    factors = jnp.concatenate(
        [-KEEP_SHARE * orthonormal, math.sqrt(row_total / rank_total) * orthonormal * scale], axis=0
    )

    place = lax.axis_index("fsdp") // 2
    if line > 4:
        gathered = lax.all_gather(codes[0], "fsdp", axis_index_groups=lines)
        count = max(1, mixed.shape[0] // 512)
        mine = [[x] for x in jnp.split(gathered, count, axis=0)]
        spots = list(range(count))
    else:
        mine = [[x[None] for x in blocks] for blocks in zip(*line_gather(codes))]
        spots = [(place - k) % line for k in range(line)]
    other = [[swap(x) for x in blocks] for blocks in mine]
    columns = [core * len(spots) + spot for spot in spots] + [(1 - core) * len(spots) + spot for spot in spots]
    return tuple(finish(momentum, grad, mine + other, jnp.stack(columns).astype(jnp.int32), factors, scale))


def solution(mesh):
    return jax.shard_map(
        on_device,
        mesh=mesh,
        in_specs=(P("fsdp", "tp"), P("fsdp", "tp"), P("fsdp", "tp"), P()),
        out_specs=(P("fsdp", "tp"), P("tp", None), P("fsdp", "tp")),
        check_vma=False,
    )
```

```python
import functools
import math

import jax
import jax.numpy as jnp
from jax import lax
from jax.experimental import pallas as pl
from jax.experimental.pallas import tpu as pltpu
from jax.sharding import PartitionSpec as P

EPSILON = 1e-06
KEEP_SHARE = 0.5
HIGH = lax.Precision.HIGHEST
PANEL = 64
TILE = 8
HEAD = 16
TOP = 32766.0
PARAMS = pltpu.CompilerParams(vmem_limit_bytes=40 * 1024 * 1024)


def split_two(x):
    high = lax.reduce_precision(x, 8, 7)
    return high.astype(jnp.bfloat16), (x - high).astype(jnp.bfloat16)


def halves(x):
    high = x.astype(jnp.bfloat16)
    return high, (x - high.astype(jnp.float32)).astype(jnp.bfloat16)


def exchange(x, axis, k):
    return lax.ppermute(x, axis, [(i, i ^ k) for i in range(lax.axis_size(axis))])


def butterfly_sum(x, axis, step=1):
    while step < lax.axis_size(axis):
        x = x + exchange(x, axis, step)
        step *= 2
    return x


def quad_sum(x, axis, step=1):
    if lax.axis_size(axis) != 4 * step:
        return butterfly_sum(x, axis, step)
    near, far, across = [exchange(x, axis, k * step) for k in range(1, 4)]
    return (x + near) + (far + across)


def whole(x):
    return pl.BlockSpec(x.shape, lambda *_: (0,) * len(x.shape))


def dot_rows(a, b):
    return lax.dot_general(a, b, (((1,), (1,)), ((), ())), precision=HIGH, preferred_element_type=jnp.float32)


def gram_kernel(column_ref, near_ref, far_ref, order_ref, unit_ref, proj_ref, scaled_ref, piece_ref, gram_ref):
    proj = jnp.dot(near_ref[...] + far_ref[...], order_ref[...], precision=HIGH, preferred_element_type=jnp.float32)
    proj_ref[...] = proj
    scaled_ref[...] = proj * unit_ref[...]
    gram_ref[...] = lax.dot_general(
        proj, proj, (((0,), (0,)), ((), ())), precision=HIGH, preferred_element_type=jnp.float32
    )
    size = piece_ref.shape[0]
    piece_ref[...] = gram_ref[pl.ds(pl.multiple_of(column_ref[0] * size, size), size), :]


def gram_parts(column, near, far, order, unit, columns):
    rows, rank = near.shape
    operands = (near, far, order, unit)
    return pl.pallas_call(
        gram_kernel,
        grid_spec=pltpu.PrefetchScalarGridSpec(
            num_scalar_prefetch=1,
            grid=(1,),
            in_specs=[whole(x) for x in operands],
            out_specs=[whole(near), whole(near), pl.BlockSpec((rank // columns, rank), lambda *_: (0, 0))],
            scratch_shapes=[pltpu.VMEM((rank, rank), jnp.float32)],
        ),
        out_shape=[
            jax.ShapeDtypeStruct((rows, rank), jnp.float32),
            jax.ShapeDtypeStruct((rows, rank), jnp.float32),
            jax.ShapeDtypeStruct((rank // columns, rank), jnp.float32),
        ],
        compiler_params=PARAMS,
        cost_estimate=pl.CostEstimate(flops=24 * rows * rank * rank, bytes_accessed=rank * rank * 12, transcendentals=0),
    )(column, *operands)


def spread(row):
    return jnp.broadcast_to(row, (TILE, 2 * PANEL))


def panel_inverse(block):
    rows = lax.broadcasted_iota(jnp.int32, (PANEL, PANEL), 0)
    cols = lax.broadcasted_iota(jnp.int32, (PANEL, PANEL), 1)
    both = jnp.concatenate([block, (rows == cols).astype(jnp.float32)], axis=1)
    count = PANEL // TILE
    tiles = [both[TILE * i : TILE * (i + 1)] for i in range(count)]
    sub = lax.broadcasted_iota(jnp.int32, (TILE, 2 * PANEL), 0)
    done = []
    for k in range(count):
        columns = [
            [spread(tiles[i][:, TILE * k + j : TILE * k + j + 1]) for j in range(TILE)] for i in range(k, count)
        ]
        own, body = columns[0], tiles[k]
        final = jnp.zeros_like(body)
        for j in range(TILE):
            here = sub == j
            pivot = spread(own[j][j : j + 1])
            inverse = 1.0 / pivot
            final = jnp.where(here, body * lax.rsqrt(pivot), final)
            reduced = spread(body[j : j + 1]) * inverse
            body = jnp.where(here, reduced, body - own[j] * reduced)
            for other in range(j + 1, TILE):
                ratio = spread(own[other][j : j + 1]) * inverse
                own[other] = jnp.where(here, ratio, own[other] - own[j] * ratio)
        done.append(final)
        for i in range(k + 1, count):
            tile = tiles[i]
            for j in range(TILE):
                tile = tile - columns[i - k][j] * spread(body[j : j + 1])
            tiles[i] = tile
    return jnp.concatenate(done, axis=0)[:, PANEL:]


def factor_kernel(place_ref, *refs):
    piece_refs, (out_ref, work) = refs[:-2], refs[-2:]
    rank = out_ref.shape[0]
    for k, piece_ref in enumerate(piece_refs):
        size = piece_ref.shape[0]
        work[pl.ds(pl.multiple_of(place_ref[k] * size, size), size), :rank] = piece_ref[...]
    rows = lax.broadcasted_iota(jnp.int32, (rank, rank), 0)
    cols = lax.broadcasted_iota(jnp.int32, (rank, rank), 1)
    work[:, rank:] = (rows == cols).astype(jnp.float32)
    for start in range(0, rank, PANEL):
        end = start + PANEL
        inverse = panel_inverse(work[start:end, start:end])
        scaled = jnp.dot(inverse, work[start:end, :], precision=HIGH, preferred_element_type=jnp.float32)
        out_ref[start:end, :] = scaled[:, rank:]
        if end < rank:
            low = end // 128 * 128
            change = lax.dot_general(
                scaled[:, low:rank],
                scaled,
                (((0,), (0,)), ((), ())),
                precision=HIGH,
                preferred_element_type=jnp.float32,
            )
            work[end:, :] = work[end:, :] - change[end - low :, :]


def factor_inverse(places, pieces):
    rank = pieces[0].shape[1]
    return pl.pallas_call(
        factor_kernel,
        grid_spec=pltpu.PrefetchScalarGridSpec(
            num_scalar_prefetch=1,
            grid=(1,),
            in_specs=[whole(x) for x in pieces],
            out_specs=pl.BlockSpec((rank, rank), lambda *_: (0, 0)),
            scratch_shapes=[pltpu.VMEM((rank, 2 * rank), jnp.float32)],
        ),
        out_shape=jax.ShapeDtypeStruct((rank, rank), jnp.float32),
        compiler_params=PARAMS,
        cost_estimate=pl.CostEstimate(flops=6 * 2 * rank**3, bytes_accessed=2 * rank * rank * 4, transcendentals=rank),
    )(places, *pieces)


def mix_kernel(code_ref, proj_ref, out_ref):
    def times(a, b):
        return lax.dot_general(a, b, (((0,), (0,)), ((), ())), preferred_element_type=jnp.float32)

    code_high, code_low = halves(code_ref[...].astype(jnp.int32).astype(jnp.float32))
    proj_high, proj_low = halves(proj_ref[...])
    part = times(code_high, proj_high) + (times(code_low, proj_high) + times(code_high, proj_low))

    @pl.when(pl.program_id(0) == 0)
    def _():
        out_ref[...] = part

    @pl.when(pl.program_id(0) > 0)
    def _():
        out_ref[...] += part


def mix(codes, projected):
    rows, cols = codes.shape
    rank = projected.shape[1]
    block = min(512, rows)
    return pl.pallas_call(
        mix_kernel,
        grid=(rows // block,),
        in_specs=[pl.BlockSpec((block, cols), lambda i: (i, 0)), pl.BlockSpec((block, rank), lambda i: (i, 0))],
        out_specs=pl.BlockSpec((cols, rank), lambda i: (0, 0)),
        out_shape=jax.ShapeDtypeStruct((cols, rank), jnp.float32),
        compiler_params=PARAMS,
        cost_estimate=pl.CostEstimate(
            flops=6 * rows * cols * rank, bytes_accessed=rows * cols * 2 + rows * rank * 4, transcendentals=0
        ),
    )(codes, projected)


def unit_of(exponent, mantissa):
    return mantissa * jnp.exp2(exponent - 13.0)


def encode_kernel(share_ref, inverse_ref, proj_ref, code_ref, ortho_ref):
    inverse = inverse_ref[...]
    ortho_ref[...] = dot_rows(proj_ref[...], inverse)
    right = dot_rows(share_ref[...], inverse)
    rows, rank = right.shape
    square = jnp.maximum(jnp.sum(right * right, axis=0, keepdims=True), 1e-34)
    square_exponent = jnp.floor(jnp.log2(square))
    fine = square * jnp.exp2(13.0 - square_exponent)
    square_high = jnp.floor(fine)
    square_low = jnp.floor((fine - square_high) * 16384.0)
    top = jnp.maximum(jnp.max(jnp.abs(right), axis=0, keepdims=True), 1e-28) * (1.0 / TOP)
    exponent = jnp.floor(jnp.log2(top))
    mantissa = jnp.floor(top * jnp.exp2(13.0 - exponent)) + 1.0
    scaled = right * (1.0 / unit_of(exponent, mantissa))
    code_ref[:rows, :] = jnp.floor(scaled + 0.5).astype(jnp.int32).astype(jnp.int16)
    place = lax.broadcasted_iota(jnp.int32, (HEAD, rank), 0)
    head = jnp.zeros((HEAD, rank), jnp.float32)
    for k, row in enumerate((exponent, mantissa, square_exponent, square_high, square_low)):
        head = jnp.where(place == k, row, head)
    code_ref[rows:, :] = head.astype(jnp.int32).astype(jnp.int16)


def encode(share, inverse_low, projected):
    rows, rank = share.shape
    return pl.pallas_call(
        encode_kernel,
        out_shape=[
            jax.ShapeDtypeStruct((rows + HEAD, rank), jnp.int16),
            jax.ShapeDtypeStruct(projected.shape, jnp.float32),
        ],
        compiler_params=PARAMS,
        cost_estimate=pl.CostEstimate(flops=12 * rows * rank * rank, bytes_accessed=rows * rank * 6, transcendentals=0),
    )(share, inverse_low, projected)


def finish_kernel(
    gain, momentum_ref, grad_ref, code_ref, ortho_ref, scale_ref, next_ref, basis_ref, update_ref, high_ref, low_ref
):
    scale = scale_ref[...]
    rows = momentum_ref.shape[0]

    @pl.when(pl.program_id(0) == 0)
    def _():
        ortho = ortho_ref[...]
        for start, factor in ((0, -KEEP_SHARE * ortho), (rows, gain * ortho * scale)):
            high, low = halves(factor)
            high_ref[start : start + rows, :] = high
            low_ref[start : start + rows, :] = low

    code = code_ref[...].astype(jnp.int32).astype(jnp.float32)
    share = code.shape[1] - HEAD
    right = code[:, :share] * unit_of(code[:, share : share + 1], code[:, share + 1 : share + 2])
    right = right.reshape(basis_ref.shape)
    basis_ref[...] = right * scale
    right_high, right_low = halves(right)

    def times(a, b):
        return lax.dot_general(a, b, (((1,), (1,)), ((), ())), preferred_element_type=jnp.float32)

    high = high_ref[...]
    both = times(high, right_high) + (times(low_ref[...], right_high) + times(high, right_low))
    next_ref[...] = momentum_ref[...] + grad_ref[...].astype(jnp.float32) + both[:rows]
    update_ref[...] = both[rows:].astype(jnp.bfloat16)


def finish(momentum, grad, codes, orthonormal, scale, gain):
    rows, cols = momentum.shape
    shares, share, rank = codes.shape
    share -= HEAD
    group = max(1, min(512 // share, shares))
    block = group * share
    wide = pl.BlockSpec((rows, block), lambda i: (0, i))
    tall = pl.BlockSpec((block, rank), lambda i: (i, 0))
    return pl.pallas_call(
        functools.partial(finish_kernel, gain),
        grid=(cols // block,),
        in_specs=[
            wide,
            wide,
            pl.BlockSpec((group, share + HEAD, rank), lambda i: (i, 0, 0)),
            whole(orthonormal),
            whole(scale),
        ],
        out_specs=[wide, tall, wide],
        out_shape=[
            jax.ShapeDtypeStruct((rows, cols), jnp.float32),
            jax.ShapeDtypeStruct((cols, rank), jnp.float32),
            jax.ShapeDtypeStruct((rows, cols), jnp.bfloat16),
        ],
        scratch_shapes=[pltpu.VMEM((2 * rows, rank), jnp.bfloat16)] * 2,
        compiler_params=PARAMS,
        cost_estimate=pl.CostEstimate(
            flops=6 * 2 * rows * cols * rank, bytes_accessed=rows * cols * 12 + cols * rank * 6, transcendentals=0
        ),
    )(momentum, grad, codes, orthonormal, scale)


def on_device(momentum, grad, q_stored, perm):
    block_rows = q_stored.shape[0]
    num_blocks = lax.axis_size("fsdp")
    num_cols = lax.axis_size("tp")
    rank_total = block_rows * num_blocks
    rows, cols = momentum.shape
    row_total, col_total = rows * num_blocks, cols * num_cols
    column = lax.axis_index("tp")

    basis = lax.all_gather(q_stored, "fsdp", axis=0, tiled=True)

    combined = momentum + grad.astype(jnp.float32)
    unit = jnp.maximum(jnp.max(jnp.abs(combined), axis=1, keepdims=True), 1e-28) * (1.0 / TOP)
    codes = jnp.floor(combined * (1.0 / unit) + 0.5).astype(jnp.int16)
    codes = codes.reshape(rows, num_blocks, cols // num_blocks).transpose(1, 0, 2)
    codes = lax.all_to_all(codes, "fsdp", split_axis=0, concat_axis=0).reshape(row_total, cols // num_blocks)
    codes, combined = lax.optimization_barrier((codes, combined))

    stacked = lax.dot_general(
        jnp.concatenate(split_two(combined), axis=0),
        basis,
        (((1,), (1,)), ((), ())),
        preferred_element_type=jnp.float32,
    )
    near = stacked[:rows] + stacked[rows:]
    step = 1
    while 2 * step < num_cols:
        near = near + exchange(near, "tp", step)
        step *= 2
    far = exchange(near, "tp", step)
    blocks = jnp.arange(num_blocks, dtype=jnp.int32)
    inverse = jnp.sum(jnp.where(perm[:, None] == blocks[None, :], blocks[:, None], 0), axis=0)
    row_ids = jnp.arange(rank_total, dtype=jnp.int32)
    order_index = inverse[row_ids // block_rows] * block_rows + row_ids % block_rows
    order = (row_ids[:, None] == order_index[None, :]).astype(jnp.float32)
    projected, scaled, piece = gram_parts(column.reshape(1), near, far, order, unit, num_cols)

    all_scaled = lax.all_gather(scaled, "fsdp", axis=0, tiled=True)
    piece = quad_sum(piece, "fsdp", 2)
    piece = piece + exchange(piece, "fsdp", 1)
    pieces = [piece] + [exchange(piece, "tp", k) for k in range(1, num_cols)]
    places = jnp.stack([column ^ k for k in range(num_cols)]).astype(jnp.int32)
    inverse_low = factor_inverse(places, pieces)
    mixed = mix(codes, all_scaled)

    code, orthonormal = encode(mixed, inverse_low, projected)
    gathered = lax.all_gather(code, "fsdp", axis=0)
    share = mixed.shape[0]
    head = gathered[:, share : share + 5].astype(jnp.float32)
    parts = (head[:, 3] + head[:, 4] * (1.0 / 16384.0)) * jnp.exp2(head[:, 2] - 13.0)
    squares = quad_sum(jnp.sum(parts, axis=0, keepdims=True), "tp")
    scale = lax.rsqrt(squares / col_total + EPSILON)
    return tuple(finish(momentum, grad, gathered, orthonormal, scale, math.sqrt(row_total / rank_total)))


def solution(mesh):
    return jax.shard_map(
        on_device,
        mesh=mesh,
        in_specs=(P("fsdp", "tp"), P("fsdp", "tp"), P("fsdp", "tp"), P()),
        out_specs=(P("fsdp", "tp"), P("tp", None), P("fsdp", "tp")),
        check_vma=False,
    )
```

```python
import functools
import math

import jax
import jax.numpy as jnp
from jax import lax
from jax.experimental import pallas as pl
from jax.experimental.pallas import tpu as pltpu
from jax.sharding import PartitionSpec as P

EPSILON = 1e-06
KEEP_SHARE = 0.5
HIGH = lax.Precision.HIGHEST
PANEL = 64
TILE = 8
HEAD = 16
TOP = 32766.0
PARAMS = pltpu.CompilerParams(vmem_limit_bytes=40 * 1024 * 1024)


def halves(x):
    high = x.astype(jnp.bfloat16)
    return high, (x - high.astype(jnp.float32)).astype(jnp.bfloat16)


def exchange(x, axis, k):
    return lax.ppermute(x, axis, [(i, i ^ k) for i in range(lax.axis_size(axis))])


def butterfly_sum(x, axis, step=1):
    while step < lax.axis_size(axis):
        x = x + exchange(x, axis, step)
        step *= 2
    return x


def quad_sum(x, axis, step=1):
    if lax.axis_size(axis) != 4 * step:
        return butterfly_sum(x, axis, step)
    near, far, across = [exchange(x, axis, k * step) for k in range(1, 4)]
    return (x + near) + (far + across)


def whole(x):
    return pl.BlockSpec(x.shape, lambda *_: (0,) * len(x.shape))


def dot_rows(a, b):
    return lax.dot_general(a, b, (((1,), (1,)), ((), ())), precision=HIGH, preferred_element_type=jnp.float32)


def code_basis(basis):
    value = basis.astype(jnp.float32)
    size = jnp.abs(value)
    normal = size >= 2.0**-126
    exponent = jnp.floor(jnp.log2(jnp.where(normal, size, 1.0)))
    code = 128.0 * (exponent + 126.0) + jnp.floor(128.0 * (size * jnp.exp2(-exponent)) + 0.5)
    return jnp.where(normal, jnp.where(value < 0.0, -code, code), 0.0).astype(jnp.int16)


def project_kernel(momentum_ref, grad_ref, code_ref, out_ref):
    code = code_ref[...].astype(jnp.int32)
    size = jnp.abs(code)
    value = ((size & 127) + 128).astype(jnp.float32) * jnp.exp2(((size >> 7) - 134).astype(jnp.float32))
    basis = jnp.where(code == 0, 0.0, jnp.where(code < 0, -value, value)).astype(jnp.bfloat16)
    high, low = halves(momentum_ref[...] + grad_ref[...].astype(jnp.float32))

    def times(a, b):
        return lax.dot_general(a, b, (((1,), (1,)), ((), ())), preferred_element_type=jnp.float32)

    part = times(high, basis) + times(low, basis)

    @pl.when(pl.program_id(0) == 0)
    def _():
        out_ref[...] = part

    @pl.when(pl.program_id(0) > 0)
    def _():
        out_ref[...] += part


def project(momentum, grad, codes):
    rows, cols = momentum.shape
    rank = codes.shape[0]
    block = min(1024, cols)
    wide = pl.BlockSpec((rows, block), lambda i: (0, i))
    return pl.pallas_call(
        project_kernel,
        grid=(cols // block,),
        in_specs=[wide, wide, pl.BlockSpec((rank, block), lambda i: (0, i))],
        out_specs=pl.BlockSpec((rows, rank), lambda i: (0, 0)),
        out_shape=jax.ShapeDtypeStruct((rows, rank), jnp.float32),
        compiler_params=PARAMS,
        cost_estimate=pl.CostEstimate(
            flops=4 * rows * cols * rank, bytes_accessed=rows * cols * 6 + rank * cols * 2, transcendentals=rank * cols
        ),
    )(momentum, grad, codes)


def gram_kernel(column_ref, near_ref, far_ref, order_ref, unit_ref, proj_ref, scaled_ref, piece_ref, gram_ref):
    proj = jnp.dot(near_ref[...] + far_ref[...], order_ref[...], precision=HIGH, preferred_element_type=jnp.float32)
    proj_ref[...] = proj
    scaled_ref[...] = proj * unit_ref[...]
    gram_ref[...] = lax.dot_general(
        proj, proj, (((0,), (0,)), ((), ())), precision=HIGH, preferred_element_type=jnp.float32
    )
    size = piece_ref.shape[0]
    piece_ref[...] = gram_ref[pl.ds(pl.multiple_of(column_ref[0] * size, size), size), :]


def gram_parts(column, near, far, order, unit, columns):
    rows, rank = near.shape
    operands = (near, far, order, unit)
    return pl.pallas_call(
        gram_kernel,
        grid_spec=pltpu.PrefetchScalarGridSpec(
            num_scalar_prefetch=1,
            grid=(1,),
            in_specs=[whole(x) for x in operands],
            out_specs=[whole(near), whole(near), pl.BlockSpec((rank // columns, rank), lambda *_: (0, 0))],
            scratch_shapes=[pltpu.VMEM((rank, rank), jnp.float32)],
        ),
        out_shape=[
            jax.ShapeDtypeStruct((rows, rank), jnp.float32),
            jax.ShapeDtypeStruct((rows, rank), jnp.float32),
            jax.ShapeDtypeStruct((rank // columns, rank), jnp.float32),
        ],
        compiler_params=PARAMS,
        cost_estimate=pl.CostEstimate(flops=24 * rows * rank * rank, bytes_accessed=rank * rank * 12, transcendentals=0),
    )(column, *operands)


def spread(row):
    return jnp.broadcast_to(row, (TILE, 2 * PANEL))


def panel_inverse(block):
    rows = lax.broadcasted_iota(jnp.int32, (PANEL, PANEL), 0)
    cols = lax.broadcasted_iota(jnp.int32, (PANEL, PANEL), 1)
    both = jnp.concatenate([block, (rows == cols).astype(jnp.float32)], axis=1)
    count = PANEL // TILE
    tiles = [both[TILE * i : TILE * (i + 1)] for i in range(count)]
    sub = lax.broadcasted_iota(jnp.int32, (TILE, 2 * PANEL), 0)
    done = []
    for k in range(count):
        columns = [
            [spread(tiles[i][:, TILE * k + j : TILE * k + j + 1]) for j in range(TILE)] for i in range(k, count)
        ]
        own, body = columns[0], tiles[k]
        final = jnp.zeros_like(body)
        for j in range(TILE):
            here = sub == j
            pivot = spread(own[j][j : j + 1])
            inverse = 1.0 / pivot
            final = jnp.where(here, body * lax.rsqrt(pivot), final)
            reduced = spread(body[j : j + 1]) * inverse
            body = jnp.where(here, reduced, body - own[j] * reduced)
            for other in range(j + 1, TILE):
                ratio = spread(own[other][j : j + 1]) * inverse
                own[other] = jnp.where(here, ratio, own[other] - own[j] * ratio)
        done.append(final)
        for i in range(k + 1, count):
            tile = tiles[i]
            for j in range(TILE):
                tile = tile - columns[i - k][j] * spread(body[j : j + 1])
            tiles[i] = tile
    return jnp.concatenate(done, axis=0)[:, PANEL:]


def factor_kernel(place_ref, *refs):
    piece_refs, (out_ref, work) = refs[:-2], refs[-2:]
    rank = out_ref.shape[0]
    for k, piece_ref in enumerate(piece_refs):
        size = piece_ref.shape[0]
        work[pl.ds(pl.multiple_of(place_ref[k] * size, size), size), :rank] = piece_ref[...]
    rows = lax.broadcasted_iota(jnp.int32, (rank, rank), 0)
    cols = lax.broadcasted_iota(jnp.int32, (rank, rank), 1)
    work[:, rank:] = (rows == cols).astype(jnp.float32)
    for start in range(0, rank, PANEL):
        end = start + PANEL
        inverse = panel_inverse(work[start:end, start:end])
        scaled = jnp.dot(inverse, work[start:end, :], precision=HIGH, preferred_element_type=jnp.float32)
        out_ref[start:end, :] = scaled[:, rank:]
        if end < rank:
            low = end // 128 * 128
            change = lax.dot_general(
                scaled[:, low:rank],
                scaled,
                (((0,), (0,)), ((), ())),
                precision=HIGH,
                preferred_element_type=jnp.float32,
            )
            work[end:, :] = work[end:, :] - change[end - low :, :]


def factor_inverse(places, pieces):
    rank = pieces[0].shape[1]
    return pl.pallas_call(
        factor_kernel,
        grid_spec=pltpu.PrefetchScalarGridSpec(
            num_scalar_prefetch=1,
            grid=(1,),
            in_specs=[whole(x) for x in pieces],
            out_specs=pl.BlockSpec((rank, rank), lambda *_: (0, 0)),
            scratch_shapes=[pltpu.VMEM((rank, 2 * rank), jnp.float32)],
        ),
        out_shape=jax.ShapeDtypeStruct((rank, rank), jnp.float32),
        compiler_params=PARAMS,
        cost_estimate=pl.CostEstimate(flops=6 * 2 * rank**3, bytes_accessed=2 * rank * rank * 4, transcendentals=rank),
    )(places, *pieces)


def unit_of(exponent, mantissa):
    return mantissa * jnp.exp2(exponent - 13.0)


def encode_kernel(source_ref, scaled_ref, inverse_ref, proj_ref, code_ref, ortho_ref, mixed_ref):
    def times(a, b):
        return lax.dot_general(a, b, (((0,), (0,)), ((), ())), preferred_element_type=jnp.float32)

    source_high, source_low = halves(source_ref[...].astype(jnp.int32).astype(jnp.float32))
    scaled_high, scaled_low = halves(scaled_ref[...])
    part = times(source_high, scaled_high) + (times(source_low, scaled_high) + times(source_high, scaled_low))
    first, last = pl.program_id(0) == 0, pl.program_id(0) == pl.num_programs(0) - 1

    @pl.when(first)
    def _():
        mixed_ref[...] = part

    @pl.when(jnp.logical_not(first))
    def _():
        mixed_ref[...] += part

    @pl.when(last)
    def _():
        inverse = inverse_ref[...]
        ortho_ref[...] = dot_rows(proj_ref[...], inverse)
        right = dot_rows(mixed_ref[...], inverse)
        rows, rank = right.shape
        square = jnp.maximum(jnp.sum(right * right, axis=0, keepdims=True), 1e-34)
        square_exponent = jnp.floor(jnp.log2(square))
        fine = square * jnp.exp2(13.0 - square_exponent)
        square_high = jnp.floor(fine)
        square_low = jnp.floor((fine - square_high) * 16384.0)
        top = jnp.maximum(jnp.max(jnp.abs(right), axis=0, keepdims=True), 1e-28) * (1.0 / TOP)
        exponent = jnp.floor(jnp.log2(top))
        mantissa = jnp.floor(top * jnp.exp2(13.0 - exponent)) + 1.0
        scaled = right * (1.0 / unit_of(exponent, mantissa))
        code_ref[:rows, :] = jnp.floor(scaled + 0.5).astype(jnp.int32).astype(jnp.int16)
        place = lax.broadcasted_iota(jnp.int32, (HEAD, rank), 0)
        head = jnp.zeros((HEAD, rank), jnp.float32)
        for k, row in enumerate((exponent, mantissa, square_exponent, square_high, square_low)):
            head = jnp.where(place == k, row, head)
        code_ref[rows:, :] = head.astype(jnp.int32).astype(jnp.int16)


def encode(source, scaled, inverse_low, projected):
    total, share = source.shape
    rank = scaled.shape[1]
    block = min(512, total)
    return pl.pallas_call(
        encode_kernel,
        grid=(total // block,),
        in_specs=[
            pl.BlockSpec((block, share), lambda i: (i, 0)),
            pl.BlockSpec((block, rank), lambda i: (i, 0)),
            whole(inverse_low),
            whole(projected),
        ],
        out_specs=[pl.BlockSpec((share + HEAD, rank), lambda i: (0, 0)), whole(projected)],
        out_shape=[
            jax.ShapeDtypeStruct((share + HEAD, rank), jnp.int16),
            jax.ShapeDtypeStruct(projected.shape, jnp.float32),
        ],
        scratch_shapes=[pltpu.VMEM((share, rank), jnp.float32)],
        compiler_params=PARAMS,
        cost_estimate=pl.CostEstimate(
            flops=6 * total * share * rank, bytes_accessed=total * (share * 2 + rank * 4), transcendentals=0
        ),
    )(source, scaled, inverse_low, projected)


def decode(code_ref):
    code = code_ref[...].astype(jnp.int32).astype(jnp.float32)
    share = code.shape[1] - HEAD
    right = code[:, :share] * unit_of(code[:, share : share + 1], code[:, share + 1 : share + 2])
    return right.reshape(code.shape[0] * share, code.shape[2])


def times_rows(high_ref, low_ref, right):
    def times(a, b):
        return lax.dot_general(a, b, (((1,), (1,)), ((), ())), preferred_element_type=jnp.float32)

    right_high, right_low = halves(right)
    high = high_ref[...]
    return times(high, right_high) + (times(low_ref[...], right_high) + times(high, right_low))


def momentum_kernel(momentum_ref, grad_ref, code_ref, ortho_ref, next_ref, high_ref, low_ref):
    @pl.when(pl.program_id(0) == 0)
    def _():
        high_ref[...], low_ref[...] = halves(-KEEP_SHARE * ortho_ref[...])

    change = times_rows(high_ref, low_ref, decode(code_ref))
    next_ref[...] = momentum_ref[...] + grad_ref[...].astype(jnp.float32) + change


def update_kernel(gain, code_ref, ortho_ref, scale_ref, basis_ref, update_ref, high_ref, low_ref):
    scale = scale_ref[...]

    @pl.when(pl.program_id(0) == 0)
    def _():
        high_ref[...], low_ref[...] = halves(gain * ortho_ref[...])

    basis = decode(code_ref) * scale
    basis_ref[...] = basis
    update_ref[...] = times_rows(high_ref, low_ref, basis).astype(jnp.bfloat16)


def finish(momentum, grad, codes, orthonormal, scale, gain):
    rows, cols = momentum.shape
    shares, share, rank = codes.shape
    share -= HEAD
    group = max(1, min(512 // share, shares))
    block = group * share
    wide = pl.BlockSpec((rows, block), lambda i: (0, i))
    tall = pl.BlockSpec((block, rank), lambda i: (i, 0))
    coded = pl.BlockSpec((group, share + HEAD, rank), lambda i: (i, 0, 0))
    split = [pltpu.VMEM((rows, rank), jnp.bfloat16)] * 2
    flops = 6 * rows * cols * rank
    momentum_next = pl.pallas_call(
        momentum_kernel,
        grid=(cols // block,),
        in_specs=[wide, wide, coded, whole(orthonormal)],
        out_specs=wide,
        out_shape=jax.ShapeDtypeStruct((rows, cols), jnp.float32),
        scratch_shapes=split,
        compiler_params=PARAMS,
        cost_estimate=pl.CostEstimate(
            flops=flops, bytes_accessed=rows * cols * 10 + cols * rank * 2, transcendentals=0
        ),
    )(momentum, grad, codes, orthonormal)
    q_next, update = pl.pallas_call(
        functools.partial(update_kernel, gain),
        grid=(cols // block,),
        in_specs=[coded, whole(orthonormal), whole(scale)],
        out_specs=[tall, wide],
        out_shape=[
            jax.ShapeDtypeStruct((cols, rank), jnp.float32),
            jax.ShapeDtypeStruct((rows, cols), jnp.bfloat16),
        ],
        scratch_shapes=split,
        compiler_params=PARAMS,
        cost_estimate=pl.CostEstimate(flops=flops, bytes_accessed=rows * cols * 2 + cols * rank * 6, transcendentals=0),
    )(codes, orthonormal, scale)
    return momentum_next, q_next, update


def on_device(momentum, grad, q_stored, perm):
    block_rows = q_stored.shape[0]
    num_blocks = lax.axis_size("fsdp")
    num_cols = lax.axis_size("tp")
    rank_total = block_rows * num_blocks
    rows, cols = momentum.shape
    row_total, col_total = rows * num_blocks, cols * num_cols
    column = lax.axis_index("tp")

    basis = lax.all_gather(code_basis(q_stored), "fsdp", axis=0, tiled=True)

    near = project(momentum, grad, basis)

    momentum_again, near = lax.optimization_barrier((momentum, near))
    combined = momentum_again + grad.astype(jnp.float32)
    unit = jnp.maximum(jnp.max(jnp.abs(combined), axis=1, keepdims=True), 1e-28) * (1.0 / TOP)
    codes = jnp.floor(combined * (1.0 / unit) + 0.5).astype(jnp.int16)
    codes = codes.reshape(rows, num_blocks, cols // num_blocks).transpose(1, 0, 2)
    codes = lax.all_to_all(codes, "fsdp", split_axis=0, concat_axis=0).reshape(row_total, cols // num_blocks)

    step = 1
    while 2 * step < num_cols:
        near = near + exchange(near, "tp", step)
        step *= 2
    far = exchange(near, "tp", step)
    blocks = jnp.arange(num_blocks, dtype=jnp.int32)
    inverse = jnp.sum(jnp.where(perm[:, None] == blocks[None, :], blocks[:, None], 0), axis=0)
    row_ids = jnp.arange(rank_total, dtype=jnp.int32)
    order_index = inverse[row_ids // block_rows] * block_rows + row_ids % block_rows
    order = (row_ids[:, None] == order_index[None, :]).astype(jnp.float32)
    projected, scaled, piece = gram_parts(column.reshape(1), near, far, order, unit, num_cols)

    all_scaled = lax.all_gather(scaled, "fsdp", axis=0, tiled=True)
    piece = quad_sum(piece, "fsdp", 2)
    piece = piece + exchange(piece, "fsdp", 1)
    pieces = [piece] + [exchange(piece, "tp", k) for k in range(1, num_cols)]
    places = jnp.stack([column ^ k for k in range(num_cols)]).astype(jnp.int32)
    inverse_low = factor_inverse(places, pieces)
    code, orthonormal = encode(codes, all_scaled, inverse_low, projected)
    gathered = lax.all_gather(code, "fsdp", axis=0)
    share = codes.shape[1]
    head = gathered[:, share : share + 5].astype(jnp.float32)
    parts = (head[:, 3] + head[:, 4] * (1.0 / 16384.0)) * jnp.exp2(head[:, 2] - 13.0)
    squares = quad_sum(jnp.sum(parts, axis=0, keepdims=True), "tp")
    scale = lax.rsqrt(squares / col_total + EPSILON)
    return tuple(finish(momentum, grad, gathered, orthonormal, scale, math.sqrt(row_total / rank_total)))


def solution(mesh):
    return jax.shard_map(
        on_device,
        mesh=mesh,
        in_specs=(P("fsdp", "tp"), P("fsdp", "tp"), P("fsdp", "tp"), P()),
        out_specs=(P("fsdp", "tp"), P("tp", None), P("fsdp", "tp")),
        check_vma=False,
    )
```

```python
import functools
import math

import jax
import jax.numpy as jnp
from jax import lax
from jax.experimental import pallas as pl
from jax.experimental.pallas import tpu as pltpu
from jax.sharding import PartitionSpec as P

EPSILON = 1e-06
KEEP_SHARE = 0.5
HIGH = lax.Precision.HIGHEST
PANEL = 64
TILE = 8
HEAD = 16
TOP = 32766.0
PARAMS = pltpu.CompilerParams(vmem_limit_bytes=40 * 1024 * 1024)


def halves(x):
    high = x.astype(jnp.bfloat16)
    return high, (x - high.astype(jnp.float32)).astype(jnp.bfloat16)


def exchange(x, axis, k):
    return lax.ppermute(x, axis, [(i, i ^ k) for i in range(lax.axis_size(axis))])


def butterfly_sum(x, axis, step=1):
    while step < lax.axis_size(axis):
        x = x + exchange(x, axis, step)
        step *= 2
    return x


def quad_sum(x, axis, step=1):
    if lax.axis_size(axis) != 4 * step:
        return butterfly_sum(x, axis, step)
    near, far, across = [exchange(x, axis, k * step) for k in range(1, 4)]
    return (x + near) + (far + across)


def whole(x):
    return pl.BlockSpec(x.shape, lambda *_: (0,) * len(x.shape))


def dot_rows(a, b):
    return lax.dot_general(a, b, (((1,), (1,)), ((), ())), precision=HIGH, preferred_element_type=jnp.float32)


def code_basis(basis):
    value = basis.astype(jnp.float32)
    size = jnp.abs(value)
    normal = size >= 2.0**-126
    exponent = jnp.floor(jnp.log2(jnp.where(normal, size, 1.0)))
    code = 128.0 * (exponent + 126.0) + jnp.floor(128.0 * (size * jnp.exp2(-exponent)) + 0.5)
    return jnp.where(normal, jnp.where(value < 0.0, -code, code), 0.0).astype(jnp.int16)


def project_kernel(momentum_ref, grad_ref, code_ref, out_ref):
    code = code_ref[...].astype(jnp.int32)
    size = jnp.abs(code)
    value = ((size & 127) + 128).astype(jnp.float32) * jnp.exp2(((size >> 7) - 134).astype(jnp.float32))
    basis = jnp.where(code == 0, 0.0, jnp.where(code < 0, -value, value)).astype(jnp.bfloat16)
    high, low = halves(momentum_ref[...] + grad_ref[...].astype(jnp.float32))

    def times(a, b):
        return lax.dot_general(a, b, (((1,), (1,)), ((), ())), preferred_element_type=jnp.float32)

    part = times(high, basis) + times(low, basis)

    @pl.when(pl.program_id(0) == 0)
    def _():
        out_ref[...] = part

    @pl.when(pl.program_id(0) > 0)
    def _():
        out_ref[...] += part


def project(momentum, grad, codes):
    rows, cols = momentum.shape
    rank = codes.shape[0]
    block = min(1024, cols)
    wide = pl.BlockSpec((rows, block), lambda i: (0, i))
    return pl.pallas_call(
        project_kernel,
        grid=(cols // block,),
        in_specs=[wide, wide, pl.BlockSpec((rank, block), lambda i: (0, i))],
        out_specs=pl.BlockSpec((rows, rank), lambda i: (0, 0)),
        out_shape=jax.ShapeDtypeStruct((rows, rank), jnp.float32),
        compiler_params=PARAMS,
        cost_estimate=pl.CostEstimate(
            flops=4 * rows * cols * rank, bytes_accessed=rows * cols * 6 + rank * cols * 2, transcendentals=rank * cols
        ),
    )(momentum, grad, codes)


def gram_kernel(column_ref, perm_ref, near_ref, far_ref, unit_ref, proj_ref, scaled_ref, piece_ref, gram_ref):
    rank = gram_ref.shape[0]
    blocks = perm_ref.shape[0]
    size = rank // blocks
    stored = lax.broadcasted_iota(jnp.int32, (rank, rank), 0)
    target = jnp.zeros((rank, rank), jnp.int32)
    for s in range(blocks):
        target = jnp.where(stored // size == s, perm_ref[s] * size + stored % size, target)
    order = (target == lax.broadcasted_iota(jnp.int32, (rank, rank), 1)).astype(jnp.float32)
    proj = jnp.dot(near_ref[...] + far_ref[...], order, precision=HIGH, preferred_element_type=jnp.float32)
    proj_ref[...] = proj
    scaled_ref[...] = proj * unit_ref[...]
    gram_ref[...] = lax.dot_general(
        proj, proj, (((0,), (0,)), ((), ())), precision=HIGH, preferred_element_type=jnp.float32
    )
    rows = piece_ref.shape[0]
    piece_ref[...] = gram_ref[pl.ds(pl.multiple_of(column_ref[0] * rows, rows), rows), :]


def gram_parts(column, perm, near, far, unit, columns):
    rows, rank = near.shape
    operands = (near, far, unit)
    return pl.pallas_call(
        gram_kernel,
        grid_spec=pltpu.PrefetchScalarGridSpec(
            num_scalar_prefetch=2,
            grid=(1,),
            in_specs=[whole(x) for x in operands],
            out_specs=[whole(near), whole(near), pl.BlockSpec((rank // columns, rank), lambda *_: (0, 0))],
            scratch_shapes=[pltpu.VMEM((rank, rank), jnp.float32)],
        ),
        out_shape=[
            jax.ShapeDtypeStruct((rows, rank), jnp.float32),
            jax.ShapeDtypeStruct((rows, rank), jnp.float32),
            jax.ShapeDtypeStruct((rank // columns, rank), jnp.float32),
        ],
        compiler_params=PARAMS,
        cost_estimate=pl.CostEstimate(flops=24 * rows * rank * rank, bytes_accessed=rank * rank * 12, transcendentals=0),
    )(column, perm, *operands)


def spread(row):
    return jnp.broadcast_to(row, (TILE, 2 * PANEL))


def panel_inverse(block):
    rows = lax.broadcasted_iota(jnp.int32, (PANEL, PANEL), 0)
    cols = lax.broadcasted_iota(jnp.int32, (PANEL, PANEL), 1)
    both = jnp.concatenate([block, (rows == cols).astype(jnp.float32)], axis=1)
    count = PANEL // TILE
    tiles = [both[TILE * i : TILE * (i + 1)] for i in range(count)]
    sub = lax.broadcasted_iota(jnp.int32, (TILE, 2 * PANEL), 0)
    done = []
    for k in range(count):
        columns = [
            [spread(tiles[i][:, TILE * k + j : TILE * k + j + 1]) for j in range(TILE)] for i in range(k, count)
        ]
        own, body = columns[0], tiles[k]
        final = jnp.zeros_like(body)
        for j in range(TILE):
            here = sub == j
            pivot = spread(own[j][j : j + 1])
            inverse = 1.0 / pivot
            final = jnp.where(here, body * lax.rsqrt(pivot), final)
            reduced = spread(body[j : j + 1]) * inverse
            body = jnp.where(here, reduced, body - own[j] * reduced)
            for other in range(j + 1, TILE):
                ratio = spread(own[other][j : j + 1]) * inverse
                own[other] = jnp.where(here, ratio, own[other] - own[j] * ratio)
        done.append(final)
        for i in range(k + 1, count):
            tile = tiles[i]
            for j in range(TILE):
                tile = tile - columns[i - k][j] * spread(body[j : j + 1])
            tiles[i] = tile
    return jnp.concatenate(done, axis=0)[:, PANEL:]


def factor_kernel(place_ref, *refs):
    piece_refs, (out_ref, work) = refs[:-2], refs[-2:]
    rank = out_ref.shape[0]
    for k, piece_ref in enumerate(piece_refs):
        size = piece_ref.shape[0]
        work[pl.ds(pl.multiple_of(place_ref[k] * size, size), size), :rank] = piece_ref[...]
    rows = lax.broadcasted_iota(jnp.int32, (rank, rank), 0)
    cols = lax.broadcasted_iota(jnp.int32, (rank, rank), 1)
    work[:, rank:] = (rows == cols).astype(jnp.float32)
    for start in range(0, rank, PANEL):
        end = start + PANEL
        inverse = panel_inverse(work[start:end, start:end])
        scaled = jnp.dot(inverse, work[start:end, :], precision=HIGH, preferred_element_type=jnp.float32)
        out_ref[start:end, :] = scaled[:, rank:]
        if end < rank:
            low = end // 128 * 128
            change = lax.dot_general(
                scaled[:, low:rank],
                scaled,
                (((0,), (0,)), ((), ())),
                precision=HIGH,
                preferred_element_type=jnp.float32,
            )
            work[end:, :] = work[end:, :] - change[end - low :, :]


def factor_inverse(places, pieces):
    rank = pieces[0].shape[1]
    return pl.pallas_call(
        factor_kernel,
        grid_spec=pltpu.PrefetchScalarGridSpec(
            num_scalar_prefetch=1,
            grid=(1,),
            in_specs=[whole(x) for x in pieces],
            out_specs=pl.BlockSpec((rank, rank), lambda *_: (0, 0)),
            scratch_shapes=[pltpu.VMEM((rank, 2 * rank), jnp.float32)],
        ),
        out_shape=jax.ShapeDtypeStruct((rank, rank), jnp.float32),
        compiler_params=PARAMS,
        cost_estimate=pl.CostEstimate(flops=6 * 2 * rank**3, bytes_accessed=2 * rank * rank * 4, transcendentals=rank),
    )(places, *pieces)


def unit_of(exponent, mantissa):
    return mantissa * jnp.exp2(exponent - 13.0)


def encode_kernel(source_ref, scaled_ref, inverse_ref, proj_ref, code_ref, ortho_ref, mixed_ref):
    def times(a, b):
        return lax.dot_general(a, b, (((0,), (0,)), ((), ())), preferred_element_type=jnp.float32)

    source_high, source_low = halves(source_ref[...].astype(jnp.int32).astype(jnp.float32))
    scaled_high, scaled_low = halves(scaled_ref[...])
    part = times(source_high, scaled_high) + (times(source_low, scaled_high) + times(source_high, scaled_low))
    first, last = pl.program_id(0) == 0, pl.program_id(0) == pl.num_programs(0) - 1

    @pl.when(first)
    def _():
        mixed_ref[...] = part

    @pl.when(jnp.logical_not(first))
    def _():
        mixed_ref[...] += part

    @pl.when(last)
    def _():
        inverse = inverse_ref[...]
        ortho_ref[...] = dot_rows(proj_ref[...], inverse)
        right = dot_rows(mixed_ref[...], inverse)
        rows, rank = right.shape
        square = jnp.maximum(jnp.sum(right * right, axis=0, keepdims=True), 1e-34)
        square_exponent = jnp.floor(jnp.log2(square))
        fine = square * jnp.exp2(13.0 - square_exponent)
        square_high = jnp.floor(fine)
        square_low = jnp.floor((fine - square_high) * 16384.0)
        top = jnp.maximum(jnp.max(jnp.abs(right), axis=0, keepdims=True), 1e-28) * (1.0 / TOP)
        exponent = jnp.floor(jnp.log2(top))
        mantissa = jnp.floor(top * jnp.exp2(13.0 - exponent)) + 1.0
        scaled = right * (1.0 / unit_of(exponent, mantissa))
        code_ref[:rows, :] = jnp.floor(scaled + 0.5).astype(jnp.int32).astype(jnp.int16)
        place = lax.broadcasted_iota(jnp.int32, (HEAD, rank), 0)
        head = jnp.zeros((HEAD, rank), jnp.float32)
        for k, row in enumerate((exponent, mantissa, square_exponent, square_high, square_low)):
            head = jnp.where(place == k, row, head)
        code_ref[rows:, :] = head.astype(jnp.int32).astype(jnp.int16)


def encode(source, scaled, inverse_low, projected):
    total, share = source.shape
    rank = scaled.shape[1]
    block = min(512, total)
    return pl.pallas_call(
        encode_kernel,
        grid=(total // block,),
        in_specs=[
            pl.BlockSpec((block, share), lambda i: (i, 0)),
            pl.BlockSpec((block, rank), lambda i: (i, 0)),
            whole(inverse_low),
            whole(projected),
        ],
        out_specs=[pl.BlockSpec((share + HEAD, rank), lambda i: (0, 0)), whole(projected)],
        out_shape=[
            jax.ShapeDtypeStruct((share + HEAD, rank), jnp.int16),
            jax.ShapeDtypeStruct(projected.shape, jnp.float32),
        ],
        scratch_shapes=[pltpu.VMEM((share, rank), jnp.float32)],
        compiler_params=PARAMS,
        cost_estimate=pl.CostEstimate(
            flops=6 * total * share * rank, bytes_accessed=total * (share * 2 + rank * 4), transcendentals=0
        ),
    )(source, scaled, inverse_low, projected)


def decode(code_ref):
    code = code_ref[...].astype(jnp.int32).astype(jnp.float32)
    share = code.shape[1] - HEAD
    right = code[:, :share] * unit_of(code[:, share : share + 1], code[:, share + 1 : share + 2])
    return right.reshape(code.shape[0] * share, code.shape[2])


def times_rows(split_ref, right):
    def times(a, b):
        return lax.dot_general(a, b, (((1,), (1,)), ((), ())), preferred_element_type=jnp.float32)

    right_high, right_low = halves(right)
    split = split_ref[...]
    rows = split.shape[0] // 2
    most = times(split, right_high)
    return most[:rows] + (most[rows:] + times(split[:rows], right_low))


def set_split(split_ref, x):
    rows = x.shape[0]

    @pl.when(pl.program_id(0) == 0)
    def _():
        split_ref[:rows], split_ref[rows:] = halves(x)


def momentum_kernel(momentum_ref, grad_ref, code_ref, ortho_ref, next_ref, split_ref):
    set_split(split_ref, -KEEP_SHARE * ortho_ref[...])
    change = times_rows(split_ref, decode(code_ref))
    next_ref[...] = momentum_ref[...] + grad_ref[...].astype(jnp.float32) + change


def update_kernel(gain, code_ref, ortho_ref, scale_ref, basis_ref, update_ref, split_ref):
    set_split(split_ref, gain * ortho_ref[...])
    basis = decode(code_ref) * scale_ref[...]
    basis_ref[...] = basis
    update_ref[...] = times_rows(split_ref, basis).astype(jnp.bfloat16)


def finish(momentum, grad, codes, orthonormal, scale, gain):
    rows, cols = momentum.shape
    shares, share, rank = codes.shape
    share -= HEAD
    group = max(1, min(1024 // share, shares))
    block = group * share
    wide = pl.BlockSpec((rows, block), lambda i: (0, i))
    tall = pl.BlockSpec((block, rank), lambda i: (i, 0))
    coded = pl.BlockSpec((group, share + HEAD, rank), lambda i: (i, 0, 0))
    split = [pltpu.VMEM((2 * rows, rank), jnp.bfloat16)]
    flops = 6 * rows * cols * rank
    momentum_next = pl.pallas_call(
        momentum_kernel,
        grid=(cols // block,),
        in_specs=[wide, wide, coded, whole(orthonormal)],
        out_specs=wide,
        out_shape=jax.ShapeDtypeStruct((rows, cols), jnp.float32),
        scratch_shapes=split,
        compiler_params=PARAMS,
        cost_estimate=pl.CostEstimate(
            flops=flops, bytes_accessed=rows * cols * 10 + cols * rank * 2, transcendentals=0
        ),
    )(momentum, grad, codes, orthonormal)
    q_next, update = pl.pallas_call(
        functools.partial(update_kernel, gain),
        grid=(cols // block,),
        in_specs=[coded, whole(orthonormal), whole(scale)],
        out_specs=[tall, wide],
        out_shape=[
            jax.ShapeDtypeStruct((cols, rank), jnp.float32),
            jax.ShapeDtypeStruct((rows, cols), jnp.bfloat16),
        ],
        scratch_shapes=split,
        compiler_params=PARAMS,
        cost_estimate=pl.CostEstimate(flops=flops, bytes_accessed=rows * cols * 2 + cols * rank * 6, transcendentals=0),
    )(codes, orthonormal, scale)
    return momentum_next, q_next, update


def on_device(momentum, grad, q_stored, perm):
    block_rows = q_stored.shape[0]
    num_blocks = lax.axis_size("fsdp")
    num_cols = lax.axis_size("tp")
    rank_total = block_rows * num_blocks
    rows, cols = momentum.shape
    row_total, col_total = rows * num_blocks, cols * num_cols
    column = lax.axis_index("tp")

    combined = momentum + grad.astype(jnp.float32)
    unit = jnp.maximum(jnp.max(jnp.abs(combined), axis=1, keepdims=True), 1e-28) * (1.0 / TOP)
    codes = jnp.floor(combined * (1.0 / unit) + 0.5).astype(jnp.int16)
    codes = codes.reshape(rows, num_blocks, cols // num_blocks).transpose(1, 0, 2)

    basis, codes = lax.optimization_barrier((code_basis(q_stored), codes))
    basis = lax.all_gather(basis, "fsdp", axis=0, tiled=True)
    codes, basis = lax.optimization_barrier((codes, basis))
    codes = lax.all_to_all(codes, "fsdp", split_axis=0, concat_axis=0).reshape(row_total, cols // num_blocks)

    near = project(momentum, grad, basis)
    step = 1
    while 2 * step < num_cols:
        near = near + exchange(near, "tp", step)
        step *= 2
    far = exchange(near, "tp", step)
    projected, scaled, piece = gram_parts(column.reshape(1), perm, near, far, unit, num_cols)

    all_scaled = lax.all_gather(scaled, "fsdp", axis=0, tiled=True)
    piece = quad_sum(piece, "fsdp", 2)
    piece = piece + exchange(piece, "fsdp", 1)
    pieces = [piece] + [exchange(piece, "tp", k) for k in range(1, num_cols)]
    places = jnp.stack([column ^ k for k in range(num_cols)]).astype(jnp.int32)
    inverse_low = factor_inverse(places, pieces)
    code, orthonormal = encode(codes, all_scaled, inverse_low, projected)
    gathered = lax.all_gather(code, "fsdp", axis=0)
    share = codes.shape[1]
    head = gathered[:, share : share + 5].astype(jnp.float32)
    parts = (head[:, 3] + head[:, 4] * (1.0 / 16384.0)) * jnp.exp2(head[:, 2] - 13.0)
    squares = quad_sum(jnp.sum(parts, axis=0, keepdims=True), "tp")
    scale = lax.rsqrt(squares / col_total + EPSILON)
    return tuple(finish(momentum, grad, gathered, orthonormal, scale, math.sqrt(row_total / rank_total)))


def solution(mesh):
    return jax.shard_map(
        on_device,
        mesh=mesh,
        in_specs=(P("fsdp", "tp"), P("fsdp", "tp"), P("fsdp", "tp"), P()),
        out_specs=(P("fsdp", "tp"), P("tp", None), P("fsdp", "tp")),
        check_vma=False,
    )
```

```python
import functools
import math

import jax
import jax.numpy as jnp
from jax import lax
from jax.experimental import pallas as pl
from jax.experimental.pallas import tpu as pltpu
from jax.sharding import PartitionSpec as P

EPSILON = 1e-06
KEEP_SHARE = 0.5
HIGH = lax.Precision.HIGHEST
PANEL = 64
TILE = 8
HEAD = 16
TOP = 32766.0
PARAMS = pltpu.CompilerParams(vmem_limit_bytes=40 * 1024 * 1024)
STREAM = pltpu.CompilerParams(vmem_limit_bytes=54 * 1024 * 1024)


def halves(x):
    high = x.astype(jnp.bfloat16)
    return high, (x - high.astype(jnp.float32)).astype(jnp.bfloat16)


def exchange(x, axis, k):
    return lax.ppermute(x, axis, [(i, i ^ k) for i in range(lax.axis_size(axis))])


def butterfly_sum(x, axis, step=1):
    while step < lax.axis_size(axis):
        x = x + exchange(x, axis, step)
        step *= 2
    return x


def quad_sum(x, axis, step=1):
    if lax.axis_size(axis) != 4 * step:
        return butterfly_sum(x, axis, step)
    near, far, across = [exchange(x, axis, k * step) for k in range(1, 4)]
    return (x + near) + (far + across)


def whole(x):
    return pl.BlockSpec(x.shape, lambda *_: (0,) * len(x.shape))


def dot_rows(a, b):
    return lax.dot_general(a, b, (((1,), (1,)), ((), ())), precision=HIGH, preferred_element_type=jnp.float32)


def code_basis(basis):
    value = basis.astype(jnp.float32)
    size = jnp.abs(value)
    normal = size >= 2.0**-126
    exponent = jnp.floor(jnp.log2(jnp.where(normal, size, 1.0)))
    code = 128.0 * (exponent + 126.0) + jnp.floor(128.0 * (size * jnp.exp2(-exponent)) + 0.5)
    return jnp.where(normal, jnp.where(value < 0.0, -code, code), 0.0).astype(jnp.int16)


def project_kernel(momentum_ref, grad_ref, code_ref, out_ref):
    code = code_ref[...].astype(jnp.int32)
    size = jnp.abs(code)
    value = ((size & 127) + 128).astype(jnp.float32) * jnp.exp2(((size >> 7) - 134).astype(jnp.float32))
    basis = jnp.where(code == 0, 0.0, jnp.where(code < 0, -value, value)).astype(jnp.bfloat16)
    high, low = halves(momentum_ref[...] + grad_ref[...].astype(jnp.float32))

    def times(a, b):
        return lax.dot_general(a, b, (((1,), (1,)), ((), ())), preferred_element_type=jnp.float32)

    part = times(high, basis) + times(low, basis)

    @pl.when(pl.program_id(0) == 0)
    def _():
        out_ref[...] = part

    @pl.when(pl.program_id(0) > 0)
    def _():
        out_ref[...] += part


def project(momentum, grad, codes):
    rows, cols = momentum.shape
    rank = codes.shape[0]
    block = min(1024, cols)
    wide = pl.BlockSpec((rows, block), lambda i: (0, i))
    return pl.pallas_call(
        project_kernel,
        grid=(cols // block,),
        in_specs=[wide, wide, pl.BlockSpec((rank, block), lambda i: (0, i))],
        out_specs=pl.BlockSpec((rows, rank), lambda i: (0, 0)),
        out_shape=jax.ShapeDtypeStruct((rows, rank), jnp.float32),
        compiler_params=PARAMS,
        cost_estimate=pl.CostEstimate(
            flops=4 * rows * cols * rank, bytes_accessed=rows * cols * 6 + rank * cols * 2, transcendentals=rank * cols
        ),
    )(momentum, grad, codes)


def gram_kernel(column_ref, perm_ref, near_ref, far_ref, unit_ref, proj_ref, scaled_ref, piece_ref, gram_ref):
    rank = gram_ref.shape[0]
    blocks = perm_ref.shape[0]
    size = rank // blocks
    stored = lax.broadcasted_iota(jnp.int32, (rank, rank), 0)
    target = jnp.zeros((rank, rank), jnp.int32)
    for s in range(blocks):
        target = jnp.where(stored // size == s, perm_ref[s] * size + stored % size, target)
    order = (target == lax.broadcasted_iota(jnp.int32, (rank, rank), 1)).astype(jnp.float32)
    proj = jnp.dot(near_ref[...] + far_ref[...], order, precision=HIGH, preferred_element_type=jnp.float32)
    proj_ref[...] = proj
    scaled_ref[...] = proj * unit_ref[...]
    gram_ref[...] = lax.dot_general(
        proj, proj, (((0,), (0,)), ((), ())), precision=HIGH, preferred_element_type=jnp.float32
    )
    rows = piece_ref.shape[0]
    piece_ref[...] = gram_ref[pl.ds(pl.multiple_of(column_ref[0] * rows, rows), rows), :]


def gram_parts(column, perm, near, far, unit, columns):
    rows, rank = near.shape
    operands = (near, far, unit)
    return pl.pallas_call(
        gram_kernel,
        grid_spec=pltpu.PrefetchScalarGridSpec(
            num_scalar_prefetch=2,
            grid=(1,),
            in_specs=[whole(x) for x in operands],
            out_specs=[whole(near), whole(near), pl.BlockSpec((rank // columns, rank), lambda *_: (0, 0))],
            scratch_shapes=[pltpu.VMEM((rank, rank), jnp.float32)],
        ),
        out_shape=[
            jax.ShapeDtypeStruct((rows, rank), jnp.float32),
            jax.ShapeDtypeStruct((rows, rank), jnp.float32),
            jax.ShapeDtypeStruct((rank // columns, rank), jnp.float32),
        ],
        compiler_params=PARAMS,
        cost_estimate=pl.CostEstimate(flops=24 * rows * rank * rank, bytes_accessed=rank * rank * 12, transcendentals=0),
    )(column, perm, *operands)


def spread(row):
    return jnp.broadcast_to(row, (TILE, 2 * PANEL))


def panel_inverse(block):
    rows = lax.broadcasted_iota(jnp.int32, (PANEL, PANEL), 0)
    cols = lax.broadcasted_iota(jnp.int32, (PANEL, PANEL), 1)
    both = jnp.concatenate([block, (rows == cols).astype(jnp.float32)], axis=1)
    count = PANEL // TILE
    tiles = [both[TILE * i : TILE * (i + 1)] for i in range(count)]
    sub = lax.broadcasted_iota(jnp.int32, (TILE, 2 * PANEL), 0)
    done = []
    for k in range(count):
        columns = [
            [spread(tiles[i][:, TILE * k + j : TILE * k + j + 1]) for j in range(TILE)] for i in range(k, count)
        ]
        own, body = columns[0], tiles[k]
        final = jnp.zeros_like(body)
        for j in range(TILE):
            here = sub == j
            pivot = spread(own[j][j : j + 1])
            inverse = 1.0 / pivot
            final = jnp.where(here, body * lax.rsqrt(pivot), final)
            reduced = spread(body[j : j + 1]) * inverse
            body = jnp.where(here, reduced, body - own[j] * reduced)
            for other in range(j + 1, TILE):
                ratio = spread(own[other][j : j + 1]) * inverse
                own[other] = jnp.where(here, ratio, own[other] - own[j] * ratio)
        done.append(final)
        for i in range(k + 1, count):
            tile = tiles[i]
            for j in range(TILE):
                tile = tile - columns[i - k][j] * spread(body[j : j + 1])
            tiles[i] = tile
    return jnp.concatenate(done, axis=0)[:, PANEL:]


def factor_kernel(place_ref, *refs):
    piece_refs, (out_ref, work) = refs[:-2], refs[-2:]
    rank = out_ref.shape[0]
    for k, piece_ref in enumerate(piece_refs):
        size = piece_ref.shape[0]
        work[pl.ds(pl.multiple_of(place_ref[k] * size, size), size), :rank] = piece_ref[...]
    rows = lax.broadcasted_iota(jnp.int32, (rank, rank), 0)
    cols = lax.broadcasted_iota(jnp.int32, (rank, rank), 1)
    work[:, rank:] = (rows == cols).astype(jnp.float32)
    for start in range(0, rank, PANEL):
        end = start + PANEL
        inverse = panel_inverse(work[start:end, start:end])
        scaled = jnp.dot(inverse, work[start:end, :], precision=HIGH, preferred_element_type=jnp.float32)
        out_ref[start:end, :] = scaled[:, rank:]
        if end < rank:
            low = end // 128 * 128
            change = lax.dot_general(
                scaled[:, low:rank],
                scaled,
                (((0,), (0,)), ((), ())),
                precision=HIGH,
                preferred_element_type=jnp.float32,
            )
            work[end:, :] = work[end:, :] - change[end - low :, :]


def factor_inverse(places, pieces):
    rank = pieces[0].shape[1]
    return pl.pallas_call(
        factor_kernel,
        grid_spec=pltpu.PrefetchScalarGridSpec(
            num_scalar_prefetch=1,
            grid=(1,),
            in_specs=[whole(x) for x in pieces],
            out_specs=pl.BlockSpec((rank, rank), lambda *_: (0, 0)),
            scratch_shapes=[pltpu.VMEM((rank, 2 * rank), jnp.float32)],
        ),
        out_shape=jax.ShapeDtypeStruct((rank, rank), jnp.float32),
        compiler_params=PARAMS,
        cost_estimate=pl.CostEstimate(flops=6 * 2 * rank**3, bytes_accessed=2 * rank * rank * 4, transcendentals=rank),
    )(places, *pieces)


def unit_of(exponent, mantissa):
    return mantissa * jnp.exp2(exponent - 13.0)


def encode_kernel(source_ref, scaled_ref, inverse_ref, proj_ref, code_ref, ortho_ref, mixed_ref):
    def times(a, b):
        return lax.dot_general(a, b, (((0,), (0,)), ((), ())), preferred_element_type=jnp.float32)

    source_high, source_low = halves(source_ref[...].astype(jnp.int32).astype(jnp.float32))
    scaled_high, scaled_low = halves(scaled_ref[...])
    part = times(source_high, scaled_high) + (times(source_low, scaled_high) + times(source_high, scaled_low))
    first, last = pl.program_id(0) == 0, pl.program_id(0) == pl.num_programs(0) - 1

    @pl.when(first)
    def _():
        mixed_ref[...] = part

    @pl.when(jnp.logical_not(first))
    def _():
        mixed_ref[...] += part

    @pl.when(last)
    def _():
        inverse = inverse_ref[...]
        ortho_ref[...] = dot_rows(proj_ref[...], inverse)
        right = dot_rows(mixed_ref[...], inverse)
        rows, rank = right.shape
        square = jnp.maximum(jnp.sum(right * right, axis=0, keepdims=True), 1e-34)
        square_exponent = jnp.floor(jnp.log2(square))
        fine = square * jnp.exp2(13.0 - square_exponent)
        square_high = jnp.floor(fine)
        square_low = jnp.floor((fine - square_high) * 16384.0)
        top = jnp.maximum(jnp.max(jnp.abs(right), axis=0, keepdims=True), 1e-28) * (1.0 / TOP)
        exponent = jnp.floor(jnp.log2(top))
        mantissa = jnp.floor(top * jnp.exp2(13.0 - exponent)) + 1.0
        scaled = right * (1.0 / unit_of(exponent, mantissa))
        code_ref[:rows, :] = jnp.floor(scaled + 0.5).astype(jnp.int32).astype(jnp.int16)
        place = lax.broadcasted_iota(jnp.int32, (HEAD, rank), 0)
        head = jnp.zeros((HEAD, rank), jnp.float32)
        for k, row in enumerate((exponent, mantissa, square_exponent, square_high, square_low)):
            head = jnp.where(place == k, row, head)
        code_ref[rows:, :] = head.astype(jnp.int32).astype(jnp.int16)


def encode(source, scaled, inverse_low, projected):
    total, share = source.shape
    rank = scaled.shape[1]
    block = min(512, total)
    return pl.pallas_call(
        encode_kernel,
        grid=(total // block,),
        in_specs=[
            pl.BlockSpec((block, share), lambda i: (i, 0)),
            pl.BlockSpec((block, rank), lambda i: (i, 0)),
            whole(inverse_low),
            whole(projected),
        ],
        out_specs=[pl.BlockSpec((share + HEAD, rank), lambda i: (0, 0)), whole(projected)],
        out_shape=[
            jax.ShapeDtypeStruct((share + HEAD, rank), jnp.int16),
            jax.ShapeDtypeStruct(projected.shape, jnp.float32),
        ],
        scratch_shapes=[pltpu.VMEM((share, rank), jnp.float32)],
        compiler_params=STREAM,
        cost_estimate=pl.CostEstimate(
            flops=6 * total * share * rank, bytes_accessed=total * (share * 2 + rank * 4), transcendentals=0
        ),
    )(source, scaled, inverse_low, projected)


def decode(code_ref):
    code = code_ref[...].astype(jnp.int32).astype(jnp.float32)
    share = code.shape[1] - HEAD
    right = code[:, :share] * unit_of(code[:, share : share + 1], code[:, share + 1 : share + 2])
    return right.reshape(code.shape[0] * share, code.shape[2])


def times_rows(split_ref, right):
    def times(a, b):
        return lax.dot_general(a, b, (((1,), (1,)), ((), ())), preferred_element_type=jnp.float32)

    right_high, right_low = halves(right)
    split = split_ref[...]
    rows = split.shape[0] // 2
    most = times(split, right_high)
    return most[:rows] + (most[rows:] + times(split[:rows], right_low))


def set_split(split_ref, x):
    rows = x.shape[0]

    @pl.when(pl.program_id(0) == 0)
    def _():
        split_ref[:rows], split_ref[rows:] = halves(x)


def momentum_kernel(momentum_ref, grad_ref, code_ref, ortho_ref, next_ref, split_ref):
    set_split(split_ref, -KEEP_SHARE * ortho_ref[...])
    change = times_rows(split_ref, decode(code_ref))
    next_ref[...] = momentum_ref[...] + grad_ref[...].astype(jnp.float32) + change


def update_kernel(gain, code_ref, ortho_ref, scale_ref, basis_ref, update_ref, split_ref):
    set_split(split_ref, gain * ortho_ref[...])
    basis = decode(code_ref) * scale_ref[...]
    basis_ref[...] = basis
    update_ref[...] = times_rows(split_ref, basis).astype(jnp.bfloat16)


def finish(momentum, grad, codes, orthonormal, scale, gain):
    rows, cols = momentum.shape
    shares, share, rank = codes.shape
    share -= HEAD
    group = max(1, min(1024 // share, shares))
    block = group * share
    wide = pl.BlockSpec((rows, block), lambda i: (0, i))
    tall = pl.BlockSpec((block, rank), lambda i: (i, 0))
    coded = pl.BlockSpec((group, share + HEAD, rank), lambda i: (i, 0, 0))
    split = [pltpu.VMEM((2 * rows, rank), jnp.bfloat16)]
    flops = 6 * rows * cols * rank
    momentum_next = pl.pallas_call(
        momentum_kernel,
        grid=(cols // block,),
        in_specs=[wide, wide, coded, whole(orthonormal)],
        out_specs=wide,
        out_shape=jax.ShapeDtypeStruct((rows, cols), jnp.float32),
        scratch_shapes=split,
        compiler_params=PARAMS,
        cost_estimate=pl.CostEstimate(
            flops=flops, bytes_accessed=rows * cols * 10 + cols * rank * 2, transcendentals=0
        ),
    )(momentum, grad, codes, orthonormal)
    q_next, update = pl.pallas_call(
        functools.partial(update_kernel, gain),
        grid=(cols // block,),
        in_specs=[coded, whole(orthonormal), whole(scale)],
        out_specs=[tall, wide],
        out_shape=[
            jax.ShapeDtypeStruct((cols, rank), jnp.float32),
            jax.ShapeDtypeStruct((rows, cols), jnp.bfloat16),
        ],
        scratch_shapes=split,
        compiler_params=PARAMS,
        cost_estimate=pl.CostEstimate(flops=flops, bytes_accessed=rows * cols * 2 + cols * rank * 6, transcendentals=0),
    )(codes, orthonormal, scale)
    return momentum_next, q_next, update


def on_device(momentum, grad, q_stored, perm):
    block_rows = q_stored.shape[0]
    num_blocks = lax.axis_size("fsdp")
    num_cols = lax.axis_size("tp")
    rank_total = block_rows * num_blocks
    rows, cols = momentum.shape
    row_total, col_total = rows * num_blocks, cols * num_cols
    column = lax.axis_index("tp")

    combined = momentum + grad.astype(jnp.float32)
    unit = jnp.maximum(jnp.max(jnp.abs(combined), axis=1, keepdims=True), 1e-28) * (1.0 / TOP)
    codes = jnp.floor(combined * (1.0 / unit) + 0.5).astype(jnp.int16)
    codes = codes.reshape(rows, num_blocks, cols // num_blocks).transpose(1, 0, 2)

    basis, codes = lax.optimization_barrier((code_basis(q_stored), codes))
    basis = lax.all_gather(basis, "fsdp", axis=0, tiled=True)
    codes, basis = lax.optimization_barrier((codes, basis))
    codes = lax.all_to_all(codes, "fsdp", split_axis=0, concat_axis=0).reshape(row_total, cols // num_blocks)

    near = project(momentum, grad, basis)
    step = 1
    while 2 * step < num_cols:
        near = near + exchange(near, "tp", step)
        step *= 2
    far = exchange(near, "tp", step)
    projected, scaled, piece = gram_parts(column.reshape(1), perm, near, far, unit, num_cols)

    piece = quad_sum(piece, "fsdp", 2)
    piece, scaled, codes = lax.optimization_barrier((piece, scaled, codes))
    all_scaled = lax.all_gather(scaled, "fsdp", axis=0, tiled=True)
    piece = piece + exchange(piece, "fsdp", 1)
    pieces = [piece] + [exchange(piece, "tp", k) for k in range(1, num_cols)]
    places = jnp.stack([column ^ k for k in range(num_cols)]).astype(jnp.int32)
    inverse_low = factor_inverse(places, pieces)
    code, orthonormal = encode(codes, all_scaled, inverse_low, projected)
    gathered = lax.all_gather(code, "fsdp", axis=0)
    share = codes.shape[1]
    head = gathered[:, share : share + 5].astype(jnp.float32)
    parts = (head[:, 3] + head[:, 4] * (1.0 / 16384.0)) * jnp.exp2(head[:, 2] - 13.0)
    squares = quad_sum(jnp.sum(parts, axis=0, keepdims=True), "tp")
    scale = lax.rsqrt(squares / col_total + EPSILON)
    return tuple(finish(momentum, grad, gathered, orthonormal, scale, math.sqrt(row_total / rank_total)))


def solution(mesh):
    return jax.shard_map(
        on_device,
        mesh=mesh,
        in_specs=(P("fsdp", "tp"), P("fsdp", "tp"), P("fsdp", "tp"), P()),
        out_specs=(P("fsdp", "tp"), P("tp", None), P("fsdp", "tp")),
        check_vma=False,
    )
```

```python
import functools
import math

import jax
import jax.numpy as jnp
from jax import lax
from jax.experimental import pallas as pl
from jax.experimental.pallas import tpu as pltpu
from jax.sharding import PartitionSpec as P

EPSILON = 1e-06
KEEP_SHARE = 0.5
HIGH = lax.Precision.HIGHEST
PANEL = 64
TILE = 8
HEAD = 16
TOP = 32766.0
PARAMS = pltpu.CompilerParams(vmem_limit_bytes=40 * 1024 * 1024)


def halves(x):
    high = x.astype(jnp.bfloat16)
    return high, (x - high.astype(jnp.float32)).astype(jnp.bfloat16)


def exchange(x, axis, k):
    return lax.ppermute(x, axis, [(i, i ^ k) for i in range(lax.axis_size(axis))])


def butterfly_sum(x, axis, step=1):
    while step < lax.axis_size(axis):
        x = x + exchange(x, axis, step)
        step *= 2
    return x


def quad_sum(x, axis, step=1):
    if lax.axis_size(axis) != 4 * step:
        return butterfly_sum(x, axis, step)
    near, far, across = [exchange(x, axis, k * step) for k in range(1, 4)]
    return (x + near) + (far + across)


def whole(x):
    return pl.BlockSpec(x.shape, lambda *_: (0,) * len(x.shape))


def dot_rows(a, b):
    return lax.dot_general(a, b, (((1,), (1,)), ((), ())), precision=HIGH, preferred_element_type=jnp.float32)


def unit_of(exponent, mantissa):
    return mantissa * jnp.exp2(exponent - 13.0)


def code_unit(top):
    top = jnp.maximum(top, 1e-28) * (1.0 / TOP)
    exponent = jnp.floor(jnp.log2(top))
    return exponent, jnp.floor(top * jnp.exp2(13.0 - exponent)) + 1.0


def whole_number(x):
    return x.astype(jnp.int32).astype(jnp.int16)


def set_head(head_ref, *rows):
    place = lax.broadcasted_iota(jnp.int32, head_ref.shape, 0)
    head = jnp.zeros(head_ref.shape, jnp.float32)
    for k, row in enumerate(rows):
        head = jnp.where(place == k, row, head)
    head_ref[...] = whole_number(head)


def code_basis(basis):
    value = basis.astype(jnp.float32)
    size = jnp.abs(value)
    normal = size >= 2.0**-126
    exponent = jnp.floor(jnp.log2(jnp.where(normal, size, 1.0)))
    code = 128.0 * (exponent + 126.0) + jnp.floor(128.0 * (size * jnp.exp2(-exponent)) + 0.5)
    return whole_number(jnp.where(normal, jnp.where(value < 0.0, -code, code), 0.0))


def prepare_kernel(momentum_ref, grad_ref, basis_ref, pack_ref, code_ref):
    rows, cols = momentum_ref.shape
    width = code_ref.shape[-1]
    spans = [slice(i, i + width) for i in range(0, cols, width)]
    combined = lambda span: momentum_ref[:, span] + grad_ref[:, span].astype(jnp.float32)
    top = functools.reduce(jnp.maximum, [jnp.abs(combined(span)) for span in spans])
    exponent, mantissa = code_unit(jnp.max(top, axis=1, keepdims=True))
    inverse = 1.0 / unit_of(exponent, mantissa)
    for k, span in enumerate(spans):
        code_ref[k] = whole_number(jnp.floor(combined(span) * inverse + 0.5))
        pack_ref[:, span] = code_basis(basis_ref[:, span])
    across = lax.broadcasted_iota(jnp.int32, (rows, rows), 0) == lax.broadcasted_iota(jnp.int32, (rows, rows), 1)
    turn = lambda x: jnp.sum(jnp.where(across, x, 0.0), axis=0, keepdims=True)
    set_head(pack_ref.at[:, cols:], turn(exponent), turn(mantissa))


def prepare(momentum, grad, basis, share):
    rows, cols = momentum.shape
    width = share if share % 128 == 0 else cols
    return pl.pallas_call(
        prepare_kernel,
        out_shape=[
            jax.ShapeDtypeStruct((basis.shape[0], cols + rows), jnp.int16),
            jax.ShapeDtypeStruct((cols // width, rows, width), jnp.int16),
        ],
        compiler_params=PARAMS,
        cost_estimate=pl.CostEstimate(flops=10 * rows * cols, bytes_accessed=rows * cols * 8, transcendentals=0),
    )(momentum, grad, basis)


def project_kernel(column_ref, momentum_ref, grad_ref, code_ref, *refs):
    out_refs, total_ref = refs[:-1], refs[-1]
    code = code_ref[...].astype(jnp.int32)
    size = jnp.abs(code)
    value = ((size & 127) + 128).astype(jnp.float32) * jnp.exp2(((size >> 7) - 134).astype(jnp.float32))
    basis = jnp.where(code == 0, 0.0, jnp.where(code < 0, -value, value)).astype(jnp.bfloat16)
    combined = momentum_ref[...] + grad_ref[...].astype(jnp.float32)
    rows = combined.shape[0]
    part = lax.dot_general(
        jnp.concatenate(halves(combined), axis=0),
        basis,
        (((1,), (1,)), ((), ())),
        preferred_element_type=jnp.float32,
    )
    part = part[:rows] + part[rows:]

    @pl.when(pl.program_id(0) == 0)
    def _():
        total_ref[...] = part

    @pl.when(pl.program_id(0) > 0)
    def _():
        total_ref[...] += part

    @pl.when(pl.program_id(0) == pl.num_programs(0) - 1)
    def _():
        for k, out_ref in enumerate(out_refs):
            piece = out_ref.shape[0]
            out_ref[...] = total_ref[pl.ds(pl.multiple_of((column_ref[0] ^ k) * piece, piece), piece), :]


def project(column, momentum, grad, codes, columns):
    rows, cols = momentum.shape
    rank = codes.shape[0]
    block = min(1024, cols)
    wide = pl.BlockSpec((rows, block), lambda i, column: (0, i))
    return pl.pallas_call(
        project_kernel,
        grid_spec=pltpu.PrefetchScalarGridSpec(
            num_scalar_prefetch=1,
            grid=(cols // block,),
            in_specs=[wide, wide, pl.BlockSpec((rank, block), lambda i, column: (0, i))],
            out_specs=[pl.BlockSpec((rows // columns, rank), lambda i, column: (0, 0))] * columns,
            scratch_shapes=[pltpu.VMEM((rows, rank), jnp.float32)],
        ),
        out_shape=[jax.ShapeDtypeStruct((rows // columns, rank), jnp.float32)] * columns,
        compiler_params=PARAMS,
        cost_estimate=pl.CostEstimate(
            flops=4 * rows * cols * rank, bytes_accessed=rows * cols * 6 + rank * cols * 2, transcendentals=rank * cols
        ),
    )(column, momentum, grad, codes)


def pack_kernel(perm_ref, *refs):
    part_refs, out_ref = refs[:-1], refs[-1]
    rows, rank = part_refs[0].shape
    blocks = perm_ref.shape[0]
    size = rank // blocks
    stored = lax.broadcasted_iota(jnp.int32, (rank, rank), 0)
    target = jnp.zeros((rank, rank), jnp.int32)
    for s in range(blocks):
        target = jnp.where(stored // size == s, perm_ref[s] * size + stored % size, target)
    order = (target == lax.broadcasted_iota(jnp.int32, (rank, rank), 1)).astype(jnp.float32)
    total = functools.reduce(jnp.add, [ref[...] for ref in part_refs])
    total = jnp.dot(total, order, precision=HIGH, preferred_element_type=jnp.float32)
    exponent, mantissa = code_unit(jnp.max(jnp.abs(total), axis=0, keepdims=True))
    value = total * (1.0 / unit_of(exponent, mantissa))
    high = jnp.floor(value + 0.5)
    out_ref[:rows] = whole_number(high)
    out_ref[rows : 2 * rows] = whole_number(jnp.floor((value - high) * 32768.0 + 0.5))
    set_head(out_ref.at[2 * rows :], exponent, mantissa)


def pack(perm, parts):
    rows, rank = parts[0].shape
    return pl.pallas_call(
        pack_kernel,
        grid_spec=pltpu.PrefetchScalarGridSpec(
            num_scalar_prefetch=1,
            grid=(1,),
            in_specs=[whole(x) for x in parts],
            out_specs=pl.BlockSpec((2 * rows + HEAD, rank), lambda *_: (0, 0)),
        ),
        out_shape=jax.ShapeDtypeStruct((2 * rows + HEAD, rank), jnp.int16),
        compiler_params=PARAMS,
        cost_estimate=pl.CostEstimate(flops=12 * rows * rank * rank, bytes_accessed=rank * rank * 4, transcendentals=0),
    )(perm, *parts)


def spread(row):
    return jnp.broadcast_to(row, (TILE, 2 * PANEL))


def panel_inverse(block):
    rows = lax.broadcasted_iota(jnp.int32, (PANEL, PANEL), 0)
    cols = lax.broadcasted_iota(jnp.int32, (PANEL, PANEL), 1)
    both = jnp.concatenate([block, (rows == cols).astype(jnp.float32)], axis=1)
    count = PANEL // TILE
    tiles = [both[TILE * i : TILE * (i + 1)] for i in range(count)]
    sub = lax.broadcasted_iota(jnp.int32, (TILE, 2 * PANEL), 0)
    done = []
    for k in range(count):
        columns = [
            [spread(tiles[i][:, TILE * k + j : TILE * k + j + 1]) for j in range(TILE)] for i in range(k, count)
        ]
        own, body = list(columns[0]), tiles[k]
        final = jnp.zeros_like(body)
        for j in range(0, TILE, 2):
            first, second = sub == j, sub == j + 1
            a, b, c = spread(own[j][j : j + 1]), spread(own[j + 1][j : j + 1]), spread(own[j + 1][j + 1 : j + 2])
            minor = a * c - b * b
            inverse = 1.0 / minor

            def solve(x):
                upper, lower = spread(x[j : j + 1]), spread(x[j + 1 : j + 2])
                return (c * upper - b * lower) * inverse, (a * lower - b * upper) * inverse

            def reduce_rows(x):
                upper, lower = solve(x)
                rest = x - own[j] * upper - own[j + 1] * lower
                return jnp.where(first, upper, jnp.where(second, lower, rest))

            ratio = 1.0 / a
            below = (body - b * ratio * spread(body[j : j + 1])) * lax.rsqrt(minor * ratio)
            final = jnp.where(first, body * lax.rsqrt(a), jnp.where(second, below, final))
            body = reduce_rows(body)
            later = {other: reduce_rows(own[other]) for other in range(j + 2, TILE)}
            for other, column in later.items():
                own[other] = column
        done.append(final)
        for i in range(k + 1, count):
            tile = tiles[i]
            for j in range(TILE):
                tile = tile - columns[i - k][j] * spread(body[j : j + 1])
            tiles[i] = tile
    return jnp.concatenate(done, axis=0)[:, PANEL:]


def lanes_up(x):
    return (x + 127) // 128 * 128


def inverse_factor(gram, out_ref, work):
    rank = gram.shape[0]
    rows = lax.broadcasted_iota(jnp.int32, (rank, rank), 0)
    cols = lax.broadcasted_iota(jnp.int32, (rank, rank), 1)
    diagonal = jnp.where(rows == cols, gram, 0.0)
    scale = lax.rsqrt(jnp.sum(diagonal, axis=0, keepdims=True))
    work[:, :rank] = gram * scale * lax.rsqrt(jnp.sum(diagonal, axis=1, keepdims=True))
    work[:, rank:] = (rows == cols).astype(jnp.float32)
    for start in range(0, rank, PANEL):
        end = start + PANEL
        left, right = start // 128 * 128, rank + lanes_up(end)
        inverse = panel_inverse(work[start:end, start:end])
        scaled = jnp.dot(inverse, work[start:end, left:right], precision=HIGH, preferred_element_type=jnp.float32)
        out_ref[start:end, : lanes_up(end)] = scaled[:, rank - left :] * scale[:, : lanes_up(end)]
        if lanes_up(end) < rank:
            out_ref[start:end, lanes_up(end) :] = jnp.zeros((PANEL, rank - lanes_up(end)), jnp.float32)
        if end < rank:
            low = end // 128 * 128
            change = lax.dot_general(
                scaled[:, low - left : rank - left],
                scaled[:, low - left :],
                (((0,), (0,)), ((), ())),
                precision=HIGH,
                preferred_element_type=jnp.float32,
            )
            work[end:, low:right] = work[end:, low:right] - change[end - low :, :]


def factor_kernel(code_ref, turned_ref, out_ref, gram_ref, work):
    count, size, rank = code_ref.shape
    size = (size - HEAD) // 2
    code = code_ref[...].astype(jnp.int32).astype(jnp.float32)
    unit = unit_of(code[:, 2 * size : 2 * size + 1], code[:, 2 * size + 1 : 2 * size + 2])
    part = (code[:, :size] + code[:, size : 2 * size] * (1.0 / 32768.0)) * unit
    turned = part.reshape(count * size, rank).T
    turned_ref[...] = turned
    gram = dot_rows(turned, turned)

    @pl.when(pl.program_id(0) == 0)
    def _():
        gram_ref[...] = gram

    @pl.when(pl.program_id(0) > 0)
    def _():
        gram_ref[...] += gram

    @pl.when(pl.program_id(0) == pl.num_programs(0) - 1)
    def _():
        inverse_factor(gram_ref[...], out_ref, work)


def factor(codes):
    devices, size, rank = codes.shape
    rows = (size - HEAD) // 2
    group = 256 // rows
    return pl.pallas_call(
        factor_kernel,
        grid=(devices // group,),
        in_specs=[pl.BlockSpec((group, size, rank), lambda i: (i, 0, 0))],
        out_specs=[pl.BlockSpec((rank, group * rows), lambda i: (0, i)), pl.BlockSpec((rank, rank), lambda i: (0, 0))],
        out_shape=[
            jax.ShapeDtypeStruct((rank, devices * rows), jnp.float32),
            jax.ShapeDtypeStruct((rank, rank), jnp.float32),
        ],
        scratch_shapes=[pltpu.VMEM((rank, rank), jnp.float32), pltpu.VMEM((rank, 2 * rank), jnp.float32)],
        compiler_params=PARAMS,
        cost_estimate=pl.CostEstimate(
            flops=12 * devices * rows * rank * rank, bytes_accessed=devices * size * rank * 4, transcendentals=rank
        ),
    )(codes)


def encode_kernel(place_ref, source_ref, turned_ref, unit_ref, inverse_ref, own_ref, code_ref, ortho_ref, mixed_ref):
    def times(a, b):
        return jnp.dot(a, b, preferred_element_type=jnp.float32)

    def turned_dot(a, b):
        return lax.dot_general(a, b, (((0,), (1,)), ((), ())), precision=HIGH, preferred_element_type=jnp.float32)

    rank = turned_ref.shape[0]
    source_high, source_low = halves(source_ref[...].astype(jnp.int32).astype(jnp.float32))
    scaled_high, scaled_low = halves(turned_ref[...] * unit_ref[...])
    most = times(jnp.concatenate([scaled_high, scaled_low], axis=0), source_high)
    part = most[:rank] + (most[rank:] + times(scaled_high, source_low))
    first, last = pl.program_id(0) == 0, pl.program_id(0) == pl.num_programs(0) - 1

    @pl.when(first)
    def _():
        mixed_ref[...] = part

    @pl.when(jnp.logical_not(first))
    def _():
        mixed_ref[...] += part

    @pl.when(last)
    def _():
        inverse = inverse_ref[...]
        ortho_ref[...] = turned_dot(own_ref[...], inverse)
        right = turned_dot(mixed_ref[...], inverse)
        rows = right.shape[0]
        square = jnp.maximum(jnp.sum(right * right, axis=0, keepdims=True), 1e-34)
        square_exponent = jnp.floor(jnp.log2(square))
        fine = square * jnp.exp2(13.0 - square_exponent)
        square_high = jnp.floor(fine)
        square_low = jnp.floor((fine - square_high) * 16384.0)
        exponent, mantissa = code_unit(jnp.max(jnp.abs(right), axis=0, keepdims=True))
        code_ref[:rows] = whole_number(jnp.floor(right * (1.0 / unit_of(exponent, mantissa)) + 0.5))
        set_head(code_ref.at[rows:], exponent, mantissa, square_exponent, square_high, square_low)


def encode(place, source, turned, unit, inverse_low, rows):
    total, share = source.shape
    rank = turned.shape[0]
    block = min(512, total)
    return pl.pallas_call(
        encode_kernel,
        grid_spec=pltpu.PrefetchScalarGridSpec(
            num_scalar_prefetch=1,
            grid=(total // block,),
            in_specs=[
                pl.BlockSpec((block, share), lambda i, place: (i, 0)),
                pl.BlockSpec((rank, block), lambda i, place: (0, i)),
                pl.BlockSpec((1, block), lambda i, place: (0, i)),
                whole(inverse_low),
                pl.BlockSpec((rank, rows), lambda i, place: (0, place[0])),
            ],
            out_specs=[
                pl.BlockSpec((share + HEAD, rank), lambda i, place: (0, 0)),
                pl.BlockSpec((rows, rank), lambda i, place: (0, 0)),
            ],
            scratch_shapes=[pltpu.VMEM((rank, share), jnp.float32)],
        ),
        out_shape=[
            jax.ShapeDtypeStruct((share + HEAD, rank), jnp.int16),
            jax.ShapeDtypeStruct((rows, rank), jnp.float32),
        ],
        compiler_params=PARAMS,
        cost_estimate=pl.CostEstimate(
            flops=6 * total * share * rank, bytes_accessed=total * (share * 2 + rank * 4), transcendentals=0
        ),
    )(place, source, turned, unit, inverse_low, turned)


def decode(code_ref):
    code = code_ref[...].astype(jnp.int32).astype(jnp.float32)
    share = code.shape[1] - HEAD
    right = code[:, :share] * unit_of(code[:, share : share + 1], code[:, share + 1 : share + 2])
    return right.reshape(code.shape[0] * share, code.shape[2])


def times_rows(split_ref, right):
    def times(a, b):
        return lax.dot_general(a, b, (((1,), (1,)), ((), ())), preferred_element_type=jnp.float32)

    right_high, right_low = halves(right)
    split = split_ref[...]
    rows = split.shape[0] // 2
    most = times(split, right_high)
    return most[:rows] + (most[rows:] + times(split[:rows], right_low))


def set_split(split_ref, x):
    rows = x.shape[0]

    @pl.when(pl.program_id(0) == 0)
    def _():
        split_ref[:rows], split_ref[rows:] = halves(x)


def momentum_kernel(momentum_ref, grad_ref, code_ref, ortho_ref, next_ref, split_ref):
    set_split(split_ref, -KEEP_SHARE * ortho_ref[...])
    change = times_rows(split_ref, decode(code_ref))
    next_ref[...] = momentum_ref[...] + grad_ref[...].astype(jnp.float32) + change


def update_kernel(gain, code_ref, ortho_ref, scale_ref, basis_ref, update_ref, split_ref):
    set_split(split_ref, gain * ortho_ref[...])
    basis = decode(code_ref) * scale_ref[...]
    basis_ref[...] = basis
    update_ref[...] = times_rows(split_ref, basis).astype(jnp.bfloat16)


def finish(momentum, grad, codes, orthonormal, scale, gain):
    rows, cols = momentum.shape
    shares, share, rank = codes.shape
    share -= HEAD
    group = max(1, min(1024 // share, shares))
    block = group * share
    wide = pl.BlockSpec((rows, block), lambda i: (0, i))
    tall = pl.BlockSpec((block, rank), lambda i: (i, 0))
    coded = pl.BlockSpec((group, share + HEAD, rank), lambda i: (i, 0, 0))
    split = [pltpu.VMEM((2 * rows, rank), jnp.bfloat16)]
    flops = 6 * rows * cols * rank
    momentum_next = pl.pallas_call(
        momentum_kernel,
        grid=(cols // block,),
        in_specs=[wide, wide, coded, whole(orthonormal)],
        out_specs=wide,
        out_shape=jax.ShapeDtypeStruct((rows, cols), jnp.float32),
        scratch_shapes=split,
        compiler_params=PARAMS,
        cost_estimate=pl.CostEstimate(
            flops=flops, bytes_accessed=rows * cols * 10 + cols * rank * 2, transcendentals=0
        ),
    )(momentum, grad, codes, orthonormal)
    q_next, update = pl.pallas_call(
        functools.partial(update_kernel, gain),
        grid=(cols // block,),
        in_specs=[coded, whole(orthonormal), whole(scale)],
        out_specs=[tall, wide],
        out_shape=[
            jax.ShapeDtypeStruct((cols, rank), jnp.float32),
            jax.ShapeDtypeStruct((rows, cols), jnp.bfloat16),
        ],
        scratch_shapes=split,
        compiler_params=PARAMS,
        cost_estimate=pl.CostEstimate(flops=flops, bytes_accessed=rows * cols * 2 + cols * rank * 6, transcendentals=0),
    )(codes, orthonormal, scale)
    return momentum_next, q_next, update


def on_device(momentum, grad, q_stored, perm):
    block_rows = q_stored.shape[0]
    num_blocks = lax.axis_size("fsdp")
    num_cols = lax.axis_size("tp")
    rank_total = block_rows * num_blocks
    rows, cols = momentum.shape
    row_total, col_total = rows * num_blocks, cols * num_cols
    column = lax.axis_index("tp")
    share = cols // num_blocks

    basis, codes = prepare(momentum, grad, q_stored, share)
    codes = codes.reshape(-1, rows, codes.shape[2] // share, share).swapaxes(1, 2).reshape(num_blocks, rows, share)
    basis = lax.all_gather(basis, "fsdp", axis=0, tiled=True)
    codes, basis = lax.optimization_barrier((codes, basis))
    codes = lax.all_to_all(codes, "fsdp", split_axis=0, concat_axis=0).reshape(row_total, share)
    head = basis.reshape(num_blocks, block_rows, cols + rows)[:, :2, cols:].astype(jnp.float32)
    unit = unit_of(head[:, 0], head[:, 1]).reshape(1, row_total)

    parts = project(column.reshape(1), momentum, grad, basis, num_cols)
    parts = [parts[0]] + [exchange(parts[k], "tp", k) for k in range(1, num_cols)]
    packed = pack(perm, parts)
    if num_blocks * num_cols <= 64:
        packed = lax.all_gather(packed, ("fsdp", "tp"), axis=0)
    else:
        packed = lax.all_gather(lax.all_gather(packed, "tp", axis=0), "fsdp", axis=0, tiled=True)
    packed, codes = lax.optimization_barrier((packed, codes))
    turned, inverse_low = factor(packed)
    code, orthonormal = encode(lax.axis_index("fsdp").reshape(1), codes, turned, unit, inverse_low, rows)
    gathered = lax.all_gather(code, "fsdp", axis=0)
    head = gathered[:, share : share + 5].astype(jnp.float32)
    parts = (head[:, 3] + head[:, 4] * (1.0 / 16384.0)) * jnp.exp2(head[:, 2] - 13.0)
    squares = quad_sum(jnp.sum(parts, axis=0, keepdims=True), "tp")
    scale = lax.rsqrt(squares / col_total + EPSILON)
    return tuple(finish(momentum, grad, gathered, orthonormal, scale, math.sqrt(row_total / rank_total)))


def solution(mesh):
    return jax.shard_map(
        on_device,
        mesh=mesh,
        in_specs=(P("fsdp", "tp"), P("fsdp", "tp"), P("fsdp", "tp"), P()),
        out_specs=(P("fsdp", "tp"), P("tp", None), P("fsdp", "tp")),
        check_vma=False,
    )
```

```python
import functools
import math

import jax
import jax.numpy as jnp
from jax import lax
from jax.experimental import pallas as pl
from jax.experimental.pallas import tpu as pltpu
from jax.sharding import PartitionSpec as P

EPSILON = 1e-06
KEEP_SHARE = 0.5
HIGH = lax.Precision.HIGHEST
PANEL = 64
TILE = 8
HEAD = 16
TOP = 32766.0
PARAMS = pltpu.CompilerParams(vmem_limit_bytes=40 * 1024 * 1024)
STREAM = pltpu.CompilerParams(vmem_limit_bytes=54 * 1024 * 1024)


def halves(x):
    high = x.astype(jnp.bfloat16)
    return high, (x - high.astype(jnp.float32)).astype(jnp.bfloat16)


def exchange(x, axis, k):
    return lax.ppermute(x, axis, [(i, i ^ k) for i in range(lax.axis_size(axis))])


def butterfly_sum(x, axis, step=1):
    while step < lax.axis_size(axis):
        x = x + exchange(x, axis, step)
        step *= 2
    return x


def quad_sum(x, axis, step=1):
    if lax.axis_size(axis) != 4 * step:
        return butterfly_sum(x, axis, step)
    near, far, across = [exchange(x, axis, k * step) for k in range(1, 4)]
    return (x + near) + (far + across)


def whole(x):
    return pl.BlockSpec(x.shape, lambda *_: (0,) * len(x.shape))


def dot_rows(a, b):
    return lax.dot_general(a, b, (((1,), (1,)), ((), ())), precision=HIGH, preferred_element_type=jnp.float32)


def unit_of(exponent, mantissa):
    return mantissa * jnp.exp2(exponent - 13.0)


def code_unit(top):
    top = jnp.maximum(top, 1e-28) * (1.0 / TOP)
    exponent = jnp.floor(jnp.log2(top))
    return exponent, jnp.floor(top * jnp.exp2(13.0 - exponent)) + 1.0


def whole_number(x):
    return x.astype(jnp.int32).astype(jnp.int16)


def set_head(head_ref, *rows):
    place = lax.broadcasted_iota(jnp.int32, head_ref.shape, 0)
    head = jnp.zeros(head_ref.shape, jnp.float32)
    for k, row in enumerate(rows):
        head = jnp.where(place == k, row, head)
    head_ref[...] = whole_number(head)


def code_basis(basis):
    value = basis.astype(jnp.float32)
    size = jnp.abs(value)
    normal = size >= 2.0**-126
    exponent = jnp.floor(jnp.log2(jnp.where(normal, size, 1.0)))
    code = 128.0 * (exponent + 126.0) + jnp.floor(128.0 * (size * jnp.exp2(-exponent)) + 0.5)
    return whole_number(jnp.where(normal, jnp.where(value < 0.0, -code, code), 0.0))


def prepare_kernel(momentum_ref, grad_ref, basis_ref, pack_ref, code_ref):
    rows, cols = momentum_ref.shape
    width = code_ref.shape[-1]
    spans = [slice(i, i + width) for i in range(0, cols, width)]
    combined = lambda span: momentum_ref[:, span] + grad_ref[:, span].astype(jnp.float32)
    top = functools.reduce(jnp.maximum, [jnp.abs(combined(span)) for span in spans])
    exponent, mantissa = code_unit(jnp.max(top, axis=1, keepdims=True))
    inverse = 1.0 / unit_of(exponent, mantissa)
    for k, span in enumerate(spans):
        code_ref[k] = whole_number(jnp.floor(combined(span) * inverse + 0.5))
        pack_ref[:, span] = code_basis(basis_ref[:, span])
    across = lax.broadcasted_iota(jnp.int32, (rows, rows), 0) == lax.broadcasted_iota(jnp.int32, (rows, rows), 1)
    turn = lambda x: jnp.sum(jnp.where(across, x, 0.0), axis=0, keepdims=True)
    set_head(pack_ref.at[:, cols:], turn(exponent), turn(mantissa))


def prepare(momentum, grad, basis, share):
    rows, cols = momentum.shape
    width = share if share % 128 == 0 else cols
    return pl.pallas_call(
        prepare_kernel,
        out_shape=[
            jax.ShapeDtypeStruct((basis.shape[0], cols + rows), jnp.int16),
            jax.ShapeDtypeStruct((cols // width, rows, width), jnp.int16),
        ],
        compiler_params=STREAM,
        cost_estimate=pl.CostEstimate(flops=10 * rows * cols, bytes_accessed=rows * cols * 8, transcendentals=0),
    )(momentum, grad, basis)


def project_kernel(momentum_ref, grad_ref, code_ref, out_ref):
    code = code_ref[...].astype(jnp.int32)
    size = jnp.abs(code)
    value = ((size & 127) + 128).astype(jnp.float32) * jnp.exp2(((size >> 7) - 134).astype(jnp.float32))
    basis = jnp.where(code == 0, 0.0, jnp.where(code < 0, -value, value)).astype(jnp.bfloat16)
    combined = momentum_ref[...] + grad_ref[...].astype(jnp.float32)
    rows = combined.shape[0]
    part = lax.dot_general(
        jnp.concatenate(halves(combined), axis=0),
        basis,
        (((1,), (1,)), ((), ())),
        preferred_element_type=jnp.float32,
    )
    part = part[:rows] + part[rows:]

    @pl.when(pl.program_id(0) == 0)
    def _():
        out_ref[...] = part

    @pl.when(pl.program_id(0) > 0)
    def _():
        out_ref[...] += part


def project(momentum, grad, codes):
    rows, cols = momentum.shape
    rank = codes.shape[0]
    block = min(1024, cols)
    wide = pl.BlockSpec((rows, block), lambda i: (0, i))
    return pl.pallas_call(
        project_kernel,
        grid=(cols // block,),
        in_specs=[wide, wide, pl.BlockSpec((rank, block), lambda i: (0, i))],
        out_specs=pl.BlockSpec((rows, rank), lambda i: (0, 0)),
        out_shape=jax.ShapeDtypeStruct((rows, rank), jnp.float32),
        compiler_params=STREAM,
        cost_estimate=pl.CostEstimate(
            flops=4 * rows * cols * rank, bytes_accessed=rows * cols * 6 + rank * cols * 2, transcendentals=rank * cols
        ),
    )(momentum, grad, codes)


def pack_kernel(perm_ref, *refs):
    part_refs, out_ref = refs[:-1], refs[-1]
    rows, rank = part_refs[0].shape
    blocks = perm_ref.shape[0]
    size = rank // blocks
    stored = lax.broadcasted_iota(jnp.int32, (rank, rank), 0)
    target = jnp.zeros((rank, rank), jnp.int32)
    for s in range(blocks):
        target = jnp.where(stored // size == s, perm_ref[s] * size + stored % size, target)
    order = (target == lax.broadcasted_iota(jnp.int32, (rank, rank), 1)).astype(jnp.float32)
    total = functools.reduce(jnp.add, [ref[...] for ref in part_refs])
    total = jnp.dot(total, order, precision=HIGH, preferred_element_type=jnp.float32)
    exponent, mantissa = code_unit(jnp.max(jnp.abs(total), axis=0, keepdims=True))
    value = total * (1.0 / unit_of(exponent, mantissa))
    high = jnp.floor(value + 0.5)
    out_ref[:rows] = whole_number(high)
    out_ref[rows : 2 * rows] = whole_number(jnp.floor((value - high) * 32768.0 + 0.5))
    set_head(out_ref.at[2 * rows :], exponent, mantissa)


def pack(perm, parts):
    rows, rank = parts[0].shape
    return pl.pallas_call(
        pack_kernel,
        grid_spec=pltpu.PrefetchScalarGridSpec(
            num_scalar_prefetch=1,
            grid=(1,),
            in_specs=[whole(x) for x in parts],
            out_specs=pl.BlockSpec((2 * rows + HEAD, rank), lambda *_: (0, 0)),
        ),
        out_shape=jax.ShapeDtypeStruct((2 * rows + HEAD, rank), jnp.int16),
        compiler_params=PARAMS,
        cost_estimate=pl.CostEstimate(flops=12 * rows * rank * rank, bytes_accessed=rank * rank * 4, transcendentals=0),
    )(perm, *parts)


def spread(row):
    return jnp.broadcast_to(row, (TILE, 2 * PANEL))


def panel_inverse(block, band):
    rows = lax.broadcasted_iota(jnp.int32, (PANEL, PANEL), 0)
    cols = lax.broadcasted_iota(jnp.int32, (PANEL, PANEL), 1)
    both = jnp.concatenate([block, (rows == cols).astype(jnp.float32)], axis=1)
    count = PANEL // TILE
    tiles = [both[TILE * i : TILE * (i + 1)] for i in range(count)]
    sub = lax.broadcasted_iota(jnp.int32, (TILE, 2 * PANEL), 0)
    row = lambda k, j: band[k, pl.ds(j, TILE, stride=0), :]
    done = []
    for k in range(count):
        columns = [
            [spread(tiles[i][:, TILE * k + j : TILE * k + j + 1]) for j in range(TILE)] for i in range(k, count)
        ]
        state = list(columns[0]) + [tiles[k]]
        for m, x in enumerate(state):
            band[m] = x
        final = jnp.zeros_like(tiles[k])
        for j in range(0, TILE, 2):
            first, second = sub == j, sub == j + 1
            a, b, c = row(j, j), row(j + 1, j), row(j + 1, j + 1)
            minor = a * c - b * b
            inverse = 1.0 / minor
            left, right = state[j], state[j + 1]
            ratio = 1.0 / a
            below = (state[TILE] - b * ratio * row(TILE, j)) * lax.rsqrt(minor * ratio)
            final = jnp.where(first, state[TILE] * lax.rsqrt(a), jnp.where(second, below, final))
            for m in range(j + 2, TILE + 1):
                upper, lower = row(m, j), row(m, j + 1)
                upper, lower = (c * upper - b * lower) * inverse, (a * lower - b * upper) * inverse
                rest = state[m] - left * upper - right * lower
                state[m] = jnp.where(first, upper, jnp.where(second, lower, rest))
            for m in range(j + 2, TILE + 1):
                band[m] = state[m]
        done.append(final)
        reduced = [row(TILE, j) for j in range(TILE)]
        for i in range(k + 1, count):
            tile = tiles[i]
            for j in range(TILE):
                tile = tile - columns[i - k][j] * reduced[j]
            tiles[i] = tile
    return jnp.concatenate(done, axis=0)[:, PANEL:]


def lanes_up(x):
    return (x + 127) // 128 * 128


def inverse_factor(gram, out_ref, work, band):
    rank = gram.shape[0]
    rows = lax.broadcasted_iota(jnp.int32, (rank, rank), 0)
    cols = lax.broadcasted_iota(jnp.int32, (rank, rank), 1)
    diagonal = jnp.where(rows == cols, gram, 0.0)
    scale = lax.rsqrt(jnp.sum(diagonal, axis=0, keepdims=True))
    work[:, :rank] = gram * scale * lax.rsqrt(jnp.sum(diagonal, axis=1, keepdims=True))
    work[:, rank:] = (rows == cols).astype(jnp.float32)
    for start in range(0, rank, PANEL):
        end = start + PANEL
        left, right = start // 128 * 128, rank + lanes_up(end)
        inverse = panel_inverse(work[start:end, start:end], band)
        scaled = jnp.dot(inverse, work[start:end, left:right], precision=HIGH, preferred_element_type=jnp.float32)
        out_ref[start:end, : lanes_up(end)] = scaled[:, rank - left :] * scale[:, : lanes_up(end)]
        if lanes_up(end) < rank:
            out_ref[start:end, lanes_up(end) :] = jnp.zeros((PANEL, rank - lanes_up(end)), jnp.float32)
        if end < rank:
            low = end // 128 * 128
            change = lax.dot_general(
                scaled[:, low - left : rank - left],
                scaled[:, low - left :],
                (((0,), (0,)), ((), ())),
                precision=HIGH,
                preferred_element_type=jnp.float32,
            )
            work[end:, low:right] = work[end:, low:right] - change[end - low :, :]


def factor_kernel(code_ref, turned_ref, out_ref, gram_ref, work, band):
    count, size, rank = code_ref.shape
    size = (size - HEAD) // 2
    code = code_ref[...].astype(jnp.int32).astype(jnp.float32)
    unit = unit_of(code[:, 2 * size : 2 * size + 1], code[:, 2 * size + 1 : 2 * size + 2])
    part = (code[:, :size] + code[:, size : 2 * size] * (1.0 / 32768.0)) * unit
    turned = part.reshape(count * size, rank).T
    turned_ref[...] = turned
    gram = dot_rows(turned, turned)

    @pl.when(pl.program_id(0) == 0)
    def _():
        gram_ref[...] = gram

    @pl.when(pl.program_id(0) > 0)
    def _():
        gram_ref[...] += gram

    @pl.when(pl.program_id(0) == pl.num_programs(0) - 1)
    def _():
        inverse_factor(gram_ref[...], out_ref, work, band)


def factor(codes):
    devices, size, rank = codes.shape
    rows = (size - HEAD) // 2
    group = 256 // rows
    return pl.pallas_call(
        factor_kernel,
        grid=(devices // group,),
        in_specs=[pl.BlockSpec((group, size, rank), lambda i: (i, 0, 0))],
        out_specs=[pl.BlockSpec((rank, group * rows), lambda i: (0, i)), pl.BlockSpec((rank, rank), lambda i: (0, 0))],
        out_shape=[
            jax.ShapeDtypeStruct((rank, devices * rows), jnp.float32),
            jax.ShapeDtypeStruct((rank, rank), jnp.float32),
        ],
        scratch_shapes=[
            pltpu.VMEM((rank, rank), jnp.float32),
            pltpu.VMEM((rank, 2 * rank), jnp.float32),
            pltpu.VMEM((TILE + 1, TILE, 2 * PANEL), jnp.float32),
        ],
        compiler_params=PARAMS,
        cost_estimate=pl.CostEstimate(
            flops=12 * devices * rows * rank * rank, bytes_accessed=devices * size * rank * 4, transcendentals=rank
        ),
    )(codes)


def encode_kernel(place_ref, source_ref, turned_ref, unit_ref, inverse_ref, own_ref, code_ref, ortho_ref, mixed_ref):
    def times(a, b):
        return jnp.dot(a, b, preferred_element_type=jnp.float32)

    def turned_dot(a, b):
        return lax.dot_general(a, b, (((0,), (1,)), ((), ())), precision=HIGH, preferred_element_type=jnp.float32)

    rank = turned_ref.shape[0]
    source_high, source_low = halves(source_ref[...].astype(jnp.int32).astype(jnp.float32))
    scaled_high, scaled_low = halves(turned_ref[...] * unit_ref[...])
    most = times(jnp.concatenate([scaled_high, scaled_low], axis=0), source_high)
    part = most[:rank] + (most[rank:] + times(scaled_high, source_low))
    first, last = pl.program_id(0) == 0, pl.program_id(0) == pl.num_programs(0) - 1

    @pl.when(first)
    def _():
        mixed_ref[...] = part

    @pl.when(jnp.logical_not(first))
    def _():
        mixed_ref[...] += part

    @pl.when(last)
    def _():
        inverse = inverse_ref[...]
        ortho_ref[...] = turned_dot(own_ref[...], inverse)
        right = turned_dot(mixed_ref[...], inverse)
        rows = right.shape[0]
        square = jnp.maximum(jnp.sum(right * right, axis=0, keepdims=True), 1e-34)
        square_exponent = jnp.floor(jnp.log2(square))
        fine = square * jnp.exp2(13.0 - square_exponent)
        square_high = jnp.floor(fine)
        square_low = jnp.floor((fine - square_high) * 16384.0)
        exponent, mantissa = code_unit(jnp.max(jnp.abs(right), axis=0, keepdims=True))
        code_ref[:rows] = whole_number(jnp.floor(right * (1.0 / unit_of(exponent, mantissa)) + 0.5))
        set_head(code_ref.at[rows:], exponent, mantissa, square_exponent, square_high, square_low)


def encode(place, source, turned, unit, inverse_low, rows):
    total, share = source.shape
    rank = turned.shape[0]
    block = min(512, total)
    return pl.pallas_call(
        encode_kernel,
        grid_spec=pltpu.PrefetchScalarGridSpec(
            num_scalar_prefetch=1,
            grid=(total // block,),
            in_specs=[
                pl.BlockSpec((block, share), lambda i, place: (i, 0)),
                pl.BlockSpec((rank, block), lambda i, place: (0, i)),
                pl.BlockSpec((1, block), lambda i, place: (0, i)),
                whole(inverse_low),
                pl.BlockSpec((rank, rows), lambda i, place: (0, place[0])),
            ],
            out_specs=[
                pl.BlockSpec((share + HEAD, rank), lambda i, place: (0, 0)),
                pl.BlockSpec((rows, rank), lambda i, place: (0, 0)),
            ],
            scratch_shapes=[pltpu.VMEM((rank, share), jnp.float32)],
        ),
        out_shape=[
            jax.ShapeDtypeStruct((share + HEAD, rank), jnp.int16),
            jax.ShapeDtypeStruct((rows, rank), jnp.float32),
        ],
        compiler_params=PARAMS,
        cost_estimate=pl.CostEstimate(
            flops=6 * total * share * rank, bytes_accessed=total * (share * 2 + rank * 4), transcendentals=0
        ),
    )(place, source, turned, unit, inverse_low, turned)


def decode(code_ref):
    code = code_ref[...].astype(jnp.int32).astype(jnp.float32)
    share = code.shape[1] - HEAD
    right = code[:, :share] * unit_of(code[:, share : share + 1], code[:, share + 1 : share + 2])
    return right.reshape(code.shape[0] * share, code.shape[2])


def times_rows(split_ref, right):
    def times(a, b):
        return lax.dot_general(a, b, (((1,), (1,)), ((), ())), preferred_element_type=jnp.float32)

    right_high, right_low = halves(right)
    split = split_ref[...]
    rows = split.shape[0] // 2
    most = times(split, right_high)
    return most[:rows] + (most[rows:] + times(split[:rows], right_low))


def set_split(split_ref, x):
    rows = x.shape[0]

    @pl.when(pl.program_id(0) == 0)
    def _():
        split_ref[:rows], split_ref[rows:] = halves(x)


def momentum_kernel(momentum_ref, grad_ref, code_ref, ortho_ref, next_ref, split_ref):
    set_split(split_ref, -KEEP_SHARE * ortho_ref[...])
    change = times_rows(split_ref, decode(code_ref))
    next_ref[...] = momentum_ref[...] + grad_ref[...].astype(jnp.float32) + change


def update_kernel(gain, code_ref, ortho_ref, scale_ref, basis_ref, update_ref, split_ref):
    set_split(split_ref, gain * ortho_ref[...])
    basis = decode(code_ref) * scale_ref[...]
    basis_ref[...] = basis
    update_ref[...] = times_rows(split_ref, basis).astype(jnp.bfloat16)


def finish(momentum, grad, codes, orthonormal, scale, gain):
    rows, cols = momentum.shape
    shares, share, rank = codes.shape
    share -= HEAD
    group = max(1, min(1024 // share, shares))
    block = group * share
    wide = pl.BlockSpec((rows, block), lambda i: (0, i))
    tall = pl.BlockSpec((block, rank), lambda i: (i, 0))
    coded = pl.BlockSpec((group, share + HEAD, rank), lambda i: (i, 0, 0))
    split = [pltpu.VMEM((2 * rows, rank), jnp.bfloat16)]
    flops = 6 * rows * cols * rank
    momentum_next = pl.pallas_call(
        momentum_kernel,
        grid=(cols // block,),
        in_specs=[wide, wide, coded, whole(orthonormal)],
        out_specs=wide,
        out_shape=jax.ShapeDtypeStruct((rows, cols), jnp.float32),
        scratch_shapes=split,
        compiler_params=PARAMS,
        cost_estimate=pl.CostEstimate(
            flops=flops, bytes_accessed=rows * cols * 10 + cols * rank * 2, transcendentals=0
        ),
    )(momentum, grad, codes, orthonormal)
    q_next, update = pl.pallas_call(
        functools.partial(update_kernel, gain),
        grid=(cols // block,),
        in_specs=[coded, whole(orthonormal), whole(scale)],
        out_specs=[tall, wide],
        out_shape=[
            jax.ShapeDtypeStruct((cols, rank), jnp.float32),
            jax.ShapeDtypeStruct((rows, cols), jnp.bfloat16),
        ],
        scratch_shapes=split,
        compiler_params=PARAMS,
        cost_estimate=pl.CostEstimate(flops=flops, bytes_accessed=rows * cols * 2 + cols * rank * 6, transcendentals=0),
    )(codes, orthonormal, scale)
    return momentum_next, q_next, update


def on_device(momentum, grad, q_stored, perm):
    block_rows = q_stored.shape[0]
    num_blocks = lax.axis_size("fsdp")
    num_cols = lax.axis_size("tp")
    rank_total = block_rows * num_blocks
    rows, cols = momentum.shape
    row_total, col_total = rows * num_blocks, cols * num_cols
    share = cols // num_blocks

    basis, codes = prepare(momentum, grad, q_stored, share)
    codes = codes.reshape(-1, rows, codes.shape[2] // share, share).swapaxes(1, 2).reshape(num_blocks, rows, share)
    basis = lax.all_gather(basis, "fsdp", axis=0, tiled=True)
    codes, basis = lax.optimization_barrier((codes, basis))
    codes = lax.all_to_all(codes, "fsdp", split_axis=0, concat_axis=0).reshape(row_total, share)
    head = basis.reshape(num_blocks, block_rows, cols + rows)[:, :2, cols:].astype(jnp.float32)
    unit = unit_of(head[:, 0], head[:, 1]).reshape(1, row_total)

    near = project(momentum, grad, basis)
    step = 1
    while 2 * step < num_cols:
        near = near + exchange(near, "tp", step)
        step *= 2
    packed = lax.all_gather(pack(perm, [near, exchange(near, "tp", step)]), "fsdp", axis=0)
    packed, codes = lax.optimization_barrier((packed, codes))
    turned, inverse_low = factor(packed)
    code, orthonormal = encode(lax.axis_index("fsdp").reshape(1), codes, turned, unit, inverse_low, rows)
    gathered = lax.all_gather(code, "fsdp", axis=0)
    head = gathered[:, share : share + 5].astype(jnp.float32)
    parts = (head[:, 3] + head[:, 4] * (1.0 / 16384.0)) * jnp.exp2(head[:, 2] - 13.0)
    squares = quad_sum(jnp.sum(parts, axis=0, keepdims=True), "tp")
    scale = lax.rsqrt(squares / col_total + EPSILON)
    return tuple(finish(momentum, grad, gathered, orthonormal, scale, math.sqrt(row_total / rank_total)))


def solution(mesh):
    return jax.shard_map(
        on_device,
        mesh=mesh,
        in_specs=(P("fsdp", "tp"), P("fsdp", "tp"), P("fsdp", "tp"), P()),
        out_specs=(P("fsdp", "tp"), P("tp", None), P("fsdp", "tp")),
        check_vma=False,
    )
```

```python
import functools
import math

import jax
import jax.numpy as jnp
from jax import lax
from jax.experimental import pallas as pl
from jax.experimental.pallas import tpu as pltpu
from jax.sharding import PartitionSpec as P

EPSILON = 1e-06
KEEP_SHARE = 0.5
HIGH = lax.Precision.HIGHEST
PANEL = 64
TILE = 8
HEAD = 16
TOP = 32766.0
PARAMS = pltpu.CompilerParams(vmem_limit_bytes=40 * 1024 * 1024)
STREAM = pltpu.CompilerParams(vmem_limit_bytes=54 * 1024 * 1024)


def halves(x):
    high = x.astype(jnp.bfloat16)
    return high, (x - high.astype(jnp.float32)).astype(jnp.bfloat16)


def exchange(x, axis, k):
    return lax.ppermute(x, axis, [(i, i ^ k) for i in range(lax.axis_size(axis))])


def butterfly_sum(x, axis, step=1):
    while step < lax.axis_size(axis):
        x = x + exchange(x, axis, step)
        step *= 2
    return x


def quad_sum(x, axis, step=1):
    if lax.axis_size(axis) != 4 * step:
        return butterfly_sum(x, axis, step)
    near, far, across = [exchange(x, axis, k * step) for k in range(1, 4)]
    return (x + near) + (far + across)


def whole(x):
    return pl.BlockSpec(x.shape, lambda *_: (0,) * len(x.shape))


def dot_rows(a, b):
    return lax.dot_general(a, b, (((1,), (1,)), ((), ())), precision=HIGH, preferred_element_type=jnp.float32)


def unit_of(exponent, mantissa):
    return mantissa * jnp.exp2(exponent - 13.0)


def code_unit(top):
    top = jnp.maximum(top, 1e-28) * (1.0 / TOP)
    exponent = jnp.floor(jnp.log2(top))
    return exponent, jnp.floor(top * jnp.exp2(13.0 - exponent)) + 1.0


def whole_number(x):
    return x.astype(jnp.int32).astype(jnp.int16)


def set_head(head_ref, *rows):
    place = lax.broadcasted_iota(jnp.int32, head_ref.shape, 0)
    head = jnp.zeros(head_ref.shape, jnp.float32)
    for k, row in enumerate(rows):
        head = jnp.where(place == k, row, head)
    head_ref[...] = whole_number(head)


def code_basis(basis):
    value = basis.astype(jnp.float32)
    size = jnp.abs(value)
    normal = size >= 2.0**-126
    exponent = jnp.floor(jnp.log2(jnp.where(normal, size, 1.0)))
    code = 128.0 * (exponent + 126.0) + jnp.floor(128.0 * (size * jnp.exp2(-exponent)) + 0.5)
    return whole_number(jnp.where(normal, jnp.where(value < 0.0, code - 32768.0, code), 0.0))


def prepare_kernel(momentum_ref, grad_ref, basis_ref, pack_ref, code_ref, head_ref):
    rows, cols = momentum_ref.shape
    width = code_ref.shape[-1]
    spans = [slice(i, i + width) for i in range(0, cols, width)]
    combined = lambda span: momentum_ref[:, span] + grad_ref[:, span].astype(jnp.float32)
    top = functools.reduce(jnp.maximum, [jnp.abs(combined(span)) for span in spans])
    exponent, mantissa = code_unit(jnp.max(top, axis=1, keepdims=True))
    inverse = 1.0 / unit_of(exponent, mantissa)
    for k, span in enumerate(spans):
        code_ref[k] = whole_number(jnp.floor(combined(span) * inverse + 0.5))
        pack_ref[:, span] = code_basis(basis_ref[:, span])
    step = pl.program_id(0)
    here = pl.ds(pl.multiple_of(step * rows, rows), rows)
    for k, column in enumerate((exponent, mantissa)):
        head_ref[k, here, :] = jnp.broadcast_to(column, (rows, head_ref.shape[2]))
    pack_ref[:, cols:] = jnp.zeros((pack_ref.shape[0], pack_ref.shape[1] - cols), jnp.int16)

    @pl.when(step == pl.num_programs(0) - 1)
    def _():
        place = lax.broadcasted_iota(jnp.int32, (pack_ref.shape[0], head_ref.shape[1]), 0)
        first, second = head_ref[0].T[:1], head_ref[1].T[:1]
        last = pack_ref.shape[0] - 1
        head = jnp.where(place == last - 1, first, jnp.where(place == last, second, 0.0))
        pack_ref[:, cols:] = whole_number(head)


def prepare(momentum, grad, basis, share):
    rows, cols = momentum.shape
    width = share if share % 128 == 0 else cols
    steps = 2 if basis.shape[0] % 32 == 0 else 1
    wide = pl.BlockSpec((rows // steps, cols), lambda i: (i, 0))
    ranks = basis.shape[0] // steps
    return pl.pallas_call(
        prepare_kernel,
        grid=(steps,),
        in_specs=[wide, wide, pl.BlockSpec((ranks, cols), lambda i: (i, 0))],
        out_specs=[
            pl.BlockSpec((ranks, cols + rows), lambda i: (i, 0)),
            pl.BlockSpec((cols // width, rows // steps, width), lambda i: (0, i, 0)),
        ],
        out_shape=[
            jax.ShapeDtypeStruct((basis.shape[0], cols + rows), jnp.int16),
            jax.ShapeDtypeStruct((cols // width, rows, width), jnp.int16),
        ],
        scratch_shapes=[pltpu.VMEM((2, rows, 128), jnp.float32)],
        compiler_params=STREAM,
        cost_estimate=pl.CostEstimate(flops=10 * rows * cols, bytes_accessed=rows * cols * 8, transcendentals=0),
    )(momentum, grad, basis)


def project_kernel(momentum_ref, grad_ref, code_ref, out_ref):
    code = code_ref[...].astype(jnp.int32)
    power = jnp.exp2(((code >> 7) & 255).astype(jnp.float32) - 134.0)
    value = ((code & 127) | 128).astype(jnp.float32) * power
    basis = jnp.where(code < 0, -value, value).astype(jnp.bfloat16)
    combined = momentum_ref[...] + grad_ref[...].astype(jnp.float32)
    rows = combined.shape[0]
    part = lax.dot_general(
        jnp.concatenate(halves(combined), axis=0),
        basis,
        (((1,), (1,)), ((), ())),
        preferred_element_type=jnp.float32,
    )
    part = part[:rows] + part[rows:]

    @pl.when(pl.program_id(0) == 0)
    def _():
        out_ref[...] = part

    @pl.when(pl.program_id(0) > 0)
    def _():
        out_ref[...] += part


def project(momentum, grad, codes):
    rows, cols = momentum.shape
    rank = codes.shape[0]
    block = min(1024, cols)
    wide = pl.BlockSpec((rows, block), lambda i: (0, i))
    return pl.pallas_call(
        project_kernel,
        grid=(cols // block,),
        in_specs=[wide, wide, pl.BlockSpec((rank, block), lambda i: (0, i))],
        out_specs=pl.BlockSpec((rows, rank), lambda i: (0, 0)),
        out_shape=jax.ShapeDtypeStruct((rows, rank), jnp.float32),
        compiler_params=STREAM,
        cost_estimate=pl.CostEstimate(
            flops=4 * rows * cols * rank, bytes_accessed=rows * cols * 6 + rank * cols * 2, transcendentals=rank * cols
        ),
    )(momentum, grad, codes)


def pack_kernel(perm_ref, *refs):
    part_refs, out_ref = refs[:-1], refs[-1]
    rows, rank = part_refs[0].shape
    blocks = perm_ref.shape[0]
    size = rank // blocks
    stored = lax.broadcasted_iota(jnp.int32, (rank, rank), 0)
    target = jnp.zeros((rank, rank), jnp.int32)
    for s in range(blocks):
        target = jnp.where(stored // size == s, perm_ref[s] * size + stored % size, target)
    order = (target == lax.broadcasted_iota(jnp.int32, (rank, rank), 1)).astype(jnp.float32)
    parts = [ref[...] for ref in part_refs]
    while len(parts) > 1:
        parts = [parts[k] + parts[k + 1] for k in range(0, len(parts), 2)]
    total = jnp.dot(parts[0], order, precision=HIGH, preferred_element_type=jnp.float32)
    exponent, mantissa = code_unit(jnp.max(jnp.abs(total), axis=0, keepdims=True))
    value = total * (1.0 / unit_of(exponent, mantissa))
    high = jnp.floor(value + 0.5)
    out_ref[:rows] = whole_number(high)
    low = jnp.minimum(jnp.floor((value - high) * 256.0 + 0.5), 127.0)
    half = rows // 2
    out_ref[rows : rows + half] = whole_number(low[:half] * 256.0 + (low[half:] + 128.0))
    set_head(out_ref.at[rows + half :], exponent, mantissa)


def pack(perm, parts):
    rows, rank = parts[0].shape
    return pl.pallas_call(
        pack_kernel,
        grid_spec=pltpu.PrefetchScalarGridSpec(
            num_scalar_prefetch=1,
            grid=(1,),
            in_specs=[whole(x) for x in parts],
            out_specs=pl.BlockSpec((rows + rows // 2 + HEAD, rank), lambda *_: (0, 0)),
        ),
        out_shape=jax.ShapeDtypeStruct((rows + rows // 2 + HEAD, rank), jnp.int16),
        compiler_params=PARAMS,
        cost_estimate=pl.CostEstimate(flops=12 * rows * rank * rank, bytes_accessed=rank * rank * 4, transcendentals=0),
    )(perm, *parts)


def reciprocal(x):
    guess = pl.reciprocal(x, approx=True)
    return guess * (2.0 - x * guess)


def spread(row):
    return jnp.broadcast_to(row, (TILE, 2 * PANEL))


def panel_inverse(block, band):
    rows = lax.broadcasted_iota(jnp.int32, (PANEL, PANEL), 0)
    cols = lax.broadcasted_iota(jnp.int32, (PANEL, PANEL), 1)
    both = jnp.concatenate([block, (rows == cols).astype(jnp.float32)], axis=1)
    count = PANEL // TILE
    tiles = [both[TILE * i : TILE * (i + 1)] for i in range(count)]
    sub = lax.broadcasted_iota(jnp.int32, (TILE, 2 * PANEL), 0)
    row = lambda k, j: band[k, pl.ds(j, TILE, stride=0), :]
    done = []
    for k in range(count):
        columns = [
            [spread(tiles[i][:, TILE * k + j : TILE * k + j + 1]) for j in range(TILE)] for i in range(k, count)
        ]
        state = list(columns[0]) + [tiles[k]]
        for m, x in enumerate(state):
            band[m] = x
        final = jnp.zeros_like(tiles[k])
        for j in range(0, TILE, 2):
            first, second = sub == j, sub == j + 1
            a, b, c = row(j, j), row(j + 1, j), row(j + 1, j + 1)
            minor = a * c - b * b
            inverse = reciprocal(minor)
            left, right = state[j], state[j + 1]
            ratio = reciprocal(a)
            below = (state[TILE] - b * ratio * row(TILE, j)) * lax.rsqrt(minor * ratio)
            final = jnp.where(first, state[TILE] * lax.rsqrt(a), jnp.where(second, below, final))
            for m in range(j + 2, TILE + 1):
                upper, lower = row(m, j), row(m, j + 1)
                upper, lower = (c * upper - b * lower) * inverse, (a * lower - b * upper) * inverse
                rest = state[m] - left * upper - right * lower
                state[m] = jnp.where(first, upper, jnp.where(second, lower, rest))
            for m in range(j + 2, TILE + 1):
                band[m] = state[m]
        done.append(final)
        reduced = [row(TILE, j) for j in range(TILE)]
        for i in range(k + 1, count):
            tile = tiles[i]
            for j in range(TILE):
                tile = tile - columns[i - k][j] * reduced[j]
            tiles[i] = tile
    return jnp.concatenate(done, axis=0)[:, PANEL:]


def lanes_up(x):
    return (x + 127) // 128 * 128


def inverse_factor(gram, out_ref, work, band):
    rank = gram.shape[0]
    rows = lax.broadcasted_iota(jnp.int32, (rank, rank), 0)
    cols = lax.broadcasted_iota(jnp.int32, (rank, rank), 1)
    diagonal = jnp.where(rows == cols, gram, 0.0)
    scale = lax.rsqrt(jnp.sum(diagonal, axis=0, keepdims=True))
    work[:, :rank] = gram * scale * lax.rsqrt(jnp.sum(diagonal, axis=1, keepdims=True))
    work[:, rank:] = (rows == cols).astype(jnp.float32)
    for start in range(0, rank, PANEL):
        end = start + PANEL
        left, right = start // 128 * 128, rank + lanes_up(end)
        inverse = panel_inverse(work[start:end, start:end], band)
        scaled = jnp.dot(inverse, work[start:end, left:right], precision=HIGH, preferred_element_type=jnp.float32)
        out_ref[start:end, : lanes_up(end)] = scaled[:, rank - left :] * scale[:, : lanes_up(end)]
        if lanes_up(end) < rank:
            out_ref[start:end, lanes_up(end) :] = jnp.zeros((PANEL, rank - lanes_up(end)), jnp.float32)
        if end < rank:
            low = end // 128 * 128
            change = lax.dot_general(
                scaled[:, low - left : rank - left],
                scaled[:, low - left :],
                (((0,), (0,)), ((), ())),
                precision=HIGH,
                preferred_element_type=jnp.float32,
            )
            work[end:, low:right] = work[end:, low:right] - change[end - low :, :]


def factor_kernel(code_ref, turned_ref, out_ref, gram_ref, work, band):
    count, size, rank = code_ref.shape
    size = (size - HEAD) * 2 // 3
    code = code_ref[...].astype(jnp.int32)
    low = code[:, size : size + size // 2]
    low = jnp.concatenate([low >> 8, (low & 255) - 128], axis=1).astype(jnp.float32)
    head = code[:, size + size // 2 :].astype(jnp.float32)
    part = (code[:, :size].astype(jnp.float32) + low * (1.0 / 256.0)) * unit_of(head[:, :1], head[:, 1:2])
    turned = part.reshape(count * size, rank).T
    turned_ref[...] = turned
    gram = dot_rows(turned, turned)

    @pl.when(pl.program_id(0) == 0)
    def _():
        gram_ref[...] = gram

    @pl.when(pl.program_id(0) > 0)
    def _():
        gram_ref[...] += gram

    @pl.when(pl.program_id(0) == pl.num_programs(0) - 1)
    def _():
        inverse_factor(gram_ref[...], out_ref, work, band)


def factor(codes):
    devices, size, rank = codes.shape
    rows = (size - HEAD) * 2 // 3
    group = 256 // rows
    return pl.pallas_call(
        factor_kernel,
        grid=(devices // group,),
        in_specs=[pl.BlockSpec((group, size, rank), lambda i: (i, 0, 0))],
        out_specs=[pl.BlockSpec((rank, group * rows), lambda i: (0, i)), pl.BlockSpec((rank, rank), lambda i: (0, 0))],
        out_shape=[
            jax.ShapeDtypeStruct((rank, devices * rows), jnp.float32),
            jax.ShapeDtypeStruct((rank, rank), jnp.float32),
        ],
        scratch_shapes=[
            pltpu.VMEM((rank, rank), jnp.float32),
            pltpu.VMEM((rank, 2 * rank), jnp.float32),
            pltpu.VMEM((TILE + 1, TILE, 2 * PANEL), jnp.float32),
        ],
        compiler_params=PARAMS,
        cost_estimate=pl.CostEstimate(
            flops=12 * devices * rows * rank * rank, bytes_accessed=devices * size * rank * 4, transcendentals=rank
        ),
    )(codes)


def encode_kernel(place_ref, source_ref, turned_ref, unit_ref, inverse_ref, own_ref, code_ref, ortho_ref, mixed_ref):
    def times(a, b):
        return jnp.dot(a, b, preferred_element_type=jnp.float32)

    def turned_dot(a, b):
        return lax.dot_general(a, b, (((0,), (1,)), ((), ())), precision=HIGH, preferred_element_type=jnp.float32)

    rank = turned_ref.shape[0]
    source_high, source_low = halves(source_ref[...].astype(jnp.int32).astype(jnp.float32))
    scaled_high, scaled_low = halves(turned_ref[...] * unit_ref[...])
    most = times(jnp.concatenate([scaled_high, scaled_low], axis=0), source_high)
    part = most[:rank] + (most[rank:] + times(scaled_high, source_low))
    first, last = pl.program_id(0) == 0, pl.program_id(0) == pl.num_programs(0) - 1

    @pl.when(first)
    def _():
        mixed_ref[...] = part

    @pl.when(jnp.logical_not(first))
    def _():
        mixed_ref[...] += part

    @pl.when(last)
    def _():
        inverse = inverse_ref[...]
        ortho_ref[...] = turned_dot(own_ref[...], inverse)
        right = turned_dot(mixed_ref[...], inverse)
        rows = right.shape[0]
        square = jnp.maximum(jnp.sum(right * right, axis=0, keepdims=True), 1e-34)
        square_exponent = jnp.floor(jnp.log2(square))
        fine = square * jnp.exp2(13.0 - square_exponent)
        square_high = jnp.floor(fine)
        square_low = jnp.floor((fine - square_high) * 16384.0)
        exponent, mantissa = code_unit(jnp.max(jnp.abs(right), axis=0, keepdims=True))
        code_ref[:rows] = whole_number(jnp.floor(right * (1.0 / unit_of(exponent, mantissa)) + 0.5))
        set_head(code_ref.at[rows:], exponent, mantissa, square_exponent, square_high, square_low)


def encode(place, source, turned, unit, inverse_low, rows):
    total, share = source.shape
    rank = turned.shape[0]
    block = min(512, total)
    return pl.pallas_call(
        encode_kernel,
        grid_spec=pltpu.PrefetchScalarGridSpec(
            num_scalar_prefetch=1,
            grid=(total // block,),
            in_specs=[
                pl.BlockSpec((block, share), lambda i, place: (i, 0)),
                pl.BlockSpec((rank, block), lambda i, place: (0, i)),
                pl.BlockSpec((1, block), lambda i, place: (0, i)),
                whole(inverse_low),
                pl.BlockSpec((rank, rows), lambda i, place: (0, place[0])),
            ],
            out_specs=[
                pl.BlockSpec((share + HEAD, rank), lambda i, place: (0, 0)),
                pl.BlockSpec((rows, rank), lambda i, place: (0, 0)),
            ],
            scratch_shapes=[pltpu.VMEM((rank, share), jnp.float32)],
        ),
        out_shape=[
            jax.ShapeDtypeStruct((share + HEAD, rank), jnp.int16),
            jax.ShapeDtypeStruct((rows, rank), jnp.float32),
        ],
        compiler_params=PARAMS,
        cost_estimate=pl.CostEstimate(
            flops=6 * total * share * rank, bytes_accessed=total * (share * 2 + rank * 4), transcendentals=0
        ),
    )(place, source, turned, unit, inverse_low, turned)


def decode(code_ref):
    code = code_ref[...].astype(jnp.int32).astype(jnp.float32)
    share = code.shape[1] - HEAD
    right = code[:, :share] * unit_of(code[:, share : share + 1], code[:, share + 1 : share + 2])
    return right.reshape(code.shape[0] * share, code.shape[2])


def times_rows(split_ref, right):
    def times(a, b):
        return lax.dot_general(a, b, (((1,), (1,)), ((), ())), preferred_element_type=jnp.float32)

    right_high, right_low = halves(right)
    split = split_ref[...]
    rows = split.shape[0] // 2
    most = times(split, right_high)
    return most[:rows] + (most[rows:] + times(split[:rows], right_low))


def set_split(split_ref, x):
    rows = x.shape[0]

    @pl.when(pl.program_id(0) == 0)
    def _():
        split_ref[:rows], split_ref[rows:] = halves(x)


def momentum_kernel(momentum_ref, grad_ref, code_ref, ortho_ref, next_ref, split_ref):
    set_split(split_ref, -KEEP_SHARE * ortho_ref[...])
    change = times_rows(split_ref, decode(code_ref))
    next_ref[...] = momentum_ref[...] + grad_ref[...].astype(jnp.float32) + change


def update_kernel(gain, code_ref, ortho_ref, scale_ref, basis_ref, update_ref, split_ref):
    set_split(split_ref, gain * ortho_ref[...])
    basis = decode(code_ref) * scale_ref[...]
    basis_ref[...] = basis
    update_ref[...] = times_rows(split_ref, basis).astype(jnp.bfloat16)


def finish(momentum, grad, codes, orthonormal, scale, gain):
    rows, cols = momentum.shape
    shares, share, rank = codes.shape
    share -= HEAD
    group = max(1, min(1024 // share, shares))
    block = group * share
    wide = pl.BlockSpec((rows, block), lambda i: (0, i))
    tall = pl.BlockSpec((block, rank), lambda i: (i, 0))
    coded = pl.BlockSpec((group, share + HEAD, rank), lambda i: (i, 0, 0))
    split = [pltpu.VMEM((2 * rows, rank), jnp.bfloat16)]
    flops = 6 * rows * cols * rank
    momentum_next = pl.pallas_call(
        momentum_kernel,
        grid=(cols // block,),
        in_specs=[wide, wide, coded, whole(orthonormal)],
        out_specs=wide,
        out_shape=jax.ShapeDtypeStruct((rows, cols), jnp.float32),
        scratch_shapes=split,
        compiler_params=PARAMS,
        cost_estimate=pl.CostEstimate(
            flops=flops, bytes_accessed=rows * cols * 10 + cols * rank * 2, transcendentals=0
        ),
    )(momentum, grad, codes, orthonormal)
    q_next, update = pl.pallas_call(
        functools.partial(update_kernel, gain),
        grid=(cols // block,),
        in_specs=[coded, whole(orthonormal), whole(scale)],
        out_specs=[tall, wide],
        out_shape=[
            jax.ShapeDtypeStruct((cols, rank), jnp.float32),
            jax.ShapeDtypeStruct((rows, cols), jnp.bfloat16),
        ],
        scratch_shapes=split,
        compiler_params=PARAMS,
        cost_estimate=pl.CostEstimate(flops=flops, bytes_accessed=rows * cols * 2 + cols * rank * 6, transcendentals=0),
    )(codes, orthonormal, scale)
    return momentum_next, q_next, update


def on_device(momentum, grad, q_stored, perm):
    block_rows = q_stored.shape[0]
    num_blocks = lax.axis_size("fsdp")
    num_cols = lax.axis_size("tp")
    rank_total = block_rows * num_blocks
    rows, cols = momentum.shape
    row_total, col_total = rows * num_blocks, cols * num_cols
    share = cols // num_blocks

    basis, codes = prepare(momentum, grad, q_stored, share)
    codes = codes.reshape(-1, rows, codes.shape[2] // share, share).swapaxes(1, 2).reshape(num_blocks, rows, share)
    basis = lax.all_gather(basis, "fsdp", axis=0, tiled=True)
    codes, basis = lax.optimization_barrier((codes, basis))
    codes = lax.all_to_all(codes, "fsdp", split_axis=0, concat_axis=0).reshape(row_total, share)
    head = basis.reshape(num_blocks, block_rows, cols + rows)[:, -2:, cols:].astype(jnp.float32)
    unit = unit_of(head[:, 0], head[:, 1]).reshape(1, row_total)

    near, step = project(momentum, grad, basis), 1
    while 4 * step < num_cols:
        near = near + exchange(near, "tp", step)
        step *= 2
    parts = [near] + [exchange(near, "tp", k) for k in range(step, num_cols, step)]
    packed = lax.all_gather(pack(perm, parts), "fsdp", axis=0)
    packed, codes = lax.optimization_barrier((packed, codes))
    turned, inverse_low = factor(packed)
    code, orthonormal = encode(lax.axis_index("fsdp").reshape(1), codes, turned, unit, inverse_low, rows)
    gathered = lax.all_gather(code, "fsdp", axis=0)
    head = gathered[:, share : share + 5].astype(jnp.float32)
    parts = (head[:, 3] + head[:, 4] * (1.0 / 16384.0)) * jnp.exp2(head[:, 2] - 13.0)
    squares = quad_sum(jnp.sum(parts, axis=0, keepdims=True), "tp")
    scale = lax.rsqrt(squares / col_total + EPSILON)
    return tuple(finish(momentum, grad, gathered, orthonormal, scale, math.sqrt(row_total / rank_total)))


def solution(mesh):
    return jax.shard_map(
        on_device,
        mesh=mesh,
        in_specs=(P("fsdp", "tp"), P("fsdp", "tp"), P("fsdp", "tp"), P()),
        out_specs=(P("fsdp", "tp"), P("tp", None), P("fsdp", "tp")),
        check_vma=False,
    )
```

```python
import functools
import math

import jax
import jax.numpy as jnp
from jax import lax
from jax.experimental import pallas as pl
from jax.experimental.pallas import tpu as pltpu
from jax.sharding import PartitionSpec as P

EPSILON = 1e-06
KEEP_SHARE = 0.5
HIGH = lax.Precision.HIGHEST
PANEL = 64
TILE = 8
HEAD = 16
TOP = 32766.0
PARAMS = pltpu.CompilerParams(vmem_limit_bytes=40 * 1024 * 1024)
FLOW = pltpu.CompilerParams(vmem_limit_bytes=53 * 1024 * 1024)
STREAM = pltpu.CompilerParams(vmem_limit_bytes=54 * 1024 * 1024)


def halves(x):
    high = x.astype(jnp.bfloat16)
    return high, (x - high.astype(jnp.float32)).astype(jnp.bfloat16)


def exchange(x, axis, k):
    return lax.ppermute(x, axis, [(i, i ^ k) for i in range(lax.axis_size(axis))])


def butterfly_sum(x, axis, step=1):
    while step < lax.axis_size(axis):
        x = x + exchange(x, axis, step)
        step *= 2
    return x


def quad_sum(x, axis, step=1):
    if lax.axis_size(axis) != 4 * step:
        return butterfly_sum(x, axis, step)
    near, far, across = [exchange(x, axis, k * step) for k in range(1, 4)]
    return (x + near) + (far + across)


def whole(x):
    return pl.BlockSpec(x.shape, lambda *_: (0,) * len(x.shape))


def dot_rows(a, b):
    return lax.dot_general(a, b, (((1,), (1,)), ((), ())), precision=HIGH, preferred_element_type=jnp.float32)


def unit_of(exponent, mantissa):
    return mantissa * jnp.exp2(exponent - 13.0)


def code_unit(top):
    top = jnp.maximum(top, 1e-28) * (1.0 / TOP)
    exponent = jnp.floor(jnp.log2(top))
    return exponent, jnp.floor(top * jnp.exp2(13.0 - exponent)) + 1.0


def whole_number(x):
    return x.astype(jnp.int32).astype(jnp.int16)


def set_head(head_ref, *rows):
    place = lax.broadcasted_iota(jnp.int32, head_ref.shape, 0)
    head = jnp.zeros(head_ref.shape, jnp.float32)
    for k, row in enumerate(rows):
        head = jnp.where(place == k, row, head)
    head_ref[...] = whole_number(head)


def code_basis(basis):
    value = basis.astype(jnp.float32)
    size = jnp.abs(value)
    normal = size >= 2.0**-126
    exponent = jnp.floor(jnp.log2(jnp.where(normal, size, 1.0)))
    code = 128.0 * (exponent + 126.0) + jnp.floor(128.0 * (size * jnp.exp2(-exponent)) + 0.5)
    return whole_number(jnp.where(normal, jnp.where(value < 0.0, code - 32768.0, code), 0.0))


def prepare_kernel(momentum_ref, grad_ref, basis_ref, pack_ref, code_ref, head_ref):
    rows, cols = momentum_ref.shape
    width = code_ref.shape[-1]
    spans = [slice(i, i + width) for i in range(0, cols, width)]
    combined = lambda span: momentum_ref[:, span] + grad_ref[:, span].astype(jnp.float32)
    top = functools.reduce(jnp.maximum, [jnp.abs(combined(span)) for span in spans])
    exponent, mantissa = code_unit(jnp.max(top, axis=1, keepdims=True))
    inverse = 1.0 / unit_of(exponent, mantissa)
    for k, span in enumerate(spans):
        code_ref[k] = whole_number(jnp.floor(combined(span) * inverse + 0.5))
        pack_ref[:, span] = code_basis(basis_ref[:, span])
    step = pl.program_id(0)
    here = pl.ds(pl.multiple_of(step * rows, rows), rows)
    for k, column in enumerate((exponent, mantissa)):
        head_ref[k, here, :] = jnp.broadcast_to(column, (rows, head_ref.shape[2]))
    pack_ref[:, cols:] = jnp.zeros((pack_ref.shape[0], pack_ref.shape[1] - cols), jnp.int16)

    @pl.when(step == pl.num_programs(0) - 1)
    def _():
        place = lax.broadcasted_iota(jnp.int32, (pack_ref.shape[0], head_ref.shape[1]), 0)
        first, second = head_ref[0].T[:1], head_ref[1].T[:1]
        last = pack_ref.shape[0] - 1
        head = jnp.where(place == last - 1, first, jnp.where(place == last, second, 0.0))
        pack_ref[:, cols:] = whole_number(head)


def prepare(momentum, grad, basis, share):
    rows, cols = momentum.shape
    width = share if share % 128 == 0 else cols
    steps = 2 if basis.shape[0] % 32 == 0 else 1
    wide = pl.BlockSpec((rows // steps, cols), lambda i: (i, 0))
    ranks = basis.shape[0] // steps
    return pl.pallas_call(
        prepare_kernel,
        grid=(steps,),
        in_specs=[wide, wide, pl.BlockSpec((ranks, cols), lambda i: (i, 0))],
        out_specs=[
            pl.BlockSpec((ranks, cols + rows), lambda i: (i, 0)),
            pl.BlockSpec((cols // width, rows // steps, width), lambda i: (0, i, 0)),
        ],
        out_shape=[
            jax.ShapeDtypeStruct((basis.shape[0], cols + rows), jnp.int16),
            jax.ShapeDtypeStruct((cols // width, rows, width), jnp.int16),
        ],
        scratch_shapes=[pltpu.VMEM((2, rows, 128), jnp.float32)],
        compiler_params=STREAM,
        cost_estimate=pl.CostEstimate(flops=10 * rows * cols, bytes_accessed=rows * cols * 8, transcendentals=0),
    )(momentum, grad, basis)


def project_kernel(momentum_ref, grad_ref, code_ref, out_ref):
    code = code_ref[...].astype(jnp.int32)
    power = jnp.exp2(((code >> 7) & 255).astype(jnp.float32) - 134.0)
    value = ((code & 127) | 128).astype(jnp.float32) * power
    basis = jnp.where(code < 0, -value, value).astype(jnp.bfloat16)
    combined = momentum_ref[...] + grad_ref[...].astype(jnp.float32)
    rows = combined.shape[0]
    part = lax.dot_general(
        jnp.concatenate(halves(combined), axis=0),
        basis,
        (((1,), (1,)), ((), ())),
        preferred_element_type=jnp.float32,
    )
    part = part[:rows] + part[rows:]

    @pl.when(pl.program_id(0) == 0)
    def _():
        out_ref[...] = part

    @pl.when(pl.program_id(0) > 0)
    def _():
        out_ref[...] += part


def project(momentum, grad, codes):
    rows, cols = momentum.shape
    rank = codes.shape[0]
    block = min(1024, cols)
    wide = pl.BlockSpec((rows, block), lambda i: (0, i))
    return pl.pallas_call(
        project_kernel,
        grid=(cols // block,),
        in_specs=[wide, wide, pl.BlockSpec((rank, block), lambda i: (0, i))],
        out_specs=pl.BlockSpec((rows, rank), lambda i: (0, 0)),
        out_shape=jax.ShapeDtypeStruct((rows, rank), jnp.float32),
        compiler_params=FLOW,
        cost_estimate=pl.CostEstimate(
            flops=4 * rows * cols * rank, bytes_accessed=rows * cols * 6 + rank * cols * 2, transcendentals=rank * cols
        ),
    )(momentum, grad, codes)


def pack_kernel(perm_ref, *refs):
    part_refs, out_ref = refs[:-1], refs[-1]
    rows, rank = part_refs[0].shape
    blocks = perm_ref.shape[0]
    size = rank // blocks
    stored = lax.broadcasted_iota(jnp.int32, (rank, rank), 0)
    target = jnp.zeros((rank, rank), jnp.int32)
    for s in range(blocks):
        target = jnp.where(stored // size == s, perm_ref[s] * size + stored % size, target)
    order = (target == lax.broadcasted_iota(jnp.int32, (rank, rank), 1)).astype(jnp.float32)
    parts = [ref[...] for ref in part_refs]
    while len(parts) > 1:
        parts = [parts[k] + parts[k + 1] for k in range(0, len(parts), 2)]
    total = jnp.dot(parts[0], order, precision=HIGH, preferred_element_type=jnp.float32)
    exponent, mantissa = code_unit(jnp.max(jnp.abs(total), axis=0, keepdims=True))
    value = total * (1.0 / unit_of(exponent, mantissa))
    high = jnp.floor(value + 0.5)
    out_ref[:rows] = whole_number(high)
    low = jnp.minimum(jnp.floor((value - high) * 256.0 + 0.5), 127.0)
    half = rows // 2
    out_ref[rows : rows + half] = whole_number(low[:half] * 256.0 + (low[half:] + 128.0))
    set_head(out_ref.at[rows + half :], exponent, mantissa)


def pack(perm, parts):
    rows, rank = parts[0].shape
    return pl.pallas_call(
        pack_kernel,
        grid_spec=pltpu.PrefetchScalarGridSpec(
            num_scalar_prefetch=1,
            grid=(1,),
            in_specs=[whole(x) for x in parts],
            out_specs=pl.BlockSpec((rows + rows // 2 + HEAD, rank), lambda *_: (0, 0)),
        ),
        out_shape=jax.ShapeDtypeStruct((rows + rows // 2 + HEAD, rank), jnp.int16),
        compiler_params=PARAMS,
        cost_estimate=pl.CostEstimate(flops=12 * rows * rank * rank, bytes_accessed=rank * rank * 4, transcendentals=0),
    )(perm, *parts)


def spread(row):
    return jnp.broadcast_to(row, (TILE, 2 * PANEL))


def panel_inverse(block, band):
    rows = lax.broadcasted_iota(jnp.int32, (PANEL, PANEL), 0)
    cols = lax.broadcasted_iota(jnp.int32, (PANEL, PANEL), 1)
    both = jnp.concatenate([block, (rows == cols).astype(jnp.float32)], axis=1)
    count = PANEL // TILE
    tiles = [both[TILE * i : TILE * (i + 1)] for i in range(count)]
    sub = lax.broadcasted_iota(jnp.int32, (TILE, 2 * PANEL), 0)
    row = lambda k, j: band[k, pl.ds(j, TILE, stride=0), :]
    done = []
    for k in range(count):
        columns = [
            [spread(tiles[i][:, TILE * k + j : TILE * k + j + 1]) for j in range(TILE)] for i in range(k, count)
        ]
        state = list(columns[0]) + [tiles[k]]
        for m, x in enumerate(state):
            band[m] = x
        final = jnp.zeros_like(tiles[k])
        for j in range(0, TILE, 2):
            first, second = sub == j, sub == j + 1
            a, b, c = row(j, j), row(j + 1, j), row(j + 1, j + 1)
            minor = a * c - b * b
            inverse = 1.0 / minor
            left, right, body = state[j], state[j + 1], state[TILE]
            ratio = 1.0 / a
            below = (body - b * ratio * row(TILE, j)) * lax.rsqrt(minor * ratio)
            final = jnp.where(first, body * lax.rsqrt(a), jnp.where(second, below, final))
            rests = {}
            for m in range(j + 2, TILE + 1):
                upper, lower = row(m, j), row(m, j + 1)
                upper, lower = c * upper - b * lower, a * lower - b * upper
                rests[m] = state[m] - (left * upper + right * lower) * inverse
                state[m] = jnp.where(first, upper * inverse, jnp.where(second, lower * inverse, rests[m]))
            for m, rest in rests.items():
                band[m] = rest
        done.append(final)
        band[TILE] = state[TILE]
        reduced = [row(TILE, j) for j in range(TILE)]
        for i in range(k + 1, count):
            terms = [columns[i - k][j] * reduced[j] for j in range(TILE)]
            while len(terms) > 1:
                terms = [terms[j] + terms[j + 1] for j in range(0, len(terms), 2)]
            tiles[i] = tiles[i] - terms[0]
    return jnp.concatenate(done, axis=0)[:, PANEL:]


def split_three(x):
    high, rest = x.astype(jnp.bfloat16), x
    rest = rest - high.astype(jnp.float32)
    middle = rest.astype(jnp.bfloat16)
    return high, middle, (rest - middle.astype(jnp.float32)).astype(jnp.bfloat16)


def short_dot(a, b):
    a1, a2, a3 = split_three(a)
    b1, b2, b3 = split_three(b)
    a = jnp.concatenate([a1, a1, a2, a2, a1, a3], axis=1)
    b = jnp.concatenate([b1, b2, b1, b2, b3, b1], axis=0)
    return jnp.dot(a, b, preferred_element_type=jnp.float32)


def lanes_up(x):
    return (x + 127) // 128 * 128


def inverse_factor(gram, out_ref, work, band):
    rank = gram.shape[0]
    rows = lax.broadcasted_iota(jnp.int32, (rank, rank), 0)
    cols = lax.broadcasted_iota(jnp.int32, (rank, rank), 1)
    diagonal = jnp.where(rows == cols, gram, 0.0)
    scale = lax.rsqrt(jnp.sum(diagonal, axis=0, keepdims=True))
    work[:, :rank] = gram * scale * lax.rsqrt(jnp.sum(diagonal, axis=1, keepdims=True))
    work[:, rank:] = (rows == cols).astype(jnp.float32)
    for start in range(0, rank, PANEL):
        end = start + PANEL
        left, right = start // 128 * 128, rank + lanes_up(end)
        inverse = panel_inverse(work[start:end, start:end], band)
        scaled = short_dot(inverse, work[start:end, left:right])
        out_ref[start:end, : lanes_up(end)] = scaled[:, rank - left :] * scale[:, : lanes_up(end)]
        if lanes_up(end) < rank:
            out_ref[start:end, lanes_up(end) :] = jnp.zeros((PANEL, rank - lanes_up(end)), jnp.float32)
        if end < rank:
            low = end // 128 * 128
            change = short_dot(scaled[:, low - left : rank - left].T, scaled[:, low - left :])
            work[end:, low:right] = work[end:, low:right] - change[end - low :, :]


def factor_kernel(code_ref, turned_ref, out_ref, gram_ref, work, band):
    count, size, rank = code_ref.shape
    size = (size - HEAD) * 2 // 3
    code = code_ref[...].astype(jnp.int32)
    low = code[:, size : size + size // 2]
    low = jnp.concatenate([low >> 8, (low & 255) - 128], axis=1).astype(jnp.float32)
    head = code[:, size + size // 2 :].astype(jnp.float32)
    part = (code[:, :size].astype(jnp.float32) + low * (1.0 / 256.0)) * unit_of(head[:, :1], head[:, 1:2])
    turned = part.reshape(count * size, rank).T
    turned_ref[...] = turned
    gram = dot_rows(turned, turned)

    @pl.when(pl.program_id(0) == 0)
    def _():
        gram_ref[...] = gram

    @pl.when(pl.program_id(0) > 0)
    def _():
        gram_ref[...] += gram

    @pl.when(pl.program_id(0) == pl.num_programs(0) - 1)
    def _():
        inverse_factor(gram_ref[...], out_ref, work, band)


def factor(codes):
    devices, size, rank = codes.shape
    rows = (size - HEAD) * 2 // 3
    group = 256 // rows
    return pl.pallas_call(
        factor_kernel,
        grid=(devices // group,),
        in_specs=[pl.BlockSpec((group, size, rank), lambda i: (i, 0, 0))],
        out_specs=[pl.BlockSpec((rank, group * rows), lambda i: (0, i)), pl.BlockSpec((rank, rank), lambda i: (0, 0))],
        out_shape=[
            jax.ShapeDtypeStruct((rank, devices * rows), jnp.float32),
            jax.ShapeDtypeStruct((rank, rank), jnp.float32),
        ],
        scratch_shapes=[
            pltpu.VMEM((rank, rank), jnp.float32),
            pltpu.VMEM((rank, 2 * rank), jnp.float32),
            pltpu.VMEM((TILE + 1, TILE, 2 * PANEL), jnp.float32),
        ],
        compiler_params=PARAMS,
        cost_estimate=pl.CostEstimate(
            flops=12 * devices * rows * rank * rank, bytes_accessed=devices * size * rank * 4, transcendentals=rank
        ),
    )(codes)


def encode_kernel(place_ref, source_ref, turned_ref, unit_ref, inverse_ref, own_ref, code_ref, ortho_ref, mixed_ref):
    def times(a, b):
        return jnp.dot(a, b, preferred_element_type=jnp.float32)

    def turned_dot(a, b):
        return lax.dot_general(a, b, (((0,), (1,)), ((), ())), precision=HIGH, preferred_element_type=jnp.float32)

    rank = turned_ref.shape[0]
    source_high, source_low = halves(source_ref[...].astype(jnp.int32).astype(jnp.float32))
    scaled_high, scaled_low = halves(turned_ref[...] * unit_ref[...])
    most = times(jnp.concatenate([scaled_high, scaled_low], axis=0), source_high)
    part = most[:rank] + (most[rank:] + times(scaled_high, source_low))
    first, last = pl.program_id(0) == 0, pl.program_id(0) == pl.num_programs(0) - 1

    @pl.when(first)
    def _():
        mixed_ref[...] = part

    @pl.when(jnp.logical_not(first))
    def _():
        mixed_ref[...] += part

    @pl.when(last)
    def _():
        inverse = inverse_ref[...]
        ortho_ref[...] = turned_dot(own_ref[...], inverse)
        right = turned_dot(mixed_ref[...], inverse)
        rows = right.shape[0]
        square = jnp.maximum(jnp.sum(right * right, axis=0, keepdims=True), 1e-34)
        square_exponent = jnp.floor(jnp.log2(square))
        fine = square * jnp.exp2(13.0 - square_exponent)
        square_high = jnp.floor(fine)
        square_low = jnp.floor((fine - square_high) * 16384.0)
        exponent, mantissa = code_unit(jnp.max(jnp.abs(right), axis=0, keepdims=True))
        code_ref[:rows] = whole_number(jnp.floor(right * (1.0 / unit_of(exponent, mantissa)) + 0.5))
        set_head(code_ref.at[rows:], exponent, mantissa, square_exponent, square_high, square_low)


def encode(place, source, turned, unit, inverse_low, rows):
    total, share = source.shape
    rank = turned.shape[0]
    block = min(512, total)
    return pl.pallas_call(
        encode_kernel,
        grid_spec=pltpu.PrefetchScalarGridSpec(
            num_scalar_prefetch=1,
            grid=(total // block,),
            in_specs=[
                pl.BlockSpec((block, share), lambda i, place: (i, 0)),
                pl.BlockSpec((rank, block), lambda i, place: (0, i)),
                pl.BlockSpec((1, block), lambda i, place: (0, i)),
                whole(inverse_low),
                pl.BlockSpec((rank, rows), lambda i, place: (0, place[0])),
            ],
            out_specs=[
                pl.BlockSpec((share + HEAD, rank), lambda i, place: (0, 0)),
                pl.BlockSpec((rows, rank), lambda i, place: (0, 0)),
            ],
            scratch_shapes=[pltpu.VMEM((rank, share), jnp.float32)],
        ),
        out_shape=[
            jax.ShapeDtypeStruct((share + HEAD, rank), jnp.int16),
            jax.ShapeDtypeStruct((rows, rank), jnp.float32),
        ],
        compiler_params=PARAMS,
        cost_estimate=pl.CostEstimate(
            flops=6 * total * share * rank, bytes_accessed=total * (share * 2 + rank * 4), transcendentals=0
        ),
    )(place, source, turned, unit, inverse_low, turned)


def decode(code_ref):
    code = code_ref[...].astype(jnp.int32).astype(jnp.float32)
    share = code.shape[1] - HEAD
    right = code[:, :share] * unit_of(code[:, share : share + 1], code[:, share + 1 : share + 2])
    return right.reshape(code.shape[0] * share, code.shape[2])


def times_rows(split_ref, right):
    def times(a, b):
        return lax.dot_general(a, b, (((1,), (1,)), ((), ())), preferred_element_type=jnp.float32)

    right_high, right_low = halves(right)
    split = split_ref[...]
    rows = split.shape[0] // 2
    most = times(split, right_high)
    return most[:rows] + (most[rows:] + times(split[:rows], right_low))


def set_split(split_ref, x):
    rows = x.shape[0]

    @pl.when(pl.program_id(0) == 0)
    def _():
        split_ref[:rows], split_ref[rows:] = halves(x)


def momentum_kernel(momentum_ref, grad_ref, code_ref, ortho_ref, next_ref, split_ref):
    set_split(split_ref, -KEEP_SHARE * ortho_ref[...])
    change = times_rows(split_ref, decode(code_ref))
    next_ref[...] = momentum_ref[...] + grad_ref[...].astype(jnp.float32) + change


def update_kernel(gain, code_ref, ortho_ref, scale_ref, basis_ref, update_ref, split_ref):
    set_split(split_ref, gain * ortho_ref[...])
    basis = decode(code_ref) * scale_ref[...]
    basis_ref[...] = basis
    update_ref[...] = times_rows(split_ref, basis).astype(jnp.bfloat16)


def finish(momentum, grad, codes, orthonormal, scale, gain):
    rows, cols = momentum.shape
    shares, share, rank = codes.shape
    share -= HEAD
    group = max(1, min(1024 // share, shares))
    block = group * share
    wide = pl.BlockSpec((rows, block), lambda i: (0, i))
    tall = pl.BlockSpec((block, rank), lambda i: (i, 0))
    coded = pl.BlockSpec((group, share + HEAD, rank), lambda i: (i, 0, 0))
    split = [pltpu.VMEM((2 * rows, rank), jnp.bfloat16)]
    flops = 6 * rows * cols * rank
    momentum_next = pl.pallas_call(
        momentum_kernel,
        grid=(cols // block,),
        in_specs=[wide, wide, coded, whole(orthonormal)],
        out_specs=wide,
        out_shape=jax.ShapeDtypeStruct((rows, cols), jnp.float32),
        scratch_shapes=split,
        compiler_params=PARAMS,
        cost_estimate=pl.CostEstimate(
            flops=flops, bytes_accessed=rows * cols * 10 + cols * rank * 2, transcendentals=0
        ),
    )(momentum, grad, codes, orthonormal)
    q_next, update = pl.pallas_call(
        functools.partial(update_kernel, gain),
        grid=(cols // block,),
        in_specs=[coded, whole(orthonormal), whole(scale)],
        out_specs=[tall, wide],
        out_shape=[
            jax.ShapeDtypeStruct((cols, rank), jnp.float32),
            jax.ShapeDtypeStruct((rows, cols), jnp.bfloat16),
        ],
        scratch_shapes=split,
        compiler_params=PARAMS,
        cost_estimate=pl.CostEstimate(flops=flops, bytes_accessed=rows * cols * 2 + cols * rank * 6, transcendentals=0),
    )(codes, orthonormal, scale)
    return momentum_next, q_next, update


def on_device(momentum, grad, q_stored, perm):
    block_rows = q_stored.shape[0]
    num_blocks = lax.axis_size("fsdp")
    num_cols = lax.axis_size("tp")
    rank_total = block_rows * num_blocks
    rows, cols = momentum.shape
    row_total, col_total = rows * num_blocks, cols * num_cols
    share = cols // num_blocks

    basis, codes = prepare(momentum, grad, q_stored, share)
    codes = codes.reshape(-1, rows, codes.shape[2] // share, share).swapaxes(1, 2).reshape(num_blocks, rows, share)
    basis = lax.all_gather(basis, "fsdp", axis=0, tiled=True)
    codes, basis = lax.optimization_barrier((codes, basis))
    codes = lax.all_to_all(codes, "fsdp", split_axis=0, concat_axis=0).reshape(row_total, share)
    head = basis.reshape(num_blocks, block_rows, cols + rows)[:, -2:, cols:].astype(jnp.float32)
    unit = unit_of(head[:, 0], head[:, 1]).reshape(1, row_total)

    near, step = project(momentum, grad, basis), 1
    while 4 * step < num_cols:
        near = near + exchange(near, "tp", step)
        step *= 2
    parts = [near] + [exchange(near, "tp", k) for k in range(step, num_cols, step)]
    packed = lax.all_gather(pack(perm, parts), "fsdp", axis=0)
    packed, codes = lax.optimization_barrier((packed, codes))
    turned, inverse_low = factor(packed)
    code, orthonormal = encode(lax.axis_index("fsdp").reshape(1), codes, turned, unit, inverse_low, rows)
    gathered = lax.all_gather(code, "fsdp", axis=0)
    head = gathered[:, share : share + 5].astype(jnp.float32)
    parts = (head[:, 3] + head[:, 4] * (1.0 / 16384.0)) * jnp.exp2(head[:, 2] - 13.0)
    squares = quad_sum(jnp.sum(parts, axis=0, keepdims=True), "tp")
    scale = lax.rsqrt(squares / col_total + EPSILON)
    return tuple(finish(momentum, grad, gathered, orthonormal, scale, math.sqrt(row_total / rank_total)))


def solution(mesh):
    return jax.shard_map(
        on_device,
        mesh=mesh,
        in_specs=(P("fsdp", "tp"), P("fsdp", "tp"), P("fsdp", "tp"), P()),
        out_specs=(P("fsdp", "tp"), P("tp", None), P("fsdp", "tp")),
        check_vma=False,
    )
```

```python
import functools
import math

import jax
import jax.numpy as jnp
from jax import lax
from jax.experimental import pallas as pl
from jax.experimental.pallas import tpu as pltpu
from jax.sharding import PartitionSpec as P

EPSILON = 1e-06
KEEP_SHARE = 0.5
HIGH = lax.Precision.HIGHEST
PANEL = 64
TILE = 16
HEAD = 16
TOP = 32766.0
PARAMS = pltpu.CompilerParams(vmem_limit_bytes=40 * 1024 * 1024)
FLOW = pltpu.CompilerParams(vmem_limit_bytes=53 * 1024 * 1024)
STREAM = pltpu.CompilerParams(vmem_limit_bytes=54 * 1024 * 1024)


def halves(x):
    high = x.astype(jnp.bfloat16)
    return high, (x - high.astype(jnp.float32)).astype(jnp.bfloat16)


def exchange(x, axis, k):
    return lax.ppermute(x, axis, [(i, i ^ k) for i in range(lax.axis_size(axis))])


def butterfly_sum(x, axis, step=1):
    while step < lax.axis_size(axis):
        x = x + exchange(x, axis, step)
        step *= 2
    return x


def quad_sum(x, axis, step=1):
    if lax.axis_size(axis) != 4 * step:
        return butterfly_sum(x, axis, step)
    near, far, across = [exchange(x, axis, k * step) for k in range(1, 4)]
    return (x + near) + (far + across)


def whole(x):
    return pl.BlockSpec(x.shape, lambda *_: (0,) * len(x.shape))


def dot_rows(a, b):
    return lax.dot_general(a, b, (((1,), (1,)), ((), ())), precision=HIGH, preferred_element_type=jnp.float32)


def unit_of(exponent, mantissa):
    return mantissa * jnp.exp2(exponent - 13.0)


def code_unit(top):
    top = jnp.maximum(top, 1e-28) * (1.0 / TOP)
    exponent = jnp.floor(jnp.log2(top))
    return exponent, jnp.floor(top * jnp.exp2(13.0 - exponent)) + 1.0


def whole_number(x):
    return x.astype(jnp.int32).astype(jnp.int16)


def set_head(head_ref, *rows):
    place = lax.broadcasted_iota(jnp.int32, head_ref.shape, 0)
    head = jnp.zeros(head_ref.shape, jnp.float32)
    for k, row in enumerate(rows):
        head = jnp.where(place == k, row, head)
    head_ref[...] = whole_number(head)


def code_basis(basis):
    value = basis.astype(jnp.float32)
    size = jnp.abs(value)
    normal = size >= 2.0**-126
    exponent = jnp.floor(jnp.log2(jnp.where(normal, size, 1.0)))
    code = 128.0 * (exponent + 126.0) + jnp.floor(128.0 * (size * jnp.exp2(-exponent)) + 0.5)
    return whole_number(jnp.where(normal, jnp.where(value < 0.0, code - 32768.0, code), 0.0))


def prepare_kernel(momentum_ref, grad_ref, basis_ref, pack_ref, code_ref, head_ref):
    rows, cols = momentum_ref.shape
    width = code_ref.shape[-1]
    spans = [slice(i, i + width) for i in range(0, cols, width)]
    combined = lambda span: momentum_ref[:, span] + grad_ref[:, span].astype(jnp.float32)
    top = functools.reduce(jnp.maximum, [jnp.abs(combined(span)) for span in spans])
    exponent, mantissa = code_unit(jnp.max(top, axis=1, keepdims=True))
    inverse = 1.0 / unit_of(exponent, mantissa)
    for k, span in enumerate(spans):
        code_ref[k] = whole_number(jnp.floor(combined(span) * inverse + 0.5))
        pack_ref[:, span] = code_basis(basis_ref[:, span])
    step = pl.program_id(0)
    here = pl.ds(pl.multiple_of(step * rows, rows), rows)
    for k, column in enumerate((exponent, mantissa)):
        head_ref[k, here, :] = jnp.broadcast_to(column, (rows, head_ref.shape[2]))
    pack_ref[:, cols:] = jnp.zeros((pack_ref.shape[0], pack_ref.shape[1] - cols), jnp.int16)

    @pl.when(step == pl.num_programs(0) - 1)
    def _():
        place = lax.broadcasted_iota(jnp.int32, (pack_ref.shape[0], head_ref.shape[1]), 0)
        first, second = head_ref[0].T[:1], head_ref[1].T[:1]
        last = pack_ref.shape[0] - 1
        head = jnp.where(place == last - 1, first, jnp.where(place == last, second, 0.0))
        pack_ref[:, cols:] = whole_number(head)


def prepare(momentum, grad, basis, share):
    rows, cols = momentum.shape
    width = share if share % 128 == 0 else cols
    steps = 2 if basis.shape[0] % 32 == 0 else 1
    wide = pl.BlockSpec((rows // steps, cols), lambda i: (i, 0))
    ranks = basis.shape[0] // steps
    return pl.pallas_call(
        prepare_kernel,
        grid=(steps,),
        in_specs=[wide, wide, pl.BlockSpec((ranks, cols), lambda i: (i, 0))],
        out_specs=[
            pl.BlockSpec((ranks, cols + rows), lambda i: (i, 0)),
            pl.BlockSpec((cols // width, rows // steps, width), lambda i: (0, i, 0)),
        ],
        out_shape=[
            jax.ShapeDtypeStruct((basis.shape[0], cols + rows), jnp.int16),
            jax.ShapeDtypeStruct((cols // width, rows, width), jnp.int16),
        ],
        scratch_shapes=[pltpu.VMEM((2, rows, 128), jnp.float32)],
        compiler_params=STREAM,
        cost_estimate=pl.CostEstimate(flops=10 * rows * cols, bytes_accessed=rows * cols * 8, transcendentals=0),
    )(momentum, grad, basis)


def project_kernel(momentum_ref, grad_ref, code_ref, out_ref):
    code = code_ref[...].astype(jnp.int32)
    power = jnp.exp2(((code >> 7) & 255).astype(jnp.float32) - 134.0)
    value = ((code & 127) | 128).astype(jnp.float32) * power
    basis = jnp.where(code < 0, -value, value).astype(jnp.bfloat16)
    combined = momentum_ref[...] + grad_ref[...].astype(jnp.float32)
    rows = combined.shape[0]
    part = lax.dot_general(
        jnp.concatenate(halves(combined), axis=0),
        basis,
        (((1,), (1,)), ((), ())),
        preferred_element_type=jnp.float32,
    )
    part = part[:rows] + part[rows:]

    @pl.when(pl.program_id(0) == 0)
    def _():
        out_ref[...] = part

    @pl.when(pl.program_id(0) > 0)
    def _():
        out_ref[...] += part


def project(momentum, grad, codes):
    rows, cols = momentum.shape
    rank = codes.shape[0]
    block = min(1024, cols)
    wide = pl.BlockSpec((rows, block), lambda i: (0, i))
    return pl.pallas_call(
        project_kernel,
        grid=(cols // block,),
        in_specs=[wide, wide, pl.BlockSpec((rank, block), lambda i: (0, i))],
        out_specs=pl.BlockSpec((rows, rank), lambda i: (0, 0)),
        out_shape=jax.ShapeDtypeStruct((rows, rank), jnp.float32),
        compiler_params=FLOW,
        cost_estimate=pl.CostEstimate(
            flops=4 * rows * cols * rank, bytes_accessed=rows * cols * 6 + rank * cols * 2, transcendentals=rank * cols
        ),
    )(momentum, grad, codes)


def pack_kernel(perm_ref, *refs):
    part_refs, out_ref = refs[:-1], refs[-1]
    rows, rank = part_refs[0].shape
    blocks = perm_ref.shape[0]
    size = rank // blocks
    stored = lax.broadcasted_iota(jnp.int32, (rank, rank), 0)
    target = jnp.zeros((rank, rank), jnp.int32)
    for s in range(blocks):
        target = jnp.where(stored // size == s, perm_ref[s] * size + stored % size, target)
    order = (target == lax.broadcasted_iota(jnp.int32, (rank, rank), 1)).astype(jnp.float32)
    parts = [ref[...] for ref in part_refs]
    while len(parts) > 1:
        parts = [parts[k] + parts[k + 1] for k in range(0, len(parts), 2)]
    total = jnp.dot(parts[0], order, precision=HIGH, preferred_element_type=jnp.float32)
    exponent, mantissa = code_unit(jnp.max(jnp.abs(total), axis=0, keepdims=True))
    value = total * (1.0 / unit_of(exponent, mantissa))
    high = jnp.floor(value + 0.5)
    out_ref[:rows] = whole_number(high)
    low = jnp.minimum(jnp.floor((value - high) * 256.0 + 0.5), 127.0)
    half = rows // 2
    out_ref[rows : rows + half] = whole_number(low[:half] * 256.0 + (low[half:] + 128.0))
    set_head(out_ref.at[rows + half :], exponent, mantissa)


def pack(perm, parts):
    rows, rank = parts[0].shape
    return pl.pallas_call(
        pack_kernel,
        grid_spec=pltpu.PrefetchScalarGridSpec(
            num_scalar_prefetch=1,
            grid=(1,),
            in_specs=[whole(x) for x in parts],
            out_specs=pl.BlockSpec((rows + rows // 2 + HEAD, rank), lambda *_: (0, 0)),
        ),
        out_shape=jax.ShapeDtypeStruct((rows + rows // 2 + HEAD, rank), jnp.int16),
        compiler_params=PARAMS,
        cost_estimate=pl.CostEstimate(flops=12 * rows * rank * rank, bytes_accessed=rank * rank * 4, transcendentals=0),
    )(perm, *parts)


def spread(row):
    return jnp.broadcast_to(row, (TILE, 2 * PANEL))


def panel_inverse(block, band):
    rows = lax.broadcasted_iota(jnp.int32, (PANEL, PANEL), 0)
    cols = lax.broadcasted_iota(jnp.int32, (PANEL, PANEL), 1)
    both = jnp.concatenate([block, (rows == cols).astype(jnp.float32)], axis=1)
    count = PANEL // TILE
    tiles = [both[TILE * i : TILE * (i + 1)] for i in range(count)]
    sub = lax.broadcasted_iota(jnp.int32, (TILE, 2 * PANEL), 0)
    row = lambda k, j: band[k, pl.ds(j, TILE, stride=0), :]
    done = []
    for k in range(count):
        columns = [
            [spread(tiles[i][:, TILE * k + j : TILE * k + j + 1]) for j in range(TILE)] for i in range(k, count)
        ]
        state = list(columns[0]) + [tiles[k]]
        for m, x in enumerate(state):
            band[m] = x
        final = jnp.zeros_like(tiles[k])
        for j in range(0, TILE, 2):
            first, second = sub == j, sub == j + 1
            a, b, c = row(j, j), row(j + 1, j), row(j + 1, j + 1)
            minor = a * c - b * b
            inverse = 1.0 / minor
            left, right, body = state[j], state[j + 1], state[TILE]
            ratio = 1.0 / a
            below = (body - b * ratio * row(TILE, j)) * lax.rsqrt(minor * ratio)
            final = jnp.where(first, body * lax.rsqrt(a), jnp.where(second, below, final))
            rests = {}
            for m in range(j + 2, TILE + 1):
                upper, lower = row(m, j), row(m, j + 1)
                upper, lower = c * upper - b * lower, a * lower - b * upper
                rests[m] = state[m] - (left * upper + right * lower) * inverse
                state[m] = jnp.where(first, upper * inverse, jnp.where(second, lower * inverse, rests[m]))
            for m, rest in rests.items():
                band[m] = rest
        done.append(final)
        band[TILE] = state[TILE]
        reduced = [row(TILE, j) for j in range(TILE)]
        for i in range(k + 1, count):
            terms = [columns[i - k][j] * reduced[j] for j in range(TILE)]
            while len(terms) > 1:
                terms = [terms[j] + terms[j + 1] for j in range(0, len(terms), 2)]
            tiles[i] = tiles[i] - terms[0]
    return jnp.concatenate(done, axis=0)[:, PANEL:]


def split_three(x):
    high, rest = x.astype(jnp.bfloat16), x
    rest = rest - high.astype(jnp.float32)
    middle = rest.astype(jnp.bfloat16)
    return high, middle, (rest - middle.astype(jnp.float32)).astype(jnp.bfloat16)


def short_dot(a, b):
    a1, a2, a3 = split_three(a)
    b1, b2, b3 = split_three(b)
    a = jnp.concatenate([a1, a1, a2, a2, a1, a3], axis=1)
    b = jnp.concatenate([b1, b2, b1, b2, b3, b1], axis=0)
    return jnp.dot(a, b, preferred_element_type=jnp.float32)


def lanes_up(x):
    return (x + 127) // 128 * 128


def inverse_factor(gram, out_ref, work, band):
    rank = gram.shape[0]
    rows = lax.broadcasted_iota(jnp.int32, (rank, rank), 0)
    cols = lax.broadcasted_iota(jnp.int32, (rank, rank), 1)
    diagonal = jnp.where(rows == cols, gram, 0.0)
    scale = lax.rsqrt(jnp.sum(diagonal, axis=0, keepdims=True))
    work[:, :rank] = gram * scale * lax.rsqrt(jnp.sum(diagonal, axis=1, keepdims=True))
    work[:, rank:] = (rows == cols).astype(jnp.float32)
    for start in range(0, rank, PANEL):
        end = start + PANEL
        left, right = start // 128 * 128, rank + lanes_up(end)
        inverse = panel_inverse(work[start:end, start:end], band)
        scaled = short_dot(inverse, work[start:end, left:right])
        out_ref[start:end, : lanes_up(end)] = scaled[:, rank - left :] * scale[:, : lanes_up(end)]
        if lanes_up(end) < rank:
            out_ref[start:end, lanes_up(end) :] = jnp.zeros((PANEL, rank - lanes_up(end)), jnp.float32)
        if end < rank:
            low = end // 128 * 128
            change = short_dot(scaled[:, low - left : rank - left].T, scaled[:, low - left :])
            work[end:, low:right] = work[end:, low:right] - change[end - low :, :]


def factor_kernel(code_ref, turned_ref, out_ref, gram_ref, mixed_ref, work, band):
    count, size, rank = code_ref.shape
    size = (size - HEAD) * 2 // 3
    code = code_ref[...].astype(jnp.int32)
    low = code[:, size : size + size // 2]
    low = jnp.concatenate([low >> 8, (low & 255) - 128], axis=1).astype(jnp.float32)
    head = code[:, size + size // 2 :].astype(jnp.float32)
    part = (code[:, :size].astype(jnp.float32) + low * (1.0 / 256.0)) * unit_of(head[:, :1], head[:, 1:2])
    turned = part.reshape(count * size, rank).T
    turned_ref[...] = turned

    def times(a, b):
        a, b = jnp.concatenate(a, axis=1), jnp.concatenate(b, axis=1)
        return lax.dot_general(a, b, (((1,), (1,)), ((), ())), preferred_element_type=jnp.float32)

    high, middle, small = split_three(turned)
    even, mixed = times((high, middle), (high, middle)), times((high, high), (middle, small))

    @pl.when(pl.program_id(0) == 0)
    def _():
        gram_ref[...] = even
        mixed_ref[...] = mixed

    @pl.when(pl.program_id(0) > 0)
    def _():
        gram_ref[...] += even
        mixed_ref[...] += mixed

    @pl.when(pl.program_id(0) == pl.num_programs(0) - 1)
    def _():
        mixed = mixed_ref[...]
        inverse_factor(gram_ref[...] + (mixed + mixed.T), out_ref, work, band)


def factor(codes):
    devices, size, rank = codes.shape
    rows = (size - HEAD) * 2 // 3
    group = 256 // rows
    return pl.pallas_call(
        factor_kernel,
        grid=(devices // group,),
        in_specs=[pl.BlockSpec((group, size, rank), lambda i: (i, 0, 0))],
        out_specs=[pl.BlockSpec((rank, group * rows), lambda i: (0, i)), pl.BlockSpec((rank, rank), lambda i: (0, 0))],
        out_shape=[
            jax.ShapeDtypeStruct((rank, devices * rows), jnp.float32),
            jax.ShapeDtypeStruct((rank, rank), jnp.float32),
        ],
        scratch_shapes=[
            pltpu.VMEM((rank, rank), jnp.float32),
            pltpu.VMEM((rank, rank), jnp.float32),
            pltpu.VMEM((rank, 2 * rank), jnp.float32),
            pltpu.VMEM((TILE + 1, TILE, 2 * PANEL), jnp.float32),
        ],
        compiler_params=PARAMS,
        cost_estimate=pl.CostEstimate(
            flops=12 * devices * rows * rank * rank, bytes_accessed=devices * size * rank * 4, transcendentals=rank
        ),
    )(codes)


def encode_kernel(place_ref, source_ref, turned_ref, unit_ref, inverse_ref, own_ref, code_ref, ortho_ref, mixed_ref):
    def times(a, b):
        return jnp.dot(a, b, preferred_element_type=jnp.float32)

    def turned_dot(a, b):
        return lax.dot_general(a, b, (((0,), (1,)), ((), ())), precision=HIGH, preferred_element_type=jnp.float32)

    rank = turned_ref.shape[0]
    source_high, source_low = halves(source_ref[...].astype(jnp.int32).astype(jnp.float32))
    scaled_high, scaled_low = halves(turned_ref[...] * unit_ref[...])
    most = times(jnp.concatenate([scaled_high, scaled_low], axis=0), source_high)
    part = most[:rank] + (most[rank:] + times(scaled_high, source_low))
    first, last = pl.program_id(0) == 0, pl.program_id(0) == pl.num_programs(0) - 1

    @pl.when(first)
    def _():
        mixed_ref[...] = part

    @pl.when(jnp.logical_not(first))
    def _():
        mixed_ref[...] += part

    @pl.when(last)
    def _():
        inverse = inverse_ref[...]
        ortho_ref[...] = turned_dot(own_ref[...], inverse)
        right = turned_dot(mixed_ref[...], inverse)
        rows = right.shape[0]
        square = jnp.maximum(jnp.sum(right * right, axis=0, keepdims=True), 1e-34)
        square_exponent = jnp.floor(jnp.log2(square))
        fine = square * jnp.exp2(13.0 - square_exponent)
        square_high = jnp.floor(fine)
        square_low = jnp.floor((fine - square_high) * 16384.0)
        exponent, mantissa = code_unit(jnp.max(jnp.abs(right), axis=0, keepdims=True))
        code_ref[:rows] = whole_number(jnp.floor(right * (1.0 / unit_of(exponent, mantissa)) + 0.5))
        set_head(code_ref.at[rows:], exponent, mantissa, square_exponent, square_high, square_low)


def encode(place, source, turned, unit, inverse_low, rows):
    total, share = source.shape
    rank = turned.shape[0]
    block = min(512, total)
    return pl.pallas_call(
        encode_kernel,
        grid_spec=pltpu.PrefetchScalarGridSpec(
            num_scalar_prefetch=1,
            grid=(total // block,),
            in_specs=[
                pl.BlockSpec((block, share), lambda i, place: (i, 0)),
                pl.BlockSpec((rank, block), lambda i, place: (0, i)),
                pl.BlockSpec((1, block), lambda i, place: (0, i)),
                whole(inverse_low),
                pl.BlockSpec((rank, rows), lambda i, place: (0, place[0])),
            ],
            out_specs=[
                pl.BlockSpec((share + HEAD, rank), lambda i, place: (0, 0)),
                pl.BlockSpec((rows, rank), lambda i, place: (0, 0)),
            ],
            scratch_shapes=[pltpu.VMEM((rank, share), jnp.float32)],
        ),
        out_shape=[
            jax.ShapeDtypeStruct((share + HEAD, rank), jnp.int16),
            jax.ShapeDtypeStruct((rows, rank), jnp.float32),
        ],
        compiler_params=PARAMS,
        cost_estimate=pl.CostEstimate(
            flops=6 * total * share * rank, bytes_accessed=total * (share * 2 + rank * 4), transcendentals=0
        ),
    )(place, source, turned, unit, inverse_low, turned)


def decode(code_ref):
    code = code_ref[...].astype(jnp.int32).astype(jnp.float32)
    share = code.shape[1] - HEAD
    right = code[:, :share] * unit_of(code[:, share : share + 1], code[:, share + 1 : share + 2])
    return right.reshape(code.shape[0] * share, code.shape[2])


def times_rows(split_ref, right):
    def times(a, b):
        return lax.dot_general(a, b, (((1,), (1,)), ((), ())), preferred_element_type=jnp.float32)

    right_high, right_low = halves(right)
    split = split_ref[...]
    rows = split.shape[0] // 2
    most = times(split, right_high)
    return most[:rows] + (most[rows:] + times(split[:rows], right_low))


def set_split(split_ref, x):
    rows = x.shape[0]

    @pl.when(pl.program_id(0) == 0)
    def _():
        split_ref[:rows], split_ref[rows:] = halves(x)


def momentum_kernel(momentum_ref, grad_ref, code_ref, ortho_ref, next_ref, split_ref):
    set_split(split_ref, -KEEP_SHARE * ortho_ref[...])
    change = times_rows(split_ref, decode(code_ref))
    next_ref[...] = momentum_ref[...] + grad_ref[...].astype(jnp.float32) + change


def update_kernel(gain, code_ref, ortho_ref, scale_ref, basis_ref, update_ref, split_ref):
    set_split(split_ref, gain * ortho_ref[...])
    basis = decode(code_ref) * scale_ref[...]
    basis_ref[...] = basis
    update_ref[...] = times_rows(split_ref, basis).astype(jnp.bfloat16)


def finish(momentum, grad, codes, orthonormal, scale, gain):
    rows, cols = momentum.shape
    shares, share, rank = codes.shape
    share -= HEAD
    group = max(1, min(1024 // share, shares))
    block = group * share
    wide = pl.BlockSpec((rows, block), lambda i: (0, i))
    tall = pl.BlockSpec((block, rank), lambda i: (i, 0))
    coded = pl.BlockSpec((group, share + HEAD, rank), lambda i: (i, 0, 0))
    split = [pltpu.VMEM((2 * rows, rank), jnp.bfloat16)]
    flops = 6 * rows * cols * rank
    momentum_next = pl.pallas_call(
        momentum_kernel,
        grid=(cols // block,),
        in_specs=[wide, wide, coded, whole(orthonormal)],
        out_specs=wide,
        out_shape=jax.ShapeDtypeStruct((rows, cols), jnp.float32),
        scratch_shapes=split,
        compiler_params=PARAMS,
        cost_estimate=pl.CostEstimate(
            flops=flops, bytes_accessed=rows * cols * 10 + cols * rank * 2, transcendentals=0
        ),
    )(momentum, grad, codes, orthonormal)
    q_next, update = pl.pallas_call(
        functools.partial(update_kernel, gain),
        grid=(cols // block,),
        in_specs=[coded, whole(orthonormal), whole(scale)],
        out_specs=[tall, wide],
        out_shape=[
            jax.ShapeDtypeStruct((cols, rank), jnp.float32),
            jax.ShapeDtypeStruct((rows, cols), jnp.bfloat16),
        ],
        scratch_shapes=split,
        compiler_params=PARAMS,
        cost_estimate=pl.CostEstimate(flops=flops, bytes_accessed=rows * cols * 2 + cols * rank * 6, transcendentals=0),
    )(codes, orthonormal, scale)
    return momentum_next, q_next, update


def on_device(momentum, grad, q_stored, perm):
    block_rows = q_stored.shape[0]
    num_blocks = lax.axis_size("fsdp")
    num_cols = lax.axis_size("tp")
    rank_total = block_rows * num_blocks
    rows, cols = momentum.shape
    row_total, col_total = rows * num_blocks, cols * num_cols
    share = cols // num_blocks

    basis, codes = prepare(momentum, grad, q_stored, share)
    codes = codes.reshape(-1, rows, codes.shape[2] // share, share).swapaxes(1, 2).reshape(num_blocks, rows, share)
    basis = lax.all_gather(basis, "fsdp", axis=0, tiled=True)
    codes, basis = lax.optimization_barrier((codes, basis))
    codes = lax.all_to_all(codes, "fsdp", split_axis=0, concat_axis=0).reshape(row_total, share)
    head = basis.reshape(num_blocks, block_rows, cols + rows)[:, -2:, cols:].astype(jnp.float32)
    unit = unit_of(head[:, 0], head[:, 1]).reshape(1, row_total)

    near, step = project(momentum, grad, basis), 1
    while 4 * step < num_cols:
        near = near + exchange(near, "tp", step)
        step *= 2
    parts = [near] + [exchange(near, "tp", k) for k in range(step, num_cols, step)]
    packed = lax.all_gather(pack(perm, parts), "fsdp", axis=0)
    packed, codes = lax.optimization_barrier((packed, codes))
    turned, inverse_low = factor(packed)
    code, orthonormal = encode(lax.axis_index("fsdp").reshape(1), codes, turned, unit, inverse_low, rows)
    gathered = lax.all_gather(code, "fsdp", axis=0)
    head = gathered[:, share : share + 5].astype(jnp.float32)
    parts = (head[:, 3] + head[:, 4] * (1.0 / 16384.0)) * jnp.exp2(head[:, 2] - 13.0)
    squares = quad_sum(jnp.sum(parts, axis=0, keepdims=True), "tp")
    scale = lax.rsqrt(squares / col_total + EPSILON)
    return tuple(finish(momentum, grad, gathered, orthonormal, scale, math.sqrt(row_total / rank_total)))


def solution(mesh):
    return jax.shard_map(
        on_device,
        mesh=mesh,
        in_specs=(P("fsdp", "tp"), P("fsdp", "tp"), P("fsdp", "tp"), P()),
        out_specs=(P("fsdp", "tp"), P("tp", None), P("fsdp", "tp")),
        check_vma=False,
    )
```

```python
import functools
import math

import jax
import jax.numpy as jnp
from jax import lax
from jax.experimental import pallas as pl
from jax.experimental.pallas import tpu as pltpu
from jax.sharding import PartitionSpec as P

EPSILON = 1e-06
KEEP_SHARE = 0.5
HIGH = lax.Precision.HIGHEST
PANEL = 64
TILE = 16
HEAD = 16
TOP = 32766.0
PARAMS = pltpu.CompilerParams(vmem_limit_bytes=40 * 1024 * 1024)
FLOW = pltpu.CompilerParams(vmem_limit_bytes=53 * 1024 * 1024)
STREAM = pltpu.CompilerParams(vmem_limit_bytes=54 * 1024 * 1024)


def halves(x):
    high = x.astype(jnp.bfloat16)
    return high, (x - high.astype(jnp.float32)).astype(jnp.bfloat16)


def exchange(x, axis, k):
    return lax.ppermute(x, axis, [(i, i ^ k) for i in range(lax.axis_size(axis))])


def butterfly_sum(x, axis, step=1):
    while step < lax.axis_size(axis):
        x = x + exchange(x, axis, step)
        step *= 2
    return x


def quad_sum(x, axis, step=1):
    if lax.axis_size(axis) != 4 * step:
        return butterfly_sum(x, axis, step)
    near, far, across = [exchange(x, axis, k * step) for k in range(1, 4)]
    return (x + near) + (far + across)


def whole(x):
    return pl.BlockSpec(x.shape, lambda *_: (0,) * len(x.shape))


def dot_rows(a, b):
    return lax.dot_general(a, b, (((1,), (1,)), ((), ())), precision=HIGH, preferred_element_type=jnp.float32)


def unit_of(exponent, mantissa):
    return mantissa * jnp.exp2(exponent - 13.0)


def code_unit(top):
    top = jnp.maximum(top, 1e-28) * (1.0 / TOP)
    exponent = jnp.floor(jnp.log2(top))
    return exponent, jnp.floor(top * jnp.exp2(13.0 - exponent)) + 1.0


def whole_number(x):
    return x.astype(jnp.int32).astype(jnp.int16)


def set_head(head_ref, *rows):
    place = lax.broadcasted_iota(jnp.int32, head_ref.shape, 0)
    head = jnp.zeros(head_ref.shape, jnp.float32)
    for k, row in enumerate(rows):
        head = jnp.where(place == k, row, head)
    head_ref[...] = whole_number(head)


def code_basis(basis):
    value = basis.astype(jnp.float32)
    size = jnp.abs(value)
    normal = size >= 2.0**-126
    exponent = jnp.floor(jnp.log2(jnp.where(normal, size, 1.0)))
    code = 128.0 * (exponent + 126.0) + jnp.floor(128.0 * (size * jnp.exp2(-exponent)) + 0.5)
    return whole_number(jnp.where(normal, jnp.where(value < 0.0, code - 32768.0, code), 0.0))


def prepare_kernel(momentum_ref, grad_ref, basis_ref, pack_ref, code_ref, head_ref):
    rows, cols = momentum_ref.shape
    width = code_ref.shape[-1]
    spans = [slice(i, i + width) for i in range(0, cols, width)]
    combined = lambda span: momentum_ref[:, span] + grad_ref[:, span].astype(jnp.float32)
    top = functools.reduce(jnp.maximum, [jnp.abs(combined(span)) for span in spans])
    exponent, mantissa = code_unit(jnp.max(top, axis=1, keepdims=True))
    inverse = 1.0 / unit_of(exponent, mantissa)
    for k, span in enumerate(spans):
        code_ref[k] = whole_number(jnp.floor(combined(span) * inverse + 0.5))
        pack_ref[:, span] = code_basis(basis_ref[:, span])
    step = pl.program_id(0)
    here = pl.ds(pl.multiple_of(step * rows, rows), rows)
    for k, column in enumerate((exponent, mantissa)):
        head_ref[k, here, :] = jnp.broadcast_to(column, (rows, head_ref.shape[2]))
    pack_ref[:, cols:] = jnp.zeros((pack_ref.shape[0], pack_ref.shape[1] - cols), jnp.int16)

    @pl.when(step == pl.num_programs(0) - 1)
    def _():
        place = lax.broadcasted_iota(jnp.int32, (pack_ref.shape[0], head_ref.shape[1]), 0)
        first, second = head_ref[0].T[:1], head_ref[1].T[:1]
        last = pack_ref.shape[0] - 1
        head = jnp.where(place == last - 1, first, jnp.where(place == last, second, 0.0))
        pack_ref[:, cols:] = whole_number(head)


def prepare(momentum, grad, basis, share):
    rows, cols = momentum.shape
    width = share if share % 128 == 0 else cols
    steps = 2 if basis.shape[0] % 32 == 0 else 1
    wide = pl.BlockSpec((rows // steps, cols), lambda i: (i, 0))
    ranks = basis.shape[0] // steps
    return pl.pallas_call(
        prepare_kernel,
        grid=(steps,),
        in_specs=[wide, wide, pl.BlockSpec((ranks, cols), lambda i: (i, 0))],
        out_specs=[
            pl.BlockSpec((ranks, cols + rows), lambda i: (i, 0)),
            pl.BlockSpec((cols // width, rows // steps, width), lambda i: (0, i, 0)),
        ],
        out_shape=[
            jax.ShapeDtypeStruct((basis.shape[0], cols + rows), jnp.int16),
            jax.ShapeDtypeStruct((cols // width, rows, width), jnp.int16),
        ],
        scratch_shapes=[pltpu.VMEM((2, rows, 128), jnp.float32)],
        compiler_params=STREAM,
        cost_estimate=pl.CostEstimate(flops=10 * rows * cols, bytes_accessed=rows * cols * 8, transcendentals=0),
    )(momentum, grad, basis)


def project_kernel(momentum_ref, grad_ref, code_ref, out_ref):
    code = code_ref[...].astype(jnp.int32)
    power = jnp.exp2(((code >> 7) & 255).astype(jnp.float32) - 134.0)
    value = ((code & 127) | 128).astype(jnp.float32) * power
    basis = jnp.where(code < 0, -value, value).astype(jnp.bfloat16)
    combined = momentum_ref[...] + grad_ref[...].astype(jnp.float32)
    rows = combined.shape[0]
    part = lax.dot_general(
        jnp.concatenate(halves(combined), axis=0),
        basis,
        (((1,), (1,)), ((), ())),
        preferred_element_type=jnp.float32,
    )
    part = part[:rows] + part[rows:]

    @pl.when(pl.program_id(0) == 0)
    def _():
        out_ref[...] = part

    @pl.when(pl.program_id(0) > 0)
    def _():
        out_ref[...] += part


def project(momentum, grad, codes):
    rows, cols = momentum.shape
    rank = codes.shape[0]
    block = min(1024, cols)
    wide = pl.BlockSpec((rows, block), lambda i: (0, i))
    return pl.pallas_call(
        project_kernel,
        grid=(cols // block,),
        in_specs=[wide, wide, pl.BlockSpec((rank, block), lambda i: (0, i))],
        out_specs=pl.BlockSpec((rows, rank), lambda i: (0, 0)),
        out_shape=jax.ShapeDtypeStruct((rows, rank), jnp.float32),
        compiler_params=FLOW,
        cost_estimate=pl.CostEstimate(
            flops=4 * rows * cols * rank, bytes_accessed=rows * cols * 6 + rank * cols * 2, transcendentals=rank * cols
        ),
    )(momentum, grad, codes)


def pack_kernel(perm_ref, *refs):
    part_refs, out_ref = refs[:-1], refs[-1]
    rows, rank = part_refs[0].shape
    blocks = perm_ref.shape[0]
    size = rank // blocks
    stored = lax.broadcasted_iota(jnp.int32, (rank, rank), 0)
    target = jnp.zeros((rank, rank), jnp.int32)
    for s in range(blocks):
        target = jnp.where(stored // size == s, perm_ref[s] * size + stored % size, target)
    order = (target == lax.broadcasted_iota(jnp.int32, (rank, rank), 1)).astype(jnp.float32)
    parts = [ref[...] for ref in part_refs]
    while len(parts) > 1:
        parts = [parts[k] + parts[k + 1] for k in range(0, len(parts), 2)]
    total = jnp.dot(parts[0], order, precision=HIGH, preferred_element_type=jnp.float32)
    exponent, mantissa = code_unit(jnp.max(jnp.abs(total), axis=0, keepdims=True))
    value = total * (1.0 / unit_of(exponent, mantissa))
    high = jnp.floor(value + 0.5)
    out_ref[:rows] = whole_number(high)
    low = jnp.minimum(jnp.floor((value - high) * 256.0 + 0.5), 127.0)
    half = rows // 2
    out_ref[rows : rows + half] = whole_number(low[:half] * 256.0 + (low[half:] + 128.0))
    set_head(out_ref.at[rows + half :], exponent, mantissa)


def pack(perm, parts):
    rows, rank = parts[0].shape
    return pl.pallas_call(
        pack_kernel,
        grid_spec=pltpu.PrefetchScalarGridSpec(
            num_scalar_prefetch=1,
            grid=(1,),
            in_specs=[whole(x) for x in parts],
            out_specs=pl.BlockSpec((rows + rows // 2 + HEAD, rank), lambda *_: (0, 0)),
        ),
        out_shape=jax.ShapeDtypeStruct((rows + rows // 2 + HEAD, rank), jnp.int16),
        compiler_params=PARAMS,
        cost_estimate=pl.CostEstimate(flops=12 * rows * rank * rank, bytes_accessed=rank * rank * 4, transcendentals=0),
    )(perm, *parts)


def spread(row):
    return jnp.broadcast_to(row, (TILE, 2 * PANEL))


def panel_inverse(block, band):
    rows = lax.broadcasted_iota(jnp.int32, (PANEL, PANEL), 0)
    cols = lax.broadcasted_iota(jnp.int32, (PANEL, PANEL), 1)
    both = jnp.concatenate([block, (rows == cols).astype(jnp.float32)], axis=1)
    count = PANEL // TILE
    tiles = [both[TILE * i : TILE * (i + 1)] for i in range(count)]
    sub = lax.broadcasted_iota(jnp.int32, (TILE, 2 * PANEL), 0)
    row = lambda k, j: band[k, pl.ds(j, TILE, stride=0), :]
    done = []
    for k in range(count):
        columns = [
            [spread(tiles[i][:, TILE * k + j : TILE * k + j + 1]) for j in range(TILE)] for i in range(k, count)
        ]
        state = list(columns[0]) + [tiles[k]]
        for m, x in enumerate(state):
            band[m] = x
        final = jnp.zeros_like(tiles[k])
        for j in range(0, TILE, 2):
            first, second = sub == j, sub == j + 1
            a, b, c = row(j, j), row(j + 1, j), row(j + 1, j + 1)
            minor = a * c - b * b
            inverse = 1.0 / minor
            left, right, body = state[j], state[j + 1], state[TILE]
            ratio = 1.0 / a
            below = (body - b * ratio * row(TILE, j)) * lax.rsqrt(minor * ratio)
            final = jnp.where(first, body * lax.rsqrt(a), jnp.where(second, below, final))
            rests = {}
            for m in range(j + 2, TILE + 1):
                upper, lower = row(m, j), row(m, j + 1)
                upper, lower = c * upper - b * lower, a * lower - b * upper
                rests[m] = state[m] - (left * upper + right * lower) * inverse
                state[m] = jnp.where(first, upper * inverse, jnp.where(second, lower * inverse, rests[m]))
            for m, rest in rests.items():
                band[m] = rest
        done.append(final)
        band[TILE] = state[TILE]
        reduced = [row(TILE, j) for j in range(TILE)]
        for i in range(k + 1, count):
            terms = [columns[i - k][j] * reduced[j] for j in range(TILE)]
            while len(terms) > 1:
                terms = [terms[j] + terms[j + 1] for j in range(0, len(terms), 2)]
            tiles[i] = tiles[i] - terms[0]
    return jnp.concatenate(done, axis=0)[:, PANEL:]


def split_three(x):
    high, rest = x.astype(jnp.bfloat16), x
    rest = rest - high.astype(jnp.float32)
    middle = rest.astype(jnp.bfloat16)
    return high, middle, (rest - middle.astype(jnp.float32)).astype(jnp.bfloat16)


def short_dot(a, b):
    a1, a2, a3 = split_three(a)
    b1, b2, b3 = split_three(b)
    a = jnp.concatenate([a1, a1, a2, a2, a1, a3], axis=1)
    b = jnp.concatenate([b1, b2, b1, b2, b3, b1], axis=0)
    return jnp.dot(a, b, preferred_element_type=jnp.float32)


def lanes_up(x):
    return (x + 127) // 128 * 128


def inverse_factor(gram, out_ref, work, band):
    rank = gram.shape[0]
    rows = lax.broadcasted_iota(jnp.int32, (rank, rank), 0)
    cols = lax.broadcasted_iota(jnp.int32, (rank, rank), 1)
    diagonal = jnp.where(rows == cols, gram, 0.0)
    scale = lax.rsqrt(jnp.sum(diagonal, axis=0, keepdims=True))
    work[:, :rank] = gram * scale * lax.rsqrt(jnp.sum(diagonal, axis=1, keepdims=True))
    work[:, rank:] = (rows == cols).astype(jnp.float32)
    for start in range(0, rank, PANEL):
        end = start + PANEL
        left, right = start // 128 * 128, rank + lanes_up(end)
        inverse = panel_inverse(work[start:end, start:end], band)
        scaled = short_dot(inverse, work[start:end, left:right])
        out_ref[start:end, : lanes_up(end)] = scaled[:, rank - left :] * scale[:, : lanes_up(end)]
        if lanes_up(end) < rank:
            out_ref[start:end, lanes_up(end) :] = jnp.zeros((PANEL, rank - lanes_up(end)), jnp.float32)
        if end < rank:
            low = end // 128 * 128
            change = short_dot(scaled[:, low - left : rank - left].T, scaled[:, low - left :])
            work[end:, low:right] = work[end:, low:right] - change[end - low :, :]


def factor_kernel(code_ref, turned_ref, out_ref, gram_ref, mixed_ref, work, band):
    count, size, rank = code_ref.shape
    size = (size - HEAD) * 2 // 3
    code = code_ref[...].astype(jnp.int32)
    low = code[:, size : size + size // 2]
    low = jnp.concatenate([low >> 8, (low & 255) - 128], axis=1).astype(jnp.float32)
    head = code[:, size + size // 2 :].astype(jnp.float32)
    part = (code[:, :size].astype(jnp.float32) + low * (1.0 / 256.0)) * unit_of(head[:, :1], head[:, 1:2])
    turned = part.reshape(count * size, rank).T
    turned_ref[...] = turned

    def times(a, b):
        a, b = jnp.concatenate(a, axis=1), jnp.concatenate(b, axis=1)
        return lax.dot_general(a, b, (((1,), (1,)), ((), ())), preferred_element_type=jnp.float32)

    high, middle, small = split_three(turned)
    even, mixed = times((high, middle), (high, middle)), times((high, high), (middle, small))

    @pl.when(pl.program_id(0) == 0)
    def _():
        gram_ref[...] = even
        mixed_ref[...] = mixed

    @pl.when(pl.program_id(0) > 0)
    def _():
        gram_ref[...] += even
        mixed_ref[...] += mixed

    @pl.when(pl.program_id(0) == pl.num_programs(0) - 1)
    def _():
        mixed = mixed_ref[...]
        inverse_factor(gram_ref[...] + (mixed + mixed.T), out_ref, work, band)


def factor(codes):
    devices, size, rank = codes.shape
    rows = (size - HEAD) * 2 // 3
    group = 256 // rows
    return pl.pallas_call(
        factor_kernel,
        grid=(devices // group,),
        in_specs=[pl.BlockSpec((group, size, rank), lambda i: (i, 0, 0))],
        out_specs=[pl.BlockSpec((rank, group * rows), lambda i: (0, i)), pl.BlockSpec((rank, rank), lambda i: (0, 0))],
        out_shape=[
            jax.ShapeDtypeStruct((rank, devices * rows), jnp.float32),
            jax.ShapeDtypeStruct((rank, rank), jnp.float32),
        ],
        scratch_shapes=[
            pltpu.VMEM((rank, rank), jnp.float32),
            pltpu.VMEM((rank, rank), jnp.float32),
            pltpu.VMEM((rank, 2 * rank), jnp.float32),
            pltpu.VMEM((TILE + 1, TILE, 2 * PANEL), jnp.float32),
        ],
        compiler_params=PARAMS,
        cost_estimate=pl.CostEstimate(
            flops=12 * devices * rows * rank * rank, bytes_accessed=devices * size * rank * 4, transcendentals=rank
        ),
    )(codes)


def encode_kernel(place_ref, source_ref, turned_ref, unit_ref, inverse_ref, own_ref, code_ref, ortho_ref, mixed_ref):
    def times(a, b):
        return jnp.dot(a, b, preferred_element_type=jnp.float32)

    rank = turned_ref.shape[0]
    source_high, source_low = halves(source_ref[...].astype(jnp.int32).astype(jnp.float32))
    scaled_high, scaled_low = halves(turned_ref[...] * unit_ref[...])
    most = times(jnp.concatenate([scaled_high, scaled_low], axis=0), source_high)
    part = most[:rank] + (most[rank:] + times(scaled_high, source_low))
    first, last = pl.program_id(0) == 0, pl.program_id(0) == pl.num_programs(0) - 1

    @pl.when(first)
    def _():
        mixed_ref[...] = part

    @pl.when(jnp.logical_not(first))
    def _():
        mixed_ref[...] += part

    @pl.when(last)
    def _():
        inverse = inverse_ref[...]
        ortho_ref[...] = lax.dot_general(
            own_ref[...], inverse, (((0,), (1,)), ((), ())), precision=HIGH, preferred_element_type=jnp.float32
        )
        right = jnp.dot(inverse, mixed_ref[...], precision=HIGH, preferred_element_type=jnp.float32)
        share = right.shape[1]
        width = code_ref.shape[1]
        square = jnp.maximum(jnp.sum(right * right, axis=1, keepdims=True), 1e-34)
        square_exponent = jnp.floor(jnp.log2(square))
        fine = square * jnp.exp2(13.0 - square_exponent)
        square_high = jnp.floor(fine)
        square_low = jnp.floor((fine - square_high) * 16384.0)
        exponent, mantissa = code_unit(jnp.max(jnp.abs(right), axis=1, keepdims=True))
        code_ref[:rank, :share] = whole_number(jnp.floor(right * (1.0 / unit_of(exponent, mantissa)) + 0.5))
        lane = lax.broadcasted_iota(jnp.int32, (rank, 128), 1)
        head = jnp.zeros((rank, 128), jnp.float32)
        for k, column in enumerate((exponent, mantissa, square_exponent, square_high, square_low)):
            head = jnp.where(lane == k, column, head)
        code_ref[rank:, :rank] = whole_number(head.T[:HEAD])
        if width > rank:
            code_ref[rank:, rank:] = jnp.zeros((HEAD, width - rank), jnp.int16)
        if width > share:
            code_ref[:rank, share:] = jnp.zeros((rank, width - share), jnp.int16)


def encode(place, source, turned, unit, inverse_low, rows):
    total, share = source.shape
    rank = turned.shape[0]
    block = min(512, total)
    return pl.pallas_call(
        encode_kernel,
        grid_spec=pltpu.PrefetchScalarGridSpec(
            num_scalar_prefetch=1,
            grid=(total // block,),
            in_specs=[
                pl.BlockSpec((block, share), lambda i, place: (i, 0)),
                pl.BlockSpec((rank, block), lambda i, place: (0, i)),
                pl.BlockSpec((1, block), lambda i, place: (0, i)),
                whole(inverse_low),
                pl.BlockSpec((rank, rows), lambda i, place: (0, place[0])),
            ],
            out_specs=[
                pl.BlockSpec((rank + HEAD, max(share, rank)), lambda i, place: (0, 0)),
                pl.BlockSpec((rows, rank), lambda i, place: (0, 0)),
            ],
            scratch_shapes=[pltpu.VMEM((rank, share), jnp.float32)],
        ),
        out_shape=[
            jax.ShapeDtypeStruct((rank + HEAD, max(share, rank)), jnp.int16),
            jax.ShapeDtypeStruct((rows, rank), jnp.float32),
        ],
        compiler_params=PARAMS,
        cost_estimate=pl.CostEstimate(
            flops=6 * total * share * rank, bytes_accessed=total * (share * 2 + rank * 4), transcendentals=0
        ),
    )(place, source, turned, unit, inverse_low, turned)


def float_of(code):
    return code if code.dtype == jnp.float32 else code.astype(jnp.int32).astype(jnp.float32)


def split_dot(left, code):
    rows = left.shape[0]
    left_high, left_low = halves(left)
    code_high, code_low = halves(code)
    most = jnp.dot(jnp.concatenate([left_high, left_low], axis=0), code_high, preferred_element_type=jnp.float32)
    return most[:rows] + (most[rows:] + jnp.dot(left_high, code_low, preferred_element_type=jnp.float32))


def momentum_kernel(momentum_ref, grad_ref, code_ref, unit_ref, ortho_ref, next_ref):
    group, _, width = code_ref.shape
    for k in range(group):
        span = slice(width * k, width * (k + 1))
        change = split_dot(-KEEP_SHARE * ortho_ref[...] * unit_ref[k], float_of(code_ref[k]))
        next_ref[:, span] = momentum_ref[:, span] + grad_ref[:, span].astype(jnp.float32) + change


def update_kernel(gain, code_ref, unit_ref, ortho_ref, scale_ref, basis_ref, update_ref):
    group, _, width = code_ref.shape
    for k in range(group):
        span = slice(width * k, width * (k + 1))
        code = float_of(code_ref[k])
        factor = unit_ref[k] * scale_ref[...]
        basis_ref[span, :] = code.T * factor
        update_ref[:, span] = split_dot(gain * ortho_ref[...] * factor, code).astype(jnp.bfloat16)


def finish(momentum, grad, codes, units, orthonormal, scale, gain):
    rows, cols = momentum.shape
    shares, _, width = codes.shape
    rank = orthonormal.shape[1]
    group = 2 if shares % 2 == 0 else 1
    block = group * width
    wide = pl.BlockSpec((rows, block), lambda i: (0, i))
    tall = pl.BlockSpec((block, rank), lambda i: (i, 0))
    coded = pl.BlockSpec((group, rank, width), lambda i: (i, 0, 0))
    unit = pl.BlockSpec((group, 1, rank), lambda i: (i, 0, 0))
    flops = 6 * rows * cols * rank
    momentum_next = pl.pallas_call(
        momentum_kernel,
        grid=(cols // block,),
        in_specs=[wide, wide, coded, unit, whole(orthonormal)],
        out_specs=wide,
        out_shape=jax.ShapeDtypeStruct((rows, cols), jnp.float32),
        compiler_params=PARAMS,
        cost_estimate=pl.CostEstimate(
            flops=flops, bytes_accessed=rows * cols * 10 + cols * rank * 2, transcendentals=0
        ),
    )(momentum, grad, codes, units, orthonormal)
    q_next, update = pl.pallas_call(
        functools.partial(update_kernel, gain),
        grid=(cols // block,),
        in_specs=[coded, unit, whole(orthonormal), whole(scale)],
        out_specs=[tall, wide],
        out_shape=[
            jax.ShapeDtypeStruct((cols, rank), jnp.float32),
            jax.ShapeDtypeStruct((rows, cols), jnp.bfloat16),
        ],
        compiler_params=PARAMS,
        cost_estimate=pl.CostEstimate(flops=flops, bytes_accessed=rows * cols * 2 + cols * rank * 6, transcendentals=0),
    )(codes, units, orthonormal, scale)
    return momentum_next, q_next, update


def on_device(momentum, grad, q_stored, perm):
    block_rows = q_stored.shape[0]
    num_blocks = lax.axis_size("fsdp")
    num_cols = lax.axis_size("tp")
    rank_total = block_rows * num_blocks
    rows, cols = momentum.shape
    row_total, col_total = rows * num_blocks, cols * num_cols
    share = cols // num_blocks

    basis, codes = prepare(momentum, grad, q_stored, share)
    codes = codes.reshape(-1, rows, codes.shape[2] // share, share).swapaxes(1, 2).reshape(num_blocks, rows, share)
    basis = lax.all_gather(basis, "fsdp", axis=0, tiled=True)
    codes, basis = lax.optimization_barrier((codes, basis))
    codes = lax.all_to_all(codes, "fsdp", split_axis=0, concat_axis=0).reshape(row_total, share)
    head = basis.reshape(num_blocks, block_rows, cols + rows)[:, -2:, cols:].astype(jnp.float32)
    unit = unit_of(head[:, 0], head[:, 1]).reshape(1, row_total)

    near, step = project(momentum, grad, basis), 1
    while 4 * step < num_cols:
        near = near + exchange(near, "tp", step)
        step *= 2
    parts = [near] + [exchange(near, "tp", k) for k in range(step, num_cols, step)]
    packed = lax.all_gather(pack(perm, parts), "fsdp", axis=0)
    packed, codes = lax.optimization_barrier((packed, codes))
    turned, inverse_low = factor(packed)
    code, orthonormal = encode(lax.axis_index("fsdp").reshape(1), codes, turned, unit, inverse_low, rows)
    gathered = lax.all_gather(code, "fsdp", axis=0)
    head = gathered[:, rank_total : rank_total + 5, :rank_total].astype(jnp.float32)
    units = unit_of(head[:, :1], head[:, 1:2])
    parts = (head[:, 3] + head[:, 4] * (1.0 / 16384.0)) * jnp.exp2(head[:, 2] - 13.0)
    squares = quad_sum(jnp.sum(parts, axis=0, keepdims=True), "tp")
    scale = lax.rsqrt(squares / col_total + EPSILON)
    if share % 128 != 0:
        gathered = gathered[:, :rank_total, :share].astype(jnp.float32) * units.swapaxes(1, 2)
        gathered = gathered.swapaxes(0, 1).reshape(1, rank_total, cols)
        units = jnp.ones((1, 1, rank_total), jnp.float32)
    return tuple(finish(momentum, grad, gathered, units, orthonormal, scale, math.sqrt(row_total / rank_total)))


def solution(mesh):
    return jax.shard_map(
        on_device,
        mesh=mesh,
        in_specs=(P("fsdp", "tp"), P("fsdp", "tp"), P("fsdp", "tp"), P()),
        out_specs=(P("fsdp", "tp"), P("tp", None), P("fsdp", "tp")),
        check_vma=False,
    )
```

```python
import functools
import math

import jax
import jax.numpy as jnp
from jax import lax
from jax.experimental import pallas as pl
from jax.experimental.pallas import tpu as pltpu
from jax.sharding import PartitionSpec as P

EPSILON = 1e-06
KEEP_SHARE = 0.5
HIGH = lax.Precision.HIGHEST
PANEL = 64
TILE = 16
HEAD = 16
TOP = 32766.0
PARAMS = pltpu.CompilerParams(vmem_limit_bytes=40 * 1024 * 1024)
FLOW = pltpu.CompilerParams(vmem_limit_bytes=53 * 1024 * 1024)
STREAM = pltpu.CompilerParams(vmem_limit_bytes=54 * 1024 * 1024)


def halves(x):
    high = x.astype(jnp.bfloat16)
    return high, (x - high.astype(jnp.float32)).astype(jnp.bfloat16)


def exchange(x, axis, k):
    return lax.ppermute(x, axis, [(i, i ^ k) for i in range(lax.axis_size(axis))])


def butterfly_sum(x, axis, step=1):
    while step < lax.axis_size(axis):
        x = x + exchange(x, axis, step)
        step *= 2
    return x


def quad_sum(x, axis, step=1):
    if lax.axis_size(axis) != 4 * step:
        return butterfly_sum(x, axis, step)
    near, far, across = [exchange(x, axis, k * step) for k in range(1, 4)]
    return (x + near) + (far + across)


def whole(x):
    return pl.BlockSpec(x.shape, lambda *_: (0,) * len(x.shape))


def dot_rows(a, b):
    return lax.dot_general(a, b, (((1,), (1,)), ((), ())), precision=HIGH, preferred_element_type=jnp.float32)


def unit_of(exponent, mantissa):
    return mantissa * jnp.exp2(exponent - 13.0)


def code_unit(top):
    top = jnp.maximum(top, 1e-28) * (1.0 / TOP)
    exponent = jnp.floor(jnp.log2(top))
    return exponent, jnp.floor(top * jnp.exp2(13.0 - exponent)) + 1.0


def whole_number(x):
    return x.astype(jnp.int32).astype(jnp.int16)


def set_head(head_ref, *rows):
    place = lax.broadcasted_iota(jnp.int32, head_ref.shape, 0)
    head = jnp.zeros(head_ref.shape, jnp.float32)
    for k, row in enumerate(rows):
        head = jnp.where(place == k, row, head)
    head_ref[...] = whole_number(head)


def code_basis(basis):
    value = basis.astype(jnp.float32)
    size = jnp.abs(value)
    normal = size >= 2.0**-126
    exponent = jnp.floor(jnp.log2(jnp.where(normal, size, 1.0)))
    code = 128.0 * (exponent + 126.0) + jnp.floor(128.0 * (size * jnp.exp2(-exponent)) + 0.5)
    return whole_number(jnp.where(normal, jnp.where(value < 0.0, code - 32768.0, code), 0.0))


def prepare_kernel(momentum_ref, grad_ref, basis_ref, basis_code_ref, code_ref, unit_ref, column_ref):
    rows, cols = momentum_ref.shape
    width = code_ref.shape[-1]
    spans = [slice(i, i + width) for i in range(0, cols, width)]
    combined = lambda span: momentum_ref[:, span] + grad_ref[:, span].astype(jnp.float32)
    top = functools.reduce(jnp.maximum, [jnp.abs(combined(span)) for span in spans])
    exponent, mantissa = code_unit(jnp.max(top, axis=1, keepdims=True))
    inverse = 1.0 / unit_of(exponent, mantissa)
    for k, span in enumerate(spans):
        code_ref[k] = whole_number(jnp.floor(combined(span) * inverse + 0.5))
        basis_code_ref[:, span] = code_basis(basis_ref[:, span])
    step = pl.program_id(0)
    here = pl.ds(pl.multiple_of(step * rows, rows), rows)
    for k, column in enumerate((exponent, mantissa)):
        column_ref[k, here, :] = jnp.broadcast_to(column, (rows, column_ref.shape[2]))

    @pl.when(step == pl.num_programs(0) - 1)
    def _():
        for k in range(2):
            unit_ref[k : k + 1, :] = column_ref[k].T[:1]


def prepare(momentum, grad, basis, share):
    rows, cols = momentum.shape
    width = share if share % 128 == 0 else cols
    steps = 2 if basis.shape[0] % 32 == 0 else 1
    wide = pl.BlockSpec((rows // steps, cols), lambda i: (i, 0))
    narrow = pl.BlockSpec((basis.shape[0] // steps, cols), lambda i: (i, 0))
    return pl.pallas_call(
        prepare_kernel,
        grid=(steps,),
        in_specs=[wide, wide, narrow],
        out_specs=[
            narrow,
            pl.BlockSpec((cols // width, rows // steps, width), lambda i: (0, i, 0)),
            pl.BlockSpec((2, rows), lambda i: (0, 0)),
        ],
        out_shape=[
            jax.ShapeDtypeStruct(basis.shape, jnp.int16),
            jax.ShapeDtypeStruct((cols // width, rows, width), jnp.int16),
            jax.ShapeDtypeStruct((2, rows), jnp.float32),
        ],
        scratch_shapes=[pltpu.VMEM((2, rows, 128), jnp.float32)],
        compiler_params=STREAM,
        cost_estimate=pl.CostEstimate(flops=10 * rows * cols, bytes_accessed=rows * cols * 8, transcendentals=0),
    )(momentum, grad, basis)


def project_kernel(momentum_ref, grad_ref, code_ref, out_ref):
    code = code_ref[...].astype(jnp.int32)
    power = jnp.exp2(((code >> 7) & 255).astype(jnp.float32) - 134.0)
    value = ((code & 127) | 128).astype(jnp.float32) * power
    basis = jnp.where(code < 0, -value, value).astype(jnp.bfloat16)
    combined = momentum_ref[...] + grad_ref[...].astype(jnp.float32)
    rows = combined.shape[0]
    part = lax.dot_general(
        jnp.concatenate(halves(combined), axis=0),
        basis,
        (((1,), (1,)), ((), ())),
        preferred_element_type=jnp.float32,
    )
    part = part[:rows] + part[rows:]

    @pl.when(pl.program_id(0) == 0)
    def _():
        out_ref[...] = part

    @pl.when(pl.program_id(0) > 0)
    def _():
        out_ref[...] += part


def project(momentum, grad, codes):
    rows, cols = momentum.shape
    rank = codes.shape[0]
    block = min(1024, cols)
    wide = pl.BlockSpec((rows, block), lambda i: (0, i))
    return pl.pallas_call(
        project_kernel,
        grid=(cols // block,),
        in_specs=[wide, wide, pl.BlockSpec((rank, block), lambda i: (0, i))],
        out_specs=pl.BlockSpec((rows, rank), lambda i: (0, 0)),
        out_shape=jax.ShapeDtypeStruct((rows, rank), jnp.float32),
        compiler_params=FLOW,
        cost_estimate=pl.CostEstimate(
            flops=4 * rows * cols * rank, bytes_accessed=rows * cols * 6 + rank * cols * 2, transcendentals=rank * cols
        ),
    )(momentum, grad, codes)


def pack_kernel(perm_ref, unit_ref, *refs):
    part_refs, out_ref = refs[:-1], refs[-1]
    rows, rank = part_refs[0].shape
    blocks = perm_ref.shape[0]
    size = rank // blocks
    stored = lax.broadcasted_iota(jnp.int32, (rank, rank), 0)
    target = jnp.zeros((rank, rank), jnp.int32)
    for s in range(blocks):
        target = jnp.where(stored // size == s, perm_ref[s] * size + stored % size, target)
    order = (target == lax.broadcasted_iota(jnp.int32, (rank, rank), 1)).astype(jnp.float32)
    parts = [ref[...] for ref in part_refs]
    while len(parts) > 1:
        parts = [parts[k] + parts[k + 1] for k in range(0, len(parts), 2)]
    total = jnp.dot(parts[0], order, precision=HIGH, preferred_element_type=jnp.float32)
    exponent, mantissa = code_unit(jnp.max(jnp.abs(total), axis=0, keepdims=True))
    value = total * (1.0 / unit_of(exponent, mantissa))
    high = jnp.floor(value + 0.5)
    out_ref[:rows] = whole_number(high)
    low = jnp.minimum(jnp.floor((value - high) * 256.0 + 0.5), 127.0)
    half = rows // 2
    out_ref[rows : rows + half] = whole_number(low[:half] * 256.0 + (low[half:] + 128.0))
    units = jnp.concatenate([unit_ref[...], jnp.zeros((2, rank - rows), jnp.float32)], axis=1)
    set_head(out_ref.at[rows + half :], exponent, mantissa, units[:1], units[1:])


def pack(perm, units, parts):
    rows, rank = parts[0].shape
    return pl.pallas_call(
        pack_kernel,
        grid_spec=pltpu.PrefetchScalarGridSpec(
            num_scalar_prefetch=1,
            grid=(1,),
            in_specs=[whole(x) for x in (units, *parts)],
            out_specs=pl.BlockSpec((rows + rows // 2 + HEAD, rank), lambda *_: (0, 0)),
        ),
        out_shape=jax.ShapeDtypeStruct((rows + rows // 2 + HEAD, rank), jnp.int16),
        compiler_params=PARAMS,
        cost_estimate=pl.CostEstimate(flops=12 * rows * rank * rank, bytes_accessed=rank * rank * 4, transcendentals=0),
    )(perm, units, *parts)


def spread(row):
    return jnp.broadcast_to(row, (TILE, 2 * PANEL))


def panel_inverse(block, band):
    rows = lax.broadcasted_iota(jnp.int32, (PANEL, PANEL), 0)
    cols = lax.broadcasted_iota(jnp.int32, (PANEL, PANEL), 1)
    both = jnp.concatenate([block, (rows == cols).astype(jnp.float32)], axis=1)
    count = PANEL // TILE
    tiles = [both[TILE * i : TILE * (i + 1)] for i in range(count)]
    sub = lax.broadcasted_iota(jnp.int32, (TILE, 2 * PANEL), 0)
    row = lambda k, j: band[k, pl.ds(j, TILE, stride=0), :]
    done = []
    for k in range(count):
        columns = [
            [spread(tiles[i][:, TILE * k + j : TILE * k + j + 1]) for j in range(TILE)] for i in range(k, count)
        ]
        state = list(columns[0]) + [tiles[k]]
        for m, x in enumerate(state):
            band[m] = x
        final = jnp.zeros_like(tiles[k])
        for j in range(0, TILE, 2):
            first, second = sub == j, sub == j + 1
            a, b, c = row(j, j), row(j + 1, j), row(j + 1, j + 1)
            minor = a * c - b * b
            inverse = 1.0 / minor
            left, right, body = state[j], state[j + 1], state[TILE]
            ratio = 1.0 / a
            below = (body - b * ratio * row(TILE, j)) * lax.rsqrt(minor * ratio)
            final = jnp.where(first, body * lax.rsqrt(a), jnp.where(second, below, final))
            rests = {}
            for m in range(j + 2, TILE + 1):
                upper, lower = row(m, j), row(m, j + 1)
                upper, lower = c * upper - b * lower, a * lower - b * upper
                rests[m] = state[m] - (left * upper + right * lower) * inverse
                state[m] = jnp.where(first, upper * inverse, jnp.where(second, lower * inverse, rests[m]))
            for m, rest in rests.items():
                band[m] = rest
        done.append(final)
        band[TILE] = state[TILE]
        reduced = [row(TILE, j) for j in range(TILE)]
        for i in range(k + 1, count):
            terms = [columns[i - k][j] * reduced[j] for j in range(TILE)]
            while len(terms) > 1:
                terms = [terms[j] + terms[j + 1] for j in range(0, len(terms), 2)]
            tiles[i] = tiles[i] - terms[0]
    return jnp.concatenate(done, axis=0)[:, PANEL:]


def split_three(x):
    high, rest = x.astype(jnp.bfloat16), x
    rest = rest - high.astype(jnp.float32)
    middle = rest.astype(jnp.bfloat16)
    return high, middle, (rest - middle.astype(jnp.float32)).astype(jnp.bfloat16)


def short_dot(a, b):
    a1, a2, a3 = split_three(a)
    b1, b2, b3 = split_three(b)
    a = jnp.concatenate([a1, a1, a2, a2, a1, a3], axis=1)
    b = jnp.concatenate([b1, b2, b1, b2, b3, b1], axis=0)
    return jnp.dot(a, b, preferred_element_type=jnp.float32)


def lanes_up(x):
    return (x + 127) // 128 * 128


def inverse_factor(gram, out_ref, work, band):
    rank = gram.shape[0]
    rows = lax.broadcasted_iota(jnp.int32, (rank, rank), 0)
    cols = lax.broadcasted_iota(jnp.int32, (rank, rank), 1)
    diagonal = jnp.where(rows == cols, gram, 0.0)
    scale = lax.rsqrt(jnp.sum(diagonal, axis=0, keepdims=True))
    work[:, :rank] = gram * scale * lax.rsqrt(jnp.sum(diagonal, axis=1, keepdims=True))
    work[:, rank:] = (rows == cols).astype(jnp.float32)
    for start in range(0, rank, PANEL):
        end = start + PANEL
        left, right = start // 128 * 128, rank + lanes_up(end)
        inverse = panel_inverse(work[start:end, start:end], band)
        scaled = short_dot(inverse, work[start:end, left:right])
        out_ref[start:end, : lanes_up(end)] = scaled[:, rank - left :] * scale[:, : lanes_up(end)]
        if lanes_up(end) < rank:
            out_ref[start:end, lanes_up(end) :] = jnp.zeros((PANEL, rank - lanes_up(end)), jnp.float32)
        if end < rank:
            low = end // 128 * 128
            change = short_dot(scaled[:, low - left : rank - left].T, scaled[:, low - left :])
            work[end:, low:right] = work[end:, low:right] - change[end - low :, :]


def factor_kernel(code_ref, turned_ref, out_ref, gram_ref, mixed_ref, work, band):
    count, size, rank = code_ref.shape
    size = (size - HEAD) * 2 // 3
    code = code_ref[...].astype(jnp.int32)
    low = code[:, size : size + size // 2]
    low = jnp.concatenate([low >> 8, (low & 255) - 128], axis=1).astype(jnp.float32)
    head = code[:, size + size // 2 :].astype(jnp.float32)
    part = (code[:, :size].astype(jnp.float32) + low * (1.0 / 256.0)) * unit_of(head[:, :1], head[:, 1:2])
    turned = part.reshape(count * size, rank).T
    turned_ref[...] = turned

    def times(a, b):
        a, b = jnp.concatenate(a, axis=1), jnp.concatenate(b, axis=1)
        return lax.dot_general(a, b, (((1,), (1,)), ((), ())), preferred_element_type=jnp.float32)

    high, middle, small = split_three(turned)
    even, mixed = times((high, middle), (high, middle)), times((high, high), (middle, small))

    @pl.when(pl.program_id(0) == 0)
    def _():
        gram_ref[...] = even
        mixed_ref[...] = mixed

    @pl.when(pl.program_id(0) > 0)
    def _():
        gram_ref[...] += even
        mixed_ref[...] += mixed

    @pl.when(pl.program_id(0) == pl.num_programs(0) - 1)
    def _():
        mixed = mixed_ref[...]
        inverse_factor(gram_ref[...] + (mixed + mixed.T), out_ref, work, band)


def factor(codes):
    devices, size, rank = codes.shape
    rows = (size - HEAD) * 2 // 3
    group = min(devices, max(1, 1024 // rows))
    return pl.pallas_call(
        factor_kernel,
        grid=(devices // group,),
        in_specs=[pl.BlockSpec((group, size, rank), lambda i: (i, 0, 0))],
        out_specs=[pl.BlockSpec((rank, group * rows), lambda i: (0, i)), pl.BlockSpec((rank, rank), lambda i: (0, 0))],
        out_shape=[
            jax.ShapeDtypeStruct((rank, devices * rows), jnp.float32),
            jax.ShapeDtypeStruct((rank, rank), jnp.float32),
        ],
        scratch_shapes=[
            pltpu.VMEM((rank, rank), jnp.float32),
            pltpu.VMEM((rank, rank), jnp.float32),
            pltpu.VMEM((rank, 2 * rank), jnp.float32),
            pltpu.VMEM((TILE + 1, TILE, 2 * PANEL), jnp.float32),
        ],
        compiler_params=PARAMS,
        cost_estimate=pl.CostEstimate(
            flops=12 * devices * rows * rank * rank, bytes_accessed=devices * size * rank * 4, transcendentals=rank
        ),
    )(codes)


def encode_kernel(place_ref, source_ref, turned_ref, head_ref, inverse_ref, own_ref, code_ref, ortho_ref, mixed_ref):
    def times(a, b):
        return jnp.dot(a, b, preferred_element_type=jnp.float32)

    def turned_dot(a, b):
        return lax.dot_general(a, b, (((0,), (1,)), ((), ())), precision=HIGH, preferred_element_type=jnp.float32)

    rank = turned_ref.shape[0]
    source_high, source_low = halves(source_ref[...].astype(jnp.int32).astype(jnp.float32))
    head = head_ref[...].astype(jnp.int32).astype(jnp.float32)
    devices = head.shape[0]
    rows = turned_ref.shape[1] // devices
    unit = jnp.concatenate([unit_of(head[k, 2:3, :rows], head[k, 3:4, :rows]) for k in range(devices)], axis=1)
    scaled_high, scaled_low = halves(turned_ref[...] * unit)
    most = times(jnp.concatenate([scaled_high, scaled_low], axis=0), source_high)
    part = most[:rank] + (most[rank:] + times(scaled_high, source_low))
    first, last = pl.program_id(0) == 0, pl.program_id(0) == pl.num_programs(0) - 1

    @pl.when(first)
    def _():
        mixed_ref[...] = part

    @pl.when(jnp.logical_not(first))
    def _():
        mixed_ref[...] += part

    @pl.when(last)
    def _():
        inverse = inverse_ref[...]
        ortho_ref[...] = turned_dot(own_ref[...], inverse)
        right = turned_dot(mixed_ref[...], inverse)
        rows = right.shape[0]
        square = jnp.maximum(jnp.sum(right * right, axis=0, keepdims=True), 1e-34)
        square_exponent = jnp.floor(jnp.log2(square))
        fine = square * jnp.exp2(13.0 - square_exponent)
        square_high = jnp.floor(fine)
        square_low = jnp.floor((fine - square_high) * 16384.0)
        exponent, mantissa = code_unit(jnp.max(jnp.abs(right), axis=0, keepdims=True))
        code_ref[:rows] = whole_number(jnp.floor(right * (1.0 / unit_of(exponent, mantissa)) + 0.5))
        set_head(code_ref.at[rows:], exponent, mantissa, square_exponent, square_high, square_low)


def encode(place, source, turned, packed, inverse_low, rows):
    total, share = source.shape
    rank = turned.shape[0]
    block = min(1024, total)
    size = packed.shape[1]
    return pl.pallas_call(
        encode_kernel,
        grid_spec=pltpu.PrefetchScalarGridSpec(
            num_scalar_prefetch=1,
            grid=(total // block,),
            in_specs=[
                pl.BlockSpec((block, share), lambda i, place: (i, 0)),
                pl.BlockSpec((rank, block), lambda i, place: (0, i)),
                pl.BlockSpec((block // rows, HEAD, rank), lambda i, place: (i, size // HEAD - 1, 0)),
                whole(inverse_low),
                pl.BlockSpec((rank, rows), lambda i, place: (0, place[0])),
            ],
            out_specs=[
                pl.BlockSpec((share + HEAD, rank), lambda i, place: (0, 0)),
                pl.BlockSpec((rows, rank), lambda i, place: (0, 0)),
            ],
            scratch_shapes=[pltpu.VMEM((rank, share), jnp.float32)],
        ),
        out_shape=[
            jax.ShapeDtypeStruct((share + HEAD, rank), jnp.int16),
            jax.ShapeDtypeStruct((rows, rank), jnp.float32),
        ],
        compiler_params=PARAMS,
        cost_estimate=pl.CostEstimate(
            flops=6 * total * share * rank, bytes_accessed=total * (share * 2 + rank * 4), transcendentals=0
        ),
    )(place, source, turned, packed, inverse_low, turned)


def decode(code_ref):
    code = code_ref[...].astype(jnp.int32).astype(jnp.float32)
    share = code.shape[1] - HEAD
    right = code[:, :share] * unit_of(code[:, share : share + 1], code[:, share + 1 : share + 2])
    return right.reshape(code.shape[0] * share, code.shape[2])


def times_rows(split_ref, right):
    def times(a, b):
        return lax.dot_general(a, b, (((1,), (1,)), ((), ())), preferred_element_type=jnp.float32)

    right_high, right_low = halves(right)
    split = split_ref[...]
    rows = split.shape[0] // 2
    most = times(split, right_high)
    return most[:rows] + (most[rows:] + times(split[:rows], right_low))


def set_split(split_ref, x):
    rows = x.shape[0]

    @pl.when(pl.program_id(0) == 0)
    def _():
        split_ref[:rows], split_ref[rows:] = halves(x)


def momentum_kernel(momentum_ref, grad_ref, code_ref, ortho_ref, next_ref, split_ref):
    set_split(split_ref, -KEEP_SHARE * ortho_ref[...])
    change = times_rows(split_ref, decode(code_ref))
    next_ref[...] = momentum_ref[...] + grad_ref[...].astype(jnp.float32) + change


def update_kernel(gain, code_ref, ortho_ref, scale_ref, basis_ref, update_ref, split_ref):
    set_split(split_ref, gain * ortho_ref[...])
    basis = decode(code_ref) * scale_ref[...]
    basis_ref[...] = basis
    update_ref[...] = times_rows(split_ref, basis).astype(jnp.bfloat16)


def finish(momentum, grad, codes, orthonormal, scale, gain):
    rows, cols = momentum.shape
    shares, share, rank = codes.shape
    share -= HEAD
    group = max(1, min(2048 // share, shares))
    block = group * share
    wide = pl.BlockSpec((rows, block), lambda i: (0, i))
    tall = pl.BlockSpec((block, rank), lambda i: (i, 0))
    coded = pl.BlockSpec((group, share + HEAD, rank), lambda i: (i, 0, 0))
    split = [pltpu.VMEM((2 * rows, rank), jnp.bfloat16)]
    flops = 6 * rows * cols * rank
    momentum_next = pl.pallas_call(
        momentum_kernel,
        grid=(cols // block,),
        in_specs=[wide, wide, coded, whole(orthonormal)],
        out_specs=wide,
        out_shape=jax.ShapeDtypeStruct((rows, cols), jnp.float32),
        scratch_shapes=split,
        compiler_params=PARAMS,
        cost_estimate=pl.CostEstimate(
            flops=flops, bytes_accessed=rows * cols * 10 + cols * rank * 2, transcendentals=0
        ),
    )(momentum, grad, codes, orthonormal)
    q_next, update = pl.pallas_call(
        functools.partial(update_kernel, gain),
        grid=(cols // block,),
        in_specs=[coded, whole(orthonormal), whole(scale)],
        out_specs=[tall, wide],
        out_shape=[
            jax.ShapeDtypeStruct((cols, rank), jnp.float32),
            jax.ShapeDtypeStruct((rows, cols), jnp.bfloat16),
        ],
        scratch_shapes=split,
        compiler_params=PARAMS,
        cost_estimate=pl.CostEstimate(flops=flops, bytes_accessed=rows * cols * 2 + cols * rank * 6, transcendentals=0),
    )(codes, orthonormal, scale)
    return momentum_next, q_next, update


def on_device(momentum, grad, q_stored, perm):
    block_rows = q_stored.shape[0]
    num_blocks = lax.axis_size("fsdp")
    num_cols = lax.axis_size("tp")
    rank_total = block_rows * num_blocks
    rows, cols = momentum.shape
    row_total, col_total = rows * num_blocks, cols * num_cols
    share = cols // num_blocks

    basis, codes, units = prepare(momentum, grad, q_stored, share)
    codes = codes.reshape(-1, rows, codes.shape[2] // share, share).swapaxes(1, 2).reshape(num_blocks, rows, share)
    basis = lax.all_gather(basis, "fsdp", axis=0, tiled=True)
    codes, basis = lax.optimization_barrier((codes, basis))
    codes = lax.all_to_all(codes, "fsdp", split_axis=0, concat_axis=0).reshape(row_total, share)

    near, step = project(momentum, grad, basis), 1
    while 4 * step < num_cols:
        near = near + exchange(near, "tp", step)
        step *= 2
    parts = [near] + [exchange(near, "tp", k) for k in range(step, num_cols, step)]
    packed = lax.all_gather(pack(perm, units, parts), "fsdp", axis=0)
    packed, codes = lax.optimization_barrier((packed, codes))
    turned, inverse_low = factor(packed)
    code, orthonormal = encode(lax.axis_index("fsdp").reshape(1), codes, turned, packed, inverse_low, rows)
    gathered = lax.all_gather(code, "fsdp", axis=0)
    head = gathered[:, share : share + 5].astype(jnp.float32)
    parts = (head[:, 3] + head[:, 4] * (1.0 / 16384.0)) * jnp.exp2(head[:, 2] - 13.0)
    squares = quad_sum(jnp.sum(parts, axis=0, keepdims=True), "tp")
    scale = lax.rsqrt(squares / col_total + EPSILON)
    return tuple(finish(momentum, grad, gathered, orthonormal, scale, math.sqrt(row_total / rank_total)))


def solution(mesh):
    return jax.shard_map(
        on_device,
        mesh=mesh,
        in_specs=(P("fsdp", "tp"), P("fsdp", "tp"), P("fsdp", "tp"), P()),
        out_specs=(P("fsdp", "tp"), P("tp", None), P("fsdp", "tp")),
        check_vma=False,
    )
```

```python
import functools
import math

import jax
import jax.numpy as jnp
from jax import lax
from jax.experimental import pallas as pl
from jax.experimental.pallas import tpu as pltpu
from jax.sharding import PartitionSpec as P

EPSILON = 1e-06
KEEP_SHARE = 0.5
HIGH = lax.Precision.HIGHEST
PANEL = 64
TILE = 16
HEAD = 16
TOP = 32766.0
PARAMS = pltpu.CompilerParams(vmem_limit_bytes=40 * 1024 * 1024)
FLOW = pltpu.CompilerParams(vmem_limit_bytes=53 * 1024 * 1024)
STREAM = pltpu.CompilerParams(vmem_limit_bytes=54 * 1024 * 1024)


def halves(x):
    high = x.astype(jnp.bfloat16)
    return high, (x - high.astype(jnp.float32)).astype(jnp.bfloat16)


def whole(x):
    return pl.BlockSpec(x.shape, lambda *_: (0,) * len(x.shape))


def dot_rows(a, b):
    return lax.dot_general(a, b, (((1,), (1,)), ((), ())), precision=HIGH, preferred_element_type=jnp.float32)


def unit_of(exponent, mantissa):
    return mantissa * jnp.exp2(exponent - 13.0)


def code_unit(top):
    top = jnp.maximum(top, 1e-28) * (1.0 / TOP)
    exponent = jnp.floor(jnp.log2(top))
    return exponent, jnp.floor(top * jnp.exp2(13.0 - exponent)) + 1.0


def whole_number(x):
    return x.astype(jnp.int32).astype(jnp.int16)


def set_head(head_ref, *rows):
    place = lax.broadcasted_iota(jnp.int32, head_ref.shape, 0)
    head = jnp.zeros(head_ref.shape, jnp.float32)
    for k, row in enumerate(rows):
        head = jnp.where(place == k, row, head)
    head_ref[...] = whole_number(head)


def code_basis(basis):
    value = basis.astype(jnp.float32)
    size = jnp.abs(value)
    normal = size >= 2.0**-126
    exponent = jnp.floor(jnp.log2(jnp.where(normal, size, 1.0)))
    code = 128.0 * (exponent + 126.0) + jnp.floor(128.0 * (size * jnp.exp2(-exponent)) + 0.5)
    return whole_number(jnp.where(normal, jnp.where(value < 0.0, code - 32768.0, code), 0.0))


def prepare_kernel(momentum_ref, grad_ref, basis_ref, basis_code_ref, code_ref, unit_ref, column_ref):
    rows, cols = momentum_ref.shape
    width = code_ref.shape[-1]
    spans = [slice(i, i + width) for i in range(0, cols, width)]
    combined = lambda span: momentum_ref[:, span] + grad_ref[:, span].astype(jnp.float32)
    top = functools.reduce(jnp.maximum, [jnp.abs(combined(span)) for span in spans])
    exponent, mantissa = code_unit(jnp.max(top, axis=1, keepdims=True))
    inverse = 1.0 / unit_of(exponent, mantissa)
    for k, span in enumerate(spans):
        code_ref[k] = whole_number(jnp.floor(combined(span) * inverse + 0.5))
        basis_code_ref[:, span] = code_basis(basis_ref[:, span])
    step = pl.program_id(0)
    here = pl.ds(pl.multiple_of(step * rows, rows), rows)
    for k, column in enumerate((exponent, mantissa)):
        column_ref[k, here, :] = jnp.broadcast_to(column, (rows, column_ref.shape[2]))

    @pl.when(step == pl.num_programs(0) - 1)
    def _():
        for k in range(2):
            unit_ref[k : k + 1, :] = column_ref[k].T[:1]


def prepare(momentum, grad, basis, share):
    rows, cols = momentum.shape
    width = share if share % 128 == 0 else cols
    steps = 2 if basis.shape[0] % 32 == 0 else 1
    wide = pl.BlockSpec((rows // steps, cols), lambda i: (i, 0))
    narrow = pl.BlockSpec((basis.shape[0] // steps, cols), lambda i: (i, 0))
    return pl.pallas_call(
        prepare_kernel,
        grid=(steps,),
        in_specs=[wide, wide, narrow],
        out_specs=[
            narrow,
            pl.BlockSpec((cols // width, rows // steps, width), lambda i: (0, i, 0)),
            pl.BlockSpec((2, rows), lambda i: (0, 0)),
        ],
        out_shape=[
            jax.ShapeDtypeStruct(basis.shape, jnp.int16),
            jax.ShapeDtypeStruct((cols // width, rows, width), jnp.int16),
            jax.ShapeDtypeStruct((2, rows), jnp.float32),
        ],
        scratch_shapes=[pltpu.VMEM((2, rows, 128), jnp.float32)],
        compiler_params=STREAM,
        cost_estimate=pl.CostEstimate(flops=10 * rows * cols, bytes_accessed=rows * cols * 8, transcendentals=0),
    )(momentum, grad, basis)


def project_kernel(momentum_ref, grad_ref, code_ref, out_ref, total_ref):
    code = code_ref[...].astype(jnp.int32)
    power = jnp.exp2(((code >> 7) & 255).astype(jnp.float32) - 134.0)
    value = ((code & 127) | 128).astype(jnp.float32) * power
    basis = jnp.where(code < 0, -value, value).astype(jnp.bfloat16)
    combined = momentum_ref[...] + grad_ref[...].astype(jnp.float32)
    rows = combined.shape[0]
    part = lax.dot_general(
        jnp.concatenate(halves(combined), axis=0),
        basis,
        (((1,), (1,)), ((), ())),
        preferred_element_type=jnp.float32,
    )
    part = part[:rows] + part[rows:]

    @pl.when(pl.program_id(0) == 0)
    def _():
        total_ref[...] = part

    @pl.when(pl.program_id(0) > 0)
    def _():
        total_ref[...] += part

    @pl.when(pl.program_id(0) == pl.num_programs(0) - 1)
    def _():
        for k in range(out_ref.shape[0]):
            out_ref[k] = total_ref[...]


def project(momentum, grad, codes, copies):
    rows, cols = momentum.shape
    rank = codes.shape[0]
    block = min(1024, cols)
    wide = pl.BlockSpec((rows, block), lambda i: (0, i))
    return pl.pallas_call(
        project_kernel,
        grid=(cols // block,),
        in_specs=[wide, wide, pl.BlockSpec((rank, block), lambda i: (0, i))],
        out_specs=pl.BlockSpec((copies, rows, rank), lambda i: (0, 0, 0)),
        out_shape=jax.ShapeDtypeStruct((copies, rows, rank), jnp.float32),
        scratch_shapes=[pltpu.VMEM((rows, rank), jnp.float32)],
        compiler_params=FLOW,
        cost_estimate=pl.CostEstimate(
            flops=4 * rows * cols * rank, bytes_accessed=rows * cols * 6 + rank * cols * 2, transcendentals=rank * cols
        ),
    )(momentum, grad, codes)


def pack_kernel(perm_ref, unit_ref, part_ref, out_ref):
    _, rows, rank = part_ref.shape
    blocks = perm_ref.shape[0]
    size = rank // blocks
    stored = lax.broadcasted_iota(jnp.int32, (rank, rank), 0)
    target = jnp.zeros((rank, rank), jnp.int32)
    for s in range(blocks):
        target = jnp.where(stored // size == s, perm_ref[s] * size + stored % size, target)
    order = (target == lax.broadcasted_iota(jnp.int32, (rank, rank), 1)).astype(jnp.float32)
    parts = [part_ref[k] for k in range(part_ref.shape[0])]
    while len(parts) > 1:
        parts = [parts[k] + parts[k + 1] for k in range(0, len(parts), 2)]
    total = jnp.dot(parts[0], order, precision=HIGH, preferred_element_type=jnp.float32)
    exponent, mantissa = code_unit(jnp.max(jnp.abs(total), axis=0, keepdims=True))
    value = total * (1.0 / unit_of(exponent, mantissa))
    high = jnp.floor(value + 0.5)
    out_ref[:rows] = whole_number(high)
    low = jnp.minimum(jnp.floor((value - high) * 256.0 + 0.5), 127.0)
    half = rows // 2
    out_ref[rows : rows + half] = whole_number(low[:half] * 256.0 + (low[half:] + 128.0))
    units = jnp.concatenate([unit_ref[...], jnp.zeros((2, rank - rows), jnp.float32)], axis=1)
    set_head(out_ref.at[rows + half :], exponent, mantissa, units[:1], units[1:])


def pack(perm, units, parts):
    _, rows, rank = parts.shape
    return pl.pallas_call(
        pack_kernel,
        grid_spec=pltpu.PrefetchScalarGridSpec(
            num_scalar_prefetch=1,
            grid=(1,),
            in_specs=[whole(units), whole(parts)],
            out_specs=pl.BlockSpec((rows + rows // 2 + HEAD, rank), lambda *_: (0, 0)),
        ),
        out_shape=jax.ShapeDtypeStruct((rows + rows // 2 + HEAD, rank), jnp.int16),
        compiler_params=PARAMS,
        cost_estimate=pl.CostEstimate(flops=12 * rows * rank * rank, bytes_accessed=rank * rank * 4, transcendentals=0),
    )(perm, units, parts)


def spread(row):
    return jnp.broadcast_to(row, (TILE, 2 * PANEL))


def panel_inverse(block, band):
    rows = lax.broadcasted_iota(jnp.int32, (PANEL, PANEL), 0)
    cols = lax.broadcasted_iota(jnp.int32, (PANEL, PANEL), 1)
    both = jnp.concatenate([block, (rows == cols).astype(jnp.float32)], axis=1)
    count = PANEL // TILE
    tiles = [both[TILE * i : TILE * (i + 1)] for i in range(count)]
    sub = lax.broadcasted_iota(jnp.int32, (TILE, 2 * PANEL), 0)
    row = lambda k, j: band[k, pl.ds(j, TILE, stride=0), :]
    done = []
    for k in range(count):
        columns = [
            [spread(tiles[i][:, TILE * k + j : TILE * k + j + 1]) for j in range(TILE)] for i in range(k, count)
        ]
        state = list(columns[0]) + [tiles[k]]
        for m, x in enumerate(state):
            band[m] = x
        final = jnp.zeros_like(tiles[k])
        for j in range(0, TILE, 2):
            first, second = sub == j, sub == j + 1
            a, b, c = row(j, j), row(j + 1, j), row(j + 1, j + 1)
            minor = a * c - b * b
            inverse = 1.0 / minor
            left, right, body = state[j], state[j + 1], state[TILE]
            ratio = 1.0 / a
            below = (body - b * ratio * row(TILE, j)) * lax.rsqrt(minor * ratio)
            final = jnp.where(first, body * lax.rsqrt(a), jnp.where(second, below, final))
            rests = {}
            for m in range(j + 2, TILE + 1):
                upper, lower = row(m, j), row(m, j + 1)
                upper, lower = c * upper - b * lower, a * lower - b * upper
                rests[m] = state[m] - (left * upper + right * lower) * inverse
                state[m] = jnp.where(first, upper * inverse, jnp.where(second, lower * inverse, rests[m]))
            for m, rest in rests.items():
                band[m] = rest
        done.append(final)
        band[TILE] = state[TILE]
        reduced = [row(TILE, j) for j in range(TILE)]
        for i in range(k + 1, count):
            terms = [columns[i - k][j] * reduced[j] for j in range(TILE)]
            while len(terms) > 1:
                terms = [terms[j] + terms[j + 1] for j in range(0, len(terms), 2)]
            tiles[i] = tiles[i] - terms[0]
    return jnp.concatenate(done, axis=0)[:, PANEL:]


def split_three(x):
    high, rest = x.astype(jnp.bfloat16), x
    rest = rest - high.astype(jnp.float32)
    middle = rest.astype(jnp.bfloat16)
    return high, middle, (rest - middle.astype(jnp.float32)).astype(jnp.bfloat16)


def short_dot(a, b):
    a1, a2, a3 = split_three(a)
    b1, b2, b3 = split_three(b)
    a = jnp.concatenate([a1, a1, a2, a2, a1, a3], axis=1)
    b = jnp.concatenate([b1, b2, b1, b2, b3, b1], axis=0)
    return jnp.dot(a, b, preferred_element_type=jnp.float32)


def lanes_up(x):
    return (x + 127) // 128 * 128


def inverse_factor(gram, out_ref, work, band):
    rank = gram.shape[0]
    rows = lax.broadcasted_iota(jnp.int32, (rank, rank), 0)
    cols = lax.broadcasted_iota(jnp.int32, (rank, rank), 1)
    diagonal = jnp.where(rows == cols, gram, 0.0)
    scale = lax.rsqrt(jnp.sum(diagonal, axis=0, keepdims=True))
    work[:, :rank] = gram * scale * lax.rsqrt(jnp.sum(diagonal, axis=1, keepdims=True))
    work[:, rank:] = (rows == cols).astype(jnp.float32)
    for start in range(0, rank, PANEL):
        end = start + PANEL
        left, right = start // 128 * 128, rank + lanes_up(end)
        inverse = panel_inverse(work[start:end, start:end], band)
        scaled = short_dot(inverse, work[start:end, left:right])
        out_ref[start:end, : lanes_up(end)] = scaled[:, rank - left :] * scale[:, : lanes_up(end)]
        if lanes_up(end) < rank:
            out_ref[start:end, lanes_up(end) :] = jnp.zeros((PANEL, rank - lanes_up(end)), jnp.float32)
        if end < rank:
            low = end // 128 * 128
            change = short_dot(scaled[:, low - left : rank - left].T, scaled[:, low - left :])
            work[end:, low:right] = work[end:, low:right] - change[end - low :, :]


def factor_kernel(code_ref, turned_ref, out_ref, gram_ref, mixed_ref, work, band):
    count, size, rank = code_ref.shape
    size = (size - HEAD) * 2 // 3
    code = code_ref[...].astype(jnp.int32)
    low = code[:, size : size + size // 2]
    low = jnp.concatenate([low >> 8, (low & 255) - 128], axis=1).astype(jnp.float32)
    head = code[:, size + size // 2 :].astype(jnp.float32)
    part = (code[:, :size].astype(jnp.float32) + low * (1.0 / 256.0)) * unit_of(head[:, :1], head[:, 1:2])
    turned = part.reshape(count * size, rank).T
    turned_ref[...] = turned

    def times(a, b):
        a, b = jnp.concatenate(a, axis=1), jnp.concatenate(b, axis=1)
        return lax.dot_general(a, b, (((1,), (1,)), ((), ())), preferred_element_type=jnp.float32)

    high, middle, small = split_three(turned)
    even, mixed = times((high, middle), (high, middle)), times((high, high), (middle, small))

    @pl.when(pl.program_id(0) == 0)
    def _():
        gram_ref[...] = even
        mixed_ref[...] = mixed

    @pl.when(pl.program_id(0) > 0)
    def _():
        gram_ref[...] += even
        mixed_ref[...] += mixed

    @pl.when(pl.program_id(0) == pl.num_programs(0) - 1)
    def _():
        mixed = mixed_ref[...]
        inverse_factor(gram_ref[...] + (mixed + mixed.T), out_ref, work, band)


def factor(codes):
    devices, size, rank = codes.shape
    rows = (size - HEAD) * 2 // 3
    group = min(devices, max(1, 1024 // rows))
    return pl.pallas_call(
        factor_kernel,
        grid=(devices // group,),
        in_specs=[pl.BlockSpec((group, size, rank), lambda i: (i, 0, 0))],
        out_specs=[pl.BlockSpec((rank, group * rows), lambda i: (0, i)), pl.BlockSpec((rank, rank), lambda i: (0, 0))],
        out_shape=[
            jax.ShapeDtypeStruct((rank, devices * rows), jnp.float32),
            jax.ShapeDtypeStruct((rank, rank), jnp.float32),
        ],
        scratch_shapes=[
            pltpu.VMEM((rank, rank), jnp.float32),
            pltpu.VMEM((rank, rank), jnp.float32),
            pltpu.VMEM((rank, 2 * rank), jnp.float32),
            pltpu.VMEM((TILE + 1, TILE, 2 * PANEL), jnp.float32),
        ],
        compiler_params=PARAMS,
        cost_estimate=pl.CostEstimate(
            flops=12 * devices * rows * rank * rank, bytes_accessed=devices * size * rank * 4, transcendentals=rank
        ),
    )(codes)


def encode_kernel(place_ref, source_ref, turned_ref, head_ref, inverse_ref, own_ref, code_ref, ortho_ref, mixed_ref):
    def times(a, b):
        return jnp.dot(a, b, preferred_element_type=jnp.float32)

    def turned_dot(a, b):
        return lax.dot_general(a, b, (((0,), (1,)), ((), ())), precision=HIGH, preferred_element_type=jnp.float32)

    rank = turned_ref.shape[0]
    source_high, source_low = halves(source_ref[...].astype(jnp.int32).astype(jnp.float32))
    head = head_ref[...].astype(jnp.int32).astype(jnp.float32)
    devices = head.shape[0]
    rows = turned_ref.shape[1] // devices
    unit = jnp.concatenate([unit_of(head[k, 2:3, :rows], head[k, 3:4, :rows]) for k in range(devices)], axis=1)
    scaled_high, scaled_low = halves(turned_ref[...] * unit)
    most = times(jnp.concatenate([scaled_high, scaled_low], axis=0), source_high)
    part = most[:rank] + (most[rank:] + times(scaled_high, source_low))
    first, last = pl.program_id(0) == 0, pl.program_id(0) == pl.num_programs(0) - 1

    @pl.when(first)
    def _():
        mixed_ref[...] = part

    @pl.when(jnp.logical_not(first))
    def _():
        mixed_ref[...] += part

    @pl.when(last)
    def _():
        inverse = inverse_ref[...]
        ortho_ref[...] = turned_dot(own_ref[...], inverse)
        right = turned_dot(mixed_ref[...], inverse)
        rows = right.shape[0]
        square = jnp.maximum(jnp.sum(right * right, axis=0, keepdims=True), 1e-34)
        square_exponent = jnp.floor(jnp.log2(square))
        fine = square * jnp.exp2(13.0 - square_exponent)
        square_high = jnp.floor(fine)
        square_low = jnp.floor((fine - square_high) * 16384.0)
        exponent, mantissa = code_unit(jnp.max(jnp.abs(right), axis=0, keepdims=True))
        code_ref[:rows] = whole_number(jnp.floor(right * (1.0 / unit_of(exponent, mantissa)) + 0.5))
        set_head(code_ref.at[rows:], exponent, mantissa, square_exponent, square_high, square_low)


def encode(place, source, turned, packed, inverse_low, rows):
    total, share = source.shape
    rank = turned.shape[0]
    block = min(1024, total)
    size = packed.shape[1]
    return pl.pallas_call(
        encode_kernel,
        grid_spec=pltpu.PrefetchScalarGridSpec(
            num_scalar_prefetch=1,
            grid=(total // block,),
            in_specs=[
                pl.BlockSpec((block, share), lambda i, place: (i, 0)),
                pl.BlockSpec((rank, block), lambda i, place: (0, i)),
                pl.BlockSpec((block // rows, HEAD, rank), lambda i, place: (i, size // HEAD - 1, 0)),
                whole(inverse_low),
                pl.BlockSpec((rank, rows), lambda i, place: (0, place[0])),
            ],
            out_specs=[
                pl.BlockSpec((share + HEAD, rank), lambda i, place: (0, 0)),
                pl.BlockSpec((rows, rank), lambda i, place: (0, 0)),
            ],
            scratch_shapes=[pltpu.VMEM((rank, share), jnp.float32)],
        ),
        out_shape=[
            jax.ShapeDtypeStruct((share + HEAD, rank), jnp.int16),
            jax.ShapeDtypeStruct((rows, rank), jnp.float32),
        ],
        compiler_params=PARAMS,
        cost_estimate=pl.CostEstimate(
            flops=6 * total * share * rank, bytes_accessed=total * (share * 2 + rank * 4), transcendentals=0
        ),
    )(place, source, turned, packed, inverse_low, turned)


def decode(code_ref):
    code = code_ref[...].astype(jnp.int32).astype(jnp.float32)
    share = code.shape[1] - HEAD
    right = code[:, :share] * unit_of(code[:, share : share + 1], code[:, share + 1 : share + 2])
    return right.reshape(code.shape[0] * share, code.shape[2])


def times_rows(split_ref, right):
    def times(a, b):
        return lax.dot_general(a, b, (((1,), (1,)), ((), ())), preferred_element_type=jnp.float32)

    right_high, right_low = halves(right)
    split = split_ref[...]
    rows = split.shape[0] // 2
    most = times(split, right_high)
    return most[:rows] + (most[rows:] + times(split[:rows], right_low))


def set_split(split_ref, x):
    rows = x.shape[0]

    @pl.when(pl.program_id(0) == 0)
    def _():
        split_ref[:rows], split_ref[rows:] = halves(x)


def momentum_kernel(momentum_ref, grad_ref, code_ref, ortho_ref, next_ref, split_ref):
    set_split(split_ref, -KEEP_SHARE * ortho_ref[...])
    change = times_rows(split_ref, decode(code_ref))
    next_ref[...] = momentum_ref[...] + grad_ref[...].astype(jnp.float32) + change


def update_kernel(gain, code_ref, ortho_ref, scale_ref, basis_ref, update_ref, split_ref):
    set_split(split_ref, gain * ortho_ref[...])
    basis = decode(code_ref) * scale_ref[...]
    basis_ref[...] = basis
    update_ref[...] = times_rows(split_ref, basis).astype(jnp.bfloat16)


def finish(momentum, grad, codes, orthonormal, scale, gain):
    rows, cols = momentum.shape
    shares, share, rank = codes.shape
    share -= HEAD
    group = max(1, min(2048 // share, shares))
    block = group * share
    wide = pl.BlockSpec((rows, block), lambda i: (0, i))
    tall = pl.BlockSpec((block, rank), lambda i: (i, 0))
    coded = pl.BlockSpec((group, share + HEAD, rank), lambda i: (i, 0, 0))
    split = [pltpu.VMEM((2 * rows, rank), jnp.bfloat16)]
    flops = 6 * rows * cols * rank
    momentum_next = pl.pallas_call(
        momentum_kernel,
        grid=(cols // block,),
        in_specs=[wide, wide, coded, whole(orthonormal)],
        out_specs=wide,
        out_shape=jax.ShapeDtypeStruct((rows, cols), jnp.float32),
        scratch_shapes=split,
        compiler_params=PARAMS,
        cost_estimate=pl.CostEstimate(
            flops=flops, bytes_accessed=rows * cols * 10 + cols * rank * 2, transcendentals=0
        ),
    )(momentum, grad, codes, orthonormal)
    q_next, update = pl.pallas_call(
        functools.partial(update_kernel, gain),
        grid=(cols // block,),
        in_specs=[coded, whole(orthonormal), whole(scale)],
        out_specs=[tall, wide],
        out_shape=[
            jax.ShapeDtypeStruct((cols, rank), jnp.float32),
            jax.ShapeDtypeStruct((rows, cols), jnp.bfloat16),
        ],
        scratch_shapes=split,
        compiler_params=PARAMS,
        cost_estimate=pl.CostEstimate(flops=flops, bytes_accessed=rows * cols * 2 + cols * rank * 6, transcendentals=0),
    )(codes, orthonormal, scale)
    return momentum_next, q_next, update


def on_device(momentum, grad, q_stored, perm):
    block_rows = q_stored.shape[0]
    num_blocks = lax.axis_size("fsdp")
    num_cols = lax.axis_size("tp")
    rank_total = block_rows * num_blocks
    rows, cols = momentum.shape
    row_total, col_total = rows * num_blocks, cols * num_cols
    share = cols // num_blocks

    basis, codes, units = prepare(momentum, grad, q_stored, share)
    codes = codes.reshape(-1, rows, codes.shape[2] // share, share).swapaxes(1, 2).reshape(num_blocks, rows, share)
    basis = lax.all_gather(basis, "fsdp", axis=0, tiled=True)
    codes, basis = lax.optimization_barrier((codes, basis))
    codes = lax.all_to_all(codes, "fsdp", split_axis=0, concat_axis=0).reshape(row_total, share)

    parts = lax.all_to_all(project(momentum, grad, basis, num_cols), "tp", split_axis=0, concat_axis=0)
    packed = lax.all_gather(pack(perm, units, parts), "fsdp", axis=0)
    packed, codes = lax.optimization_barrier((packed, codes))
    turned, inverse_low = factor(packed)
    code, orthonormal = encode(lax.axis_index("fsdp").reshape(1), codes, turned, packed, inverse_low, rows)
    gathered = lax.all_gather(code, "fsdp", axis=0)
    head = gathered[:, share : share + 5].astype(jnp.float32)
    parts = (head[:, 3] + head[:, 4] * (1.0 / 16384.0)) * jnp.exp2(head[:, 2] - 13.0)
    squares = jnp.broadcast_to(jnp.sum(parts, axis=0), (num_cols, 1, rank_total))
    squares = jnp.sum(lax.all_to_all(squares, "tp", split_axis=0, concat_axis=0), axis=0)
    scale = lax.rsqrt(squares / col_total + EPSILON)
    return tuple(finish(momentum, grad, gathered, orthonormal, scale, math.sqrt(row_total / rank_total)))


def solution(mesh):
    return jax.shard_map(
        on_device,
        mesh=mesh,
        in_specs=(P("fsdp", "tp"), P("fsdp", "tp"), P("fsdp", "tp"), P()),
        out_specs=(P("fsdp", "tp"), P("tp", None), P("fsdp", "tp")),
        check_vma=False,
    )
```

```python
import functools
import math

import jax
import jax.numpy as jnp
from jax import lax
from jax.experimental import pallas as pl
from jax.experimental.pallas import tpu as pltpu
from jax.sharding import PartitionSpec as P

EPSILON = 1e-06
KEEP_SHARE = 0.5
HIGH = lax.Precision.HIGHEST
PANEL = 64
TILE = 16
HEAD = 16
TOP = 32766.0
PARAMS = pltpu.CompilerParams(vmem_limit_bytes=40 * 1024 * 1024)
FLOW = pltpu.CompilerParams(vmem_limit_bytes=53 * 1024 * 1024)
STREAM = pltpu.CompilerParams(vmem_limit_bytes=54 * 1024 * 1024)


def halves(x):
    high = x.astype(jnp.bfloat16)
    return high, (x - high.astype(jnp.float32)).astype(jnp.bfloat16)


def exchange(x, axis, k):
    return lax.ppermute(x, axis, [(i, i ^ k) for i in range(lax.axis_size(axis))])


def butterfly_sum(x, axis, step=1):
    while step < lax.axis_size(axis):
        x = x + exchange(x, axis, step)
        step *= 2
    return x


def quad_sum(x, axis, step=1):
    if lax.axis_size(axis) != 4 * step:
        return butterfly_sum(x, axis, step)
    near, far, across = [exchange(x, axis, k * step) for k in range(1, 4)]
    return (x + near) + (far + across)


def whole(x):
    return pl.BlockSpec(x.shape, lambda *_: (0,) * len(x.shape))


def dot_rows(a, b):
    return lax.dot_general(a, b, (((1,), (1,)), ((), ())), precision=HIGH, preferred_element_type=jnp.float32)


def unit_of(exponent, mantissa):
    return mantissa * jnp.exp2(exponent - 13.0)


def code_unit(top):
    top = jnp.maximum(top, 1e-28) * (1.0 / TOP)
    exponent = jnp.floor(jnp.log2(top))
    return exponent, jnp.floor(top * jnp.exp2(13.0 - exponent)) + 1.0


def whole_number(x):
    return x.astype(jnp.int32).astype(jnp.int16)


def set_head(head_ref, *rows):
    place = lax.broadcasted_iota(jnp.int32, head_ref.shape, 0)
    head = jnp.zeros(head_ref.shape, jnp.float32)
    for k, row in enumerate(rows):
        head = jnp.where(place == k, row, head)
    head_ref[...] = whole_number(head)


def code_basis(basis):
    value = basis.astype(jnp.float32)
    size = jnp.abs(value)
    normal = size >= 2.0**-126
    exponent = jnp.floor(jnp.log2(jnp.where(normal, size, 1.0)))
    code = 128.0 * (exponent + 126.0) + jnp.floor(128.0 * (size * jnp.exp2(-exponent)) + 0.5)
    return whole_number(jnp.where(normal, jnp.where(value < 0.0, code - 32768.0, code), 0.0))


def prepare_kernel(momentum_ref, grad_ref, basis_ref, basis_code_ref, *refs):
    code_refs, (unit_ref, column_ref) = refs[:-2], refs[-2:]
    rows, cols = momentum_ref.shape
    width = sum(ref.shape[-1] for ref in code_refs)
    spans = [slice(i, i + width) for i in range(0, cols, width)]
    combined = lambda span: momentum_ref[:, span] + grad_ref[:, span].astype(jnp.float32)
    top = functools.reduce(jnp.maximum, [jnp.abs(combined(span)) for span in spans])
    exponent, mantissa = code_unit(jnp.max(top, axis=1, keepdims=True))
    inverse = 1.0 / unit_of(exponent, mantissa)
    for k, span in enumerate(spans):
        code = whole_number(jnp.floor(combined(span) * inverse + 0.5))
        start = 0
        for ref in code_refs:
            end = start + ref.shape[-1]
            ref[k] = code[:, start:end]
            start = end
        basis_code_ref[:, span] = code_basis(basis_ref[:, span])
    step = pl.program_id(0)
    here = pl.ds(pl.multiple_of(step * rows, rows), rows)
    for k, column in enumerate((exponent, mantissa)):
        column_ref[k, here, :] = jnp.broadcast_to(column, (rows, column_ref.shape[2]))

    @pl.when(step == pl.num_programs(0) - 1)
    def _():
        for k in range(2):
            unit_ref[k : k + 1, :] = column_ref[k].T[:1]


def prepare(momentum, grad, basis, widths):
    rows, cols = momentum.shape
    count = cols // sum(widths)
    steps = 2 if basis.shape[0] % 32 == 0 else 1
    wide = pl.BlockSpec((rows // steps, cols), lambda i: (i, 0))
    narrow = pl.BlockSpec((basis.shape[0] // steps, cols), lambda i: (i, 0))
    out = pl.pallas_call(
        prepare_kernel,
        grid=(steps,),
        in_specs=[wide, wide, narrow],
        out_specs=[narrow]
        + [pl.BlockSpec((count, rows // steps, width), lambda i: (0, i, 0)) for width in widths]
        + [pl.BlockSpec((2, rows), lambda i: (0, 0))],
        out_shape=[jax.ShapeDtypeStruct(basis.shape, jnp.int16)]
        + [jax.ShapeDtypeStruct((count, rows, width), jnp.int16) for width in widths]
        + [jax.ShapeDtypeStruct((2, rows), jnp.float32)],
        scratch_shapes=[pltpu.VMEM((2, rows, 128), jnp.float32)],
        compiler_params=STREAM,
        cost_estimate=pl.CostEstimate(flops=10 * rows * cols, bytes_accessed=rows * cols * 8, transcendentals=0),
    )(momentum, grad, basis)
    return out[0], out[1:-1], out[-1]


def project_kernel(momentum_ref, grad_ref, code_ref, out_ref):
    code = code_ref[...].astype(jnp.int32)
    power = jnp.exp2(((code >> 7) & 255).astype(jnp.float32) - 134.0)
    value = ((code & 127) | 128).astype(jnp.float32) * power
    basis = jnp.where(code < 0, -value, value).astype(jnp.bfloat16)
    combined = momentum_ref[...] + grad_ref[...].astype(jnp.float32)
    rows = combined.shape[0]
    part = lax.dot_general(
        jnp.concatenate(halves(combined), axis=0),
        basis,
        (((1,), (1,)), ((), ())),
        preferred_element_type=jnp.float32,
    )
    part = part[:rows] + part[rows:]

    @pl.when(pl.program_id(0) == 0)
    def _():
        out_ref[...] = part

    @pl.when(pl.program_id(0) > 0)
    def _():
        out_ref[...] += part


def project(momentum, grad, codes):
    rows, cols = momentum.shape
    rank = codes.shape[0]
    block = min(1024, cols)
    wide = pl.BlockSpec((rows, block), lambda i: (0, i))
    return pl.pallas_call(
        project_kernel,
        grid=(cols // block,),
        in_specs=[wide, wide, pl.BlockSpec((rank, block), lambda i: (0, i))],
        out_specs=pl.BlockSpec((rows, rank), lambda i: (0, 0)),
        out_shape=jax.ShapeDtypeStruct((rows, rank), jnp.float32),
        compiler_params=FLOW,
        cost_estimate=pl.CostEstimate(
            flops=4 * rows * cols * rank, bytes_accessed=rows * cols * 6 + rank * cols * 2, transcendentals=rank * cols
        ),
    )(momentum, grad, codes)


def pack_kernel(perm_ref, unit_ref, *refs):
    part_refs, out_ref = refs[:-1], refs[-1]
    rows, rank = part_refs[0].shape
    blocks = perm_ref.shape[0]
    size = rank // blocks
    stored = lax.broadcasted_iota(jnp.int32, (rank, rank), 0)
    target = jnp.zeros((rank, rank), jnp.int32)
    for s in range(blocks):
        target = jnp.where(stored // size == s, perm_ref[s] * size + stored % size, target)
    order = (target == lax.broadcasted_iota(jnp.int32, (rank, rank), 1)).astype(jnp.float32)
    parts = [ref[...] for ref in part_refs]
    while len(parts) > 1:
        parts = [parts[k] + parts[k + 1] for k in range(0, len(parts), 2)]
    total = jnp.dot(parts[0], order, precision=HIGH, preferred_element_type=jnp.float32)
    exponent, mantissa = code_unit(jnp.max(jnp.abs(total), axis=0, keepdims=True))
    value = total * (1.0 / unit_of(exponent, mantissa))
    high = jnp.floor(value + 0.5)
    out_ref[:rows] = whole_number(high)
    low = jnp.minimum(jnp.floor((value - high) * 256.0 + 0.5), 127.0)
    half = rows // 2
    out_ref[rows : rows + half] = whole_number(low[:half] * 256.0 + (low[half:] + 128.0))
    units = jnp.concatenate([unit_ref[...], jnp.zeros((2, rank - rows), jnp.float32)], axis=1)
    set_head(out_ref.at[rows + half :], exponent, mantissa, units[:1], units[1:])


def pack(perm, units, parts):
    rows, rank = parts[0].shape
    return pl.pallas_call(
        pack_kernel,
        grid_spec=pltpu.PrefetchScalarGridSpec(
            num_scalar_prefetch=1,
            grid=(1,),
            in_specs=[whole(x) for x in (units, *parts)],
            out_specs=pl.BlockSpec((rows + rows // 2 + HEAD, rank), lambda *_: (0, 0)),
        ),
        out_shape=jax.ShapeDtypeStruct((rows + rows // 2 + HEAD, rank), jnp.int16),
        compiler_params=PARAMS,
        cost_estimate=pl.CostEstimate(flops=12 * rows * rank * rank, bytes_accessed=rank * rank * 4, transcendentals=0),
    )(perm, units, *parts)


def spread(row):
    return jnp.broadcast_to(row, (TILE, 2 * PANEL))


def panel_inverse(block, band):
    rows = lax.broadcasted_iota(jnp.int32, (PANEL, PANEL), 0)
    cols = lax.broadcasted_iota(jnp.int32, (PANEL, PANEL), 1)
    both = jnp.concatenate([block, (rows == cols).astype(jnp.float32)], axis=1)
    count = PANEL // TILE
    tiles = [both[TILE * i : TILE * (i + 1)] for i in range(count)]
    sub = lax.broadcasted_iota(jnp.int32, (TILE, 2 * PANEL), 0)
    row = lambda k, j: band[k, pl.ds(j, TILE, stride=0), :]
    done = []
    for k in range(count):
        columns = [
            [spread(tiles[i][:, TILE * k + j : TILE * k + j + 1]) for j in range(TILE)] for i in range(k, count)
        ]
        state = list(columns[0]) + [tiles[k]]
        for m, x in enumerate(state):
            band[m] = x
        final = jnp.zeros_like(tiles[k])
        for j in range(0, TILE, 2):
            first, second = sub == j, sub == j + 1
            a, b, c = row(j, j), row(j + 1, j), row(j + 1, j + 1)
            minor = a * c - b * b
            inverse = 1.0 / minor
            left, right, body = state[j], state[j + 1], state[TILE]
            ratio = 1.0 / a
            below = (body - b * ratio * row(TILE, j)) * lax.rsqrt(minor * ratio)
            final = jnp.where(first, body * lax.rsqrt(a), jnp.where(second, below, final))
            rests = {}
            for m in range(j + 2, TILE + 1):
                upper, lower = row(m, j), row(m, j + 1)
                upper, lower = c * upper - b * lower, a * lower - b * upper
                rests[m] = state[m] - (left * upper + right * lower) * inverse
                state[m] = jnp.where(first, upper * inverse, jnp.where(second, lower * inverse, rests[m]))
            for m, rest in rests.items():
                band[m] = rest
        done.append(final)
        band[TILE] = state[TILE]
        reduced = [row(TILE, j) for j in range(TILE)]
        for i in range(k + 1, count):
            terms = [columns[i - k][j] * reduced[j] for j in range(TILE)]
            while len(terms) > 1:
                terms = [terms[j] + terms[j + 1] for j in range(0, len(terms), 2)]
            tiles[i] = tiles[i] - terms[0]
    return jnp.concatenate(done, axis=0)[:, PANEL:]


def split_three(x):
    high, rest = x.astype(jnp.bfloat16), x
    rest = rest - high.astype(jnp.float32)
    middle = rest.astype(jnp.bfloat16)
    return high, middle, (rest - middle.astype(jnp.float32)).astype(jnp.bfloat16)


def short_dot(a, b):
    a1, a2, a3 = split_three(a)
    b1, b2, b3 = split_three(b)
    a = jnp.concatenate([a1, a1, a2, a2, a1, a3], axis=1)
    b = jnp.concatenate([b1, b2, b1, b2, b3, b1], axis=0)
    return jnp.dot(a, b, preferred_element_type=jnp.float32)


def lanes_up(x):
    return (x + 127) // 128 * 128


def inverse_factor(gram, out_ref, work, band):
    rank = gram.shape[0]
    rows = lax.broadcasted_iota(jnp.int32, (rank, rank), 0)
    cols = lax.broadcasted_iota(jnp.int32, (rank, rank), 1)
    diagonal = jnp.where(rows == cols, gram, 0.0)
    scale = lax.rsqrt(jnp.sum(diagonal, axis=0, keepdims=True))
    work[:, :rank] = gram * scale * lax.rsqrt(jnp.sum(diagonal, axis=1, keepdims=True))
    work[:, rank:] = (rows == cols).astype(jnp.float32)
    for start in range(0, rank, PANEL):
        end = start + PANEL
        left, right = start // 128 * 128, rank + lanes_up(end)
        inverse = panel_inverse(work[start:end, start:end], band)
        scaled = short_dot(inverse, work[start:end, left:right])
        out_ref[start:end, : lanes_up(end)] = scaled[:, rank - left :] * scale[:, : lanes_up(end)]
        if lanes_up(end) < rank:
            out_ref[start:end, lanes_up(end) :] = jnp.zeros((PANEL, rank - lanes_up(end)), jnp.float32)
        if end < rank:
            low = end // 128 * 128
            change = short_dot(scaled[:, low - left : rank - left].T, scaled[:, low - left :])
            work[end:, low:right] = work[end:, low:right] - change[end - low :, :]


def factor_kernel(code_ref, turned_ref, out_ref, gram_ref, mixed_ref, work, band):
    count, size, rank = code_ref.shape
    size = (size - HEAD) * 2 // 3
    code = code_ref[...].astype(jnp.int32)
    low = code[:, size : size + size // 2]
    low = jnp.concatenate([low >> 8, (low & 255) - 128], axis=1).astype(jnp.float32)
    head = code[:, size + size // 2 :].astype(jnp.float32)
    part = (code[:, :size].astype(jnp.float32) + low * (1.0 / 256.0)) * unit_of(head[:, :1], head[:, 1:2])
    turned = part.reshape(count * size, rank).T
    turned_ref[...] = turned

    def times(a, b):
        a, b = jnp.concatenate(a, axis=1), jnp.concatenate(b, axis=1)
        return lax.dot_general(a, b, (((1,), (1,)), ((), ())), preferred_element_type=jnp.float32)

    high, middle, small = split_three(turned)
    even, mixed = times((high, middle), (high, middle)), times((high, high), (middle, small))

    @pl.when(pl.program_id(0) == 0)
    def _():
        gram_ref[...] = even
        mixed_ref[...] = mixed

    @pl.when(pl.program_id(0) > 0)
    def _():
        gram_ref[...] += even
        mixed_ref[...] += mixed

    @pl.when(pl.program_id(0) == pl.num_programs(0) - 1)
    def _():
        mixed = mixed_ref[...]
        inverse_factor(gram_ref[...] + (mixed + mixed.T), out_ref, work, band)


def factor(codes):
    devices, size, rank = codes.shape
    rows = (size - HEAD) * 2 // 3
    group = min(devices, max(1, 1024 // rows))
    return pl.pallas_call(
        factor_kernel,
        grid=(devices // group,),
        in_specs=[pl.BlockSpec((group, size, rank), lambda i: (i, 0, 0))],
        out_specs=[pl.BlockSpec((rank, group * rows), lambda i: (0, i)), pl.BlockSpec((rank, rank), lambda i: (0, 0))],
        out_shape=[
            jax.ShapeDtypeStruct((rank, devices * rows), jnp.float32),
            jax.ShapeDtypeStruct((rank, rank), jnp.float32),
        ],
        scratch_shapes=[
            pltpu.VMEM((rank, rank), jnp.float32),
            pltpu.VMEM((rank, rank), jnp.float32),
            pltpu.VMEM((rank, 2 * rank), jnp.float32),
            pltpu.VMEM((TILE + 1, TILE, 2 * PANEL), jnp.float32),
        ],
        compiler_params=PARAMS,
        cost_estimate=pl.CostEstimate(
            flops=12 * devices * rows * rank * rank, bytes_accessed=devices * size * rank * 4, transcendentals=rank
        ),
    )(codes)


def encode_kernel(place_ref, *refs):
    def times(a, b):
        return jnp.dot(a, b, preferred_element_type=jnp.float32)

    def turned_dot(a, b):
        return lax.dot_general(a, b, (((0,), (1,)), ((), ())), precision=HIGH, preferred_element_type=jnp.float32)

    source_refs = refs[:-7]
    turned_ref, head_ref, inverse_ref, own_ref, code_ref, ortho_ref, mixed_ref = refs[-7:]
    rank = turned_ref.shape[0]
    source = jnp.concatenate([ref[...].astype(jnp.int32).astype(jnp.float32) for ref in source_refs], axis=1)
    source_high, source_low = halves(source)
    head = head_ref[...].astype(jnp.int32).astype(jnp.float32)
    devices = head.shape[0]
    rows = turned_ref.shape[1] // devices
    unit = jnp.concatenate([unit_of(head[k, 2:3, :rows], head[k, 3:4, :rows]) for k in range(devices)], axis=1)
    scaled_high, scaled_low = halves(turned_ref[...] * unit)
    most = times(jnp.concatenate([scaled_high, scaled_low], axis=0), source_high)
    part = most[:rank] + (most[rank:] + times(scaled_high, source_low))
    first, last = pl.program_id(0) == 0, pl.program_id(0) == pl.num_programs(0) - 1

    @pl.when(first)
    def _():
        mixed_ref[...] = part

    @pl.when(jnp.logical_not(first))
    def _():
        mixed_ref[...] += part

    @pl.when(last)
    def _():
        inverse = inverse_ref[...]
        ortho_ref[...] = turned_dot(own_ref[...], inverse)
        right = turned_dot(mixed_ref[...], inverse)
        rows = right.shape[0]
        square = jnp.maximum(jnp.sum(right * right, axis=0, keepdims=True), 1e-34)
        square_exponent = jnp.floor(jnp.log2(square))
        fine = square * jnp.exp2(13.0 - square_exponent)
        square_high = jnp.floor(fine)
        square_low = jnp.floor((fine - square_high) * 16384.0)
        exponent, mantissa = code_unit(jnp.max(jnp.abs(right), axis=0, keepdims=True))
        code_ref[:rows] = whole_number(jnp.floor(right * (1.0 / unit_of(exponent, mantissa)) + 0.5))
        set_head(code_ref.at[rows:], exponent, mantissa, square_exponent, square_high, square_low)


def encode(place, sources, turned, packed, inverse_low, rows):
    total, share = sources[0].shape[0], sum(x.shape[1] for x in sources)
    rank = turned.shape[0]
    block = min(1024, total)
    size = packed.shape[1]
    return pl.pallas_call(
        encode_kernel,
        grid_spec=pltpu.PrefetchScalarGridSpec(
            num_scalar_prefetch=1,
            grid=(total // block,),
            in_specs=[
                *[pl.BlockSpec((block, x.shape[1]), lambda i, place: (i, 0)) for x in sources],
                pl.BlockSpec((rank, block), lambda i, place: (0, i)),
                pl.BlockSpec((block // rows, HEAD, rank), lambda i, place: (i, size // HEAD - 1, 0)),
                whole(inverse_low),
                pl.BlockSpec((rank, rows), lambda i, place: (0, place[0])),
            ],
            out_specs=[
                pl.BlockSpec((share + HEAD, rank), lambda i, place: (0, 0)),
                pl.BlockSpec((rows, rank), lambda i, place: (0, 0)),
            ],
            scratch_shapes=[pltpu.VMEM((rank, share), jnp.float32)],
        ),
        out_shape=[
            jax.ShapeDtypeStruct((share + HEAD, rank), jnp.int16),
            jax.ShapeDtypeStruct((rows, rank), jnp.float32),
        ],
        compiler_params=PARAMS,
        cost_estimate=pl.CostEstimate(
            flops=6 * total * share * rank, bytes_accessed=total * (share * 2 + rank * 4), transcendentals=0
        ),
    )(place, *sources, turned, packed, inverse_low, turned)


def decode(code_ref):
    code = code_ref[...].astype(jnp.int32).astype(jnp.float32)
    share = code.shape[1] - HEAD
    right = code[:, :share] * unit_of(code[:, share : share + 1], code[:, share + 1 : share + 2])
    return right.reshape(code.shape[0] * share, code.shape[2])


def times_rows(split_ref, right):
    def times(a, b):
        return lax.dot_general(a, b, (((1,), (1,)), ((), ())), preferred_element_type=jnp.float32)

    right_high, right_low = halves(right)
    split = split_ref[...]
    rows = split.shape[0] // 2
    most = times(split, right_high)
    return most[:rows] + (most[rows:] + times(split[:rows], right_low))


def set_split(split_ref, x):
    rows = x.shape[0]

    @pl.when(pl.program_id(0) == 0)
    def _():
        split_ref[:rows], split_ref[rows:] = halves(x)


def momentum_kernel(momentum_ref, grad_ref, code_ref, ortho_ref, next_ref, split_ref):
    set_split(split_ref, -KEEP_SHARE * ortho_ref[...])
    change = times_rows(split_ref, decode(code_ref))
    next_ref[...] = momentum_ref[...] + grad_ref[...].astype(jnp.float32) + change


def update_kernel(gain, code_ref, ortho_ref, scale_ref, basis_ref, update_ref, split_ref):
    set_split(split_ref, gain * ortho_ref[...])
    basis = decode(code_ref) * scale_ref[...]
    basis_ref[...] = basis
    update_ref[...] = times_rows(split_ref, basis).astype(jnp.bfloat16)


def finish(momentum, grad, codes, orthonormal, scale, gain):
    rows, cols = momentum.shape
    shares, share, rank = codes.shape
    share -= HEAD
    group = max(1, min(2048 // share, shares))
    block = group * share
    wide = pl.BlockSpec((rows, block), lambda i: (0, i))
    tall = pl.BlockSpec((block, rank), lambda i: (i, 0))
    coded = pl.BlockSpec((group, share + HEAD, rank), lambda i: (i, 0, 0))
    split = [pltpu.VMEM((2 * rows, rank), jnp.bfloat16)]
    flops = 6 * rows * cols * rank
    momentum_next = pl.pallas_call(
        momentum_kernel,
        grid=(cols // block,),
        in_specs=[wide, wide, coded, whole(orthonormal)],
        out_specs=wide,
        out_shape=jax.ShapeDtypeStruct((rows, cols), jnp.float32),
        scratch_shapes=split,
        compiler_params=PARAMS,
        cost_estimate=pl.CostEstimate(
            flops=flops, bytes_accessed=rows * cols * 10 + cols * rank * 2, transcendentals=0
        ),
    )(momentum, grad, codes, orthonormal)
    q_next, update = pl.pallas_call(
        functools.partial(update_kernel, gain),
        grid=(cols // block,),
        in_specs=[coded, whole(orthonormal), whole(scale)],
        out_specs=[tall, wide],
        out_shape=[
            jax.ShapeDtypeStruct((cols, rank), jnp.float32),
            jax.ShapeDtypeStruct((rows, cols), jnp.bfloat16),
        ],
        scratch_shapes=split,
        compiler_params=PARAMS,
        cost_estimate=pl.CostEstimate(flops=flops, bytes_accessed=rows * cols * 2 + cols * rank * 6, transcendentals=0),
    )(codes, orthonormal, scale)
    return momentum_next, q_next, update


def on_device(momentum, grad, q_stored, perm):
    block_rows = q_stored.shape[0]
    num_blocks = lax.axis_size("fsdp")
    num_cols = lax.axis_size("tp")
    rank_total = block_rows * num_blocks
    rows, cols = momentum.shape
    row_total, col_total = rows * num_blocks, cols * num_cols
    share = cols // num_blocks

    late = share // 4 if share % 512 == 0 else 0
    widths = [share - late, late] if late else [share if share % 128 == 0 else cols]
    basis, codes, units = prepare(momentum, grad, q_stored, widths)
    if share % 128 != 0:
        codes = [codes[0].reshape(rows, num_blocks, share).swapaxes(0, 1)]
    trade = lambda x: lax.all_to_all(x, "fsdp", split_axis=0, concat_axis=0).reshape(row_total, x.shape[2])
    basis = lax.all_gather(basis, "fsdp", axis=0, tiled=True)
    first, basis = lax.optimization_barrier((codes[0], basis))
    first = trade(first)

    near, step = project(momentum, grad, basis), 1
    while 4 * step < num_cols:
        near = near + exchange(near, "tp", step)
        step *= 2
    parts = [near] + [exchange(near, "tp", k) for k in range(step, num_cols, step)]
    packed = lax.all_gather(pack(perm, units, parts), "fsdp", axis=0)
    packed, first, rest = lax.optimization_barrier((packed, first, codes[1:]))
    sources = [first] + [trade(x) for x in rest]
    turned, inverse_low = factor(packed)
    code, orthonormal = encode(lax.axis_index("fsdp").reshape(1), sources, turned, packed, inverse_low, rows)
    gathered = lax.all_gather(code, "fsdp", axis=0)
    head = gathered[:, share : share + 5].astype(jnp.float32)
    parts = (head[:, 3] + head[:, 4] * (1.0 / 16384.0)) * jnp.exp2(head[:, 2] - 13.0)
    squares = quad_sum(jnp.sum(parts, axis=0, keepdims=True), "tp")
    scale = lax.rsqrt(squares / col_total + EPSILON)
    return tuple(finish(momentum, grad, gathered, orthonormal, scale, math.sqrt(row_total / rank_total)))


def solution(mesh):
    return jax.shard_map(
        on_device,
        mesh=mesh,
        in_specs=(P("fsdp", "tp"), P("fsdp", "tp"), P("fsdp", "tp"), P()),
        out_specs=(P("fsdp", "tp"), P("tp", None), P("fsdp", "tp")),
        check_vma=False,
    )
```

```python
import functools
import math

import jax
import jax.numpy as jnp
from jax import lax
from jax.experimental import pallas as pl
from jax.experimental.pallas import tpu as pltpu
from jax.sharding import PartitionSpec as P

EPSILON = 1e-06
KEEP_SHARE = 0.5
HIGH = lax.Precision.HIGHEST
PANEL = 64
TILE = 16
HEAD = 16
TOP = 32766.0
PARAMS = pltpu.CompilerParams(vmem_limit_bytes=40 * 1024 * 1024)
FLOW = pltpu.CompilerParams(vmem_limit_bytes=53 * 1024 * 1024)
STREAM = pltpu.CompilerParams(vmem_limit_bytes=54 * 1024 * 1024)


def halves(x):
    high = x.astype(jnp.bfloat16)
    return high, (x - high.astype(jnp.float32)).astype(jnp.bfloat16)


def exchange(x, axis, k):
    return lax.ppermute(x, axis, [(i, i ^ k) for i in range(lax.axis_size(axis))])


def butterfly_sum(x, axis, step=1):
    while step < lax.axis_size(axis):
        x = x + exchange(x, axis, step)
        step *= 2
    return x


def quad_sum(x, axis, step=1):
    if lax.axis_size(axis) != 4 * step:
        return butterfly_sum(x, axis, step)
    near, far, across = [exchange(x, axis, k * step) for k in range(1, 4)]
    return (x + near) + (far + across)


def whole(x):
    return pl.BlockSpec(x.shape, lambda *_: (0,) * len(x.shape))


def dot_rows(a, b):
    return lax.dot_general(a, b, (((1,), (1,)), ((), ())), precision=HIGH, preferred_element_type=jnp.float32)


def unit_of(exponent, mantissa):
    return mantissa * jnp.exp2(exponent - 13.0)


def code_unit(top):
    top = jnp.maximum(top, 1e-28) * (1.0 / TOP)
    exponent = jnp.floor(jnp.log2(top))
    return exponent, jnp.floor(top * jnp.exp2(13.0 - exponent)) + 1.0


def whole_number(x):
    return x.astype(jnp.int32).astype(jnp.int16)


def set_head(head_ref, *rows):
    place = lax.broadcasted_iota(jnp.int32, head_ref.shape, 0)
    head = jnp.zeros(head_ref.shape, jnp.float32)
    for k, row in enumerate(rows):
        head = jnp.where(place == k, row, head)
    head_ref[...] = whole_number(head)


def code_basis(basis):
    value = basis.astype(jnp.float32)
    size = jnp.abs(value)
    normal = size >= 2.0**-126
    exponent = jnp.floor(jnp.log2(jnp.where(normal, size, 1.0)))
    code = 128.0 * (exponent + 126.0) + jnp.floor(128.0 * (size * jnp.exp2(-exponent)) + 0.5)
    return whole_number(jnp.where(normal, jnp.where(value < 0.0, code - 32768.0, code), 0.0))


def prepare_kernel(momentum_ref, grad_ref, basis_ref, basis_code_ref, code_ref, unit_ref, column_ref):
    rows, cols = momentum_ref.shape
    width = code_ref.shape[-1]
    spans = [slice(i, i + width) for i in range(0, cols, width)]
    combined = lambda span: momentum_ref[:, span] + grad_ref[:, span].astype(jnp.float32)
    top = functools.reduce(jnp.maximum, [jnp.abs(combined(span)) for span in spans])
    exponent, mantissa = code_unit(jnp.max(top, axis=1, keepdims=True))
    inverse = 1.0 / unit_of(exponent, mantissa)
    for k, span in enumerate(spans):
        code_ref[k] = whole_number(jnp.floor(combined(span) * inverse + 0.5))
        basis_code_ref[:, span] = code_basis(basis_ref[:, span])
    step = pl.program_id(0)
    here = pl.ds(pl.multiple_of(step * rows, rows), rows)
    for k, column in enumerate((exponent, mantissa)):
        column_ref[k, here, :] = jnp.broadcast_to(column, (rows, column_ref.shape[2]))

    @pl.when(step == pl.num_programs(0) - 1)
    def _():
        for k in range(2):
            unit_ref[k : k + 1, :] = column_ref[k].T[:1]


def prepare(momentum, grad, basis, share):
    rows, cols = momentum.shape
    width = share if share % 128 == 0 else cols
    steps = 2 if basis.shape[0] % 32 == 0 else 1
    wide = pl.BlockSpec((rows // steps, cols), lambda i: (i, 0))
    narrow = pl.BlockSpec((basis.shape[0] // steps, cols), lambda i: (i, 0))
    return pl.pallas_call(
        prepare_kernel,
        grid=(steps,),
        in_specs=[wide, wide, narrow],
        out_specs=[
            narrow,
            pl.BlockSpec((cols // width, rows // steps, width), lambda i: (0, i, 0)),
            pl.BlockSpec((2, rows), lambda i: (0, 0)),
        ],
        out_shape=[
            jax.ShapeDtypeStruct(basis.shape, jnp.int16),
            jax.ShapeDtypeStruct((cols // width, rows, width), jnp.int16),
            jax.ShapeDtypeStruct((2, rows), jnp.float32),
        ],
        scratch_shapes=[pltpu.VMEM((2, rows, 128), jnp.float32)],
        compiler_params=STREAM,
        cost_estimate=pl.CostEstimate(flops=10 * rows * cols, bytes_accessed=rows * cols * 8, transcendentals=0),
    )(momentum, grad, basis)


def project_kernel(momentum_ref, grad_ref, code_ref, out_ref):
    code = code_ref[...].astype(jnp.int32)
    power = jnp.exp2(((code >> 7) & 255).astype(jnp.float32) - 134.0)
    value = ((code & 127) | 128).astype(jnp.float32) * power
    basis = jnp.where(code < 0, -value, value).astype(jnp.bfloat16)
    combined = momentum_ref[...] + grad_ref[...].astype(jnp.float32)
    rows = combined.shape[0]
    part = lax.dot_general(
        jnp.concatenate(halves(combined), axis=0),
        basis,
        (((1,), (1,)), ((), ())),
        preferred_element_type=jnp.float32,
    )
    part = part[:rows] + part[rows:]

    @pl.when(pl.program_id(0) == 0)
    def _():
        out_ref[...] = part

    @pl.when(pl.program_id(0) > 0)
    def _():
        out_ref[...] += part


def project(momentum, grad, codes):
    rows, cols = momentum.shape
    rank = codes.shape[0]
    block = min(1024, cols)
    wide = pl.BlockSpec((rows, block), lambda i: (0, i))
    return pl.pallas_call(
        project_kernel,
        grid=(cols // block,),
        in_specs=[wide, wide, pl.BlockSpec((rank, block), lambda i: (0, i))],
        out_specs=pl.BlockSpec((rows, rank), lambda i: (0, 0)),
        out_shape=jax.ShapeDtypeStruct((rows, rank), jnp.float32),
        compiler_params=FLOW,
        cost_estimate=pl.CostEstimate(
            flops=4 * rows * cols * rank, bytes_accessed=rows * cols * 6 + rank * cols * 2, transcendentals=rank * cols
        ),
    )(momentum, grad, codes)


def pack_kernel(perm_ref, unit_ref, *refs):
    part_refs, out_ref = refs[:-1], refs[-1]
    rows, rank = part_refs[0].shape
    blocks = perm_ref.shape[0]
    size = rank // blocks
    stored = lax.broadcasted_iota(jnp.int32, (rank, rank), 0)
    target = jnp.zeros((rank, rank), jnp.int32)
    for s in range(blocks):
        target = jnp.where(stored // size == s, perm_ref[s] * size + stored % size, target)
    order = (target == lax.broadcasted_iota(jnp.int32, (rank, rank), 1)).astype(jnp.float32)
    parts = [ref[...] for ref in part_refs]
    while len(parts) > 1:
        parts = [parts[k] + parts[k + 1] for k in range(0, len(parts), 2)]
    total = jnp.dot(parts[0], order, precision=HIGH, preferred_element_type=jnp.float32)
    exponent, mantissa = code_unit(jnp.max(jnp.abs(total), axis=0, keepdims=True))
    value = total * (1.0 / unit_of(exponent, mantissa))
    high = jnp.floor(value + 0.5)
    out_ref[:rows] = whole_number(high)
    low = jnp.minimum(jnp.floor((value - high) * 16.0 + 0.5), 7.0)
    part = rows // 4
    packed = low[:part]
    for k in range(1, 4):
        packed = packed * 16.0 + (low[part * k : part * (k + 1)] + 8.0)
    out_ref[rows : rows + part] = whole_number(packed)
    units = jnp.concatenate([unit_ref[...], jnp.zeros((2, rank - rows), jnp.float32)], axis=1)
    set_head(out_ref.at[rows + part :], exponent, mantissa, units[:1], units[1:])


def pack(perm, units, parts):
    rows, rank = parts[0].shape
    return pl.pallas_call(
        pack_kernel,
        grid_spec=pltpu.PrefetchScalarGridSpec(
            num_scalar_prefetch=1,
            grid=(1,),
            in_specs=[whole(x) for x in (units, *parts)],
            out_specs=pl.BlockSpec((rows + rows // 4 + HEAD, rank), lambda *_: (0, 0)),
        ),
        out_shape=jax.ShapeDtypeStruct((rows + rows // 4 + HEAD, rank), jnp.int16),
        compiler_params=PARAMS,
        cost_estimate=pl.CostEstimate(flops=12 * rows * rank * rank, bytes_accessed=rank * rank * 4, transcendentals=0),
    )(perm, units, *parts)


def spread(row):
    return jnp.broadcast_to(row, (TILE, 2 * PANEL))


def panel_inverse(block, band):
    rows = lax.broadcasted_iota(jnp.int32, (PANEL, PANEL), 0)
    cols = lax.broadcasted_iota(jnp.int32, (PANEL, PANEL), 1)
    both = jnp.concatenate([block, (rows == cols).astype(jnp.float32)], axis=1)
    count = PANEL // TILE
    tiles = [both[TILE * i : TILE * (i + 1)] for i in range(count)]
    sub = lax.broadcasted_iota(jnp.int32, (TILE, 2 * PANEL), 0)
    row = lambda k, j: band[k, pl.ds(j, TILE, stride=0), :]
    done = []
    for k in range(count):
        columns = [
            [spread(tiles[i][:, TILE * k + j : TILE * k + j + 1]) for j in range(TILE)] for i in range(k, count)
        ]
        state = list(columns[0]) + [tiles[k]]
        for m, x in enumerate(state):
            band[m] = x
        final = jnp.zeros_like(tiles[k])
        for j in range(0, TILE, 2):
            first, second = sub == j, sub == j + 1
            a, b, c = row(j, j), row(j + 1, j), row(j + 1, j + 1)
            minor = a * c - b * b
            inverse = 1.0 / minor
            left, right, body = state[j], state[j + 1], state[TILE]
            ratio = 1.0 / a
            below = (body - b * ratio * row(TILE, j)) * lax.rsqrt(minor * ratio)
            final = jnp.where(first, body * lax.rsqrt(a), jnp.where(second, below, final))
            rests = {}
            for m in range(j + 2, TILE + 1):
                upper, lower = row(m, j), row(m, j + 1)
                upper, lower = c * upper - b * lower, a * lower - b * upper
                rests[m] = state[m] - (left * upper + right * lower) * inverse
                state[m] = jnp.where(first, upper * inverse, jnp.where(second, lower * inverse, rests[m]))
            for m, rest in rests.items():
                band[m] = rest
        done.append(final)
        band[TILE] = state[TILE]
        reduced = [row(TILE, j) for j in range(TILE)]
        for i in range(k + 1, count):
            terms = [columns[i - k][j] * reduced[j] for j in range(TILE)]
            while len(terms) > 1:
                terms = [terms[j] + terms[j + 1] for j in range(0, len(terms), 2)]
            tiles[i] = tiles[i] - terms[0]
    return jnp.concatenate(done, axis=0)[:, PANEL:]


def split_three(x):
    high, rest = x.astype(jnp.bfloat16), x
    rest = rest - high.astype(jnp.float32)
    middle = rest.astype(jnp.bfloat16)
    return high, middle, (rest - middle.astype(jnp.float32)).astype(jnp.bfloat16)


def short_dot(a, b):
    a1, a2, a3 = split_three(a)
    b1, b2, b3 = split_three(b)
    a = jnp.concatenate([a1, a1, a2, a2, a1, a3], axis=1)
    b = jnp.concatenate([b1, b2, b1, b2, b3, b1], axis=0)
    return jnp.dot(a, b, preferred_element_type=jnp.float32)


def lanes_up(x):
    return (x + 127) // 128 * 128


def inverse_factor(gram, out_ref, work, band):
    rank = gram.shape[0]
    rows = lax.broadcasted_iota(jnp.int32, (rank, rank), 0)
    cols = lax.broadcasted_iota(jnp.int32, (rank, rank), 1)
    diagonal = jnp.where(rows == cols, gram, 0.0)
    scale = lax.rsqrt(jnp.sum(diagonal, axis=0, keepdims=True))
    work[:, :rank] = gram * scale * lax.rsqrt(jnp.sum(diagonal, axis=1, keepdims=True))
    work[:, rank:] = (rows == cols).astype(jnp.float32)
    block = work[:PANEL, :PANEL]
    for start in range(0, rank, PANEL):
        end = start + PANEL
        left, right = start // 128 * 128, rank + lanes_up(end)
        inverse = panel_inverse(block, band)
        if end < rank:
            after = slice(end, end + PANEL)
            ahead = short_dot(inverse, work[start:end, after])
            block = work[after, after] - short_dot(ahead.T, ahead)
        scaled = short_dot(inverse, work[start:end, left:right])
        out_ref[start:end, : lanes_up(end)] = scaled[:, rank - left :] * scale[:, : lanes_up(end)]
        if lanes_up(end) < rank:
            out_ref[start:end, lanes_up(end) :] = jnp.zeros((PANEL, rank - lanes_up(end)), jnp.float32)
        if end < rank:
            low = end // 128 * 128
            change = short_dot(scaled[:, low - left : rank - left].T, scaled[:, low - left :])
            work[end:, low:right] = work[end:, low:right] - change[end - low :, :]


def factor_kernel(code_ref, turned_ref, out_ref, gram_ref, mixed_ref, work, band):
    count, size, rank = code_ref.shape
    size = (size - HEAD) * 4 // 5
    code = code_ref[...].astype(jnp.int32)
    low = code[:, size : size + size // 4]
    low = jnp.concatenate([low >> 12, *[((low >> shift) & 15) - 8 for shift in (8, 4, 0)]], axis=1)
    head = code[:, size + size // 4 :].astype(jnp.float32)
    part = code[:, :size].astype(jnp.float32) + low.astype(jnp.float32) * (1.0 / 16.0)
    part = part * unit_of(head[:, :1], head[:, 1:2])
    turned = part.reshape(count * size, rank).T
    turned_ref[...] = turned

    def times(a, b):
        a, b = jnp.concatenate(a, axis=1), jnp.concatenate(b, axis=1)
        return lax.dot_general(a, b, (((1,), (1,)), ((), ())), preferred_element_type=jnp.float32)

    high, middle, small = split_three(turned)
    even, mixed = times((high, middle), (high, middle)), times((high, high), (middle, small))

    @pl.when(pl.program_id(0) == 0)
    def _():
        gram_ref[...] = even
        mixed_ref[...] = mixed

    @pl.when(pl.program_id(0) > 0)
    def _():
        gram_ref[...] += even
        mixed_ref[...] += mixed

    @pl.when(pl.program_id(0) == pl.num_programs(0) - 1)
    def _():
        mixed = mixed_ref[...]
        inverse_factor(gram_ref[...] + (mixed + mixed.T), out_ref, work, band)


def factor(codes):
    devices, size, rank = codes.shape
    rows = (size - HEAD) * 4 // 5
    group = min(devices, max(1, 1024 // rows))
    return pl.pallas_call(
        factor_kernel,
        grid=(devices // group,),
        in_specs=[pl.BlockSpec((group, size, rank), lambda i: (i, 0, 0))],
        out_specs=[pl.BlockSpec((rank, group * rows), lambda i: (0, i)), pl.BlockSpec((rank, rank), lambda i: (0, 0))],
        out_shape=[
            jax.ShapeDtypeStruct((rank, devices * rows), jnp.float32),
            jax.ShapeDtypeStruct((rank, rank), jnp.float32),
        ],
        scratch_shapes=[
            pltpu.VMEM((rank, rank), jnp.float32),
            pltpu.VMEM((rank, rank), jnp.float32),
            pltpu.VMEM((rank, 2 * rank), jnp.float32),
            pltpu.VMEM((TILE + 1, TILE, 2 * PANEL), jnp.float32),
        ],
        compiler_params=PARAMS,
        cost_estimate=pl.CostEstimate(
            flops=12 * devices * rows * rank * rank, bytes_accessed=devices * size * rank * 4, transcendentals=rank
        ),
    )(codes)


def encode_kernel(place_ref, source_ref, turned_ref, head_ref, inverse_ref, own_ref, code_ref, ortho_ref, mixed_ref):
    def times(a, b):
        return jnp.dot(a, b, preferred_element_type=jnp.float32)

    def turned_dot(a, b):
        return lax.dot_general(a, b, (((0,), (1,)), ((), ())), precision=HIGH, preferred_element_type=jnp.float32)

    rank = turned_ref.shape[0]
    source_high, source_low = halves(source_ref[...].astype(jnp.int32).astype(jnp.float32))
    head = head_ref[...].astype(jnp.int32).astype(jnp.float32)
    devices = head.shape[0]
    rows = turned_ref.shape[1] // devices
    unit = jnp.concatenate([unit_of(head[k, 2:3, :rows], head[k, 3:4, :rows]) for k in range(devices)], axis=1)
    scaled_high, scaled_low = halves(turned_ref[...] * unit)
    most = times(jnp.concatenate([scaled_high, scaled_low], axis=0), source_high)
    part = most[:rank] + (most[rank:] + times(scaled_high, source_low))
    first, last = pl.program_id(0) == 0, pl.program_id(0) == pl.num_programs(0) - 1

    @pl.when(first)
    def _():
        mixed_ref[...] = part

    @pl.when(jnp.logical_not(first))
    def _():
        mixed_ref[...] += part

    @pl.when(last)
    def _():
        inverse = inverse_ref[...]
        ortho_ref[...] = turned_dot(own_ref[...], inverse)
        right = turned_dot(mixed_ref[...], inverse)
        rows = right.shape[0]
        square = jnp.maximum(jnp.sum(right * right, axis=0, keepdims=True), 1e-34)
        square_exponent = jnp.floor(jnp.log2(square))
        fine = square * jnp.exp2(13.0 - square_exponent)
        square_high = jnp.floor(fine)
        square_low = jnp.floor((fine - square_high) * 16384.0)
        exponent, mantissa = code_unit(jnp.max(jnp.abs(right), axis=0, keepdims=True))
        code_ref[:rows] = whole_number(jnp.floor(right * (1.0 / unit_of(exponent, mantissa)) + 0.5))
        set_head(code_ref.at[rows:], exponent, mantissa, square_exponent, square_high, square_low)


def encode(place, source, turned, packed, inverse_low, rows):
    total, share = source.shape
    rank = turned.shape[0]
    block = min(1024, total)
    size = packed.shape[1]
    return pl.pallas_call(
        encode_kernel,
        grid_spec=pltpu.PrefetchScalarGridSpec(
            num_scalar_prefetch=1,
            grid=(total // block,),
            in_specs=[
                pl.BlockSpec((block, share), lambda i, place: (i, 0)),
                pl.BlockSpec((rank, block), lambda i, place: (0, i)),
                pl.BlockSpec((block // rows, HEAD, rank), lambda i, place: (i, size // HEAD - 1, 0)),
                whole(inverse_low),
                pl.BlockSpec((rank, rows), lambda i, place: (0, place[0])),
            ],
            out_specs=[
                pl.BlockSpec((share + HEAD, rank), lambda i, place: (0, 0)),
                pl.BlockSpec((rows, rank), lambda i, place: (0, 0)),
            ],
            scratch_shapes=[pltpu.VMEM((rank, share), jnp.float32)],
        ),
        out_shape=[
            jax.ShapeDtypeStruct((share + HEAD, rank), jnp.int16),
            jax.ShapeDtypeStruct((rows, rank), jnp.float32),
        ],
        compiler_params=PARAMS,
        cost_estimate=pl.CostEstimate(
            flops=6 * total * share * rank, bytes_accessed=total * (share * 2 + rank * 4), transcendentals=0
        ),
    )(place, source, turned, packed, inverse_low, turned)


def decode(code_ref):
    code = code_ref[...].astype(jnp.int32).astype(jnp.float32)
    share = code.shape[1] - HEAD
    right = code[:, :share] * unit_of(code[:, share : share + 1], code[:, share + 1 : share + 2])
    return right.reshape(code.shape[0] * share, code.shape[2])


def times_rows(split_ref, right):
    def times(a, b):
        return lax.dot_general(a, b, (((1,), (1,)), ((), ())), preferred_element_type=jnp.float32)

    right_high, right_low = halves(right)
    split = split_ref[...]
    rows = split.shape[0] // 2
    most = times(split, right_high)
    return most[:rows] + (most[rows:] + times(split[:rows], right_low))


def set_split(split_ref, x):
    rows = x.shape[0]

    @pl.when(pl.program_id(0) == 0)
    def _():
        split_ref[:rows], split_ref[rows:] = halves(x)


def momentum_kernel(momentum_ref, grad_ref, code_ref, ortho_ref, next_ref, split_ref):
    set_split(split_ref, -KEEP_SHARE * ortho_ref[...])
    change = times_rows(split_ref, decode(code_ref))
    next_ref[...] = momentum_ref[...] + grad_ref[...].astype(jnp.float32) + change


def update_kernel(gain, code_ref, ortho_ref, scale_ref, basis_ref, update_ref, split_ref):
    set_split(split_ref, gain * ortho_ref[...])
    basis = decode(code_ref) * scale_ref[...]
    basis_ref[...] = basis
    update_ref[...] = times_rows(split_ref, basis).astype(jnp.bfloat16)


def finish(momentum, grad, codes, orthonormal, scale, gain):
    rows, cols = momentum.shape
    shares, share, rank = codes.shape
    share -= HEAD
    group = max(1, min(2048 // share, shares))
    block = group * share
    wide = pl.BlockSpec((rows, block), lambda i: (0, i))
    tall = pl.BlockSpec((block, rank), lambda i: (i, 0))
    coded = pl.BlockSpec((group, share + HEAD, rank), lambda i: (i, 0, 0))
    split = [pltpu.VMEM((2 * rows, rank), jnp.bfloat16)]
    flops = 6 * rows * cols * rank
    momentum_next = pl.pallas_call(
        momentum_kernel,
        grid=(cols // block,),
        in_specs=[wide, wide, coded, whole(orthonormal)],
        out_specs=wide,
        out_shape=jax.ShapeDtypeStruct((rows, cols), jnp.float32),
        scratch_shapes=split,
        compiler_params=PARAMS,
        cost_estimate=pl.CostEstimate(
            flops=flops, bytes_accessed=rows * cols * 10 + cols * rank * 2, transcendentals=0
        ),
    )(momentum, grad, codes, orthonormal)
    q_next, update = pl.pallas_call(
        functools.partial(update_kernel, gain),
        grid=(cols // block,),
        in_specs=[coded, whole(orthonormal), whole(scale)],
        out_specs=[tall, wide],
        out_shape=[
            jax.ShapeDtypeStruct((cols, rank), jnp.float32),
            jax.ShapeDtypeStruct((rows, cols), jnp.bfloat16),
        ],
        scratch_shapes=split,
        compiler_params=PARAMS,
        cost_estimate=pl.CostEstimate(flops=flops, bytes_accessed=rows * cols * 2 + cols * rank * 6, transcendentals=0),
    )(codes, orthonormal, scale)
    return momentum_next, q_next, update


def on_device(momentum, grad, q_stored, perm):
    block_rows = q_stored.shape[0]
    num_blocks = lax.axis_size("fsdp")
    num_cols = lax.axis_size("tp")
    rank_total = block_rows * num_blocks
    rows, cols = momentum.shape
    row_total, col_total = rows * num_blocks, cols * num_cols
    share = cols // num_blocks

    basis, codes, units = prepare(momentum, grad, q_stored, share)
    codes = codes.reshape(-1, rows, codes.shape[2] // share, share).swapaxes(1, 2).reshape(num_blocks, rows, share)
    basis = lax.all_gather(basis, "fsdp", axis=0, tiled=True)
    codes, basis = lax.optimization_barrier((codes, basis))
    codes = lax.all_to_all(codes, "fsdp", split_axis=0, concat_axis=0).reshape(row_total, share)

    near, step = project(momentum, grad, basis), 1
    while 4 * step < num_cols:
        near = near + exchange(near, "tp", step)
        step *= 2
    parts = [near] + [exchange(near, "tp", k) for k in range(step, num_cols, step)]
    packed = lax.all_gather(pack(perm, units, parts), "fsdp", axis=0)
    packed, codes = lax.optimization_barrier((packed, codes))
    turned, inverse_low = factor(packed)
    code, orthonormal = encode(lax.axis_index("fsdp").reshape(1), codes, turned, packed, inverse_low, rows)
    gathered = lax.all_gather(code, "fsdp", axis=0)
    head = gathered[:, share : share + 5].astype(jnp.float32)
    parts = (head[:, 3] + head[:, 4] * (1.0 / 16384.0)) * jnp.exp2(head[:, 2] - 13.0)
    squares = quad_sum(jnp.sum(parts, axis=0, keepdims=True), "tp")
    scale = lax.rsqrt(squares / col_total + EPSILON)
    return tuple(finish(momentum, grad, gathered, orthonormal, scale, math.sqrt(row_total / rank_total)))


def solution(mesh):
    return jax.shard_map(
        on_device,
        mesh=mesh,
        in_specs=(P("fsdp", "tp"), P("fsdp", "tp"), P("fsdp", "tp"), P()),
        out_specs=(P("fsdp", "tp"), P("tp", None), P("fsdp", "tp")),
        check_vma=False,
    )
```

```python
import functools
import math

import jax
import jax.numpy as jnp
from jax import lax
from jax.experimental import pallas as pl
from jax.experimental.pallas import tpu as pltpu
from jax.sharding import PartitionSpec as P

EPSILON = 1e-06
KEEP_SHARE = 0.5
HIGH = lax.Precision.HIGHEST
PANEL = 64
TILE = 16
HEAD = 16
TOP = 32766.0
PARAMS = pltpu.CompilerParams(vmem_limit_bytes=40 * 1024 * 1024)
FLOW = pltpu.CompilerParams(vmem_limit_bytes=53 * 1024 * 1024)
STREAM = pltpu.CompilerParams(vmem_limit_bytes=54 * 1024 * 1024)


def halves(x):
    high = x.astype(jnp.bfloat16)
    return high, (x - high.astype(jnp.float32)).astype(jnp.bfloat16)


def exchange(x, axis, k):
    return lax.ppermute(x, axis, [(i, i ^ k) for i in range(lax.axis_size(axis))])


def butterfly_sum(x, axis, step=1):
    while step < lax.axis_size(axis):
        x = x + exchange(x, axis, step)
        step *= 2
    return x


def quad_sum(x, axis, step=1):
    if lax.axis_size(axis) != 4 * step:
        return butterfly_sum(x, axis, step)
    near, far, across = [exchange(x, axis, k * step) for k in range(1, 4)]
    return (x + near) + (far + across)


def whole(x):
    return pl.BlockSpec(x.shape, lambda *_: (0,) * len(x.shape))


def dot_rows(a, b):
    return lax.dot_general(a, b, (((1,), (1,)), ((), ())), precision=HIGH, preferred_element_type=jnp.float32)


def unit_of(exponent, mantissa):
    return mantissa * jnp.exp2(exponent - 13.0)


def code_unit(top):
    top = jnp.maximum(top, 1e-28) * (1.0 / TOP)
    exponent = jnp.floor(jnp.log2(top))
    return exponent, jnp.floor(top * jnp.exp2(13.0 - exponent)) + 1.0


def whole_number(x):
    return x.astype(jnp.int32).astype(jnp.int16)


def set_head(head_ref, *rows):
    place = lax.broadcasted_iota(jnp.int32, head_ref.shape, 0)
    head = jnp.zeros(head_ref.shape, jnp.float32)
    for k, row in enumerate(rows):
        head = jnp.where(place == k, row, head)
    head_ref[...] = whole_number(head)


def code_basis(basis):
    value = basis.astype(jnp.float32)
    size = jnp.abs(value)
    normal = size >= 2.0**-126
    exponent = jnp.floor(jnp.log2(jnp.where(normal, size, 1.0)))
    code = 128.0 * (exponent + 126.0) + jnp.floor(128.0 * (size * jnp.exp2(-exponent)) + 0.5)
    return whole_number(jnp.where(normal, jnp.where(value < 0.0, code - 32768.0, code), 0.0))


def prepare_kernel(momentum_ref, grad_ref, basis_ref, basis_code_ref, code_ref, unit_ref, column_ref):
    rows, cols = momentum_ref.shape
    width = code_ref.shape[-1]
    spans = [slice(i, i + width) for i in range(0, cols, width)]
    combined = lambda span: momentum_ref[:, span] + grad_ref[:, span].astype(jnp.float32)
    top = functools.reduce(jnp.maximum, [jnp.abs(combined(span)) for span in spans])
    exponent, mantissa = code_unit(jnp.max(top, axis=1, keepdims=True))
    inverse = 1.0 / unit_of(exponent, mantissa)
    for k, span in enumerate(spans):
        code_ref[k] = whole_number(jnp.floor(combined(span) * inverse + 0.5))
        basis_code_ref[:, span] = code_basis(basis_ref[:, span])
    step = pl.program_id(0)
    here = pl.ds(pl.multiple_of(step * rows, rows), rows)
    for k, column in enumerate((exponent, mantissa)):
        column_ref[k, here, :] = jnp.broadcast_to(column, (rows, column_ref.shape[2]))

    @pl.when(step == pl.num_programs(0) - 1)
    def _():
        for k in range(2):
            unit_ref[k : k + 1, :] = column_ref[k].T[:1]


def prepare(momentum, grad, basis, share):
    rows, cols = momentum.shape
    width = share if share % 128 == 0 else cols
    steps = 2 if basis.shape[0] % 32 == 0 else 1
    wide = pl.BlockSpec((rows // steps, cols), lambda i: (i, 0))
    narrow = pl.BlockSpec((basis.shape[0] // steps, cols), lambda i: (i, 0))
    return pl.pallas_call(
        prepare_kernel,
        grid=(steps,),
        in_specs=[wide, wide, narrow],
        out_specs=[
            narrow,
            pl.BlockSpec((cols // width, rows // steps, width), lambda i: (0, i, 0)),
            pl.BlockSpec((2, rows), lambda i: (0, 0)),
        ],
        out_shape=[
            jax.ShapeDtypeStruct(basis.shape, jnp.int16),
            jax.ShapeDtypeStruct((cols // width, rows, width), jnp.int16),
            jax.ShapeDtypeStruct((2, rows), jnp.float32),
        ],
        scratch_shapes=[pltpu.VMEM((2, rows, 128), jnp.float32)],
        compiler_params=STREAM,
        cost_estimate=pl.CostEstimate(flops=10 * rows * cols, bytes_accessed=rows * cols * 8, transcendentals=0),
    )(momentum, grad, basis)


def project_kernel(momentum_ref, grad_ref, code_ref, out_ref):
    code = code_ref[...].astype(jnp.int32)
    power = jnp.exp2(((code >> 7) & 255).astype(jnp.float32) - 134.0)
    value = ((code & 127) | 128).astype(jnp.float32) * power
    basis = jnp.where(code < 0, -value, value).astype(jnp.bfloat16)
    combined = momentum_ref[...] + grad_ref[...].astype(jnp.float32)
    rows = combined.shape[0]
    part = lax.dot_general(
        jnp.concatenate(halves(combined), axis=0),
        basis,
        (((1,), (1,)), ((), ())),
        preferred_element_type=jnp.float32,
    )
    part = part[:rows] + part[rows:]

    @pl.when(pl.program_id(0) == 0)
    def _():
        out_ref[...] = part

    @pl.when(pl.program_id(0) > 0)
    def _():
        out_ref[...] += part


def project(momentum, grad, codes):
    rows, cols = momentum.shape
    rank = codes.shape[0]
    block = min(1024, cols)
    wide = pl.BlockSpec((rows, block), lambda i: (0, i))
    return pl.pallas_call(
        project_kernel,
        grid=(cols // block,),
        in_specs=[wide, wide, pl.BlockSpec((rank, block), lambda i: (0, i))],
        out_specs=pl.BlockSpec((rows, rank), lambda i: (0, 0)),
        out_shape=jax.ShapeDtypeStruct((rows, rank), jnp.float32),
        compiler_params=FLOW,
        cost_estimate=pl.CostEstimate(
            flops=4 * rows * cols * rank, bytes_accessed=rows * cols * 6 + rank * cols * 2, transcendentals=rank * cols
        ),
    )(momentum, grad, codes)


def pack_kernel(perm_ref, unit_ref, *refs):
    part_refs, out_ref = refs[:-1], refs[-1]
    rows, rank = part_refs[0].shape
    blocks = perm_ref.shape[0]
    size = rank // blocks
    stored = lax.broadcasted_iota(jnp.int32, (rank, rank), 0)
    target = jnp.zeros((rank, rank), jnp.int32)
    for s in range(blocks):
        target = jnp.where(stored // size == s, perm_ref[s] * size + stored % size, target)
    order = (target == lax.broadcasted_iota(jnp.int32, (rank, rank), 1)).astype(jnp.float32)
    parts = [ref[...] for ref in part_refs]
    while len(parts) > 1:
        parts = [parts[k] + parts[k + 1] for k in range(0, len(parts), 2)]
    total = jnp.dot(parts[0], order, precision=HIGH, preferred_element_type=jnp.float32)
    exponent, mantissa = code_unit(jnp.max(jnp.abs(total), axis=0, keepdims=True))
    value = total * (1.0 / unit_of(exponent, mantissa))
    high = jnp.floor(value + 0.5)
    out_ref[:rows] = whole_number(high)
    low = jnp.minimum(jnp.floor((value - high) * 16.0 + 0.5), 7.0)
    part = rows // 4
    packed = low[:part]
    for k in range(1, 4):
        packed = packed * 16.0 + (low[part * k : part * (k + 1)] + 8.0)
    out_ref[rows : rows + part] = whole_number(packed)
    units = jnp.concatenate([unit_ref[...], jnp.zeros((2, rank - rows), jnp.float32)], axis=1)
    set_head(out_ref.at[rows + part :], exponent, mantissa, units[:1], units[1:])


def pack(perm, units, parts):
    rows, rank = parts[0].shape
    return pl.pallas_call(
        pack_kernel,
        grid_spec=pltpu.PrefetchScalarGridSpec(
            num_scalar_prefetch=1,
            grid=(1,),
            in_specs=[whole(x) for x in (units, *parts)],
            out_specs=pl.BlockSpec((rows + rows // 4 + HEAD, rank), lambda *_: (0, 0)),
        ),
        out_shape=jax.ShapeDtypeStruct((rows + rows // 4 + HEAD, rank), jnp.int16),
        compiler_params=PARAMS,
        cost_estimate=pl.CostEstimate(flops=12 * rows * rank * rank, bytes_accessed=rank * rank * 4, transcendentals=0),
    )(perm, units, *parts)


def spread(row):
    return jnp.broadcast_to(row, (TILE, 2 * PANEL))


def panel_inverse(block, band):
    rows = lax.broadcasted_iota(jnp.int32, (PANEL, PANEL), 0)
    cols = lax.broadcasted_iota(jnp.int32, (PANEL, PANEL), 1)
    both = jnp.concatenate([block, (rows == cols).astype(jnp.float32)], axis=1)
    count = PANEL // TILE
    tiles = [both[TILE * i : TILE * (i + 1)] for i in range(count)]
    sub = lax.broadcasted_iota(jnp.int32, (TILE, 2 * PANEL), 0)
    row = lambda k, j: band[k, pl.ds(j, TILE, stride=0), :]
    done = []
    for k in range(count):
        columns = [
            [spread(tiles[i][:, TILE * k + j : TILE * k + j + 1]) for j in range(TILE)] for i in range(k, count)
        ]
        state = list(columns[0]) + [tiles[k]]
        for m, x in enumerate(state):
            band[m] = x
        final = jnp.zeros_like(tiles[k])
        for j in range(0, TILE, 2):
            first, second = sub == j, sub == j + 1
            a, b, c = row(j, j), row(j + 1, j), row(j + 1, j + 1)
            minor = a * c - b * b
            inverse = 1.0 / minor
            left, right, body = state[j], state[j + 1], state[TILE]
            ratio = 1.0 / a
            below = (body - b * ratio * row(TILE, j)) * lax.rsqrt(minor * ratio)
            final = jnp.where(first, body * lax.rsqrt(a), jnp.where(second, below, final))
            rests = {}
            for m in range(j + 2, TILE + 1):
                upper, lower = row(m, j), row(m, j + 1)
                upper, lower = c * upper - b * lower, a * lower - b * upper
                rests[m] = state[m] - (left * upper + right * lower) * inverse
                state[m] = jnp.where(first, upper * inverse, jnp.where(second, lower * inverse, rests[m]))
            for m, rest in rests.items():
                band[m] = rest
        done.append(final)
        band[TILE] = state[TILE]
        reduced = [row(TILE, j) for j in range(TILE)]
        for i in range(k + 1, count):
            terms = [columns[i - k][j] * reduced[j] for j in range(TILE)]
            while len(terms) > 1:
                terms = [terms[j] + terms[j + 1] for j in range(0, len(terms), 2)]
            tiles[i] = tiles[i] - terms[0]
    return jnp.concatenate(done, axis=0)[:, PANEL:]


def split_three(x):
    high, rest = x.astype(jnp.bfloat16), x
    rest = rest - high.astype(jnp.float32)
    middle = rest.astype(jnp.bfloat16)
    return high, middle, (rest - middle.astype(jnp.float32)).astype(jnp.bfloat16)


def short_dot(a, b):
    a1, a2, a3 = split_three(a)
    b1, b2, b3 = split_three(b)
    a = jnp.concatenate([a1, a1, a2, a2, a1, a3], axis=1)
    b = jnp.concatenate([b1, b2, b1, b2, b3, b1], axis=0)
    return jnp.dot(a, b, preferred_element_type=jnp.float32)


def lanes_up(x):
    return (x + 127) // 128 * 128


def inverse_factor(gram, out_ref, work, band):
    rank = gram.shape[0]
    rows = lax.broadcasted_iota(jnp.int32, (rank, rank), 0)
    cols = lax.broadcasted_iota(jnp.int32, (rank, rank), 1)
    diagonal = jnp.where(rows == cols, gram, 0.0)
    scale = lax.rsqrt(jnp.sum(diagonal, axis=0, keepdims=True))
    work[:, :rank] = gram * scale * lax.rsqrt(jnp.sum(diagonal, axis=1, keepdims=True))
    work[:, rank:] = (rows == cols).astype(jnp.float32)
    block = work[:PANEL, :PANEL]
    for start in range(0, rank, PANEL):
        end = start + PANEL
        left, right = start // 128 * 128, rank + lanes_up(end)
        inverse = panel_inverse(block, band)
        if end < rank:
            after = slice(end, end + PANEL)
            ahead = short_dot(inverse, work[start:end, after])
            block = work[after, after] - short_dot(ahead.T, ahead)
        scaled = short_dot(inverse, work[start:end, left:right])
        out_ref[start:end, : lanes_up(end)] = scaled[:, rank - left :] * scale[:, : lanes_up(end)]
        if lanes_up(end) < rank:
            out_ref[start:end, lanes_up(end) :] = jnp.zeros((PANEL, rank - lanes_up(end)), jnp.float32)
        if end < rank:
            low = end // 128 * 128
            change = short_dot(scaled[:, low - left : rank - left].T, scaled[:, low - left :])
            work[end:, low:right] = work[end:, low:right] - change[end - low :, :]


def factor_kernel(code_ref, turned_ref, out_ref, gram_ref, mixed_ref, work, band):
    count, size, rank = code_ref.shape
    size = (size - HEAD) * 4 // 5
    code = code_ref[...].astype(jnp.int32)
    low = code[:, size : size + size // 4]
    low = jnp.concatenate([low >> 12, *[((low >> shift) & 15) - 8 for shift in (8, 4, 0)]], axis=1)
    head = code[:, size + size // 4 :].astype(jnp.float32)
    part = code[:, :size].astype(jnp.float32) + low.astype(jnp.float32) * (1.0 / 16.0)
    part = part * unit_of(head[:, :1], head[:, 1:2])
    turned = part.reshape(count * size, rank).T
    turned_ref[...] = turned

    def times(a, b):
        a, b = jnp.concatenate(a, axis=1), jnp.concatenate(b, axis=1)
        return lax.dot_general(a, b, (((1,), (1,)), ((), ())), preferred_element_type=jnp.float32)

    high, middle, small = split_three(turned)
    even, mixed = times((high, middle), (high, middle)), times((high, high), (middle, small))

    @pl.when(pl.program_id(0) == 0)
    def _():
        gram_ref[...] = even
        mixed_ref[...] = mixed

    @pl.when(pl.program_id(0) > 0)
    def _():
        gram_ref[...] += even
        mixed_ref[...] += mixed

    @pl.when(pl.program_id(0) == pl.num_programs(0) - 1)
    def _():
        mixed = mixed_ref[...]
        inverse_factor(gram_ref[...] + (mixed + mixed.T), out_ref, work, band)


def factor(codes):
    devices, size, rank = codes.shape
    rows = (size - HEAD) * 4 // 5
    group = min(devices, max(1, 1024 // rows))
    return pl.pallas_call(
        factor_kernel,
        grid=(devices // group,),
        in_specs=[pl.BlockSpec((group, size, rank), lambda i: (i, 0, 0))],
        out_specs=[pl.BlockSpec((rank, group * rows), lambda i: (0, i)), pl.BlockSpec((rank, rank), lambda i: (0, 0))],
        out_shape=[
            jax.ShapeDtypeStruct((rank, devices * rows), jnp.float32),
            jax.ShapeDtypeStruct((rank, rank), jnp.float32),
        ],
        scratch_shapes=[
            pltpu.VMEM((rank, rank), jnp.float32),
            pltpu.VMEM((rank, rank), jnp.float32),
            pltpu.VMEM((rank, 2 * rank), jnp.float32),
            pltpu.VMEM((TILE + 1, TILE, 2 * PANEL), jnp.float32),
        ],
        compiler_params=PARAMS,
        cost_estimate=pl.CostEstimate(
            flops=12 * devices * rows * rank * rank, bytes_accessed=devices * size * rank * 4, transcendentals=rank
        ),
    )(codes)


def encode_kernel(place_ref, source_ref, turned_ref, head_ref, inverse_ref, own_ref, code_ref, ortho_ref, mixed_ref):
    def times(a, b):
        return jnp.dot(a, b, preferred_element_type=jnp.float32)

    def turned_dot(a, b):
        return lax.dot_general(a, b, (((0,), (1,)), ((), ())), precision=HIGH, preferred_element_type=jnp.float32)

    rank = turned_ref.shape[0]
    source_high, source_low = halves(source_ref[...].astype(jnp.int32).astype(jnp.float32))
    head = head_ref[...].astype(jnp.int32).astype(jnp.float32)
    devices = head.shape[0]
    rows = turned_ref.shape[1] // devices
    unit = jnp.concatenate([unit_of(head[k, 2:3, :rows], head[k, 3:4, :rows]) for k in range(devices)], axis=1)
    scaled_high, scaled_low = halves(turned_ref[...] * unit)
    most = times(jnp.concatenate([scaled_high, scaled_low], axis=0), source_high)
    part = most[:rank] + (most[rank:] + times(scaled_high, source_low))
    first, last = pl.program_id(0) == 0, pl.program_id(0) == pl.num_programs(0) - 1

    @pl.when(first)
    def _():
        mixed_ref[...] = part

    @pl.when(jnp.logical_not(first))
    def _():
        mixed_ref[...] += part

    @pl.when(last)
    def _():
        inverse = inverse_ref[...]
        ortho_ref[...] = turned_dot(own_ref[...], inverse)
        right = turned_dot(mixed_ref[...], inverse)
        rows = right.shape[0]
        square = jnp.maximum(jnp.sum(right * right, axis=0, keepdims=True), 1e-34)
        square_exponent = jnp.floor(jnp.log2(square))
        fine = square * jnp.exp2(13.0 - square_exponent)
        square_high = jnp.floor(fine)
        square_low = jnp.floor((fine - square_high) * 16384.0)
        exponent, mantissa = code_unit(jnp.max(jnp.abs(right), axis=0, keepdims=True))
        code_ref[:rows] = whole_number(jnp.floor(right * (1.0 / unit_of(exponent, mantissa)) + 0.5))
        set_head(code_ref.at[rows:], exponent, mantissa, square_exponent, square_high, square_low)


def encode(place, source, turned, packed, inverse_low, rows):
    total, share = source.shape
    rank = turned.shape[0]
    block = min(1024, total)
    size = packed.shape[1]
    return pl.pallas_call(
        encode_kernel,
        grid_spec=pltpu.PrefetchScalarGridSpec(
            num_scalar_prefetch=1,
            grid=(total // block,),
            in_specs=[
                pl.BlockSpec((block, share), lambda i, place: (i, 0)),
                pl.BlockSpec((rank, block), lambda i, place: (0, i)),
                pl.BlockSpec((block // rows, HEAD, rank), lambda i, place: (i, size // HEAD - 1, 0)),
                whole(inverse_low),
                pl.BlockSpec((rank, rows), lambda i, place: (0, place[0])),
            ],
            out_specs=[
                pl.BlockSpec((share + HEAD, rank), lambda i, place: (0, 0)),
                pl.BlockSpec((rows, rank), lambda i, place: (0, 0)),
            ],
            scratch_shapes=[pltpu.VMEM((rank, share), jnp.float32)],
        ),
        out_shape=[
            jax.ShapeDtypeStruct((share + HEAD, rank), jnp.int16),
            jax.ShapeDtypeStruct((rows, rank), jnp.float32),
        ],
        compiler_params=PARAMS,
        cost_estimate=pl.CostEstimate(
            flops=6 * total * share * rank, bytes_accessed=total * (share * 2 + rank * 4), transcendentals=0
        ),
    )(place, source, turned, packed, inverse_low, turned)


def decode(code_ref):
    code = code_ref[...].astype(jnp.int32).astype(jnp.float32)
    share = code.shape[1] - HEAD
    right = code[:, :share] * unit_of(code[:, share : share + 1], code[:, share + 1 : share + 2])
    return right.reshape(code.shape[0] * share, code.shape[2])


def times_rows(split_ref, right):
    def times(a, b):
        return lax.dot_general(a, b, (((1,), (1,)), ((), ())), preferred_element_type=jnp.float32)

    right_high, right_low = halves(right)
    split = split_ref[...]
    rows = split.shape[0] // 2
    most = times(split, right_high)
    return most[:rows] + (most[rows:] + times(split[:rows], right_low))


def finish_kernel(
    gain, momentum_ref, grad_ref, code_ref, ortho_ref, scale_ref, next_ref, basis_ref, update_ref, split_ref
):
    rows = momentum_ref.shape[0]
    scale = scale_ref[...]

    @pl.when(pl.program_id(0) == 0)
    def _():
        ortho = ortho_ref[...]
        for k, factor in enumerate((-KEEP_SHARE * ortho, gain * ortho * scale)):
            high, low = halves(factor)
            split_ref[rows * k : rows * (k + 1)] = high
            split_ref[rows * (k + 2) : rows * (k + 3)] = low

    right = decode(code_ref)
    basis_ref[...] = right * scale
    both = times_rows(split_ref, right)
    next_ref[...] = momentum_ref[...] + grad_ref[...].astype(jnp.float32) + both[:rows]
    update_ref[...] = both[rows:].astype(jnp.bfloat16)


def finish(momentum, grad, codes, orthonormal, scale, gain):
    rows, cols = momentum.shape
    shares, share, rank = codes.shape
    share -= HEAD
    group = max(1, min(1024 // share, shares))
    block = group * share
    wide = pl.BlockSpec((rows, block), lambda i: (0, i))
    tall = pl.BlockSpec((block, rank), lambda i: (i, 0))
    coded = pl.BlockSpec((group, share + HEAD, rank), lambda i: (i, 0, 0))
    return pl.pallas_call(
        functools.partial(finish_kernel, gain),
        grid=(cols // block,),
        in_specs=[wide, wide, coded, whole(orthonormal), whole(scale)],
        out_specs=[wide, tall, wide],
        out_shape=[
            jax.ShapeDtypeStruct((rows, cols), jnp.float32),
            jax.ShapeDtypeStruct((cols, rank), jnp.float32),
            jax.ShapeDtypeStruct((rows, cols), jnp.bfloat16),
        ],
        scratch_shapes=[pltpu.VMEM((4 * rows, rank), jnp.bfloat16)],
        compiler_params=PARAMS,
        cost_estimate=pl.CostEstimate(
            flops=12 * rows * cols * rank, bytes_accessed=rows * cols * 12 + cols * rank * 6, transcendentals=0
        ),
    )(momentum, grad, codes, orthonormal, scale)


def on_device(momentum, grad, q_stored, perm):
    block_rows = q_stored.shape[0]
    num_blocks = lax.axis_size("fsdp")
    num_cols = lax.axis_size("tp")
    rank_total = block_rows * num_blocks
    rows, cols = momentum.shape
    row_total, col_total = rows * num_blocks, cols * num_cols
    share = cols // num_blocks

    basis, codes, units = prepare(momentum, grad, q_stored, share)
    codes = codes.reshape(-1, rows, codes.shape[2] // share, share).swapaxes(1, 2).reshape(num_blocks, rows, share)
    basis = lax.all_gather(basis, "fsdp", axis=0, tiled=True)
    codes, basis = lax.optimization_barrier((codes, basis))
    codes = lax.all_to_all(codes, "fsdp", split_axis=0, concat_axis=0).reshape(row_total, share)

    near, step = project(momentum, grad, basis), 1
    while 4 * step < num_cols:
        near = near + exchange(near, "tp", step)
        step *= 2
    parts = [near] + [exchange(near, "tp", k) for k in range(step, num_cols, step)]
    packed = lax.all_gather(pack(perm, units, parts), "fsdp", axis=0)
    packed, codes = lax.optimization_barrier((packed, codes))
    turned, inverse_low = factor(packed)
    code, orthonormal = encode(lax.axis_index("fsdp").reshape(1), codes, turned, packed, inverse_low, rows)
    gathered = lax.all_gather(code, "fsdp", axis=0)
    head = gathered[:, share : share + 5].astype(jnp.float32)
    parts = (head[:, 3] + head[:, 4] * (1.0 / 16384.0)) * jnp.exp2(head[:, 2] - 13.0)
    squares = quad_sum(jnp.sum(parts, axis=0, keepdims=True), "tp")
    scale = lax.rsqrt(squares / col_total + EPSILON)
    return tuple(finish(momentum, grad, gathered, orthonormal, scale, math.sqrt(row_total / rank_total)))


def solution(mesh):
    return jax.shard_map(
        on_device,
        mesh=mesh,
        in_specs=(P("fsdp", "tp"), P("fsdp", "tp"), P("fsdp", "tp"), P()),
        out_specs=(P("fsdp", "tp"), P("tp", None), P("fsdp", "tp")),
        check_vma=False,
    )
```

```python
import functools
import math

import jax
import jax.numpy as jnp
from jax import lax
from jax.experimental import pallas as pl
from jax.experimental.pallas import tpu as pltpu
from jax.sharding import PartitionSpec as P

EPSILON = 1e-06
KEEP_SHARE = 0.5
HIGH = lax.Precision.HIGHEST
PANEL = 64
TILE = 16
HEAD = 16
TOP = 32766.0
PARAMS = pltpu.CompilerParams(vmem_limit_bytes=40 * 1024 * 1024)
FLOW = pltpu.CompilerParams(vmem_limit_bytes=53 * 1024 * 1024)
STREAM = pltpu.CompilerParams(vmem_limit_bytes=54 * 1024 * 1024)


def halves(x):
    high = x.astype(jnp.bfloat16)
    return high, (x - high.astype(jnp.float32)).astype(jnp.bfloat16)


def exchange(x, axis, k):
    return lax.ppermute(x, axis, [(i, i ^ k) for i in range(lax.axis_size(axis))])


def butterfly_sum(x, axis, step=1):
    while step < lax.axis_size(axis):
        x = x + exchange(x, axis, step)
        step *= 2
    return x


def quad_sum(x, axis, step=1):
    if lax.axis_size(axis) != 4 * step:
        return butterfly_sum(x, axis, step)
    near, far, across = [exchange(x, axis, k * step) for k in range(1, 4)]
    return (x + near) + (far + across)


def whole(x):
    return pl.BlockSpec(x.shape, lambda *_: (0,) * len(x.shape))


def dot_rows(a, b):
    return lax.dot_general(a, b, (((1,), (1,)), ((), ())), precision=HIGH, preferred_element_type=jnp.float32)


def unit_of(exponent, mantissa):
    return mantissa * jnp.exp2(exponent - 13.0)


def code_unit(top):
    top = jnp.maximum(top, 1e-28) * (1.0 / TOP)
    exponent = jnp.floor(jnp.log2(top))
    return exponent, jnp.floor(top * jnp.exp2(13.0 - exponent)) + 1.0


def whole_number(x):
    return x.astype(jnp.int32).astype(jnp.int16)


def cut(value, group):
    step = 2.0 ** (16 // group)
    high = jnp.floor(value + 0.5)
    low = jnp.minimum(jnp.floor((value - high) * step + 0.5), 0.5 * step - 1.0)
    part = value.shape[0] // group
    packed = low[:part]
    for k in range(1, group):
        packed = packed * step + (low[part * k : part * (k + 1)] + 0.5 * step)
    return jnp.concatenate([whole_number(high), whole_number(packed)], axis=0)


def join(code, size, group):
    bits = 16 // group
    step = 2**bits
    low = code[:, size : size + size // group]
    shifts = [bits * k for k in reversed(range(group))]
    lows = [low >> shifts[0]] + [((low >> shift) & (step - 1)) - step // 2 for shift in shifts[1:]]
    low = jnp.concatenate(lows, axis=1).astype(jnp.float32)
    return code[:, :size].astype(jnp.float32) + low * (1.0 / step)


def set_head(head_ref, *rows):
    place = lax.broadcasted_iota(jnp.int32, head_ref.shape, 0)
    head = jnp.zeros(head_ref.shape, jnp.float32)
    for k, row in enumerate(rows):
        head = jnp.where(place == k, row, head)
    head_ref[...] = whole_number(head)


def code_basis(basis):
    value = basis.astype(jnp.float32)
    size = jnp.abs(value)
    normal = size >= 2.0**-126
    exponent = jnp.floor(jnp.log2(jnp.where(normal, size, 1.0)))
    code = 128.0 * (exponent + 126.0) + jnp.floor(128.0 * (size * jnp.exp2(-exponent)) + 0.5)
    return whole_number(jnp.where(normal, jnp.where(value < 0.0, code - 32768.0, code), 0.0))


def prepare_kernel(momentum_ref, grad_ref, basis_ref, basis_code_ref, code_ref, unit_ref, column_ref):
    rows, cols = momentum_ref.shape
    width = code_ref.shape[-1]
    spans = [slice(i, i + width) for i in range(0, cols, width)]
    combined = lambda span: momentum_ref[:, span] + grad_ref[:, span].astype(jnp.float32)
    top = functools.reduce(jnp.maximum, [jnp.abs(combined(span)) for span in spans])
    exponent, mantissa = code_unit(jnp.max(top, axis=1, keepdims=True))
    inverse = 1.0 / unit_of(exponent, mantissa)
    for k, span in enumerate(spans):
        code_ref[k] = cut(combined(span) * inverse, 4)
        basis_code_ref[:, span] = code_basis(basis_ref[:, span])
    step = pl.program_id(0)
    here = pl.ds(pl.multiple_of(step * rows, rows), rows)
    for k, column in enumerate((exponent, mantissa)):
        column_ref[k, here, :] = jnp.broadcast_to(column, (rows, column_ref.shape[2]))

    @pl.when(step == pl.num_programs(0) - 1)
    def _():
        for k in range(2):
            unit_ref[k : k + 1, :] = column_ref[k].T[:1]


def row_steps(basis):
    return 2 if basis.shape[0] % 32 == 0 else 1


def prepare(momentum, grad, basis, share):
    rows, cols = momentum.shape
    width = share if share % 128 == 0 else cols
    steps = row_steps(basis)
    wide = pl.BlockSpec((rows // steps, cols), lambda i: (i, 0))
    narrow = pl.BlockSpec((basis.shape[0] // steps, cols), lambda i: (i, 0))
    return pl.pallas_call(
        prepare_kernel,
        grid=(steps,),
        in_specs=[wide, wide, narrow],
        out_specs=[
            narrow,
            pl.BlockSpec((cols // width, rows // steps * 5 // 4, width), lambda i: (0, i, 0)),
            pl.BlockSpec((2, rows), lambda i: (0, 0)),
        ],
        out_shape=[
            jax.ShapeDtypeStruct(basis.shape, jnp.int16),
            jax.ShapeDtypeStruct((cols // width, rows * 5 // 4, width), jnp.int16),
            jax.ShapeDtypeStruct((2, rows), jnp.float32),
        ],
        scratch_shapes=[pltpu.VMEM((2, rows, 128), jnp.float32)],
        compiler_params=STREAM,
        cost_estimate=pl.CostEstimate(flops=10 * rows * cols, bytes_accessed=rows * cols * 8, transcendentals=0),
    )(momentum, grad, basis)


def project_kernel(momentum_ref, grad_ref, code_ref, out_ref):
    code = code_ref[...].astype(jnp.int32)
    power = jnp.exp2(((code >> 7) & 255).astype(jnp.float32) - 134.0)
    value = ((code & 127) | 128).astype(jnp.float32) * power
    basis = jnp.where(code < 0, -value, value).astype(jnp.bfloat16)
    combined = momentum_ref[...] + grad_ref[...].astype(jnp.float32)
    rows = combined.shape[0]
    part = lax.dot_general(
        jnp.concatenate(split_three(combined), axis=0),
        basis,
        (((1,), (1,)), ((), ())),
        preferred_element_type=jnp.float32,
    )
    part = part[:rows] + (part[rows : 2 * rows] + part[2 * rows :])

    @pl.when(pl.program_id(0) == 0)
    def _():
        out_ref[...] = part

    @pl.when(pl.program_id(0) > 0)
    def _():
        out_ref[...] += part


def project(momentum, grad, codes):
    rows, cols = momentum.shape
    rank = codes.shape[0]
    block = min(1024, cols)
    wide = pl.BlockSpec((rows, block), lambda i: (0, i))
    return pl.pallas_call(
        project_kernel,
        grid=(cols // block,),
        in_specs=[wide, wide, pl.BlockSpec((rank, block), lambda i: (0, i))],
        out_specs=pl.BlockSpec((rows, rank), lambda i: (0, 0)),
        out_shape=jax.ShapeDtypeStruct((rows, rank), jnp.float32),
        compiler_params=FLOW,
        cost_estimate=pl.CostEstimate(
            flops=4 * rows * cols * rank, bytes_accessed=rows * cols * 6 + rank * cols * 2, transcendentals=rank * cols
        ),
    )(momentum, grad, codes)


def pack_kernel(perm_ref, unit_ref, *refs):
    part_refs, out_ref = refs[:-1], refs[-1]
    rows, rank = part_refs[0].shape
    blocks = perm_ref.shape[0]
    size = rank // blocks
    stored = lax.broadcasted_iota(jnp.int32, (rank, rank), 0)
    target = jnp.zeros((rank, rank), jnp.int32)
    for s in range(blocks):
        target = jnp.where(stored // size == s, perm_ref[s] * size + stored % size, target)
    order = (target == lax.broadcasted_iota(jnp.int32, (rank, rank), 1)).astype(jnp.float32)
    parts = [ref[...] for ref in part_refs]
    while len(parts) > 1:
        parts = [parts[k] + parts[k + 1] for k in range(0, len(parts), 2)]
    total = jnp.dot(parts[0], order, precision=HIGH, preferred_element_type=jnp.float32)
    exponent, mantissa = code_unit(jnp.max(jnp.abs(total), axis=0, keepdims=True))
    coded = rows + rows // 2
    out_ref[:coded] = cut(total * (1.0 / unit_of(exponent, mantissa)), 2)
    units = jnp.concatenate([unit_ref[...], jnp.zeros((2, rank - rows), jnp.float32)], axis=1)
    set_head(out_ref.at[coded:], exponent, mantissa, units[:1], units[1:])


def pack(perm, units, parts):
    rows, rank = parts[0].shape
    return pl.pallas_call(
        pack_kernel,
        grid_spec=pltpu.PrefetchScalarGridSpec(
            num_scalar_prefetch=1,
            grid=(1,),
            in_specs=[whole(x) for x in (units, *parts)],
            out_specs=pl.BlockSpec((rows + rows // 2 + HEAD, rank), lambda *_: (0, 0)),
        ),
        out_shape=jax.ShapeDtypeStruct((rows + rows // 2 + HEAD, rank), jnp.int16),
        compiler_params=PARAMS,
        cost_estimate=pl.CostEstimate(flops=12 * rows * rank * rank, bytes_accessed=rank * rank * 4, transcendentals=0),
    )(perm, units, *parts)


def spread(row):
    return jnp.broadcast_to(row, (TILE, 2 * PANEL))


def panel_inverse(block, band):
    rows = lax.broadcasted_iota(jnp.int32, (PANEL, PANEL), 0)
    cols = lax.broadcasted_iota(jnp.int32, (PANEL, PANEL), 1)
    both = jnp.concatenate([block, (rows == cols).astype(jnp.float32)], axis=1)
    count = PANEL // TILE
    tiles = [both[TILE * i : TILE * (i + 1)] for i in range(count)]
    sub = lax.broadcasted_iota(jnp.int32, (TILE, 2 * PANEL), 0)
    row = lambda k, j: band[k, pl.ds(j, TILE, stride=0), :]
    done = []
    for k in range(count):
        columns = [
            [spread(tiles[i][:, TILE * k + j : TILE * k + j + 1]) for j in range(TILE)] for i in range(k, count)
        ]
        state = list(columns[0]) + [tiles[k]]
        for m, x in enumerate(state):
            band[m] = x
        final = jnp.zeros_like(tiles[k])
        for j in range(0, TILE, 2):
            first, second = sub == j, sub == j + 1
            a, b, c = row(j, j), row(j + 1, j), row(j + 1, j + 1)
            minor = a * c - b * b
            inverse = 1.0 / minor
            left, right, body = state[j], state[j + 1], state[TILE]
            ratio = 1.0 / a
            below = (body - b * ratio * row(TILE, j)) * lax.rsqrt(minor * ratio)
            final = jnp.where(first, body * lax.rsqrt(a), jnp.where(second, below, final))
            rests = {}
            for m in range(j + 2, TILE + 1):
                upper, lower = row(m, j), row(m, j + 1)
                upper, lower = c * upper - b * lower, a * lower - b * upper
                rests[m] = state[m] - (left * upper + right * lower) * inverse
                state[m] = jnp.where(first, upper * inverse, jnp.where(second, lower * inverse, rests[m]))
            for m, rest in rests.items():
                band[m] = rest
        done.append(final)
        band[TILE] = state[TILE]
        reduced = [row(TILE, j) for j in range(TILE)]
        for i in range(k + 1, count):
            terms = [columns[i - k][j] * reduced[j] for j in range(TILE)]
            while len(terms) > 1:
                terms = [terms[j] + terms[j + 1] for j in range(0, len(terms), 2)]
            tiles[i] = tiles[i] - terms[0]
    return jnp.concatenate(done, axis=0)[:, PANEL:]


def split_three(x):
    high, rest = x.astype(jnp.bfloat16), x
    rest = rest - high.astype(jnp.float32)
    middle = rest.astype(jnp.bfloat16)
    return high, middle, (rest - middle.astype(jnp.float32)).astype(jnp.bfloat16)


def short_dot(a, b):
    a1, a2, a3 = split_three(a)
    b1, b2, b3 = split_three(b)
    a = jnp.concatenate([a1, a1, a2, a2, a1, a3], axis=1)
    b = jnp.concatenate([b1, b2, b1, b2, b3, b1], axis=0)
    return jnp.dot(a, b, preferred_element_type=jnp.float32)


def lanes_up(x):
    return (x + 127) // 128 * 128


def inverse_factor(gram, out_ref, work, band):
    rank = gram.shape[0]
    rows = lax.broadcasted_iota(jnp.int32, (rank, rank), 0)
    cols = lax.broadcasted_iota(jnp.int32, (rank, rank), 1)
    diagonal = jnp.where(rows == cols, gram, 0.0)
    scale = lax.rsqrt(jnp.sum(diagonal, axis=0, keepdims=True))
    work[:, :rank] = gram * scale * lax.rsqrt(jnp.sum(diagonal, axis=1, keepdims=True))
    work[:, rank:] = (rows == cols).astype(jnp.float32)
    block = work[:PANEL, :PANEL]
    for start in range(0, rank, PANEL):
        end = start + PANEL
        left, right = start // 128 * 128, rank + lanes_up(end)
        inverse = panel_inverse(block, band)
        if end < rank:
            after = slice(end, end + PANEL)
            ahead = short_dot(inverse, work[start:end, after])
            block = work[after, after] - short_dot(ahead.T, ahead)
        scaled = short_dot(inverse, work[start:end, left:right])
        out_ref[start:end, : lanes_up(end)] = scaled[:, rank - left :] * scale[:, : lanes_up(end)]
        if lanes_up(end) < rank:
            out_ref[start:end, lanes_up(end) :] = jnp.zeros((PANEL, rank - lanes_up(end)), jnp.float32)
        if end < rank:
            low = end // 128 * 128
            change = short_dot(scaled[:, low - left : rank - left].T, scaled[:, low - left :])
            work[end:, low:right] = work[end:, low:right] - change[end - low :, :]


def factor_kernel(code_ref, turned_ref, out_ref, gram_ref, mixed_ref, work, band):
    count, size, rank = code_ref.shape
    size = (size - HEAD) * 2 // 3
    code = code_ref[...].astype(jnp.int32)
    head = code[:, size + size // 2 :].astype(jnp.float32)
    part = join(code, size, 2) * unit_of(head[:, :1], head[:, 1:2])
    turned = part.reshape(count * size, rank).T
    turned_ref[...] = turned

    def times(a, b):
        a, b = jnp.concatenate(a, axis=1), jnp.concatenate(b, axis=1)
        return lax.dot_general(a, b, (((1,), (1,)), ((), ())), preferred_element_type=jnp.float32)

    high, middle, small = split_three(turned)
    even, mixed = times((high, middle), (high, middle)), times((high, high), (middle, small))

    @pl.when(pl.program_id(0) == 0)
    def _():
        gram_ref[...] = even
        mixed_ref[...] = mixed

    @pl.when(pl.program_id(0) > 0)
    def _():
        gram_ref[...] += even
        mixed_ref[...] += mixed

    @pl.when(pl.program_id(0) == pl.num_programs(0) - 1)
    def _():
        mixed = mixed_ref[...]
        inverse_factor(gram_ref[...] + (mixed + mixed.T), out_ref, work, band)


def factor(codes):
    devices, size, rank = codes.shape
    rows = (size - HEAD) * 2 // 3
    group = min(devices, max(1, 1024 // rows))
    return pl.pallas_call(
        factor_kernel,
        grid=(devices // group,),
        in_specs=[pl.BlockSpec((group, size, rank), lambda i: (i, 0, 0))],
        out_specs=[pl.BlockSpec((rank, group * rows), lambda i: (0, i)), pl.BlockSpec((rank, rank), lambda i: (0, 0))],
        out_shape=[
            jax.ShapeDtypeStruct((rank, devices * rows), jnp.float32),
            jax.ShapeDtypeStruct((rank, rank), jnp.float32),
        ],
        scratch_shapes=[
            pltpu.VMEM((rank, rank), jnp.float32),
            pltpu.VMEM((rank, rank), jnp.float32),
            pltpu.VMEM((rank, 2 * rank), jnp.float32),
            pltpu.VMEM((TILE + 1, TILE, 2 * PANEL), jnp.float32),
        ],
        compiler_params=PARAMS,
        cost_estimate=pl.CostEstimate(
            flops=12 * devices * rows * rank * rank, bytes_accessed=devices * size * rank * 4, transcendentals=rank
        ),
    )(codes)


def encode_kernel(chunk, place_ref, source_ref, turned_ref, head_ref, inverse_ref, own_ref, code_ref, ortho_ref, mixed_ref):
    def times(a, b):
        return jnp.dot(a, b, preferred_element_type=jnp.float32)

    def turned_dot(a, b):
        return lax.dot_general(a, b, (((0,), (1,)), ((), ())), precision=HIGH, preferred_element_type=jnp.float32)

    rank = turned_ref.shape[0]
    code = source_ref[...].astype(jnp.int32)
    share = code.shape[1]
    source_high, source_low = halves(join(code.reshape(-1, chunk * 5 // 4, share), chunk, 4).reshape(-1, share))
    head = head_ref[...].astype(jnp.int32).astype(jnp.float32)
    devices = head.shape[0]
    rows = turned_ref.shape[1] // devices
    unit = jnp.concatenate([unit_of(head[k, 2:3, :rows], head[k, 3:4, :rows]) for k in range(devices)], axis=1)
    scaled = split_three(turned_ref[...] * unit)
    most = times(jnp.concatenate(scaled, axis=0), source_high)
    less = times(jnp.concatenate(scaled[:2], axis=0), source_low)
    part = most[:rank] + (most[rank : 2 * rank] + less[:rank] + (most[2 * rank :] + less[rank:]))
    first, last = pl.program_id(0) == 0, pl.program_id(0) == pl.num_programs(0) - 1

    @pl.when(first)
    def _():
        mixed_ref[...] = part

    @pl.when(jnp.logical_not(first))
    def _():
        mixed_ref[...] += part

    @pl.when(last)
    def _():
        inverse = inverse_ref[...]
        ortho_ref[...] = turned_dot(own_ref[...], inverse)
        right = turned_dot(mixed_ref[...], inverse)
        rows = right.shape[0]
        square = jnp.maximum(jnp.sum(right * right, axis=0, keepdims=True), 1e-34)
        square_exponent = jnp.floor(jnp.log2(square))
        fine = square * jnp.exp2(13.0 - square_exponent)
        square_high = jnp.floor(fine)
        square_low = jnp.floor((fine - square_high) * 16384.0)
        exponent, mantissa = code_unit(jnp.max(jnp.abs(right), axis=0, keepdims=True))
        code_ref[:rows] = whole_number(jnp.floor(right * (1.0 / unit_of(exponent, mantissa)) + 0.5))
        set_head(code_ref.at[rows:], exponent, mantissa, square_exponent, square_high, square_low)


def encode(place, source, turned, packed, inverse_low, rows, chunk):
    share = source.shape[1]
    rank, total = turned.shape
    block = min(1024, total)
    size = packed.shape[1]
    return pl.pallas_call(
        functools.partial(encode_kernel, chunk),
        grid_spec=pltpu.PrefetchScalarGridSpec(
            num_scalar_prefetch=1,
            grid=(total // block,),
            in_specs=[
                pl.BlockSpec((block * 5 // 4, share), lambda i, place: (i, 0)),
                pl.BlockSpec((rank, block), lambda i, place: (0, i)),
                pl.BlockSpec((block // rows, HEAD, rank), lambda i, place: (i, size // HEAD - 1, 0)),
                whole(inverse_low),
                pl.BlockSpec((rank, rows), lambda i, place: (0, place[0])),
            ],
            out_specs=[
                pl.BlockSpec((share + HEAD, rank), lambda i, place: (0, 0)),
                pl.BlockSpec((rows, rank), lambda i, place: (0, 0)),
            ],
            scratch_shapes=[pltpu.VMEM((rank, share), jnp.float32)],
        ),
        out_shape=[
            jax.ShapeDtypeStruct((share + HEAD, rank), jnp.int16),
            jax.ShapeDtypeStruct((rows, rank), jnp.float32),
        ],
        compiler_params=PARAMS,
        cost_estimate=pl.CostEstimate(
            flops=6 * total * share * rank, bytes_accessed=total * (share * 2 + rank * 4), transcendentals=0
        ),
    )(place, source, turned, packed, inverse_low, turned)


def decode(code_ref):
    code = code_ref[...].astype(jnp.int32).astype(jnp.float32)
    share = code.shape[1] - HEAD
    right = code[:, :share] * unit_of(code[:, share : share + 1], code[:, share + 1 : share + 2])
    return right.reshape(code.shape[0] * share, code.shape[2])


def times_rows(split_ref, right):
    def times(a, b):
        return lax.dot_general(a, b, (((1,), (1,)), ((), ())), preferred_element_type=jnp.float32)

    right_high, right_low = halves(right)
    split = split_ref[...]
    rows = split.shape[0] // 2
    most = times(split, right_high)
    return most[:rows] + (most[rows:] + times(split[:rows], right_low))


def finish_kernel(
    gain, momentum_ref, grad_ref, code_ref, ortho_ref, scale_ref, next_ref, basis_ref, update_ref, split_ref
):
    rows = momentum_ref.shape[0]
    scale = scale_ref[...]

    @pl.when(pl.program_id(0) == 0)
    def _():
        ortho = ortho_ref[...]
        for k, factor in enumerate((-KEEP_SHARE * ortho, gain * ortho * scale)):
            high, low = halves(factor)
            split_ref[rows * k : rows * (k + 1)] = high
            split_ref[rows * (k + 2) : rows * (k + 3)] = low

    right = decode(code_ref)
    basis_ref[...] = right * scale
    both = times_rows(split_ref, right)
    next_ref[...] = momentum_ref[...] + grad_ref[...].astype(jnp.float32) + both[:rows]
    update_ref[...] = both[rows:].astype(jnp.bfloat16)


def finish(momentum, grad, codes, orthonormal, scale, gain):
    rows, cols = momentum.shape
    shares, share, rank = codes.shape
    share -= HEAD
    group = max(1, min(1024 // share, shares))
    block = group * share
    wide = pl.BlockSpec((rows, block), lambda i: (0, i))
    tall = pl.BlockSpec((block, rank), lambda i: (i, 0))
    coded = pl.BlockSpec((group, share + HEAD, rank), lambda i: (i, 0, 0))
    return pl.pallas_call(
        functools.partial(finish_kernel, gain),
        grid=(cols // block,),
        in_specs=[wide, wide, coded, whole(orthonormal), whole(scale)],
        out_specs=[wide, tall, wide],
        out_shape=[
            jax.ShapeDtypeStruct((rows, cols), jnp.float32),
            jax.ShapeDtypeStruct((cols, rank), jnp.float32),
            jax.ShapeDtypeStruct((rows, cols), jnp.bfloat16),
        ],
        scratch_shapes=[pltpu.VMEM((4 * rows, rank), jnp.bfloat16)],
        compiler_params=PARAMS,
        cost_estimate=pl.CostEstimate(
            flops=12 * rows * cols * rank, bytes_accessed=rows * cols * 12 + cols * rank * 6, transcendentals=0
        ),
    )(momentum, grad, codes, orthonormal, scale)


def on_device(momentum, grad, q_stored, perm):
    block_rows = q_stored.shape[0]
    num_blocks = lax.axis_size("fsdp")
    num_cols = lax.axis_size("tp")
    rank_total = block_rows * num_blocks
    rows, cols = momentum.shape
    row_total, col_total = rows * num_blocks, cols * num_cols
    share = cols // num_blocks

    basis, codes, units = prepare(momentum, grad, q_stored, share)
    coded = rows * 5 // 4
    codes = codes.reshape(-1, coded, codes.shape[2] // share, share).swapaxes(1, 2).reshape(num_blocks, coded, share)
    basis = lax.all_gather(basis, "fsdp", axis=0, tiled=True)
    codes, basis = lax.optimization_barrier((codes, basis))
    codes = lax.all_to_all(codes, "fsdp", split_axis=0, concat_axis=0).reshape(num_blocks * coded, share)

    near, step = project(momentum, grad, basis), 1
    while 4 * step < num_cols:
        near = near + exchange(near, "tp", step)
        step *= 2
    parts = [near] + [exchange(near, "tp", k) for k in range(step, num_cols, step)]
    packed = lax.all_gather(pack(perm, units, parts), "fsdp", axis=0)
    packed, codes = lax.optimization_barrier((packed, codes))
    turned, inverse_low = factor(packed)
    chunk = rows // row_steps(q_stored)
    code, orthonormal = encode(lax.axis_index("fsdp").reshape(1), codes, turned, packed, inverse_low, rows, chunk)
    gathered = lax.all_gather(code, "fsdp", axis=0)
    head = gathered[:, share : share + 5].astype(jnp.float32)
    parts = (head[:, 3] + head[:, 4] * (1.0 / 16384.0)) * jnp.exp2(head[:, 2] - 13.0)
    squares = quad_sum(jnp.sum(parts, axis=0, keepdims=True), "tp")
    scale = lax.rsqrt(squares / col_total + EPSILON)
    return tuple(finish(momentum, grad, gathered, orthonormal, scale, math.sqrt(row_total / rank_total)))


def solution(mesh):
    return jax.shard_map(
        on_device,
        mesh=mesh,
        in_specs=(P("fsdp", "tp"), P("fsdp", "tp"), P("fsdp", "tp"), P()),
        out_specs=(P("fsdp", "tp"), P("tp", None), P("fsdp", "tp")),
        check_vma=False,
    )
```

```python
import functools
import math

import jax
import jax.numpy as jnp
from jax import lax
from jax.experimental import pallas as pl
from jax.experimental.pallas import tpu as pltpu
from jax.sharding import PartitionSpec as P

EPSILON = 1e-06
KEEP_SHARE = 0.5
HIGH = lax.Precision.HIGHEST
PANEL = 64
TILE = 16
HEAD = 16
TOP = 32766.0
PARAMS = pltpu.CompilerParams(vmem_limit_bytes=40 * 1024 * 1024)
FLOW = pltpu.CompilerParams(vmem_limit_bytes=53 * 1024 * 1024)
STREAM = pltpu.CompilerParams(vmem_limit_bytes=54 * 1024 * 1024)


def halves(x):
    high = x.astype(jnp.bfloat16)
    return high, (x - high.astype(jnp.float32)).astype(jnp.bfloat16)


def exchange(x, axis, k):
    return lax.ppermute(x, axis, [(i, i ^ k) for i in range(lax.axis_size(axis))])


def butterfly_sum(x, axis, step=1):
    while step < lax.axis_size(axis):
        x = x + exchange(x, axis, step)
        step *= 2
    return x


def quad_sum(x, axis, step=1):
    if lax.axis_size(axis) != 4 * step:
        return butterfly_sum(x, axis, step)
    near, far, across = [exchange(x, axis, k * step) for k in range(1, 4)]
    return (x + near) + (far + across)


def whole(x):
    return pl.BlockSpec(x.shape, lambda *_: (0,) * len(x.shape))


def dot_rows(a, b):
    return lax.dot_general(a, b, (((1,), (1,)), ((), ())), precision=HIGH, preferred_element_type=jnp.float32)


def unit_of(exponent, mantissa):
    return mantissa * jnp.exp2(exponent - 13.0)


def code_unit(top):
    top = jnp.maximum(top, 1e-28) * (1.0 / TOP)
    exponent = jnp.floor(jnp.log2(top))
    return exponent, jnp.floor(top * jnp.exp2(13.0 - exponent)) + 1.0


def whole_number(x):
    return x.astype(jnp.int32).astype(jnp.int16)


def cut(value, group):
    step = 2.0 ** (16 // group)
    high = jnp.floor(value + 0.5)
    low = jnp.minimum(jnp.floor((value - high) * step + 0.5), 0.5 * step - 1.0)
    part = value.shape[0] // group
    packed = low[:part]
    for k in range(1, group):
        packed = packed * step + (low[part * k : part * (k + 1)] + 0.5 * step)
    return whole_number(high), whole_number(packed)


def join(high, low, group):
    bits = 16 // group
    step = 2**bits
    shifts = [bits * k for k in reversed(range(group))]
    lows = [low >> shifts[0]] + [((low >> shift) & (step - 1)) - step // 2 for shift in shifts[1:]]
    low = jnp.concatenate(lows, axis=1).astype(jnp.float32)
    return high.astype(jnp.float32) + low * (1.0 / step)


def set_head(head_ref, *rows):
    place = lax.broadcasted_iota(jnp.int32, head_ref.shape, 0)
    head = jnp.zeros(head_ref.shape, jnp.float32)
    for k, row in enumerate(rows):
        head = jnp.where(place == k, row, head)
    head_ref[...] = whole_number(head)


def code_basis(basis):
    value = basis.astype(jnp.float32)
    size = jnp.abs(value)
    normal = size >= 2.0**-126
    exponent = jnp.floor(jnp.log2(jnp.where(normal, size, 1.0)))
    code = 128.0 * (exponent + 126.0) + jnp.floor(128.0 * (size * jnp.exp2(-exponent)) + 0.5)
    return whole_number(jnp.where(normal, jnp.where(value < 0.0, code - 32768.0, code), 0.0))


def prepare_kernel(momentum_ref, grad_ref, basis_ref, basis_code_ref, code_ref, low_ref, unit_ref, column_ref):
    rows, cols = momentum_ref.shape
    width = code_ref.shape[-1]
    spans = [slice(i, i + width) for i in range(0, cols, width)]
    combined = lambda span: momentum_ref[:, span] + grad_ref[:, span].astype(jnp.float32)
    top = functools.reduce(jnp.maximum, [jnp.abs(combined(span)) for span in spans])
    exponent, mantissa = code_unit(jnp.max(top, axis=1, keepdims=True))
    inverse = 1.0 / unit_of(exponent, mantissa)
    for k, span in enumerate(spans):
        code_ref[k], low_ref[k] = cut(combined(span) * inverse, 4)
        basis_code_ref[:, span] = code_basis(basis_ref[:, span])
    step = pl.program_id(0)
    here = pl.ds(pl.multiple_of(step * rows, rows), rows)
    for k, column in enumerate((exponent, mantissa)):
        column_ref[k, here, :] = jnp.broadcast_to(column, (rows, column_ref.shape[2]))

    @pl.when(step == pl.num_programs(0) - 1)
    def _():
        for k in range(2):
            unit_ref[k : k + 1, :] = column_ref[k].T[:1]


def row_steps(basis):
    return 2 if basis.shape[0] % 32 == 0 else 1


def prepare(momentum, grad, basis, share):
    rows, cols = momentum.shape
    width = share if share % 128 == 0 else cols
    steps = row_steps(basis)
    wide = pl.BlockSpec((rows // steps, cols), lambda i: (i, 0))
    narrow = pl.BlockSpec((basis.shape[0] // steps, cols), lambda i: (i, 0))
    return pl.pallas_call(
        prepare_kernel,
        grid=(steps,),
        in_specs=[wide, wide, narrow],
        out_specs=[
            narrow,
            pl.BlockSpec((cols // width, rows // steps, width), lambda i: (0, i, 0)),
            pl.BlockSpec((cols // width, rows // steps // 4, width), lambda i: (0, i, 0)),
            pl.BlockSpec((2, rows), lambda i: (0, 0)),
        ],
        out_shape=[
            jax.ShapeDtypeStruct(basis.shape, jnp.int16),
            jax.ShapeDtypeStruct((cols // width, rows, width), jnp.int16),
            jax.ShapeDtypeStruct((cols // width, rows // 4, width), jnp.int16),
            jax.ShapeDtypeStruct((2, rows), jnp.float32),
        ],
        scratch_shapes=[pltpu.VMEM((2, rows, 128), jnp.float32)],
        compiler_params=STREAM,
        cost_estimate=pl.CostEstimate(flops=10 * rows * cols, bytes_accessed=rows * cols * 8, transcendentals=0),
    )(momentum, grad, basis)


def project_kernel(momentum_ref, grad_ref, code_ref, out_ref):
    code = code_ref[...].astype(jnp.int32)
    power = jnp.exp2(((code >> 7) & 255).astype(jnp.float32) - 134.0)
    value = ((code & 127) | 128).astype(jnp.float32) * power
    basis = jnp.where(code < 0, -value, value).astype(jnp.bfloat16)
    combined = momentum_ref[...] + grad_ref[...].astype(jnp.float32)
    rows = combined.shape[0]
    part = lax.dot_general(
        jnp.concatenate(split_three(combined), axis=0),
        basis,
        (((1,), (1,)), ((), ())),
        preferred_element_type=jnp.float32,
    )
    part = part[:rows] + (part[rows : 2 * rows] + part[2 * rows :])

    @pl.when(pl.program_id(0) == 0)
    def _():
        out_ref[...] = part

    @pl.when(pl.program_id(0) > 0)
    def _():
        out_ref[...] += part


def project(momentum, grad, codes):
    rows, cols = momentum.shape
    rank = codes.shape[0]
    block = min(1024, cols)
    wide = pl.BlockSpec((rows, block), lambda i: (0, i))
    return pl.pallas_call(
        project_kernel,
        grid=(cols // block,),
        in_specs=[wide, wide, pl.BlockSpec((rank, block), lambda i: (0, i))],
        out_specs=pl.BlockSpec((rows, rank), lambda i: (0, 0)),
        out_shape=jax.ShapeDtypeStruct((rows, rank), jnp.float32),
        compiler_params=FLOW,
        cost_estimate=pl.CostEstimate(
            flops=4 * rows * cols * rank, bytes_accessed=rows * cols * 6 + rank * cols * 2, transcendentals=rank * cols
        ),
    )(momentum, grad, codes)


def pack_kernel(perm_ref, unit_ref, *refs):
    part_refs, out_ref = refs[:-1], refs[-1]
    rows, rank = part_refs[0].shape
    blocks = perm_ref.shape[0]
    size = rank // blocks
    stored = lax.broadcasted_iota(jnp.int32, (rank, rank), 0)
    target = jnp.zeros((rank, rank), jnp.int32)
    for s in range(blocks):
        target = jnp.where(stored // size == s, perm_ref[s] * size + stored % size, target)
    order = (target == lax.broadcasted_iota(jnp.int32, (rank, rank), 1)).astype(jnp.float32)
    parts = [ref[...] for ref in part_refs]
    while len(parts) > 1:
        parts = [parts[k] + parts[k + 1] for k in range(0, len(parts), 2)]
    total = jnp.dot(parts[0], order, precision=HIGH, preferred_element_type=jnp.float32)
    exponent, mantissa = code_unit(jnp.max(jnp.abs(total), axis=0, keepdims=True))
    coded = rows + rows // 2
    out_ref[:rows], out_ref[rows:coded] = cut(total * (1.0 / unit_of(exponent, mantissa)), 2)
    units = jnp.concatenate([unit_ref[...], jnp.zeros((2, rank - rows), jnp.float32)], axis=1)
    set_head(out_ref.at[coded:], exponent, mantissa, units[:1], units[1:])


def pack(perm, units, parts):
    rows, rank = parts[0].shape
    return pl.pallas_call(
        pack_kernel,
        grid_spec=pltpu.PrefetchScalarGridSpec(
            num_scalar_prefetch=1,
            grid=(1,),
            in_specs=[whole(x) for x in (units, *parts)],
            out_specs=pl.BlockSpec((rows + rows // 2 + HEAD, rank), lambda *_: (0, 0)),
        ),
        out_shape=jax.ShapeDtypeStruct((rows + rows // 2 + HEAD, rank), jnp.int16),
        compiler_params=PARAMS,
        cost_estimate=pl.CostEstimate(flops=12 * rows * rank * rank, bytes_accessed=rank * rank * 4, transcendentals=0),
    )(perm, units, *parts)


def spread(row):
    return jnp.broadcast_to(row, (TILE, 2 * PANEL))


def panel_inverse(block, band):
    rows = lax.broadcasted_iota(jnp.int32, (PANEL, PANEL), 0)
    cols = lax.broadcasted_iota(jnp.int32, (PANEL, PANEL), 1)
    both = jnp.concatenate([block, (rows == cols).astype(jnp.float32)], axis=1)
    count = PANEL // TILE
    tiles = [both[TILE * i : TILE * (i + 1)] for i in range(count)]
    sub = lax.broadcasted_iota(jnp.int32, (TILE, 2 * PANEL), 0)
    row = lambda k, j: band[k, pl.ds(j, TILE, stride=0), :]
    done = []
    for k in range(count):
        columns = [
            [spread(tiles[i][:, TILE * k + j : TILE * k + j + 1]) for j in range(TILE)] for i in range(k, count)
        ]
        state = list(columns[0]) + [tiles[k]]
        for m, x in enumerate(state):
            band[m] = x
        final = jnp.zeros_like(tiles[k])
        for j in range(0, TILE, 2):
            first, second = sub == j, sub == j + 1
            a, b, c = row(j, j), row(j + 1, j), row(j + 1, j + 1)
            minor = a * c - b * b
            inverse = 1.0 / minor
            left, right, body = state[j], state[j + 1], state[TILE]
            ratio = 1.0 / a
            below = (body - b * ratio * row(TILE, j)) * lax.rsqrt(minor * ratio)
            final = jnp.where(first, body * lax.rsqrt(a), jnp.where(second, below, final))
            rests = {}
            for m in range(j + 2, TILE + 1):
                upper, lower = row(m, j), row(m, j + 1)
                upper, lower = c * upper - b * lower, a * lower - b * upper
                rests[m] = state[m] - (left * upper + right * lower) * inverse
                state[m] = jnp.where(first, upper * inverse, jnp.where(second, lower * inverse, rests[m]))
            for m, rest in rests.items():
                band[m] = rest
        done.append(final)
        band[TILE] = state[TILE]
        reduced = [row(TILE, j) for j in range(TILE)]
        for i in range(k + 1, count):
            terms = [columns[i - k][j] * reduced[j] for j in range(TILE)]
            while len(terms) > 1:
                terms = [terms[j] + terms[j + 1] for j in range(0, len(terms), 2)]
            tiles[i] = tiles[i] - terms[0]
    return jnp.concatenate(done, axis=0)[:, PANEL:]


def split_three(x):
    high, rest = x.astype(jnp.bfloat16), x
    rest = rest - high.astype(jnp.float32)
    middle = rest.astype(jnp.bfloat16)
    return high, middle, (rest - middle.astype(jnp.float32)).astype(jnp.bfloat16)


def short_dot(a, b):
    a1, a2, a3 = split_three(a)
    b1, b2, b3 = split_three(b)
    a = jnp.concatenate([a1, a1, a2, a2, a1, a3], axis=1)
    b = jnp.concatenate([b1, b2, b1, b2, b3, b1], axis=0)
    return jnp.dot(a, b, preferred_element_type=jnp.float32)


def lanes_up(x):
    return (x + 127) // 128 * 128


def inverse_factor(gram, out_ref, work, band):
    rank = gram.shape[0]
    rows = lax.broadcasted_iota(jnp.int32, (rank, rank), 0)
    cols = lax.broadcasted_iota(jnp.int32, (rank, rank), 1)
    diagonal = jnp.where(rows == cols, gram, 0.0)
    scale = lax.rsqrt(jnp.sum(diagonal, axis=0, keepdims=True))
    work[:, :rank] = gram * scale * lax.rsqrt(jnp.sum(diagonal, axis=1, keepdims=True))
    work[:, rank:] = (rows == cols).astype(jnp.float32)
    block = work[:PANEL, :PANEL]
    for start in range(0, rank, PANEL):
        end = start + PANEL
        left, right = start // 128 * 128, rank + lanes_up(end)
        inverse = panel_inverse(block, band)
        if end < rank:
            after = slice(end, end + PANEL)
            ahead = short_dot(inverse, work[start:end, after])
            block = work[after, after] - short_dot(ahead.T, ahead)
        scaled = short_dot(inverse, work[start:end, left:right])
        out_ref[start:end, : lanes_up(end)] = scaled[:, rank - left :] * scale[:, : lanes_up(end)]
        if lanes_up(end) < rank:
            out_ref[start:end, lanes_up(end) :] = jnp.zeros((PANEL, rank - lanes_up(end)), jnp.float32)
        if end < rank:
            low = end // 128 * 128
            change = short_dot(scaled[:, low - left : rank - left].T, scaled[:, low - left :])
            work[end:, low:right] = work[end:, low:right] - change[end - low :, :]


def factor_kernel(code_ref, turned_ref, out_ref, gram_ref, mixed_ref, work, band):
    count, size, rank = code_ref.shape
    size = (size - HEAD) * 2 // 3
    code = code_ref[...].astype(jnp.int32)
    head = code[:, size + size // 2 :].astype(jnp.float32)
    part = join(code[:, :size], code[:, size : size + size // 2], 2) * unit_of(head[:, :1], head[:, 1:2])
    turned = part.reshape(count * size, rank).T
    turned_ref[...] = turned

    def times(a, b):
        a, b = jnp.concatenate(a, axis=1), jnp.concatenate(b, axis=1)
        return lax.dot_general(a, b, (((1,), (1,)), ((), ())), preferred_element_type=jnp.float32)

    high, middle, small = split_three(turned)
    even, mixed = times((high, middle), (high, middle)), times((high, high), (middle, small))

    @pl.when(pl.program_id(0) == 0)
    def _():
        gram_ref[...] = even
        mixed_ref[...] = mixed

    @pl.when(pl.program_id(0) > 0)
    def _():
        gram_ref[...] += even
        mixed_ref[...] += mixed

    @pl.when(pl.program_id(0) == pl.num_programs(0) - 1)
    def _():
        mixed = mixed_ref[...]
        inverse_factor(gram_ref[...] + (mixed + mixed.T), out_ref, work, band)


def factor(codes):
    devices, size, rank = codes.shape
    rows = (size - HEAD) * 2 // 3
    group = min(devices, max(1, 1024 // rows))
    return pl.pallas_call(
        factor_kernel,
        grid=(devices // group,),
        in_specs=[pl.BlockSpec((group, size, rank), lambda i: (i, 0, 0))],
        out_specs=[pl.BlockSpec((rank, group * rows), lambda i: (0, i)), pl.BlockSpec((rank, rank), lambda i: (0, 0))],
        out_shape=[
            jax.ShapeDtypeStruct((rank, devices * rows), jnp.float32),
            jax.ShapeDtypeStruct((rank, rank), jnp.float32),
        ],
        scratch_shapes=[
            pltpu.VMEM((rank, rank), jnp.float32),
            pltpu.VMEM((rank, rank), jnp.float32),
            pltpu.VMEM((rank, 2 * rank), jnp.float32),
            pltpu.VMEM((TILE + 1, TILE, 2 * PANEL), jnp.float32),
        ],
        compiler_params=PARAMS,
        cost_estimate=pl.CostEstimate(
            flops=12 * devices * rows * rank * rank, bytes_accessed=devices * size * rank * 4, transcendentals=rank
        ),
    )(codes)


def encode_kernel(chunk, place_ref, source_ref, low_ref, turned_ref, head_ref, inverse_ref, own_ref, code_ref, ortho_ref, mixed_ref):
    def times(a, b):
        return jnp.dot(a, b, preferred_element_type=jnp.float32)

    def turned_dot(a, b):
        return lax.dot_general(a, b, (((0,), (1,)), ((), ())), precision=HIGH, preferred_element_type=jnp.float32)

    rank = turned_ref.shape[0]
    share = source_ref.shape[1]
    high, low = source_ref[...].astype(jnp.int32), low_ref[...].astype(jnp.int32)
    source = join(high.reshape(-1, chunk, share), low.reshape(-1, chunk // 4, share), 4)
    source_high, source_low = halves(source.reshape(-1, share))
    head = head_ref[...].astype(jnp.int32).astype(jnp.float32)
    devices = head.shape[0]
    rows = turned_ref.shape[1] // devices
    unit = jnp.concatenate([unit_of(head[k, 2:3, :rows], head[k, 3:4, :rows]) for k in range(devices)], axis=1)
    scaled = split_three(turned_ref[...] * unit)
    most = times(jnp.concatenate(scaled, axis=0), source_high)
    less = times(jnp.concatenate(scaled[:2], axis=0), source_low)
    part = most[:rank] + (most[rank : 2 * rank] + less[:rank] + (most[2 * rank :] + less[rank:]))
    first, last = pl.program_id(0) == 0, pl.program_id(0) == pl.num_programs(0) - 1

    @pl.when(first)
    def _():
        mixed_ref[...] = part

    @pl.when(jnp.logical_not(first))
    def _():
        mixed_ref[...] += part

    @pl.when(last)
    def _():
        inverse = inverse_ref[...]
        ortho_ref[...] = turned_dot(own_ref[...], inverse)
        right = turned_dot(mixed_ref[...], inverse)
        rows = right.shape[0]
        square = jnp.maximum(jnp.sum(right * right, axis=0, keepdims=True), 1e-34)
        square_exponent = jnp.floor(jnp.log2(square))
        fine = square * jnp.exp2(13.0 - square_exponent)
        square_high = jnp.floor(fine)
        square_low = jnp.floor((fine - square_high) * 16384.0)
        exponent, mantissa = code_unit(jnp.max(jnp.abs(right), axis=0, keepdims=True))
        code_ref[:rows] = whole_number(jnp.floor(right * (1.0 / unit_of(exponent, mantissa)) + 0.5))
        set_head(code_ref.at[rows:], exponent, mantissa, square_exponent, square_high, square_low)


def encode(place, source, low, turned, packed, inverse_low, rows, chunk):
    share = source.shape[1]
    rank, total = turned.shape
    block = min(1024, total)
    size = packed.shape[1]
    return pl.pallas_call(
        functools.partial(encode_kernel, chunk),
        grid_spec=pltpu.PrefetchScalarGridSpec(
            num_scalar_prefetch=1,
            grid=(total // block,),
            in_specs=[
                pl.BlockSpec((block, share), lambda i, place: (i, 0)),
                pl.BlockSpec((block // 4, share), lambda i, place: (i, 0)),
                pl.BlockSpec((rank, block), lambda i, place: (0, i)),
                pl.BlockSpec((block // rows, HEAD, rank), lambda i, place: (i, size // HEAD - 1, 0)),
                whole(inverse_low),
                pl.BlockSpec((rank, rows), lambda i, place: (0, place[0])),
            ],
            out_specs=[
                pl.BlockSpec((share + HEAD, rank), lambda i, place: (0, 0)),
                pl.BlockSpec((rows, rank), lambda i, place: (0, 0)),
            ],
            scratch_shapes=[pltpu.VMEM((rank, share), jnp.float32)],
        ),
        out_shape=[
            jax.ShapeDtypeStruct((share + HEAD, rank), jnp.int16),
            jax.ShapeDtypeStruct((rows, rank), jnp.float32),
        ],
        compiler_params=PARAMS,
        cost_estimate=pl.CostEstimate(
            flops=6 * total * share * rank, bytes_accessed=total * (share * 2 + rank * 4), transcendentals=0
        ),
    )(place, source, low, turned, packed, inverse_low, turned)


def decode(code_ref):
    code = code_ref[...].astype(jnp.int32).astype(jnp.float32)
    share = code.shape[1] - HEAD
    right = code[:, :share] * unit_of(code[:, share : share + 1], code[:, share + 1 : share + 2])
    return right.reshape(code.shape[0] * share, code.shape[2])


def times_rows(split_ref, right):
    def times(a, b):
        return lax.dot_general(a, b, (((1,), (1,)), ((), ())), preferred_element_type=jnp.float32)

    right_high, right_low = halves(right)
    split = split_ref[...]
    rows = split.shape[0] // 2
    most = times(split, right_high)
    return most[:rows] + (most[rows:] + times(split[:rows], right_low))


def finish_kernel(
    gain, momentum_ref, grad_ref, code_ref, ortho_ref, scale_ref, next_ref, basis_ref, update_ref, split_ref
):
    rows = momentum_ref.shape[0]
    scale = scale_ref[...]

    @pl.when(pl.program_id(0) == 0)
    def _():
        ortho = ortho_ref[...]
        for k, factor in enumerate((-KEEP_SHARE * ortho, gain * ortho * scale)):
            high, low = halves(factor)
            split_ref[rows * k : rows * (k + 1)] = high
            split_ref[rows * (k + 2) : rows * (k + 3)] = low

    right = decode(code_ref)
    basis_ref[...] = right * scale
    both = times_rows(split_ref, right)
    next_ref[...] = momentum_ref[...] + grad_ref[...].astype(jnp.float32) + both[:rows]
    update_ref[...] = both[rows:].astype(jnp.bfloat16)


def finish(momentum, grad, codes, orthonormal, scale, gain):
    rows, cols = momentum.shape
    shares, share, rank = codes.shape
    share -= HEAD
    group = max(1, min(1024 // share, shares))
    block = group * share
    wide = pl.BlockSpec((rows, block), lambda i: (0, i))
    tall = pl.BlockSpec((block, rank), lambda i: (i, 0))
    coded = pl.BlockSpec((group, share + HEAD, rank), lambda i: (i, 0, 0))
    return pl.pallas_call(
        functools.partial(finish_kernel, gain),
        grid=(cols // block,),
        in_specs=[wide, wide, coded, whole(orthonormal), whole(scale)],
        out_specs=[wide, tall, wide],
        out_shape=[
            jax.ShapeDtypeStruct((rows, cols), jnp.float32),
            jax.ShapeDtypeStruct((cols, rank), jnp.float32),
            jax.ShapeDtypeStruct((rows, cols), jnp.bfloat16),
        ],
        scratch_shapes=[pltpu.VMEM((4 * rows, rank), jnp.bfloat16)],
        compiler_params=PARAMS,
        cost_estimate=pl.CostEstimate(
            flops=12 * rows * cols * rank, bytes_accessed=rows * cols * 12 + cols * rank * 6, transcendentals=0
        ),
    )(momentum, grad, codes, orthonormal, scale)


def on_device(momentum, grad, q_stored, perm):
    block_rows = q_stored.shape[0]
    num_blocks = lax.axis_size("fsdp")
    num_cols = lax.axis_size("tp")
    rank_total = block_rows * num_blocks
    rows, cols = momentum.shape
    row_total, col_total = rows * num_blocks, cols * num_cols
    share = cols // num_blocks

    basis, codes, lows, units = prepare(momentum, grad, q_stored, share)

    def trade(x):
        x = x.reshape(-1, x.shape[1], x.shape[2] // share, share).swapaxes(1, 2).reshape(num_blocks, -1, share)
        return lax.all_to_all(x, "fsdp", split_axis=0, concat_axis=0).reshape(-1, share)

    basis = lax.all_gather(basis, "fsdp", axis=0, tiled=True)
    codes, basis = lax.optimization_barrier((codes, basis))
    codes = trade(codes)

    near, step = project(momentum, grad, basis), 1
    while 4 * step < num_cols:
        near = near + exchange(near, "tp", step)
        step *= 2
    parts = [near] + [exchange(near, "tp", k) for k in range(step, num_cols, step)]
    packed = lax.all_gather(pack(perm, units, parts), "fsdp", axis=0)
    packed, codes, lows = lax.optimization_barrier((packed, codes, lows))
    lows = trade(lows)
    turned, inverse_low = factor(packed)
    chunk = rows // row_steps(q_stored)
    code, orthonormal = encode(lax.axis_index("fsdp").reshape(1), codes, lows, turned, packed, inverse_low, rows, chunk)
    gathered = lax.all_gather(code, "fsdp", axis=0)
    head = gathered[:, share : share + 5].astype(jnp.float32)
    parts = (head[:, 3] + head[:, 4] * (1.0 / 16384.0)) * jnp.exp2(head[:, 2] - 13.0)
    squares = quad_sum(jnp.sum(parts, axis=0, keepdims=True), "tp")
    scale = lax.rsqrt(squares / col_total + EPSILON)
    return tuple(finish(momentum, grad, gathered, orthonormal, scale, math.sqrt(row_total / rank_total)))


def solution(mesh):
    return jax.shard_map(
        on_device,
        mesh=mesh,
        in_specs=(P("fsdp", "tp"), P("fsdp", "tp"), P("fsdp", "tp"), P()),
        out_specs=(P("fsdp", "tp"), P("tp", None), P("fsdp", "tp")),
        check_vma=False,
    )
```

```python
import functools
import math

import jax
import jax.numpy as jnp
from jax import lax
from jax.experimental import pallas as pl
from jax.experimental.pallas import tpu as pltpu
from jax.sharding import PartitionSpec as P

EPSILON = 1e-06
KEEP_SHARE = 0.5
HIGH = lax.Precision.HIGHEST
PANEL = 64
TILE = 16
HEAD = 16
TOP = 32766.0
PARAMS = pltpu.CompilerParams(vmem_limit_bytes=40 * 1024 * 1024)
FLOW = pltpu.CompilerParams(vmem_limit_bytes=53 * 1024 * 1024)
STREAM = pltpu.CompilerParams(vmem_limit_bytes=54 * 1024 * 1024)


def halves(x):
    high = x.astype(jnp.bfloat16)
    return high, (x - high.astype(jnp.float32)).astype(jnp.bfloat16)


def exchange(x, axis, k):
    return lax.ppermute(x, axis, [(i, i ^ k) for i in range(lax.axis_size(axis))])


def butterfly_sum(x, axis, step=1):
    while step < lax.axis_size(axis):
        x = x + exchange(x, axis, step)
        step *= 2
    return x


def quad_sum(x, axis, step=1):
    if lax.axis_size(axis) != 4 * step:
        return butterfly_sum(x, axis, step)
    near, far, across = [exchange(x, axis, k * step) for k in range(1, 4)]
    return (x + near) + (far + across)


def whole(x):
    return pl.BlockSpec(x.shape, lambda *_: (0,) * len(x.shape))


def dot_rows(a, b):
    return lax.dot_general(a, b, (((1,), (1,)), ((), ())), precision=HIGH, preferred_element_type=jnp.float32)


def unit_of(exponent, mantissa):
    return mantissa * jnp.exp2(exponent - 13.0)


def code_unit(top):
    top = jnp.maximum(top, 1e-28) * (1.0 / TOP)
    exponent = jnp.floor(jnp.log2(top))
    return exponent, jnp.floor(top * jnp.exp2(13.0 - exponent)) + 1.0


def whole_number(x):
    return x.astype(jnp.int32).astype(jnp.int16)


def cut(value, group):
    step = 2.0 ** (16 // group)
    high = jnp.floor(value + 0.5)
    low = jnp.minimum(jnp.floor((value - high) * step + 0.5), 0.5 * step - 1.0)
    part = value.shape[0] // group
    packed = low[:part]
    for k in range(1, group):
        packed = packed * step + (low[part * k : part * (k + 1)] + 0.5 * step)
    return whole_number(high), whole_number(packed)


def join(high, low, group):
    bits = 16 // group
    step = 2**bits
    shifts = [bits * k for k in reversed(range(group))]
    lows = [low >> shifts[0]] + [((low >> shift) & (step - 1)) - step // 2 for shift in shifts[1:]]
    low = jnp.concatenate(lows, axis=1).astype(jnp.float32)
    return high.astype(jnp.float32) + low * (1.0 / step)


def set_head(head_ref, *rows):
    place = lax.broadcasted_iota(jnp.int32, head_ref.shape, 0)
    head = jnp.zeros(head_ref.shape, jnp.float32)
    for k, row in enumerate(rows):
        head = jnp.where(place == k, row, head)
    head_ref[...] = whole_number(head)


def code_basis(basis):
    value = basis.astype(jnp.float32)
    size = jnp.abs(value)
    normal = size >= 2.0**-126
    exponent = jnp.floor(jnp.log2(jnp.where(normal, size, 1.0)))
    code = 128.0 * (exponent + 126.0) + jnp.floor(128.0 * (size * jnp.exp2(-exponent)) + 0.5)
    return whole_number(jnp.where(normal, jnp.where(value < 0.0, code - 32768.0, code), 0.0))


def prepare_kernel(momentum_ref, grad_ref, basis_ref, basis_code_ref, code_ref, low_ref, unit_ref, column_ref):
    rows, cols = momentum_ref.shape
    width = code_ref.shape[-1]
    spans = [slice(i, i + width) for i in range(0, cols, width)]
    combined = lambda span: momentum_ref[:, span] + grad_ref[:, span].astype(jnp.float32)
    top = functools.reduce(jnp.maximum, [jnp.abs(combined(span)) for span in spans])
    exponent, mantissa = code_unit(jnp.max(top, axis=1, keepdims=True))
    inverse = 1.0 / unit_of(exponent, mantissa)
    for k, span in enumerate(spans):
        code_ref[k], low_ref[k] = cut(combined(span) * inverse, 4)
        basis_code_ref[:, span] = code_basis(basis_ref[:, span])
    step = pl.program_id(0)
    here = pl.ds(pl.multiple_of(step * rows, rows), rows)
    for k, column in enumerate((exponent, mantissa)):
        column_ref[k, here, :] = jnp.broadcast_to(column, (rows, column_ref.shape[2]))

    @pl.when(step == pl.num_programs(0) - 1)
    def _():
        for k in range(2):
            unit_ref[k : k + 1, :] = column_ref[k].T[:1]


def row_steps(basis):
    return 2 if basis.shape[0] % 32 == 0 else 1


def prepare(momentum, grad, basis, share):
    rows, cols = momentum.shape
    width = share if share % 128 == 0 else cols
    steps = row_steps(basis)
    wide = pl.BlockSpec((rows // steps, cols), lambda i: (i, 0))
    narrow = pl.BlockSpec((basis.shape[0] // steps, cols), lambda i: (i, 0))
    return pl.pallas_call(
        prepare_kernel,
        grid=(steps,),
        in_specs=[wide, wide, narrow],
        out_specs=[
            narrow,
            pl.BlockSpec((cols // width, rows // steps, width), lambda i: (0, i, 0)),
            pl.BlockSpec((cols // width, rows // steps // 4, width), lambda i: (0, i, 0)),
            pl.BlockSpec((2, rows), lambda i: (0, 0)),
        ],
        out_shape=[
            jax.ShapeDtypeStruct(basis.shape, jnp.int16),
            jax.ShapeDtypeStruct((cols // width, rows, width), jnp.int16),
            jax.ShapeDtypeStruct((cols // width, rows // 4, width), jnp.int16),
            jax.ShapeDtypeStruct((2, rows), jnp.float32),
        ],
        scratch_shapes=[pltpu.VMEM((2, rows, 128), jnp.float32)],
        compiler_params=STREAM,
        cost_estimate=pl.CostEstimate(flops=10 * rows * cols, bytes_accessed=rows * cols * 8, transcendentals=0),
    )(momentum, grad, basis)


def project_kernel(momentum_ref, grad_ref, code_ref, out_ref):
    code = code_ref[...].astype(jnp.int32)
    power = jnp.exp2(((code >> 7) & 255).astype(jnp.float32) - 134.0)
    value = ((code & 127) | 128).astype(jnp.float32) * power
    basis = jnp.where(code < 0, -value, value).astype(jnp.bfloat16)
    combined = momentum_ref[...] + grad_ref[...].astype(jnp.float32)
    rows = combined.shape[0]
    part = lax.dot_general(
        jnp.concatenate(split_three(combined), axis=0),
        basis,
        (((1,), (1,)), ((), ())),
        preferred_element_type=jnp.float32,
    )
    part = part[:rows] + (part[rows : 2 * rows] + part[2 * rows :])

    @pl.when(pl.program_id(0) == 0)
    def _():
        out_ref[...] = part

    @pl.when(pl.program_id(0) > 0)
    def _():
        out_ref[...] += part


def project(momentum, grad, codes):
    rows, cols = momentum.shape
    rank = codes.shape[0]
    block = min(1024, cols)
    wide = pl.BlockSpec((rows, block), lambda i: (0, i))
    return pl.pallas_call(
        project_kernel,
        grid=(cols // block,),
        in_specs=[wide, wide, pl.BlockSpec((rank, block), lambda i: (0, i))],
        out_specs=pl.BlockSpec((rows, rank), lambda i: (0, 0)),
        out_shape=jax.ShapeDtypeStruct((rows, rank), jnp.float32),
        compiler_params=FLOW,
        cost_estimate=pl.CostEstimate(
            flops=4 * rows * cols * rank, bytes_accessed=rows * cols * 6 + rank * cols * 2, transcendentals=rank * cols
        ),
    )(momentum, grad, codes)


def pack_kernel(perm_ref, unit_ref, *refs):
    part_refs, out_ref = refs[:-1], refs[-1]
    rows, rank = part_refs[0].shape
    blocks = perm_ref.shape[0]
    size = rank // blocks
    stored = lax.broadcasted_iota(jnp.int32, (rank, rank), 0)
    target = jnp.zeros((rank, rank), jnp.int32)
    for s in range(blocks):
        target = jnp.where(stored // size == s, perm_ref[s] * size + stored % size, target)
    order = (target == lax.broadcasted_iota(jnp.int32, (rank, rank), 1)).astype(jnp.float32)
    parts = [ref[...] for ref in part_refs]
    while len(parts) > 1:
        parts = [parts[k] + parts[k + 1] for k in range(0, len(parts), 2)]
    total = jnp.dot(parts[0], order, precision=HIGH, preferred_element_type=jnp.float32)
    exponent, mantissa = code_unit(jnp.max(jnp.abs(total), axis=0, keepdims=True))
    coded = rows + rows // 4
    out_ref[:rows], out_ref[rows:coded] = cut(total * (1.0 / unit_of(exponent, mantissa)), 4)
    units = jnp.concatenate([unit_ref[...], jnp.zeros((2, rank - rows), jnp.float32)], axis=1)
    set_head(out_ref.at[coded:], exponent, mantissa, units[:1], units[1:])


def pack(perm, units, parts):
    rows, rank = parts[0].shape
    return pl.pallas_call(
        pack_kernel,
        grid_spec=pltpu.PrefetchScalarGridSpec(
            num_scalar_prefetch=1,
            grid=(1,),
            in_specs=[whole(x) for x in (units, *parts)],
            out_specs=pl.BlockSpec((rows + rows // 4 + HEAD, rank), lambda *_: (0, 0)),
        ),
        out_shape=jax.ShapeDtypeStruct((rows + rows // 4 + HEAD, rank), jnp.int16),
        compiler_params=PARAMS,
        cost_estimate=pl.CostEstimate(flops=12 * rows * rank * rank, bytes_accessed=rank * rank * 4, transcendentals=0),
    )(perm, units, *parts)


def spread(row):
    return jnp.broadcast_to(row, (TILE, 2 * PANEL))


def panel_inverse(block, band):
    rows = lax.broadcasted_iota(jnp.int32, (PANEL, PANEL), 0)
    cols = lax.broadcasted_iota(jnp.int32, (PANEL, PANEL), 1)
    both = jnp.concatenate([block, (rows == cols).astype(jnp.float32)], axis=1)
    count = PANEL // TILE
    tiles = [both[TILE * i : TILE * (i + 1)] for i in range(count)]
    sub = lax.broadcasted_iota(jnp.int32, (TILE, 2 * PANEL), 0)
    row = lambda k, j: band[k, pl.ds(j, TILE, stride=0), :]
    done = []
    for k in range(count):
        columns = [
            [spread(tiles[i][:, TILE * k + j : TILE * k + j + 1]) for j in range(TILE)] for i in range(k, count)
        ]
        state = list(columns[0]) + [tiles[k]]
        for m, x in enumerate(state):
            band[m] = x
        final = jnp.zeros_like(tiles[k])
        for j in range(0, TILE, 2):
            first, second = sub == j, sub == j + 1
            a, b, c = row(j, j), row(j + 1, j), row(j + 1, j + 1)
            minor = a * c - b * b
            inverse = 1.0 / minor
            left, right, body = state[j], state[j + 1], state[TILE]
            ratio = 1.0 / a
            below = (body - b * ratio * row(TILE, j)) * lax.rsqrt(minor * ratio)
            final = jnp.where(first, body * lax.rsqrt(a), jnp.where(second, below, final))
            rests = {}
            for m in range(j + 2, TILE + 1):
                upper, lower = row(m, j), row(m, j + 1)
                upper, lower = c * upper - b * lower, a * lower - b * upper
                rests[m] = state[m] - (left * upper + right * lower) * inverse
                state[m] = jnp.where(first, upper * inverse, jnp.where(second, lower * inverse, rests[m]))
            for m, rest in rests.items():
                band[m] = rest
        done.append(final)
        band[TILE] = state[TILE]
        reduced = [row(TILE, j) for j in range(TILE)]
        for i in range(k + 1, count):
            terms = [columns[i - k][j] * reduced[j] for j in range(TILE)]
            while len(terms) > 1:
                terms = [terms[j] + terms[j + 1] for j in range(0, len(terms), 2)]
            tiles[i] = tiles[i] - terms[0]
    return jnp.concatenate(done, axis=0)[:, PANEL:]


def split_three(x):
    high, rest = x.astype(jnp.bfloat16), x
    rest = rest - high.astype(jnp.float32)
    middle = rest.astype(jnp.bfloat16)
    return high, middle, (rest - middle.astype(jnp.float32)).astype(jnp.bfloat16)


def short_dot(a, b):
    a1, a2, a3 = split_three(a)
    b1, b2, b3 = split_three(b)
    a = jnp.concatenate([a1, a1, a2, a2, a1, a3], axis=1)
    b = jnp.concatenate([b1, b2, b1, b2, b3, b1], axis=0)
    return jnp.dot(a, b, preferred_element_type=jnp.float32)


def lanes_up(x):
    return (x + 127) // 128 * 128


def inverse_factor(gram, out_ref, work, band):
    rank = gram.shape[0]
    rows = lax.broadcasted_iota(jnp.int32, (rank, rank), 0)
    cols = lax.broadcasted_iota(jnp.int32, (rank, rank), 1)
    diagonal = jnp.where(rows == cols, gram, 0.0)
    scale = lax.rsqrt(jnp.sum(diagonal, axis=0, keepdims=True))
    work[:, :rank] = gram * scale * lax.rsqrt(jnp.sum(diagonal, axis=1, keepdims=True))
    work[:, rank:] = (rows == cols).astype(jnp.float32)
    block = work[:PANEL, :PANEL]
    for start in range(0, rank, PANEL):
        end = start + PANEL
        left, right = start // 128 * 128, rank + lanes_up(end)
        inverse = panel_inverse(block, band)
        if end < rank:
            after = slice(end, end + PANEL)
            ahead = short_dot(inverse, work[start:end, after])
            block = work[after, after] - short_dot(ahead.T, ahead)
        scaled = short_dot(inverse, work[start:end, left:right])
        out_ref[start:end, : lanes_up(end)] = scaled[:, rank - left :] * scale[:, : lanes_up(end)]
        if lanes_up(end) < rank:
            out_ref[start:end, lanes_up(end) :] = jnp.zeros((PANEL, rank - lanes_up(end)), jnp.float32)
        if end < rank:
            low = end // 128 * 128
            change = short_dot(scaled[:, low - left : rank - left].T, scaled[:, low - left :])
            work[end:, low:right] = work[end:, low:right] - change[end - low :, :]


def factor_kernel(code_ref, turned_ref, out_ref, gram_ref, mixed_ref, work, band):
    count, size, rank = code_ref.shape
    size = (size - HEAD) * 4 // 5
    code = code_ref[...].astype(jnp.int32)
    head = code[:, size + size // 4 :].astype(jnp.float32)
    part = join(code[:, :size], code[:, size : size + size // 4], 4) * unit_of(head[:, :1], head[:, 1:2])
    turned = part.reshape(count * size, rank).T
    turned_ref[...] = turned

    def times(a, b):
        a, b = jnp.concatenate(a, axis=1), jnp.concatenate(b, axis=1)
        return lax.dot_general(a, b, (((1,), (1,)), ((), ())), preferred_element_type=jnp.float32)

    high, middle, small = split_three(turned)
    even, mixed = times((high, middle), (high, middle)), times((high, high), (middle, small))

    @pl.when(pl.program_id(0) == 0)
    def _():
        gram_ref[...] = even
        mixed_ref[...] = mixed

    @pl.when(pl.program_id(0) > 0)
    def _():
        gram_ref[...] += even
        mixed_ref[...] += mixed

    @pl.when(pl.program_id(0) == pl.num_programs(0) - 1)
    def _():
        mixed = mixed_ref[...]
        inverse_factor(gram_ref[...] + (mixed + mixed.T), out_ref, work, band)


def factor(codes):
    devices, size, rank = codes.shape
    rows = (size - HEAD) * 4 // 5
    group = min(devices, max(1, 1024 // rows))
    return pl.pallas_call(
        factor_kernel,
        grid=(devices // group,),
        in_specs=[pl.BlockSpec((group, size, rank), lambda i: (i, 0, 0))],
        out_specs=[pl.BlockSpec((rank, group * rows), lambda i: (0, i)), pl.BlockSpec((rank, rank), lambda i: (0, 0))],
        out_shape=[
            jax.ShapeDtypeStruct((rank, devices * rows), jnp.float32),
            jax.ShapeDtypeStruct((rank, rank), jnp.float32),
        ],
        scratch_shapes=[
            pltpu.VMEM((rank, rank), jnp.float32),
            pltpu.VMEM((rank, rank), jnp.float32),
            pltpu.VMEM((rank, 2 * rank), jnp.float32),
            pltpu.VMEM((TILE + 1, TILE, 2 * PANEL), jnp.float32),
        ],
        compiler_params=PARAMS,
        cost_estimate=pl.CostEstimate(
            flops=12 * devices * rows * rank * rank, bytes_accessed=devices * size * rank * 4, transcendentals=rank
        ),
    )(codes)


def encode_kernel(chunk, place_ref, source_ref, low_ref, turned_ref, head_ref, inverse_ref, own_ref, code_ref, ortho_ref, mixed_ref):
    def times(a, b):
        return jnp.dot(a, b, preferred_element_type=jnp.float32)

    def turned_dot(a, b):
        return lax.dot_general(a, b, (((0,), (1,)), ((), ())), precision=HIGH, preferred_element_type=jnp.float32)

    rank = turned_ref.shape[0]
    share = source_ref.shape[1]
    high, low = source_ref[...].astype(jnp.int32), low_ref[...].astype(jnp.int32)
    source = join(high.reshape(-1, chunk, share), low.reshape(-1, chunk // 4, share), 4)
    source_high, source_low = halves(source.reshape(-1, share))
    head = head_ref[...].astype(jnp.int32).astype(jnp.float32)
    devices = head.shape[0]
    rows = turned_ref.shape[1] // devices
    unit = jnp.concatenate([unit_of(head[k, 2:3, :rows], head[k, 3:4, :rows]) for k in range(devices)], axis=1)
    scaled = split_three(turned_ref[...] * unit)
    most = times(jnp.concatenate(scaled, axis=0), source_high)
    less = times(jnp.concatenate(scaled[:2], axis=0), source_low)
    part = most[:rank] + (most[rank : 2 * rank] + less[:rank] + (most[2 * rank :] + less[rank:]))
    first, last = pl.program_id(0) == 0, pl.program_id(0) == pl.num_programs(0) - 1

    @pl.when(first)
    def _():
        mixed_ref[...] = part

    @pl.when(jnp.logical_not(first))
    def _():
        mixed_ref[...] += part

    @pl.when(last)
    def _():
        inverse = inverse_ref[...]
        ortho_ref[...] = turned_dot(own_ref[...], inverse)
        right = turned_dot(mixed_ref[...], inverse)
        rows = right.shape[0]
        square = jnp.maximum(jnp.sum(right * right, axis=0, keepdims=True), 1e-34)
        square_exponent = jnp.floor(jnp.log2(square))
        fine = square * jnp.exp2(13.0 - square_exponent)
        square_high = jnp.floor(fine)
        square_low = jnp.floor((fine - square_high) * 16384.0)
        exponent, mantissa = code_unit(jnp.max(jnp.abs(right), axis=0, keepdims=True))
        code_ref[:rows] = whole_number(jnp.floor(right * (1.0 / unit_of(exponent, mantissa)) + 0.5))
        set_head(code_ref.at[rows:], exponent, mantissa, square_exponent, square_high, square_low)


def encode(place, source, low, turned, packed, inverse_low, rows, chunk):
    share = source.shape[1]
    rank, total = turned.shape
    block = min(1024, total)
    size = packed.shape[1]
    return pl.pallas_call(
        functools.partial(encode_kernel, chunk),
        grid_spec=pltpu.PrefetchScalarGridSpec(
            num_scalar_prefetch=1,
            grid=(total // block,),
            in_specs=[
                pl.BlockSpec((block, share), lambda i, place: (i, 0)),
                pl.BlockSpec((block // 4, share), lambda i, place: (i, 0)),
                pl.BlockSpec((rank, block), lambda i, place: (0, i)),
                pl.BlockSpec((block // rows, HEAD, rank), lambda i, place: (i, size // HEAD - 1, 0)),
                whole(inverse_low),
                pl.BlockSpec((rank, rows), lambda i, place: (0, place[0])),
            ],
            out_specs=[
                pl.BlockSpec((share + HEAD, rank), lambda i, place: (0, 0)),
                pl.BlockSpec((rows, rank), lambda i, place: (0, 0)),
            ],
            scratch_shapes=[pltpu.VMEM((rank, share), jnp.float32)],
        ),
        out_shape=[
            jax.ShapeDtypeStruct((share + HEAD, rank), jnp.int16),
            jax.ShapeDtypeStruct((rows, rank), jnp.float32),
        ],
        compiler_params=PARAMS,
        cost_estimate=pl.CostEstimate(
            flops=6 * total * share * rank, bytes_accessed=total * (share * 2 + rank * 4), transcendentals=0
        ),
    )(place, source, low, turned, packed, inverse_low, turned)


def decode(code_ref):
    code = code_ref[...].astype(jnp.int32).astype(jnp.float32)
    share = code.shape[1] - HEAD
    right = code[:, :share] * unit_of(code[:, share : share + 1], code[:, share + 1 : share + 2])
    return right.reshape(code.shape[0] * share, code.shape[2])


def times_rows(split_ref, right):
    def times(a, b):
        return lax.dot_general(a, b, (((1,), (1,)), ((), ())), preferred_element_type=jnp.float32)

    right_high, right_low = halves(right)
    split = split_ref[...]
    rows = split.shape[0] // 2
    most = times(split, right_high)
    return most[:rows] + (most[rows:] + times(split[:rows], right_low))


def finish_kernel(
    gain, momentum_ref, grad_ref, code_ref, ortho_ref, scale_ref, next_ref, basis_ref, update_ref, split_ref
):
    rows = momentum_ref.shape[0]
    scale = scale_ref[...]

    @pl.when(pl.program_id(0) == 0)
    def _():
        ortho = ortho_ref[...]
        for k, factor in enumerate((-KEEP_SHARE * ortho, gain * ortho * scale)):
            high, low = halves(factor)
            split_ref[rows * k : rows * (k + 1)] = high
            split_ref[rows * (k + 2) : rows * (k + 3)] = low

    right = decode(code_ref)
    basis_ref[...] = right * scale
    both = times_rows(split_ref, right)
    next_ref[...] = momentum_ref[...] + grad_ref[...].astype(jnp.float32) + both[:rows]
    update_ref[...] = both[rows:].astype(jnp.bfloat16)


def finish(momentum, grad, codes, orthonormal, scale, gain):
    rows, cols = momentum.shape
    shares, share, rank = codes.shape
    share -= HEAD
    group = max(1, min(2048 // share, shares))
    block = group * share
    wide = pl.BlockSpec((rows, block), lambda i: (0, i))
    tall = pl.BlockSpec((block, rank), lambda i: (i, 0))
    coded = pl.BlockSpec((group, share + HEAD, rank), lambda i: (i, 0, 0))
    return pl.pallas_call(
        functools.partial(finish_kernel, gain),
        grid=(cols // block,),
        in_specs=[wide, wide, coded, whole(orthonormal), whole(scale)],
        out_specs=[wide, tall, wide],
        out_shape=[
            jax.ShapeDtypeStruct((rows, cols), jnp.float32),
            jax.ShapeDtypeStruct((cols, rank), jnp.float32),
            jax.ShapeDtypeStruct((rows, cols), jnp.bfloat16),
        ],
        scratch_shapes=[pltpu.VMEM((4 * rows, rank), jnp.bfloat16)],
        compiler_params=PARAMS,
        cost_estimate=pl.CostEstimate(
            flops=12 * rows * cols * rank, bytes_accessed=rows * cols * 12 + cols * rank * 6, transcendentals=0
        ),
    )(momentum, grad, codes, orthonormal, scale)


def on_device(momentum, grad, q_stored, perm):
    block_rows = q_stored.shape[0]
    num_blocks = lax.axis_size("fsdp")
    num_cols = lax.axis_size("tp")
    rank_total = block_rows * num_blocks
    rows, cols = momentum.shape
    row_total, col_total = rows * num_blocks, cols * num_cols
    share = cols // num_blocks

    basis, codes, lows, units = prepare(momentum, grad, q_stored, share)

    def trade(x):
        x = x.reshape(-1, x.shape[1], x.shape[2] // share, share).swapaxes(1, 2).reshape(num_blocks, -1, share)
        return lax.all_to_all(x, "fsdp", split_axis=0, concat_axis=0).reshape(-1, share)

    basis = lax.all_gather(basis, "fsdp", axis=0, tiled=True)
    codes, basis = lax.optimization_barrier((codes, basis))
    codes = trade(codes)

    near, step = project(momentum, grad, basis), 1
    while 4 * step < num_cols:
        near = near + exchange(near, "tp", step)
        step *= 2
    parts = [near] + [exchange(near, "tp", k) for k in range(step, num_cols, step)]
    packed = lax.all_gather(pack(perm, units, parts), "fsdp", axis=0)
    packed, codes, lows = lax.optimization_barrier((packed, codes, lows))
    lows = trade(lows)
    turned, inverse_low = factor(packed)
    chunk = rows // row_steps(q_stored)
    code, orthonormal = encode(lax.axis_index("fsdp").reshape(1), codes, lows, turned, packed, inverse_low, rows, chunk)
    gathered = lax.all_gather(code, "fsdp", axis=0)
    head = gathered[:, share : share + 5].astype(jnp.float32)
    parts = (head[:, 3] + head[:, 4] * (1.0 / 16384.0)) * jnp.exp2(head[:, 2] - 13.0)
    squares = quad_sum(jnp.sum(parts, axis=0, keepdims=True), "tp")
    scale = lax.rsqrt(squares / col_total + EPSILON)
    return tuple(finish(momentum, grad, gathered, orthonormal, scale, math.sqrt(row_total / rank_total)))


def solution(mesh):
    return jax.shard_map(
        on_device,
        mesh=mesh,
        in_specs=(P("fsdp", "tp"), P("fsdp", "tp"), P("fsdp", "tp"), P()),
        out_specs=(P("fsdp", "tp"), P("tp", None), P("fsdp", "tp")),
        check_vma=False,
    )
```
